32 devices in a mesh: tok: 4 (over y, x), ch: 8 (over z, core).
Axes of the slice: x: 2, y: 2, z: 4, core: 2. Of those that a mesh axis runs over, the one named last changes fastest.
Arguments:
- block_input: bfloat16 [4096, 2048], P(('tok', 'ch')), may hold values from -6 to 6
- norm_gain: bfloat16 [2048], replicated, may hold values from 0.5 to 1.5
- in_weight: bfloat16 [3, 2048, 8192], P(None, None, 'ch'), may hold values from -0.125 to 0.125
- x_weight: bfloat16 [3, 160, 4096], P(None, None, 'ch'), may hold values from -0.09375 to 0.09375
- dt_weight: bfloat16 [3, 128, 4096], P(None, None, 'ch'), may hold values from -0.5 to 0.5
- dt_bias: bfloat16 [3, 4096], P(None, 'ch'), may hold values from -3 to 0
- conv_weight: bfloat16 [4, 4096], P(None, 'ch'), may hold values from -0.5 to 0.5
- conv_bias: bfloat16 [4096], P('ch'), may hold values from -0.5 to 0.5
- a_log: bfloat16 [16, 4096], P(None, 'ch'), may hold values from 0 to 2
- skip_gain: bfloat16 [4096], P('ch'), may hold values from 0.5 to 1.5
- out_weight: bfloat16 [3, 4096, 2048], P(None, 'ch'), may hold values from -0.75 to 0.75
- modality: int32 [4096], P(('tok', 'ch')), may hold values from 0 to 2
- cotangent: bfloat16 [4096, 2048], P(('tok', 'ch')), may hold values from -6 to 6
Outputs:
- block_out: bfloat16 [4096, 2048], P(('tok', 'ch'))
- input_grad: float32 [4096, 2048], P(('tok', 'ch'))
- gain_grad: float32 [2048], P('ch')
- in_weight_grad: float32 [3, 2048, 8192], P(None, None, 'ch')
- x_weight_grad: float32 [3, 160, 4096], P(None, None, 'ch')
- dt_weight_grad: float32 [3, 128, 4096], P(None, None, 'ch')
- dt_bias_grad: float32 [3, 4096], P(None, 'ch')
- conv_weight_grad: float32 [4, 4096], P(None, 'ch')
- conv_bias_grad: float32 [4096], P('ch')
- a_log_grad: float32 [16, 4096], P(None, 'ch')
- skip_gain_grad: float32 [4096], P('ch')
- out_weight_grad: float32 [3, 4096, 2048], P(None, 'ch')
The draws below stay inside these ranges and needn't reach their ends.
All inputs are finite; a program needn't handle non-finite values.
Results may differ from the reference program's by a relative error of at most 0.0096.
Values may be sent and summed in bfloat16 or wider, within the bound.
A program may use at most 448 MiB of HBM per device.

```python
import jax
import jax.numpy as jnp
from jax import lax

D = 2048
E = 4096
S = 16
R = 128
K = 4
MODS = 3
TOK_DEV = 128
TOKENS = 4096


def draw_modality(key, part):
    key = jax.random.fold_in(key, 7)
    lean_key, pick_key, other_key = jax.random.split(key, 3)
    sequences = TOKENS // TOK_DEV
    leaning = jax.random.randint(lean_key, (sequences, 1), 0, MODS)
    picks = jax.random.randint(pick_key, (sequences, TOK_DEV), 0, 8)
    others = jax.random.randint(other_key, (sequences, TOK_DEV), 0, MODS)
    return jnp.where(picks < 5, leaning, others).reshape(TOKENS).astype(jnp.int32)


def steps_of(rng, extent, shards, least, high):
    factor_of, own = 1.0, jax.random.fold_in(rng, 6)
    for axis_at, blocks in shards:
        steps = jnp.exp(jax.random.uniform(jax.random.fold_in(own, axis_at), (blocks,), jnp.float32, least / len(shards), high / len(shards)))
        factor_of = factor_of * jnp.repeat(steps, extent[axis_at] // blocks).reshape([-1 if axis == axis_at else 1 for axis in range(len(extent))])
    return factor_of


def bell_draw(own_key, dims, scale, reach, shards=(), held_as=jnp.bfloat16):
    entries = scale * jax.random.normal(own_key, dims, jnp.float32)
    if shards:
        entries = entries * steps_of(own_key, dims, shards, -0.22, 0.18)
    return jnp.clip(entries, -reach, reach).astype(held_as)


def setup_inputs(seed: int = 0) -> dict:
    arg_keys = jax.random.split(jax.random.key(seed), 14)
    block_input = bell_draw(arg_keys[0], (TOKENS, D), 1.0, 6.0, ((0, 32),))
    norm_gain = jnp.clip(1.0 + 0.1 * jax.random.normal(arg_keys[1], (D,), jnp.float32), 0.5, 1.5).astype(jnp.bfloat16)
    in_weight = bell_draw(arg_keys[2], (MODS, D, 2 * E), D ** -0.5, 0.125, ((2, 8),))
    x_weight = bell_draw(arg_keys[3], (MODS, R + 2 * S, E), E ** -0.5, 0.09375, ((2, 8),))
    dt_weight = bell_draw(arg_keys[4], (MODS, R, E), R ** -0.5, 0.5, ((2, 8),))
    dt_bias = jnp.clip(-3.0 + 3.0 * jax.random.uniform(arg_keys[5], (MODS, E), jnp.float32) ** steps_of(arg_keys[5], (MODS, E), ((1, 8),), -0.2, 0.2), -3.0, 0.0).astype(jnp.bfloat16)
    conv_weight = jnp.clip(jax.random.uniform(arg_keys[6], (K, E), jnp.float32, -0.5, 0.5) * steps_of(arg_keys[6], (K, E), ((1, 8),), -0.4, 0.0), -0.5, 0.5).astype(jnp.bfloat16)
    conv_bias = jnp.clip(jax.random.uniform(arg_keys[7], (E,), jnp.float32, -0.5, 0.5) * steps_of(arg_keys[7], (E,), ((0, 8),), -0.4, 0.0), -0.5, 0.5).astype(jnp.bfloat16)
    a_log = jnp.clip(2.0 * jax.random.uniform(arg_keys[8], (S, E), jnp.float32) ** steps_of(arg_keys[8], (S, E), ((1, 8),), -0.2, 0.2), 0.0, 2.0).astype(jnp.bfloat16)
    skip_gain = jnp.clip(0.5 + 1.0 * jax.random.uniform(arg_keys[9], (E,), jnp.float32) ** steps_of(arg_keys[9], (E,), ((0, 8),), -0.2, 0.2), 0.5, 1.5).astype(jnp.bfloat16)
    out_weight = bell_draw(arg_keys[10], (MODS, E, D), (E // 64) ** -0.5, 0.75, ((1, 8),))
    modality = draw_modality(jax.random.fold_in(arg_keys[13], 71), 0)
    cotangent = bell_draw(arg_keys[12], (TOKENS, D), 1.0, 6.0, ((0, 32),))
    return {"block_input": block_input, "norm_gain": norm_gain, "in_weight": in_weight, "x_weight": x_weight, "dt_weight": dt_weight, "dt_bias": dt_bias, "conv_weight": conv_weight, "conv_bias": conv_bias, "a_log": a_log, "skip_gain": skip_gain, "out_weight": out_weight, "modality": modality, "cotangent": cotangent}


@jax.custom_vjp
def low(v):
    return lax.optimization_barrier(v.astype(jnp.bfloat16)).astype(jnp.float32)

@jax.custom_vjp
def low_back(v):
    return v

def low_keep(v):
    return (low(v), None)

def low_pass(kept, grad):
    return (grad,)

def back_keep(v):
    return (v, None)

def back_low(kept, grad):
    return (low(grad),)
low.defvjp(low_keep, low_pass)
low_back.defvjp(back_keep, back_low)
highest = lax.Precision.HIGHEST

def mixer(xz_value, onehot, x_weight, dt_weight, dt_bias, conv_weight, conv_bias, a_log, skip_gain):
    channels = conv_weight.shape[1]
    tap_count = conv_weight.shape[0]
    length = xz_value.shape[0]
    inner_part = xz_value[:, :channels]
    gate_in = xz_value[:, channels:]
    padded = jnp.concatenate([jnp.zeros((tap_count - 1, channels), jnp.float32), inner_part], axis=0)
    convolved = conv_bias[None, :]
    for tap in range(tap_count):
        convolved = convolved + conv_weight[tap][None, :] * padded[tap:tap + length]
    active = jax.nn.silu(convolved)
    modalities = x_weight.shape[0]
    low_width = dt_weight.shape[1]
    states = a_log.shape[0]
    mixed = jnp.zeros((length, x_weight.shape[1]), jnp.float32)
    for index in range(modalities):
        mixed = mixed + onehot[:, index:index + 1] * jnp.dot(active, x_weight[index].T, precision=highest)
    low_rank = mixed[:, :low_width]
    b_part = mixed[:, low_width:low_width + states]
    c_part = mixed[:, low_width + states:]
    speed_pre = jnp.zeros((length, channels), jnp.float32)
    for index in range(modalities):
        speed_pre = speed_pre + onehot[:, index:index + 1] * (jnp.dot(low_rank, dt_weight[index], precision=highest) + dt_bias[index][None, :])
    step_size = jax.nn.softplus(speed_pre)
    decay_rates = -jnp.exp(a_log)

    def advance(carry_state, inputs):
        step_now, drive, b_row, c_row = inputs
        carry_state = jnp.exp(step_now[None, :] * decay_rates) * carry_state + b_row[:, None] * drive[None, :]
        return (carry_state, jnp.dot(c_row, carry_state, precision=highest))
    start_state = jnp.zeros((states, channels), jnp.float32)
    _, scanned = lax.scan(advance, start_state, (step_size, step_size * active, b_part, c_part))
    return (scanned + skip_gain[None, :] * active) * jax.nn.silu(gate_in)

def block(params, rows, onehot):
    gain, in_weight, x_weight, dt_weight, dt_bias, conv_weight, conv_bias, a_log, skip_gain, out_weight = params
    inverse = lax.rsqrt(lax.optimization_barrier(jnp.mean(rows * rows, axis=-1, keepdims=True)) + 1e-05)
    scaled = low(rows * inverse * gain[None, :])
    modalities = in_weight.shape[0]
    projected = jnp.zeros((rows.shape[0], in_weight.shape[2]), jnp.float32)
    for index in range(modalities):
        projected = projected + jnp.dot(scaled * onehot[:, index:index + 1], in_weight[index], precision=highest)
    xz_value = low(low_back(projected))
    count = rows.shape[0] // TOK_DEV
    mixed = jax.vmap(mixer, in_axes=(0, 0, None, None, None, None, None, None, None))(xz_value.reshape(count, TOK_DEV, -1), onehot.reshape(count, TOK_DEV, -1), x_weight, dt_weight, dt_bias, conv_weight, conv_bias, a_log, skip_gain)
    gated = low(low_back(mixed.reshape(rows.shape[0], -1)))
    branch = jnp.zeros(rows.shape, jnp.float32)
    for index in range(modalities):
        branch = branch + jnp.dot(gated * onehot[:, index:index + 1], out_weight[index], precision=highest)
    return rows + branch

def reference(block_input, norm_gain, in_weight, x_weight, dt_weight, dt_bias, conv_weight, conv_bias, a_log, skip_gain, out_weight, modality, cotangent):
    group = min(TOKENS, 4096 // TOK_DEV * TOK_DEV)
    groups = TOKENS // group
    params = tuple((value.astype(jnp.float32) for value in (norm_gain, in_weight, x_weight, dt_weight, dt_bias, conv_weight, conv_bias, a_log, skip_gain, out_weight)))
    onehot = (modality[:, None] == jnp.arange(MODS, dtype=jnp.int32)[None, :]).astype(jnp.float32)
    width = block_input.shape[1]

    def one_group(totals, inputs):
        rows, group_hot, group_cot = inputs
        result, pullback = jax.vjp(lambda values, given: block(values, given, group_hot), params, rows)
        grads, row_grad = pullback(group_cot)
        totals = jax.tree.map(jnp.add, totals, grads)
        return (totals, (result.astype(jnp.bfloat16), row_grad))
    zeros = jax.tree.map(jnp.zeros_like, params)
    totals, (outputs, row_grads) = lax.scan(one_group, zeros, (block_input.astype(jnp.float32).reshape(groups, group, width), onehot.reshape(groups, group, MODS), cotangent.astype(jnp.float32).reshape(groups, group, width)))
    return (outputs.reshape(TOKENS, width), row_grads.reshape(TOKENS, width), totals[0], totals[1], totals[2], totals[3], totals[4], totals[5], totals[6], totals[7], totals[8], totals[9])
```

```python
import functools
import math

import jax
import jax.numpy as jnp
from jax import lax
from jax.experimental import pallas as pl
from jax.experimental.pallas import tpu as pltpu
from jax.sharding import PartitionSpec as P

F32 = jnp.float32
BF16 = jnp.bfloat16
LOG2E = math.log2(math.e)
LN2 = math.log(2.0)
GROUP = 8
VMEM_LIMIT = 58 << 20


def params(**kw):
    return pltpu.CompilerParams(vmem_limit_bytes=VMEM_LIMIT, **kw)


def dot(a, b):
    return lax.dot_general(a, b, (((1,), (0,)), ((), ())), preferred_element_type=F32)


def dot_bt(a, b):
    return lax.dot_general(a, b, (((1,), (1,)), ((), ())), preferred_element_type=F32)


def dot_at(a, b):
    return lax.dot_general(a, b, (((0,), (0,)), ((), ())), preferred_element_type=F32)


def halves(x):
    high = x.astype(BF16)
    return high, (x - high.astype(F32)).astype(BF16)


def pick(parts, label):
    total = parts[-1]
    for index in range(len(parts) - 2, -1, -1):
        total = jnp.where(label == index, parts[index], total)
    return total


def sigmoid(x):
    return 1.0 / (1.0 + jnp.exp(-x))


def select_kernel(transposed, x_ref, label_ref, w_ref, out_ref):
    x = x_ref[...]
    label = label_ref[...]
    product = dot_bt if transposed else dot
    parts = [product(x, w_ref[m]) for m in range(w_ref.shape[0])]
    out_ref[...] = pick(parts, label).astype(out_ref.dtype)


def routed_select(x, label, w, tile, transposed):
    rows, depth = x.shape
    mods = w.shape[0]
    outer = w.shape[1] if transposed else w.shape[2]
    tile = min(tile, outer)
    block = min(rows, 1024)
    if transposed:
        w_spec = pl.BlockSpec((mods, tile, depth), lambda i, j: (0, j, 0))
    else:
        w_spec = pl.BlockSpec((mods, depth, tile), lambda i, j: (0, 0, j))
    return pl.pallas_call(
        functools.partial(select_kernel, transposed),
        out_shape=jax.ShapeDtypeStruct((rows, outer), BF16),
        grid=(rows // block, outer // tile),
        in_specs=[
            pl.BlockSpec((block, depth), lambda i, j: (i, 0)),
            pl.BlockSpec((block, 1), lambda i, j: (i, 0)),
            w_spec,
        ],
        out_specs=pl.BlockSpec((block, tile), lambda i, j: (i, j)),
        compiler_params=params(),
        cost_estimate=pl.CostEstimate(
            flops=2 * rows * depth * outer * mods, bytes_accessed=2 * mods * depth * outer + 2 * rows * (depth + outer), transcendentals=0
        ),
        name="routed_select",
    )(x, label, w)


def spread_kernel(transposed, x_ref, label_ref, w_ref, out_ref):
    x = x_ref[...]
    label = label_ref[...]
    product = dot_bt if transposed else dot
    total = None
    for m in range(w_ref.shape[0]):
        part = product(jnp.where(label == m, x, jnp.zeros_like(x)), w_ref[m])
        total = part if total is None else total + part
    out_ref[...] = total.astype(out_ref.dtype)


def routed_spread(x, label, w, tile, transposed, dtype):
    rows, depth = x.shape
    mods = w.shape[0]
    outer = w.shape[1] if transposed else w.shape[2]
    tile = min(tile, outer)
    block = min(rows, 1024)
    if transposed:
        w_spec = pl.BlockSpec((mods, tile, depth), lambda i, j: (0, j, 0))
    else:
        w_spec = pl.BlockSpec((mods, depth, tile), lambda i, j: (0, 0, j))
    return pl.pallas_call(
        functools.partial(spread_kernel, transposed),
        out_shape=jax.ShapeDtypeStruct((rows, outer), dtype),
        grid=(rows // block, outer // tile),
        in_specs=[
            pl.BlockSpec((block, depth), lambda i, j: (i, 0)),
            pl.BlockSpec((block, 1), lambda i, j: (i, 0)),
            w_spec,
        ],
        out_specs=pl.BlockSpec((block, tile), lambda i, j: (i, j)),
        compiler_params=params(),
        cost_estimate=pl.CostEstimate(
            flops=2 * rows * depth * outer * mods, bytes_accessed=2 * mods * depth * outer + 2 * rows * (depth + outer), transcendentals=0
        ),
        name="routed_spread",
    )(x, label, w)


def by_time(x):
    rows, width = x.shape
    return jnp.swapaxes(x.astype(F32).reshape(GROUP, rows // GROUP, width), 0, 1).reshape(rows, width)


def by_sequence(x):
    rows, width = x.shape
    return jnp.swapaxes(x.reshape(rows // GROUP, GROUP, width), 0, 1).reshape(rows, width)


def conv_kernel(inner_ref, label_ref, cw_ref, cb_ref, xw_ref, conv_ref, inner_out_ref, proj_ref, pad_ref):
    rows, channels = inner_ref.shape
    taps = cw_ref.shape[0]
    lead = (taps - 1) * GROUP
    inner = by_time(inner_ref[...])
    inner_out_ref[...] = inner.astype(BF16)
    pad_ref[pl.ds(0, lead), :] = jnp.zeros((lead, channels), F32)
    pad_ref[pl.ds(lead, rows), :] = inner
    conv = jnp.broadcast_to(cb_ref[...].astype(F32), (rows, channels))
    for tap in range(taps):
        conv = conv + cw_ref[pl.ds(tap, 1), :].astype(F32) * pad_ref[pl.ds(tap * GROUP, rows), :]
    conv_ref[...] = conv
    high, low = halves(conv * sigmoid(conv))
    label = label_ref[...]
    parts = [dot_bt(high, xw_ref[m]) + dot_bt(low, xw_ref[m]) for m in range(xw_ref.shape[0])]
    proj_ref[...] = pick(parts, label)


def conv_forward(inner, label, cw, cb, xw):
    rows, channels = inner.shape
    wide = xw.shape[1]
    lead = (cw.shape[0] - 1) * GROUP
    return pl.pallas_call(
        conv_kernel,
        out_shape=(
            jax.ShapeDtypeStruct((rows, channels), F32),
            jax.ShapeDtypeStruct((rows, channels), BF16),
            jax.ShapeDtypeStruct((rows, wide), F32),
        ),
        scratch_shapes=[pltpu.VMEM((rows + lead, channels), F32)],
        compiler_params=params(),
        name="conv_forward",
    )(inner, label, cw, cb[None, :], xw)


def scan_kernel(
    conv_ref, proj_ref, gate_ref, grad_ref, label_ref, dtw_ref, dtb_ref, alog_ref, skip_ref,
    gated_ref, dgate_ref, dact_ref, dproj_ref, ddtw_ref, ddtb_ref, dalog_ref, dskip_ref,
    hist, mix, prod, rate, drate, act, step, slope, dout, scanned, ddrive, dstep, dlow,
):
    rows, width = conv_ref.shape
    length = rows // GROUP
    states = alog_ref.shape[0]
    mods, low_width = dtw_ref.shape[0], dtw_ref.shape[1]
    tile = pl.program_id(0)
    label = label_ref[...]

    @pl.when(tile == 0)
    def _():
        prod[...] = jnp.zeros_like(prod)
        dlow[...] = jnp.zeros_like(dlow)
        for s in range(2 * states):
            mix[s] = jnp.broadcast_to(proj_ref[:, pl.ds(low_width + s, 1)], (rows, width))

    low_rank = proj_ref[:, pl.ds(0, low_width)]
    low_high, low_low = halves(low_rank)
    parts = [
        dot(low_high, dtw_ref[m]) + dot(low_low, dtw_ref[m]) + dtb_ref[pl.ds(m, 1), :].astype(F32) for m in range(mods)
    ]
    speed = pick(parts, label)
    step[...] = jnp.maximum(speed, 0.0) + jnp.log1p(jnp.exp(-jnp.abs(speed)))
    slope[...] = sigmoid(speed)
    conv = conv_ref[...]
    act[...] = conv * sigmoid(conv)
    for s in range(states):
        rate[s] = jnp.broadcast_to(-LOG2E * jnp.exp(alog_ref[pl.ds(s, 1), :].astype(F32)), (GROUP, width))
        drate[s] = jnp.zeros((GROUP, width), F32)
        hist[0, s] = jnp.zeros((GROUP, width), F32)

    def forward(t, state):
        at = pl.ds(pl.multiple_of(t * GROUP, GROUP), GROUP)
        now = step[at, :]
        drive = now * act[at, :]
        total = None
        new = []
        for s in range(states):
            value = jnp.exp2(now * rate[s]) * state[s] + mix[s, at, :] * drive
            hist[t + 1, s] = value
            new.append(value)
            term = mix[states + s, at, :] * value
            total = term if total is None else total + term
        scanned[at, :] = total
        return tuple(new)

    zero = jnp.zeros((GROUP, width), F32)
    lax.fori_loop(0, length, forward, (zero,) * states)

    gate = by_time(gate_ref[...])
    grad = by_time(grad_ref[...])
    soft = sigmoid(gate)
    opened = gate * soft
    skip = skip_ref[...].astype(F32)
    summed = scanned[...] + skip * act[...]
    gated_ref[...] = by_sequence(summed * opened).astype(BF16)
    dgate = grad * summed * (soft + opened * (1.0 - soft))
    dgate_ref[...] = by_sequence(dgate).astype(BF16)
    dsummed = grad * opened
    dout[...] = dsummed
    dskip_ref[...] = jnp.sum(dsummed * act[...], axis=0, keepdims=True)

    def backward(i, carry):
        t = length - 1 - i
        at = pl.ds(pl.multiple_of(t * GROUP, GROUP), GROUP)
        now = step[at, :]
        drive = now * act[at, :]
        out = dout[at, :]
        dd, ds = None, None
        new = []
        for s in range(states):
            decay = jnp.exp2(now * rate[s])
            dstate = carry[s] + mix[states + s, at, :] * out
            prod[states + s, at, :] += out * hist[t + 1, s]
            prod[s, at, :] += dstate * drive
            term = dstate * mix[s, at, :]
            dd = term if dd is None else dd + term
            passed = dstate * decay
            new.append(passed)
            change = passed * hist[t, s]
            term = change * rate[s]
            ds = term if ds is None else ds + term
            drate[s] += change * now
        ddrive[at, :] = dd
        dstep[at, :] = ds
        return tuple(new)

    lax.fori_loop(0, length, backward, (zero,) * states)

    for s in range(states):
        dalog_ref[pl.ds(s, 1), :] = LN2 * jnp.sum(drate[s] * rate[s], axis=0, keepdims=True)
    dact_ref[...] = ddrive[...] * step[...] + skip * dout[...]
    dspeed = (dstep[...] * LN2 + ddrive[...] * act[...]) * slope[...]
    high, low = halves(dspeed)
    parts = [dot_bt(high, dtw_ref[m]) + dot_bt(low, dtw_ref[m]) for m in range(mods)]
    dlow[...] += pick(parts, label)
    for m in range(mods):
        own = label == m
        masked = jnp.where(own, dspeed, 0.0)
        high, low = halves(masked)
        ddtw_ref[m] = dot_at(low_high, high) + dot_at(low_high, low) + dot_at(low_low, high)
        ddtb_ref[pl.ds(m, 1), :] = jnp.sum(masked, axis=0, keepdims=True)

    @pl.when(tile == pl.num_programs(0) - 1)
    def _():
        column = lax.broadcasted_iota(jnp.int32, (rows, 2 * states), 1)
        sums = jnp.zeros((rows, 2 * states), F32)
        for s in range(2 * states):
            sums = jnp.where(column == s, jnp.sum(prod[s], axis=1, keepdims=True), sums)
        dproj_ref[:, pl.ds(0, low_width)] = dlow[...]
        dproj_ref[:, pl.ds(low_width, 2 * states)] = sums


def scan_both(conv, proj, gate, grad, label, dtw, dtb, alog, skip):
    rows, channels = conv.shape
    width = min(128, channels)
    length = rows // GROUP
    states = alog.shape[0]
    mods, low_width = dtw.shape[0], dtw.shape[1]
    wide = proj.shape[1]

    def whole(shape):
        return pl.BlockSpec(shape, lambda j: (0,) * len(shape), pipeline_mode=pl.Buffered(1))

    def cut(*shape):
        return pl.BlockSpec(shape + (width,), lambda j: (0,) * len(shape) + (j,))

    plane = (GROUP, width)
    flat = pltpu.VMEM((rows, width), F32)
    return pl.pallas_call(
        scan_kernel,
        out_shape=(
            jax.ShapeDtypeStruct((rows, channels), BF16),
            jax.ShapeDtypeStruct((rows, channels), BF16),
            jax.ShapeDtypeStruct((rows, channels), F32),
            jax.ShapeDtypeStruct((rows, wide), F32),
            jax.ShapeDtypeStruct((mods, low_width, channels), F32),
            jax.ShapeDtypeStruct((mods, channels), F32),
            jax.ShapeDtypeStruct((states, channels), F32),
            jax.ShapeDtypeStruct((1, channels), F32),
        ),
        grid=(channels // width,),
        in_specs=[
            cut(rows), whole((rows, wide)), cut(rows), cut(rows), whole((rows, 1)),
            cut(mods, low_width), cut(mods), cut(states), cut(1),
        ],
        out_specs=(
            cut(rows), cut(rows), cut(rows), whole((rows, wide)), cut(mods, low_width), cut(mods), cut(states), cut(1),
        ),
        scratch_shapes=[
            pltpu.VMEM((length + 1, states) + plane, F32),
            pltpu.VMEM((2 * states, rows, width), F32),
            pltpu.VMEM((2 * states, rows, width), F32),
            pltpu.VMEM((states,) + plane, F32),
            pltpu.VMEM((states,) + plane, F32),
            flat, flat, flat, flat, flat, flat, flat,
            pltpu.VMEM((rows, low_width), F32),
        ],
        compiler_params=params(),
        name="scan_both",
    )(conv, proj, gate, grad, label, dtw, dtb, alog, skip[None, :])


def conv_back_kernel(
    conv_ref, inner_ref, dact_ref, dproj_ref, label_ref, cw_ref, xw_ref,
    dinner_ref, dxw_ref, dcw_ref, dcb_ref, pad_ref,
):
    rows, channels = conv_ref.shape
    taps = cw_ref.shape[0]
    tail = (taps - 1) * GROUP
    label = label_ref[...]
    conv = conv_ref[...]
    soft = sigmoid(conv)
    act = conv * soft
    dproj = dproj_ref[...]
    high, low = halves(dproj)
    parts = [dot(high, xw_ref[m]) + dot(low, xw_ref[m]) for m in range(xw_ref.shape[0])]
    dact = dact_ref[...] + pick(parts, label)
    act_high, act_low = halves(act)
    for m in range(xw_ref.shape[0]):
        high, low = halves(jnp.where(label == m, dproj, 0.0))
        dxw_ref[m] = dot_at(high, act_high) + dot_at(low, act_high) + dot_at(high, act_low)
    dconv = dact * (soft + act * (1.0 - soft))
    dcb_ref[...] = jnp.sum(dconv, axis=0, keepdims=True)
    pad_ref[pl.ds(0, rows), :] = dconv
    pad_ref[pl.ds(rows, tail), :] = jnp.zeros((tail, channels), F32)
    inner = inner_ref[...].astype(F32)
    total = None
    for tap in range(taps):
        shift = (taps - 1 - tap) * GROUP
        later = pad_ref[pl.ds(shift, rows), :]
        term = cw_ref[pl.ds(tap, 1), :].astype(F32) * later
        total = term if total is None else total + term
        dcw_ref[pl.ds(tap, 1), :] = jnp.sum(later * inner, axis=0, keepdims=True)
    dinner_ref[...] = by_sequence(total).astype(BF16)


def conv_backward(conv, inner, dact, dproj, label, cw, xw):
    rows, channels = conv.shape
    mods, wide = xw.shape[0], xw.shape[1]
    taps = cw.shape[0]
    return pl.pallas_call(
        conv_back_kernel,
        out_shape=(
            jax.ShapeDtypeStruct((rows, channels), BF16),
            jax.ShapeDtypeStruct((mods, wide, channels), F32),
            jax.ShapeDtypeStruct((taps, channels), F32),
            jax.ShapeDtypeStruct((1, channels), F32),
        ),
        scratch_shapes=[pltpu.VMEM((rows + (taps - 1) * GROUP, channels), F32)],
        compiler_params=params(),
        name="conv_backward",
    )(conv, inner, dact, dproj, label, cw, xw)


def by_groups(fn, count, arrays, joined):
    if count == 1:
        return fn(*arrays)
    size = arrays[0].shape[0] // count
    outs = [fn(*(a[i * size : (i + 1) * size] for a in arrays)) for i in range(count)]
    return tuple(
        jnp.concatenate(values, axis=0) if at < joined else functools.reduce(jnp.add, values)
        for at, values in enumerate(zip(*outs, strict=True))
    )


def exchange_pairs(n):
    half = n // 2
    first = [(c, 2 * c) if c < half else (c, 2 * (c - half) + 1) for c in range(n)]
    second = [(c, 2 * c + 1) if c < half else (c, 2 * (c - half)) for c in range(n)]
    return first, second


def to_owners(xz, n):
    first, second = exchange_pairs(n)
    c = lax.axis_index("ch")
    width = xz.shape[1] // 2
    left, right = xz[:, :width], xz[:, width:]
    lower = c < n // 2
    one = lax.ppermute(jnp.where(lower, left, right), "ch", first)
    two = lax.ppermute(jnp.where(lower, right, left), "ch", second)
    even = c % 2 == 0
    return jnp.where(even, one, two), jnp.where(even, two, one)


def to_columns(dinner, dgate, n):
    first, second = exchange_pairs(n)
    c = lax.axis_index("ch")
    even = c % 2 == 0
    one = lax.ppermute(jnp.where(even, dinner, dgate), "ch", [(b, a) for a, b in first])
    two = lax.ppermute(jnp.where(even, dgate, dinner), "ch", [(b, a) for a, b in second])
    lower = c < n // 2
    return jnp.concatenate([jnp.where(lower, one, two), jnp.where(lower, two, one)], axis=1)


def weight_grad(left, right, label, mods, spread_left):
    parts = []
    for m in range(mods):
        own = (label == m)[:, None]
        if spread_left:
            parts.append(dot_at(jnp.where(own, left, jnp.zeros_like(left)), right))
        else:
            parts.append(dot_at(left, jnp.where(own, right, jnp.zeros_like(right))))
    return jnp.stack(parts)


def on_device(
    n,
    block_input,
    norm_gain,
    in_weight,
    x_weight,
    dt_weight,
    dt_bias,
    conv_weight,
    conv_bias,
    a_log,
    skip_gain,
    out_weight,
    modality,
    cotangent,
):
    mods = in_weight.shape[0]
    length = block_input.shape[0]
    count = n // GROUP
    rows_float = block_input.astype(F32)
    gain = norm_gain.astype(F32)
    inverse = lax.rsqrt(jnp.mean(rows_float * rows_float, axis=-1, keepdims=True) + 1e-05)
    normed = rows_float * inverse
    scaled = (normed * gain[None, :]).astype(BF16)

    group_rows = lax.all_gather(scaled, "ch", axis=0, tiled=True)
    every_label = lax.all_gather(modality, ("tok", "ch"), axis=0, tiled=True)
    token_group = n * length
    group_label = lax.dynamic_slice_in_dim(every_label, lax.axis_index("tok") * token_group, token_group, 0)
    label = group_label[:, None]
    label_by_time = group_label.reshape(count, GROUP, length).transpose(0, 2, 1).reshape(token_group, 1)

    xz = routed_select(group_rows, label, in_weight, 256, False)
    inner, gate = to_owners(xz, n)
    group_cot = lax.all_gather(cotangent, "ch", axis=0, tiled=True)
    gated_grad = routed_select(group_cot, label, out_weight, 128, True)

    conv, inner_by_time, proj_part = by_groups(
        lambda a, b: conv_forward(a, b, conv_weight, conv_bias, x_weight), count, (inner, label_by_time), 3
    )
    proj = lax.psum(proj_part, "ch")

    gated, dgate, dact, dproj_part, ddtw, ddtb, dalog, dskip = by_groups(
        lambda a, b, c, d, e: scan_both(a, b, c, d, e, dt_weight, dt_bias, a_log, skip_gain),
        count,
        (conv, proj, gate, gated_grad, label_by_time),
        4,
    )
    dproj = lax.psum(dproj_part, "ch")

    dinner, dxw, dcw, dcb = by_groups(
        lambda a, b, c, d, e: conv_backward(a, b, c, d, e, conv_weight, x_weight),
        count,
        (conv, inner_by_time, dact, dproj, label_by_time),
        1,
    )
    xz_grad = to_columns(dinner, dgate, n)

    branch_part = routed_spread(gated, label, out_weight, 512, False, BF16)
    branch = lax.psum_scatter(branch_part, "ch", scatter_dimension=0, tiled=True).astype(F32)
    block_out = (rows_float + branch).astype(BF16)

    scaled_part = routed_spread(xz_grad, label, in_weight, 256, True, BF16)
    scaled_grad = lax.psum_scatter(scaled_part, "ch", scatter_dimension=0, tiled=True).astype(F32)
    gain_grad = jnp.sum(scaled_grad * normed, axis=0)
    ng = scaled_grad * gain[None, :]
    row_grad = cotangent.astype(F32) + inverse * (ng - normed * jnp.mean(ng * normed, axis=-1, keepdims=True))

    every_scaled = lax.all_gather(scaled, ("tok", "ch"), axis=0, tiled=True)
    every_cot = lax.all_gather(cotangent, ("tok", "ch"), axis=0, tiled=True)
    every_gated = lax.all_gather(gated, "tok", axis=0, tiled=True)
    every_grad = lax.all_gather(xz_grad, "tok", axis=0, tiled=True)
    out_weight_grad = weight_grad(every_gated, every_cot, every_label, mods, True)
    in_weight_grad = weight_grad(every_scaled, every_grad, every_label, mods, False)

    small = lax.psum((dxw, ddtw, ddtb, dcw, dcb, dalog, dskip), "tok")
    gain_grad = lax.psum(gain_grad, ("tok", "ch"))
    own = gain_grad.shape[0] // n
    gain_grad = lax.dynamic_slice_in_dim(gain_grad, lax.axis_index("ch") * own, own, 0)
    dxw, ddtw, ddtb, dcw, dcb, dalog, dskip = small
    return (
        block_out,
        row_grad,
        gain_grad,
        in_weight_grad,
        dxw,
        ddtw,
        ddtb,
        dcw,
        dcb[0],
        dalog,
        dskip[0],
        out_weight_grad,
    )


def solution(mesh):
    placed = (
        P(("tok", "ch"), None),
        P(),
        P(None, None, "ch"),
        P(None, None, "ch"),
        P(None, None, "ch"),
        P(None, "ch"),
        P(None, "ch"),
        P("ch"),
        P(None, "ch"),
        P("ch"),
        P(None, "ch", None),
        P(("tok", "ch")),
        P(("tok", "ch"), None),
    )
    return jax.shard_map(
        functools.partial(on_device, mesh.shape["ch"]),
        mesh=mesh,
        in_specs=placed,
        out_specs=(
            P(("tok", "ch"), None),
            P(("tok", "ch"), None),
            P("ch"),
            P(None, None, "ch"),
            P(None, None, "ch"),
            P(None, None, "ch"),
            P(None, "ch"),
            P(None, "ch"),
            P("ch"),
            P(None, "ch"),
            P("ch"),
            P(None, "ch", None),
        ),
        check_vma=False,
    )
```

```python
import functools
import math

import jax
import jax.numpy as jnp
from jax import lax
from jax.experimental import pallas as pl
from jax.experimental.pallas import tpu as pltpu
from jax.sharding import PartitionSpec as P

F32 = jnp.float32
BF16 = jnp.bfloat16
LOG2E = math.log2(math.e)
LN2 = math.log(2.0)
GROUP = 8
VMEM_LIMIT = 58 << 20


def params(**kw):
    return pltpu.CompilerParams(vmem_limit_bytes=VMEM_LIMIT, **kw)


def dot(a, b):
    return lax.dot_general(a, b, (((1,), (0,)), ((), ())), preferred_element_type=F32)


def dot_bt(a, b):
    return lax.dot_general(a, b, (((1,), (1,)), ((), ())), preferred_element_type=F32)


def dot_at(a, b):
    return lax.dot_general(a, b, (((0,), (0,)), ((), ())), preferred_element_type=F32)


def halves(x):
    high = x.astype(BF16)
    return high, (x - high.astype(F32)).astype(BF16)


def pick(parts, label):
    total = parts[-1]
    for index in range(len(parts) - 2, -1, -1):
        total = jnp.where(label == index, parts[index], total)
    return total


def sigmoid(x):
    return 1.0 / (1.0 + jnp.exp(-x))


def select_kernel(transposed, x_ref, label_ref, w_ref, out_ref):
    x = x_ref[...]
    label = label_ref[...]
    product = dot_bt if transposed else dot
    parts = [product(x, w_ref[m]) for m in range(w_ref.shape[0])]
    out_ref[...] = pick(parts, label).astype(out_ref.dtype)


def routed_select(x, label, w, tile, transposed):
    rows, depth = x.shape
    mods = w.shape[0]
    outer = w.shape[1] if transposed else w.shape[2]
    tile = min(tile, outer)
    block = min(rows, 1024)
    if transposed:
        w_spec = pl.BlockSpec((mods, tile, depth), lambda i, j: (0, j, 0))
    else:
        w_spec = pl.BlockSpec((mods, depth, tile), lambda i, j: (0, 0, j))
    return pl.pallas_call(
        functools.partial(select_kernel, transposed),
        out_shape=jax.ShapeDtypeStruct((rows, outer), BF16),
        grid=(rows // block, outer // tile),
        in_specs=[
            pl.BlockSpec((block, depth), lambda i, j: (i, 0)),
            pl.BlockSpec((block, 1), lambda i, j: (i, 0)),
            w_spec,
        ],
        out_specs=pl.BlockSpec((block, tile), lambda i, j: (i, j)),
        compiler_params=params(),
        cost_estimate=pl.CostEstimate(
            flops=2 * rows * depth * outer * mods, bytes_accessed=2 * mods * depth * outer + 2 * rows * (depth + outer), transcendentals=0
        ),
        name="routed_select",
    )(x, label, w)


def spread_kernel(transposed, x_ref, label_ref, w_ref, out_ref):
    x = x_ref[...]
    label = label_ref[...]
    product = dot_bt if transposed else dot
    total = None
    for m in range(w_ref.shape[0]):
        part = product(jnp.where(label == m, x, jnp.zeros_like(x)), w_ref[m])
        total = part if total is None else total + part
    out_ref[...] = total.astype(out_ref.dtype)


def routed_spread(x, label, w, tile, transposed, dtype):
    rows, depth = x.shape
    mods = w.shape[0]
    outer = w.shape[1] if transposed else w.shape[2]
    tile = min(tile, outer)
    block = min(rows, 1024)
    if transposed:
        w_spec = pl.BlockSpec((mods, tile, depth), lambda i, j: (0, j, 0))
    else:
        w_spec = pl.BlockSpec((mods, depth, tile), lambda i, j: (0, 0, j))
    return pl.pallas_call(
        functools.partial(spread_kernel, transposed),
        out_shape=jax.ShapeDtypeStruct((rows, outer), dtype),
        grid=(rows // block, outer // tile),
        in_specs=[
            pl.BlockSpec((block, depth), lambda i, j: (i, 0)),
            pl.BlockSpec((block, 1), lambda i, j: (i, 0)),
            w_spec,
        ],
        out_specs=pl.BlockSpec((block, tile), lambda i, j: (i, j)),
        compiler_params=params(),
        cost_estimate=pl.CostEstimate(
            flops=2 * rows * depth * outer * mods, bytes_accessed=2 * mods * depth * outer + 2 * rows * (depth + outer), transcendentals=0
        ),
        name="routed_spread",
    )(x, label, w)


def by_time(x):
    rows, width = x.shape
    return jnp.swapaxes(x.astype(F32).reshape(GROUP, rows // GROUP, width), 0, 1).reshape(rows, width)


def by_sequence(x):
    rows, width = x.shape
    return jnp.swapaxes(x.reshape(rows // GROUP, GROUP, width), 0, 1).reshape(rows, width)


def conv_kernel(inner_ref, label_ref, cw_ref, cb_ref, xw_ref, conv_ref, inner_out_ref, proj_ref, pad_ref):
    rows, channels = inner_ref.shape
    taps = cw_ref.shape[0]
    lead = (taps - 1) * GROUP
    inner = by_time(inner_ref[...])
    inner_out_ref[...] = inner.astype(BF16)
    pad_ref[pl.ds(0, lead), :] = jnp.zeros((lead, channels), F32)
    pad_ref[pl.ds(lead, rows), :] = inner
    conv = jnp.broadcast_to(cb_ref[...].astype(F32), (rows, channels))
    for tap in range(taps):
        conv = conv + cw_ref[pl.ds(tap, 1), :].astype(F32) * pad_ref[pl.ds(tap * GROUP, rows), :]
    conv_ref[...] = conv
    high, low = halves(conv * sigmoid(conv))
    label = label_ref[...]
    parts = [dot_bt(xw_ref[m], high) + dot_bt(xw_ref[m], low) for m in range(xw_ref.shape[0])]
    proj_ref[...] = pick(parts, label)


def conv_forward(inner, label, cw, cb, xw):
    rows, channels = inner.shape
    wide = xw.shape[1]
    lead = (cw.shape[0] - 1) * GROUP
    return pl.pallas_call(
        conv_kernel,
        out_shape=(
            jax.ShapeDtypeStruct((rows, channels), F32),
            jax.ShapeDtypeStruct((rows, channels), BF16),
            jax.ShapeDtypeStruct((wide, rows), F32),
        ),
        scratch_shapes=[pltpu.VMEM((rows + lead, channels), F32)],
        compiler_params=params(),
        name="conv_forward",
    )(inner, label, cw, cb[None, :], xw)


def scan_kernel(
    conv_ref, proj_ref, gate_ref, grad_ref, label_ref, label_row_ref, dtw_ref, dtb_ref, alog_ref, skip_ref,
    gated_ref, dgate_ref, dact_ref, dproj_ref, ddtw_ref, ddtb_ref, dalog_ref, dskip_ref,
    hist, mix, prod, rate, drate, act, step, slope, dout, scanned, ddrive, dstep, dlow,
):
    rows, width = conv_ref.shape
    length = rows // GROUP
    states = alog_ref.shape[0]
    mods, low_width = dtw_ref.shape[0], dtw_ref.shape[1]
    tile = pl.program_id(0)
    label = label_ref[...]

    @pl.when(tile == 0)
    def _():
        prod[...] = jnp.zeros_like(prod)
        dlow[...] = jnp.zeros_like(dlow)
        high, low = halves(proj_ref[pl.ds(low_width, 2 * states), :])
        row = lax.broadcasted_iota(jnp.int32, (2 * states, width), 0)
        for s in range(2 * states):
            spread = (row == s).astype(BF16)
            mix[s] = dot_at(high, spread) + dot_at(low, spread)

    low_high, low_low = halves(proj_ref[pl.ds(0, low_width), :])
    parts = [
        dot_at(low_high, dtw_ref[m]) + dot_at(low_low, dtw_ref[m]) + dtb_ref[pl.ds(m, 1), :].astype(F32) for m in range(mods)
    ]
    speed = pick(parts, label)
    step[...] = jnp.maximum(speed, 0.0) + jnp.log1p(jnp.exp(-jnp.abs(speed)))
    slope[...] = sigmoid(speed)
    conv = conv_ref[...]
    act[...] = conv * sigmoid(conv)
    for s in range(states):
        rate[s] = jnp.broadcast_to(-LOG2E * jnp.exp(alog_ref[pl.ds(s, 1), :].astype(F32)), (GROUP, width))
        drate[s] = jnp.zeros((GROUP, width), F32)
        hist[0, s] = jnp.zeros((GROUP, width), F32)

    def forward(t, state):
        at = pl.ds(pl.multiple_of(t * GROUP, GROUP), GROUP)
        now = step[at, :]
        drive = now * act[at, :]
        total = None
        new = []
        for s in range(states):
            value = jnp.exp2(now * rate[s]) * state[s] + mix[s, at, :] * drive
            hist[t + 1, s] = value
            new.append(value)
            term = mix[states + s, at, :] * value
            total = term if total is None else total + term
        scanned[at, :] = total
        return tuple(new)

    zero = jnp.zeros((GROUP, width), F32)
    lax.fori_loop(0, length, forward, (zero,) * states)

    gate = by_time(gate_ref[...])
    grad = by_time(grad_ref[...])
    soft = sigmoid(gate)
    opened = gate * soft
    skip = skip_ref[...].astype(F32)
    summed = scanned[...] + skip * act[...]
    gated_ref[...] = by_sequence(summed * opened).astype(BF16)
    dgate = grad * summed * (soft + opened * (1.0 - soft))
    dgate_ref[...] = by_sequence(dgate).astype(BF16)
    dsummed = grad * opened
    dout[...] = dsummed
    dskip_ref[...] = jnp.sum(dsummed * act[...], axis=0, keepdims=True)

    def backward(i, carry):
        t = length - 1 - i
        at = pl.ds(pl.multiple_of(t * GROUP, GROUP), GROUP)
        now = step[at, :]
        drive = now * act[at, :]
        out = dout[at, :]
        dd, ds = None, None
        new = []
        for s in range(states):
            decay = jnp.exp2(now * rate[s])
            dstate = carry[s] + mix[states + s, at, :] * out
            prod[states + s, at, :] += out * hist[t + 1, s]
            prod[s, at, :] += dstate * drive
            term = dstate * mix[s, at, :]
            dd = term if dd is None else dd + term
            passed = dstate * decay
            new.append(passed)
            change = passed * hist[t, s]
            term = change * rate[s]
            ds = term if ds is None else ds + term
            drate[s] += change * now
        ddrive[at, :] = dd
        dstep[at, :] = ds
        return tuple(new)

    lax.fori_loop(0, length, backward, (zero,) * states)

    for s in range(states):
        dalog_ref[pl.ds(s, 1), :] = LN2 * jnp.sum(drate[s] * rate[s], axis=0, keepdims=True)
    dact_ref[...] = ddrive[...] * step[...] + skip * dout[...]
    dspeed = (dstep[...] * LN2 + ddrive[...] * act[...]) * slope[...]
    high, low = halves(dspeed)
    parts = [dot_bt(dtw_ref[m], high) + dot_bt(dtw_ref[m], low) for m in range(mods)]
    dlow[...] += pick(parts, label_row_ref[...])
    for m in range(mods):
        own = label == m
        masked = jnp.where(own, dspeed, 0.0)
        high, low = halves(masked)
        ddtw_ref[m] = dot(low_high, high) + dot(low_high, low) + dot(low_low, high)
        ddtb_ref[pl.ds(m, 1), :] = jnp.sum(masked, axis=0, keepdims=True)

    @pl.when(tile == pl.num_programs(0) - 1)
    def _():
        column = lax.broadcasted_iota(jnp.int32, (width, 2 * states), 1)
        sums = jnp.zeros((rows, 2 * states), F32)
        for s in range(2 * states):
            gather = (column == s).astype(BF16)
            high, low = halves(prod[s])
            sums = sums + (dot(high, gather) + dot(low, gather))
        dproj_ref[pl.ds(0, low_width), :] = dlow[...]
        dproj_ref[pl.ds(low_width, 2 * states), :] = sums.T


def scan_both(conv, proj, gate, grad, label, label_row, dtw, dtb, alog, skip):
    rows, channels = conv.shape
    width = min(128, channels)
    length = rows // GROUP
    states = alog.shape[0]
    mods, low_width = dtw.shape[0], dtw.shape[1]
    wide = proj.shape[0]

    def whole(shape):
        return pl.BlockSpec(shape, lambda j: (0,) * len(shape), pipeline_mode=pl.Buffered(1))

    def cut(*shape):
        return pl.BlockSpec(shape + (width,), lambda j: (0,) * len(shape) + (j,))

    plane = (GROUP, width)
    flat = pltpu.VMEM((rows, width), F32)
    return pl.pallas_call(
        scan_kernel,
        out_shape=(
            jax.ShapeDtypeStruct((rows, channels), BF16),
            jax.ShapeDtypeStruct((rows, channels), BF16),
            jax.ShapeDtypeStruct((rows, channels), F32),
            jax.ShapeDtypeStruct((wide, rows), F32),
            jax.ShapeDtypeStruct((mods, low_width, channels), F32),
            jax.ShapeDtypeStruct((mods, channels), F32),
            jax.ShapeDtypeStruct((states, channels), F32),
            jax.ShapeDtypeStruct((1, channels), F32),
        ),
        grid=(channels // width,),
        in_specs=[
            cut(rows), whole((wide, rows)), cut(rows), cut(rows), whole((rows, 1)), whole((1, rows)),
            cut(mods, low_width), cut(mods), cut(states), cut(1),
        ],
        out_specs=(
            cut(rows), cut(rows), cut(rows), whole((wide, rows)), cut(mods, low_width), cut(mods), cut(states), cut(1),
        ),
        scratch_shapes=[
            pltpu.VMEM((length + 1, states) + plane, F32),
            pltpu.VMEM((2 * states, rows, width), F32),
            pltpu.VMEM((2 * states, rows, width), F32),
            pltpu.VMEM((states,) + plane, F32),
            pltpu.VMEM((states,) + plane, F32),
            flat, flat, flat, flat, flat, flat, flat,
            pltpu.VMEM((low_width, rows), F32),
        ],
        compiler_params=params(),
        cost_estimate=pl.CostEstimate(flops=5000 * rows * channels * states, bytes_accessed=20 * rows * channels, transcendentals=0),
        name="scan_both",
    )(conv, proj, gate, grad, label, label_row, dtw, dtb, alog, skip[None, :])


def conv_back_kernel(
    conv_ref, inner_ref, dact_ref, dproj_ref, label_ref, label_row_ref, cw_ref, xw_ref,
    dinner_ref, dxw_ref, dcw_ref, dcb_ref, pad_ref,
):
    rows, channels = conv_ref.shape
    taps = cw_ref.shape[0]
    tail = (taps - 1) * GROUP
    label, label_row = label_ref[...], label_row_ref[...]
    conv = conv_ref[...]
    soft = sigmoid(conv)
    act = conv * soft
    dproj = dproj_ref[...]
    high, low = halves(dproj)
    parts = [dot_at(high, xw_ref[m]) + dot_at(low, xw_ref[m]) for m in range(xw_ref.shape[0])]
    dact = dact_ref[...] + pick(parts, label)
    act_high, act_low = halves(act)
    for m in range(xw_ref.shape[0]):
        high, low = halves(jnp.where(label_row == m, dproj, 0.0))
        dxw_ref[m] = dot(high, act_high) + dot(low, act_high) + dot(high, act_low)
    dconv = dact * (soft + act * (1.0 - soft))
    dcb_ref[...] = jnp.sum(dconv, axis=0, keepdims=True)
    pad_ref[pl.ds(0, rows), :] = dconv
    pad_ref[pl.ds(rows, tail), :] = jnp.zeros((tail, channels), F32)
    inner = inner_ref[...].astype(F32)
    total = None
    for tap in range(taps):
        shift = (taps - 1 - tap) * GROUP
        later = pad_ref[pl.ds(shift, rows), :]
        term = cw_ref[pl.ds(tap, 1), :].astype(F32) * later
        total = term if total is None else total + term
        dcw_ref[pl.ds(tap, 1), :] = jnp.sum(later * inner, axis=0, keepdims=True)
    dinner_ref[...] = by_sequence(total).astype(BF16)


def conv_backward(conv, inner, dact, dproj, label, label_row, cw, xw):
    rows, channels = conv.shape
    mods, wide = xw.shape[0], xw.shape[1]
    taps = cw.shape[0]
    return pl.pallas_call(
        conv_back_kernel,
        out_shape=(
            jax.ShapeDtypeStruct((rows, channels), BF16),
            jax.ShapeDtypeStruct((mods, wide, channels), F32),
            jax.ShapeDtypeStruct((taps, channels), F32),
            jax.ShapeDtypeStruct((1, channels), F32),
        ),
        scratch_shapes=[pltpu.VMEM((rows + (taps - 1) * GROUP, channels), F32)],
        compiler_params=params(),
        name="conv_backward",
    )(conv, inner, dact, dproj, label, label_row, cw, xw)


MESH = pl.DeviceIdType.MESH


def sum_kernel(chips, x_ref, out_ref, near, mine, far, total, every, other, near_sems, far_sems, back_sems, other_sems):
    wide, rows = x_ref.shape
    half, part = rows // 2, rows // 2 // chips
    tok, ch = lax.axis_index("tok"), lax.axis_index("ch")
    chip, core = ch // 2, ch % 2
    partner = (tok, 2 * chip + 1 - core)
    chips_away = [(tok, 2 * (chip ^ d) + core) for d in range(1, chips)]

    barrier = pltpu.get_barrier_semaphore()
    for device in [partner] + chips_away:
        pl.semaphore_signal(barrier, inc=1, device_id=device, device_id_type=MESH)
    pl.semaphore_wait(barrier, chips)

    def send(src, dst, sems, device):
        copy = pltpu.make_async_remote_copy(
            src_ref=src, dst_ref=dst, send_sem=sems.at[0], recv_sem=sems.at[1], device_id=device, device_id_type=MESH
        )
        copy.start()
        return copy

    def columns(index, size):
        return pl.ds(pl.multiple_of(index * size, size), size)

    copy = send(x_ref.at[:, columns(1 - core, half)], near, near_sems, partner)
    copy.wait()
    mine[...] = (x_ref[:, columns(core, half)] + near[...]).astype(BF16)
    copies = [
        send(mine.at[:, columns(chip ^ d, part)], far.at[d - 1], far_sems.at[d - 1], chips_away[d - 1])
        for d in range(1, chips)
    ]
    value = mine[:, columns(chip, part)].astype(F32)
    for d, copy in enumerate(copies):
        copy.wait()
        value = value + far[d].astype(F32)
    total[...] = value.astype(BF16)
    copies = [send(total, every.at[d - 1], back_sems.at[d - 1], chips_away[d - 1]) for d in range(1, chips)]
    copies += [send(total, other.at[0], other_sems.at[0], partner)]
    out_ref[:, columns(core * chips + chip, part)] = total[...].astype(F32)
    for d in range(1, chips):
        copies[d - 1].wait()
        copies += [send(every.at[d - 1], other.at[d], other_sems.at[d], partner)]
        out_ref[:, columns(core * chips + (chip ^ d), part)] = every[d - 1].astype(F32)
    for d in range(chips):
        copies[chips - 1 + d].wait()
        out_ref[:, columns((1 - core) * chips + (chip ^ d), part)] = other[d].astype(F32)


def sum_over_ch(x, n, collective_id):
    wide, rows = x.shape
    chips = n // 2
    half, part = rows // 2, rows // 2 // chips
    dma = pltpu.SemaphoreType.DMA
    return pl.pallas_call(
        functools.partial(sum_kernel, chips),
        out_shape=jax.ShapeDtypeStruct((wide, rows), F32),
        in_specs=[pl.BlockSpec(memory_space=pltpu.VMEM)],
        out_specs=pl.BlockSpec(memory_space=pltpu.VMEM),
        scratch_shapes=[
            pltpu.VMEM((wide, half), F32),
            pltpu.VMEM((wide, half), BF16),
            pltpu.VMEM((chips - 1, wide, part), BF16),
            pltpu.VMEM((wide, part), BF16),
            pltpu.VMEM((chips - 1, wide, part), BF16),
            pltpu.VMEM((chips, wide, part), BF16),
            dma((2,)), dma((chips - 1, 2)), dma((chips - 1, 2)), dma((chips, 2)),
        ],
        compiler_params=pltpu.CompilerParams(collective_id=collective_id, has_side_effects=True, vmem_limit_bytes=16 << 20),
        name="sum_over_ch",
    )(x)


def total_over_ch(x, n, collective_id):
    if x.shape[1] // n % 128 == 0 and n // 2 & (n // 2 - 1) == 0 and n <= 8:
        return sum_over_ch(x, n, collective_id)
    return lax.psum(x, "ch")


def grad_kernel(left_ref, right_ref, label_ref, out_ref):
    left, right, label = left_ref[...], right_ref[...], label_ref[...]
    turned = left.T
    for m in range(out_ref.shape[0]):
        out_ref[m] = dot(jnp.where(label == m, turned, jnp.zeros_like(turned)), right)


def grad_part_kernel(left_ref, right_ref, label_ref, out_ref):
    left, right, label = left_ref[...], right_ref[...], label_ref[...]
    turned = left.T
    first = pl.program_id(1) == 0
    for m in range(out_ref.shape[0]):
        part = dot(jnp.where(label == m, turned, jnp.zeros_like(turned)), right)
        out_ref[m] = jnp.where(first, part, out_ref[m] + part)


def weight_grad(left, right, label, mods, tile):
    rows, deep = left.shape
    wide = right.shape[1]
    block = min(rows, 4096)
    tile = min(tile, deep)
    return pl.pallas_call(
        grad_kernel if block == rows else grad_part_kernel,
        out_shape=jax.ShapeDtypeStruct((mods, deep, wide), F32),
        grid=(deep // tile, rows // block),
        in_specs=[
            pl.BlockSpec((block, tile), lambda i, j: (j, i)),
            pl.BlockSpec((block, wide), lambda i, j: (j, 0)),
            pl.BlockSpec((1, block), lambda i, j: (0, j)),
        ],
        out_specs=pl.BlockSpec((mods, tile, wide), lambda i, j: (0, i, 0)),
        compiler_params=params(),
        cost_estimate=pl.CostEstimate(
            flops=2 * mods * rows * deep * wide,
            bytes_accessed=2 * rows * (deep + wide) + 4 * mods * deep * wide,
            transcendentals=0,
        ),
        name="weight_grad",
    )(left, right, label)


def by_groups(fn, count, arrays, axes, joined):
    if count == 1:
        return fn(*arrays)

    def cut(a, axis, i):
        size = a.shape[axis] // count
        return lax.slice_in_dim(a, i * size, (i + 1) * size, axis=axis)

    outs = [fn(*(cut(a, axis, i) for a, axis in zip(arrays, axes, strict=True))) for i in range(count)]
    return tuple(
        jnp.concatenate(values, axis=joined[at]) if at < len(joined) else functools.reduce(jnp.add, values)
        for at, values in enumerate(zip(*outs, strict=True))
    )


def exchange_pairs(n):
    half = n // 2
    first = [(c, 2 * c) if c < half else (c, 2 * (c - half) + 1) for c in range(n)]
    second = [(c, 2 * c + 1) if c < half else (c, 2 * (c - half)) for c in range(n)]
    return first, second


def to_owners(xz, n):
    first, second = exchange_pairs(n)
    c = lax.axis_index("ch")
    width = xz.shape[1] // 2
    left, right = xz[:, :width], xz[:, width:]
    lower = c < n // 2
    one = lax.ppermute(jnp.where(lower, left, right), "ch", first)
    two = lax.ppermute(jnp.where(lower, right, left), "ch", second)
    even = c % 2 == 0
    return jnp.where(even, one, two), jnp.where(even, two, one)


def to_columns(dinner, dgate, n):
    first, second = exchange_pairs(n)
    c = lax.axis_index("ch")
    even = c % 2 == 0
    one = lax.ppermute(jnp.where(even, dinner, dgate), "ch", [(b, a) for a, b in first])
    two = lax.ppermute(jnp.where(even, dgate, dinner), "ch", [(b, a) for a, b in second])
    lower = c < n // 2
    return jnp.concatenate([jnp.where(lower, one, two), jnp.where(lower, two, one)], axis=1)


def on_device(
    n,
    block_input,
    norm_gain,
    in_weight,
    x_weight,
    dt_weight,
    dt_bias,
    conv_weight,
    conv_bias,
    a_log,
    skip_gain,
    out_weight,
    modality,
    cotangent,
):
    mods = in_weight.shape[0]
    length = block_input.shape[0]
    count = n // GROUP
    rows_float = block_input.astype(F32)
    gain = norm_gain.astype(F32)
    inverse = lax.rsqrt(jnp.mean(rows_float * rows_float, axis=-1, keepdims=True) + 1e-05)
    normed = rows_float * inverse
    scaled = (normed * gain[None, :]).astype(BF16)

    group_rows = lax.all_gather(scaled, "ch", axis=0, tiled=True)
    every_label = lax.all_gather(modality, ("tok", "ch"), axis=0, tiled=True)
    token_group = n * length
    group_label = lax.dynamic_slice_in_dim(every_label, lax.axis_index("tok") * token_group, token_group, 0)
    label = group_label[:, None]
    label_by_time = group_label.reshape(count, GROUP, length).transpose(0, 2, 1).reshape(token_group, 1)
    label_row = label_by_time.reshape(1, token_group)

    every_scaled = lax.all_gather(scaled, ("tok", "ch"), axis=0, tiled=True)
    every_cot = lax.all_gather(cotangent, ("tok", "ch"), axis=0, tiled=True)
    xz = routed_select(group_rows, label, in_weight, 256, False)
    inner, gate = to_owners(xz, n)
    group_cot = lax.all_gather(cotangent, "ch", axis=0, tiled=True)
    gated_grad = routed_select(group_cot, label, out_weight, 128, True)

    conv, inner_by_time, proj_part = by_groups(
        lambda a, b: conv_forward(a, b, conv_weight, conv_bias, x_weight), count, (inner, label_row), (0, 1), (0, 0, 1)
    )
    proj = total_over_ch(proj_part, n, 0)

    gated, dgate, dact, dproj_part, ddtw, ddtb, dalog, dskip = by_groups(
        lambda a, b, c, d, e, f: scan_both(a, b, c, d, e, f, dt_weight, dt_bias, a_log, skip_gain),
        count,
        (conv, proj, gate, gated_grad, label_by_time, label_row),
        (0, 1, 0, 0, 0, 1),
        (0, 0, 0, 1),
    )
    if count == 1:
        dproj_part, every_scaled = lax.optimization_barrier((dproj_part, every_scaled))
    dproj = total_over_ch(dproj_part, n, 1)

    dinner, dxw, dcw, dcb = by_groups(
        lambda a, b, c, d, e, f: conv_backward(a, b, c, d, e, f, conv_weight, x_weight),
        count,
        (conv, inner_by_time, dact, dproj, label_by_time, label_row),
        (0, 0, 0, 1, 0, 1),
        (0,),
    )
    xz_grad = to_columns(dinner, dgate, n)

    if count == 1:
        xz_grad, every_cot = lax.optimization_barrier((xz_grad, every_cot))
    branch_part = routed_spread(gated, label, out_weight, 512, False, BF16)
    branch = lax.psum_scatter(branch_part, "ch", scatter_dimension=0, tiled=True).astype(F32)
    block_out = (rows_float + branch).astype(BF16)

    scaled_part = routed_spread(xz_grad, label, in_weight, 256, True, BF16)
    scaled_grad = lax.psum_scatter(scaled_part, "ch", scatter_dimension=0, tiled=True).astype(F32)
    gain_grad = jnp.sum(scaled_grad * normed, axis=0)
    ng = scaled_grad * gain[None, :]
    row_grad = cotangent.astype(F32) + inverse * (ng - normed * jnp.mean(ng * normed, axis=-1, keepdims=True))

    every_gated = lax.all_gather(gated, "tok", axis=0, tiled=True)
    every_grad = lax.all_gather(xz_grad, "tok", axis=0, tiled=True)
    every_label = every_label[None, :]
    out_weight_grad = weight_grad(every_gated, every_cot, every_label, mods, 128)
    in_weight_grad = weight_grad(every_scaled, every_grad, every_label, mods, 256)

    small = lax.psum((dxw, ddtw, ddtb, dcw, dcb, dalog, dskip), "tok")
    gain_grad = lax.psum(gain_grad, ("tok", "ch"))
    own = gain_grad.shape[0] // n
    gain_grad = lax.dynamic_slice_in_dim(gain_grad, lax.axis_index("ch") * own, own, 0)
    dxw, ddtw, ddtb, dcw, dcb, dalog, dskip = small
    return (
        block_out,
        row_grad,
        gain_grad,
        in_weight_grad,
        dxw,
        ddtw,
        ddtb,
        dcw,
        dcb[0],
        dalog,
        dskip[0],
        out_weight_grad,
    )


def solution(mesh):
    placed = (
        P(("tok", "ch"), None),
        P(),
        P(None, None, "ch"),
        P(None, None, "ch"),
        P(None, None, "ch"),
        P(None, "ch"),
        P(None, "ch"),
        P("ch"),
        P(None, "ch"),
        P("ch"),
        P(None, "ch", None),
        P(("tok", "ch")),
        P(("tok", "ch"), None),
    )
    return jax.shard_map(
        functools.partial(on_device, mesh.shape["ch"]),
        mesh=mesh,
        in_specs=placed,
        out_specs=(
            P(("tok", "ch"), None),
            P(("tok", "ch"), None),
            P("ch"),
            P(None, None, "ch"),
            P(None, None, "ch"),
            P(None, None, "ch"),
            P(None, "ch"),
            P(None, "ch"),
            P("ch"),
            P(None, "ch"),
            P("ch"),
            P(None, "ch", None),
        ),
        check_vma=False,
    )
```

```python
import functools
import math

import jax
import jax.numpy as jnp
from jax import lax
from jax.experimental import pallas as pl
from jax.experimental.pallas import tpu as pltpu
from jax.sharding import PartitionSpec as P

F32 = jnp.float32
BF16 = jnp.bfloat16
LOG2E = math.log2(math.e)
LN2 = math.log(2.0)
GROUP = 8
VMEM_LIMIT = 58 << 20


def params(**kw):
    return pltpu.CompilerParams(vmem_limit_bytes=VMEM_LIMIT, **kw)


def dot(a, b):
    return lax.dot_general(a, b, (((1,), (0,)), ((), ())), preferred_element_type=F32)


def dot_bt(a, b):
    return lax.dot_general(a, b, (((1,), (1,)), ((), ())), preferred_element_type=F32)


def dot_at(a, b):
    return lax.dot_general(a, b, (((0,), (0,)), ((), ())), preferred_element_type=F32)


def halves(x):
    high = x.astype(BF16)
    return high, (x - high.astype(F32)).astype(BF16)


def pick(parts, label):
    total = parts[-1]
    for index in range(len(parts) - 2, -1, -1):
        total = jnp.where(label == index, parts[index], total)
    return total


def sigmoid(x):
    return 1.0 / (1.0 + jnp.exp(-x))


def select_kernel(transposed, x_ref, label_ref, w_ref, out_ref):
    x = x_ref[...]
    label = label_ref[...]
    product = dot_bt if transposed else dot
    parts = [product(x, w_ref[m]) for m in range(w_ref.shape[0])]
    out_ref[...] = pick(parts, label).astype(out_ref.dtype)


def routed_select(x, label, w, tile, transposed):
    rows, depth = x.shape
    mods = w.shape[0]
    outer = w.shape[1] if transposed else w.shape[2]
    tile = min(tile, outer)
    block = min(rows, 1024)
    if transposed:
        w_spec = pl.BlockSpec((mods, tile, depth), lambda i, j: (0, j, 0))
    else:
        w_spec = pl.BlockSpec((mods, depth, tile), lambda i, j: (0, 0, j))
    return pl.pallas_call(
        functools.partial(select_kernel, transposed),
        out_shape=jax.ShapeDtypeStruct((rows, outer), BF16),
        grid=(rows // block, outer // tile),
        in_specs=[
            pl.BlockSpec((block, depth), lambda i, j: (i, 0)),
            pl.BlockSpec((block, 1), lambda i, j: (i, 0)),
            w_spec,
        ],
        out_specs=pl.BlockSpec((block, tile), lambda i, j: (i, j)),
        compiler_params=params(),
        cost_estimate=pl.CostEstimate(
            flops=2 * rows * depth * outer * mods, bytes_accessed=2 * mods * depth * outer + 2 * rows * (depth + outer), transcendentals=0
        ),
        name="routed_select",
    )(x, label, w)


def spread_kernel(transposed, x_ref, label_ref, w_ref, out_ref):
    x = x_ref[...]
    label = label_ref[...]
    product = dot_bt if transposed else dot
    total = None
    for m in range(w_ref.shape[0]):
        part = product(jnp.where(label == m, x, jnp.zeros_like(x)), w_ref[m])
        total = part if total is None else total + part
    out_ref[...] = total.astype(out_ref.dtype)


def routed_spread(x, label, w, tile, transposed, dtype):
    rows, depth = x.shape
    mods = w.shape[0]
    outer = w.shape[1] if transposed else w.shape[2]
    tile = min(tile, outer)
    block = min(rows, 1024)
    if transposed:
        w_spec = pl.BlockSpec((mods, tile, depth), lambda i, j: (0, j, 0))
    else:
        w_spec = pl.BlockSpec((mods, depth, tile), lambda i, j: (0, 0, j))
    return pl.pallas_call(
        functools.partial(spread_kernel, transposed),
        out_shape=jax.ShapeDtypeStruct((rows, outer), dtype),
        grid=(rows // block, outer // tile),
        in_specs=[
            pl.BlockSpec((block, depth), lambda i, j: (i, 0)),
            pl.BlockSpec((block, 1), lambda i, j: (i, 0)),
            w_spec,
        ],
        out_specs=pl.BlockSpec((block, tile), lambda i, j: (i, j)),
        compiler_params=params(),
        cost_estimate=pl.CostEstimate(
            flops=2 * rows * depth * outer * mods, bytes_accessed=2 * mods * depth * outer + 2 * rows * (depth + outer), transcendentals=0
        ),
        name="routed_spread",
    )(x, label, w)


def by_time(x):
    rows, width = x.shape
    return jnp.swapaxes(x.astype(F32).reshape(GROUP, rows // GROUP, width), 0, 1).reshape(rows, width)


def by_sequence(x):
    rows, width = x.shape
    return jnp.swapaxes(x.reshape(rows // GROUP, GROUP, width), 0, 1).reshape(rows, width)


def conv_kernel(inner_ref, label_ref, cw_ref, cb_ref, xw_ref, conv_ref, inner_out_ref, proj_ref, pad_ref):
    rows, channels = inner_ref.shape
    taps = cw_ref.shape[0]
    lead = (taps - 1) * GROUP
    inner = by_time(inner_ref[...])
    inner_out_ref[...] = inner.astype(BF16)
    pad_ref[pl.ds(0, lead), :] = jnp.zeros((lead, channels), F32)
    pad_ref[pl.ds(lead, rows), :] = inner
    conv = jnp.broadcast_to(cb_ref[...].astype(F32), (rows, channels))
    for tap in range(taps):
        conv = conv + cw_ref[pl.ds(tap, 1), :].astype(F32) * pad_ref[pl.ds(tap * GROUP, rows), :]
    conv_ref[...] = conv
    high, low = halves(conv * sigmoid(conv))
    label = label_ref[...]
    parts = [dot_bt(xw_ref[m], high) + dot_bt(xw_ref[m], low) for m in range(xw_ref.shape[0])]
    proj_ref[...] = pick(parts, label)


def conv_forward(inner, label, cw, cb, xw):
    rows, channels = inner.shape
    wide = xw.shape[1]
    lead = (cw.shape[0] - 1) * GROUP
    return pl.pallas_call(
        conv_kernel,
        out_shape=(
            jax.ShapeDtypeStruct((rows, channels), F32),
            jax.ShapeDtypeStruct((rows, channels), BF16),
            jax.ShapeDtypeStruct((wide, rows), F32),
        ),
        scratch_shapes=[pltpu.VMEM((rows + lead, channels), F32)],
        compiler_params=params(),
        name="conv_forward",
    )(inner, label, cw, cb[None, :], xw)


def scan_kernel(
    conv_ref, proj_ref, gate_ref, grad_ref, label_ref, label_row_ref, dtw_ref, dtb_ref, alog_ref, skip_ref,
    gated_ref, dgate_ref, dact_ref, dproj_ref, ddtw_ref, ddtb_ref, dalog_ref, dskip_ref,
    hist, mix, prod, rate, drate, act, step, slope, dout, scanned, ddrive, dstep, dlow,
):
    rows, width = conv_ref.shape
    length = rows // GROUP
    states = alog_ref.shape[0]
    mods, low_width = dtw_ref.shape[0], dtw_ref.shape[1]
    tile = pl.program_id(0)
    label = label_ref[...]

    @pl.when(tile == 0)
    def _():
        prod[...] = jnp.zeros_like(prod)
        dlow[...] = jnp.zeros_like(dlow)
        high, low = halves(proj_ref[pl.ds(low_width, 2 * states), :])
        row = lax.broadcasted_iota(jnp.int32, (2 * states, width), 0)
        for s in range(2 * states):
            spread = (row == s).astype(BF16)
            mix[s] = dot_at(high, spread) + dot_at(low, spread)

    low_high, low_low = halves(proj_ref[pl.ds(0, low_width), :])
    parts = [
        dot_at(low_high, dtw_ref[m]) + dot_at(low_low, dtw_ref[m]) + dtb_ref[pl.ds(m, 1), :].astype(F32) for m in range(mods)
    ]
    speed = pick(parts, label)
    step[...] = jnp.maximum(speed, 0.0) + jnp.log1p(jnp.exp(-jnp.abs(speed)))
    slope[...] = sigmoid(speed)
    conv = conv_ref[...]
    act[...] = conv * sigmoid(conv)
    for s in range(states):
        rate[s] = jnp.broadcast_to(-LOG2E * jnp.exp(alog_ref[pl.ds(s, 1), :].astype(F32)), (GROUP, width))
        drate[s] = jnp.zeros((GROUP, width), F32)
        hist[0, s] = jnp.zeros((GROUP, width), F32)

    def forward(t, state):
        at = pl.ds(pl.multiple_of(t * GROUP, GROUP), GROUP)
        now = step[at, :]
        drive = now * act[at, :]
        total = None
        new = []
        for s in range(states):
            value = jnp.exp2(now * rate[s]) * state[s] + mix[s, at, :] * drive
            hist[t + 1, s] = value
            new.append(value)
            term = mix[states + s, at, :] * value
            total = term if total is None else total + term
        scanned[at, :] = total
        return tuple(new)

    zero = jnp.zeros((GROUP, width), F32)
    lax.fori_loop(0, length, forward, (zero,) * states)

    gate = by_time(gate_ref[...])
    grad = by_time(grad_ref[...])
    soft = sigmoid(gate)
    opened = gate * soft
    skip = skip_ref[...].astype(F32)
    summed = scanned[...] + skip * act[...]
    gated_ref[...] = by_sequence(summed * opened).astype(BF16)
    dgate = grad * summed * (soft + opened * (1.0 - soft))
    dgate_ref[...] = by_sequence(dgate).astype(BF16)
    dsummed = grad * opened
    dout[...] = dsummed
    dskip_ref[...] = jnp.sum(dsummed * act[...], axis=0, keepdims=True)

    def backward(i, carry):
        t = length - 1 - i
        at = pl.ds(pl.multiple_of(t * GROUP, GROUP), GROUP)
        now = step[at, :]
        drive = now * act[at, :]
        out = dout[at, :]
        dd, ds = None, None
        new = []
        for s in range(states):
            decay = jnp.exp2(now * rate[s])
            dstate = carry[s] + mix[states + s, at, :] * out
            prod[states + s, at, :] += out * hist[t + 1, s]
            prod[s, at, :] += dstate * drive
            term = dstate * mix[s, at, :]
            dd = term if dd is None else dd + term
            passed = dstate * decay
            new.append(passed)
            change = passed * hist[t, s]
            term = change * rate[s]
            ds = term if ds is None else ds + term
            drate[s] += change * now
        ddrive[at, :] = dd
        dstep[at, :] = ds
        return tuple(new)

    lax.fori_loop(0, length, backward, (zero,) * states)

    for s in range(states):
        dalog_ref[pl.ds(s, 1), :] = LN2 * jnp.sum(drate[s] * rate[s], axis=0, keepdims=True)
    dact_ref[...] = ddrive[...] * step[...] + skip * dout[...]
    dspeed = (dstep[...] * LN2 + ddrive[...] * act[...]) * slope[...]
    high, low = halves(dspeed)
    parts = [dot_bt(dtw_ref[m], high) + dot_bt(dtw_ref[m], low) for m in range(mods)]
    dlow[...] += pick(parts, label_row_ref[...])
    for m in range(mods):
        own = label == m
        masked = jnp.where(own, dspeed, 0.0)
        high, low = halves(masked)
        ddtw_ref[m] = dot(low_high, high) + dot(low_high, low) + dot(low_low, high)
        ddtb_ref[pl.ds(m, 1), :] = jnp.sum(masked, axis=0, keepdims=True)

    @pl.when(tile == pl.num_programs(0) - 1)
    def _():
        column = lax.broadcasted_iota(jnp.int32, (width, 2 * states), 1)
        sums = jnp.zeros((rows, 2 * states), F32)
        for s in range(2 * states):
            gather = (column == s).astype(BF16)
            high, low = halves(prod[s])
            sums = sums + (dot(high, gather) + dot(low, gather))
        dproj_ref[pl.ds(0, low_width), :] = dlow[...]
        dproj_ref[pl.ds(low_width, 2 * states), :] = sums.T


def scan_both(conv, proj, gate, grad, label, label_row, dtw, dtb, alog, skip):
    rows, channels = conv.shape
    width = min(128, channels)
    length = rows // GROUP
    states = alog.shape[0]
    mods, low_width = dtw.shape[0], dtw.shape[1]
    wide = proj.shape[0]

    def whole(shape):
        return pl.BlockSpec(shape, lambda j: (0,) * len(shape), pipeline_mode=pl.Buffered(1))

    def cut(*shape):
        return pl.BlockSpec(shape + (width,), lambda j: (0,) * len(shape) + (j,))

    plane = (GROUP, width)
    flat = pltpu.VMEM((rows, width), F32)
    return pl.pallas_call(
        scan_kernel,
        out_shape=(
            jax.ShapeDtypeStruct((rows, channels), BF16),
            jax.ShapeDtypeStruct((rows, channels), BF16),
            jax.ShapeDtypeStruct((rows, channels), F32),
            jax.ShapeDtypeStruct((wide, rows), F32),
            jax.ShapeDtypeStruct((mods, low_width, channels), F32),
            jax.ShapeDtypeStruct((mods, channels), F32),
            jax.ShapeDtypeStruct((states, channels), F32),
            jax.ShapeDtypeStruct((1, channels), F32),
        ),
        grid=(channels // width,),
        in_specs=[
            cut(rows), whole((wide, rows)), cut(rows), cut(rows), whole((rows, 1)), whole((1, rows)),
            cut(mods, low_width), cut(mods), cut(states), cut(1),
        ],
        out_specs=(
            cut(rows), cut(rows), cut(rows), whole((wide, rows)), cut(mods, low_width), cut(mods), cut(states), cut(1),
        ),
        scratch_shapes=[
            pltpu.VMEM((length + 1, states) + plane, F32),
            pltpu.VMEM((2 * states, rows, width), F32),
            pltpu.VMEM((2 * states, rows, width), F32),
            pltpu.VMEM((states,) + plane, F32),
            pltpu.VMEM((states,) + plane, F32),
            flat, flat, flat, flat, flat, flat, flat,
            pltpu.VMEM((low_width, rows), F32),
        ],
        compiler_params=params(),
        cost_estimate=pl.CostEstimate(flops=5000 * rows * channels * states, bytes_accessed=20 * rows * channels, transcendentals=0),
        name="scan_both",
    )(conv, proj, gate, grad, label, label_row, dtw, dtb, alog, skip[None, :])


def conv_back_kernel(
    conv_ref, inner_ref, dact_ref, dproj_ref, label_ref, label_row_ref, cw_ref, xw_ref,
    dinner_ref, dxw_ref, dcw_ref, dcb_ref, pad_ref,
):
    rows, channels = conv_ref.shape
    taps = cw_ref.shape[0]
    tail = (taps - 1) * GROUP
    label, label_row = label_ref[...], label_row_ref[...]
    conv = conv_ref[...]
    soft = sigmoid(conv)
    act = conv * soft
    dproj = dproj_ref[...]
    high, low = halves(dproj)
    parts = [dot_at(high, xw_ref[m]) + dot_at(low, xw_ref[m]) for m in range(xw_ref.shape[0])]
    dact = dact_ref[...] + pick(parts, label)
    act_high, act_low = halves(act)
    for m in range(xw_ref.shape[0]):
        high, low = halves(jnp.where(label_row == m, dproj, 0.0))
        dxw_ref[m] = dot(high, act_high) + dot(low, act_high) + dot(high, act_low)
    dconv = dact * (soft + act * (1.0 - soft))
    dcb_ref[...] = jnp.sum(dconv, axis=0, keepdims=True)
    pad_ref[pl.ds(0, rows), :] = dconv
    pad_ref[pl.ds(rows, tail), :] = jnp.zeros((tail, channels), F32)
    inner = inner_ref[...].astype(F32)
    total = None
    for tap in range(taps):
        shift = (taps - 1 - tap) * GROUP
        later = pad_ref[pl.ds(shift, rows), :]
        term = cw_ref[pl.ds(tap, 1), :].astype(F32) * later
        total = term if total is None else total + term
        dcw_ref[pl.ds(tap, 1), :] = jnp.sum(later * inner, axis=0, keepdims=True)
    dinner_ref[...] = by_sequence(total).astype(BF16)


def conv_backward(conv, inner, dact, dproj, label, label_row, cw, xw):
    rows, channels = conv.shape
    mods, wide = xw.shape[0], xw.shape[1]
    taps = cw.shape[0]
    return pl.pallas_call(
        conv_back_kernel,
        out_shape=(
            jax.ShapeDtypeStruct((rows, channels), BF16),
            jax.ShapeDtypeStruct((mods, wide, channels), F32),
            jax.ShapeDtypeStruct((taps, channels), F32),
            jax.ShapeDtypeStruct((1, channels), F32),
        ),
        scratch_shapes=[pltpu.VMEM((rows + (taps - 1) * GROUP, channels), F32)],
        compiler_params=params(),
        name="conv_backward",
    )(conv, inner, dact, dproj, label, label_row, cw, xw)


MESH = pl.DeviceIdType.MESH


def sum_body(chips, x_ref, out_ref, near, mine, far, total, every, other, near_sems, far_sems, back_sems, other_sems):
    wide, rows = x_ref.shape
    half, part = rows // 2, rows // 2 // chips
    tok, ch = lax.axis_index("tok"), lax.axis_index("ch")
    chip, core = ch // 2, ch % 2
    partner = (tok, 2 * chip + 1 - core)
    chips_away = [(tok, 2 * (chip ^ d) + core) for d in range(1, chips)]

    def send(src, dst, sems, device):
        copy = pltpu.make_async_remote_copy(
            src_ref=src, dst_ref=dst, send_sem=sems.at[0], recv_sem=sems.at[1], device_id=device, device_id_type=MESH
        )
        copy.start()
        return copy

    def columns(index, size):
        return pl.ds(pl.multiple_of(index * size, size), size)

    copy = send(x_ref.at[:, columns(1 - core, half)], near, near_sems, partner)
    copy.wait()
    mine[...] = (x_ref[:, columns(core, half)] + near[...]).astype(BF16)
    copies = [
        send(mine.at[:, columns(chip ^ d, part)], far.at[d - 1], far_sems.at[d - 1], chips_away[d - 1])
        for d in range(1, chips)
    ]
    value = mine[:, columns(chip, part)].astype(F32)
    for d, copy in enumerate(copies):
        copy.wait()
        value = value + far[d].astype(F32)
    total[...] = value.astype(BF16)
    copies = [send(total, every.at[d - 1], back_sems.at[d - 1], chips_away[d - 1]) for d in range(1, chips)]
    copies += [send(total, other.at[0], other_sems.at[0], partner)]
    out_ref[:, columns(core * chips + chip, part)] = total[...].astype(F32)
    for d in range(1, chips):
        copies[d - 1].wait()
        copies += [send(every.at[d - 1], other.at[d], other_sems.at[d], partner)]
        out_ref[:, columns(core * chips + (chip ^ d), part)] = every[d - 1].astype(F32)
    for d in range(chips):
        copies[chips - 1 + d].wait()
        out_ref[:, columns((1 - core) * chips + (chip ^ d), part)] = other[d].astype(F32)


def sum_kernel(chips, *refs):
    tok, ch = lax.axis_index("tok"), lax.axis_index("ch")
    barrier = pltpu.get_barrier_semaphore()
    for device in [(tok, ch ^ 1)] + [(tok, ch ^ (2 * d)) for d in range(1, chips)]:
        pl.semaphore_signal(barrier, inc=1, device_id=device, device_id_type=MESH)
    pl.semaphore_wait(barrier, chips)
    sum_body(chips, *refs)


def sum_scratch(wide, rows, chips):
    half, part = rows // 2, rows // 2 // chips
    dma = pltpu.SemaphoreType.DMA
    return [
        pltpu.VMEM((wide, half), F32),
        pltpu.VMEM((wide, half), BF16),
        pltpu.VMEM((chips - 1, wide, part), BF16),
        pltpu.VMEM((wide, part), BF16),
        pltpu.VMEM((chips - 1, wide, part), BF16),
        pltpu.VMEM((chips, wide, part), BF16),
        dma((2,)),
        dma((chips - 1, 2)),
        dma((chips - 1, 2)),
        dma((chips, 2)),
    ]


def sum_over_ch(x, n, collective_id):
    wide, rows = x.shape
    return pl.pallas_call(
        functools.partial(sum_kernel, n // 2),
        out_shape=jax.ShapeDtypeStruct((wide, rows), F32),
        in_specs=[pl.BlockSpec(memory_space=pltpu.VMEM)],
        out_specs=pl.BlockSpec(memory_space=pltpu.VMEM),
        scratch_shapes=sum_scratch(wide, rows, n // 2),
        compiler_params=pltpu.CompilerParams(collective_id=collective_id, has_side_effects=True, vmem_limit_bytes=16 << 20),
        name="sum_over_ch",
    )(x)


def front_kernel(
    chips, input_ref, gain_ref, cot_ref, label_ref, iw_ref, ow_ref, cw_ref, cb_ref, xw_ref,
    scaled_ref, core_cot_ref, near_cot_ref, labels_ref, gate_ref, gated_grad_ref, conv_ref, inner_out_ref, proj_ref,
    own_rows, in_w, out_w, chunk_rows, staged, xz, proj_part, pad,
    in_sem, out_sem, load_sem, own_sem,
    line_send, line_recv, near_send, near_recv, tok_send, tok_recv, diag_send, diag_recv,
    xz_send, xz_recv, lab_send, lab_recv, lab_tok_send, lab_tok_recv, *sum_refs,
):
    n = 2 * chips
    length, deep = input_ref.shape
    group, chunk = n * length, 2 * length
    mods, width = ow_ref.shape[0], ow_ref.shape[1]
    tok, ch = lax.axis_index("tok"), lax.axis_index("ch")
    chip, core = ch // 2, ch % 2

    fetch_in = pltpu.make_async_copy(iw_ref, in_w, in_sem)
    fetch_in.start()
    fetch_out = pltpu.make_async_copy(ow_ref, out_w, out_sem)
    fetch_out.start()

    rows = input_ref[...].astype(F32)
    inverse = lax.rsqrt(jnp.mean(rows * rows, axis=-1, keepdims=True) + 1e-05)
    own_rows[...] = (rows * inverse * gain_ref[...].astype(F32)).astype(BF16)
    labels_ref[tok, ch] = label_ref[...]

    def block(g, device):
        return pl.ds(pl.multiple_of(g * group + device * length, length), length)

    own = (
        pltpu.make_async_copy(own_rows, scaled_ref.at[block(tok, ch)], own_sem.at[0]),
        pltpu.make_async_copy(cot_ref, core_cot_ref.at[pl.ds(pl.multiple_of(chip * length, length), length)], own_sem.at[1]),
    )
    for copy in own:
        copy.start()

    barrier = pltpu.get_barrier_semaphore()
    peers = [(tok, ch ^ e) for e in range(1, n)] + [(tok ^ g, ch) for g in range(1, 4)]
    for device in peers:
        pl.semaphore_signal(barrier, inc=1, device_id=device, device_id_type=MESH)
    pl.semaphore_wait(barrier, len(peers))

    def remote(src, dst, send_sem, recv_sem, device):
        return pltpu.make_async_remote_copy(
            src_ref=src, dst_ref=dst, send_sem=send_sem, recv_sem=recv_sem, device_id=device, device_id_type=MESH
        )

    def arrive(ref, sem):
        pltpu.make_async_copy(ref, ref, sem).wait()

    label_copies = [
        remote(labels_ref.at[tok, ch], labels_ref.at[tok, ch], lab_send.at[e - 1], lab_recv.at[e - 1], (tok, ch ^ e))
        for e in range(1, n)
    ]
    for copy in label_copies:
        copy.start()

    def from_line(x, o):
        if x == 0:
            return scaled_ref.at[block(tok, 2 * o + core)]
        return core_cot_ref.at[pl.ds(pl.multiple_of(o * length, length), length)]

    def line_copy(x, o, side):
        ref = from_line(x, o)
        target = lax.rem(ch + (2 if side == 0 else n - 2), n)
        return remote(ref, ref, line_send.at[x, side, o], line_recv.at[x, o], (tok, target))

    def near_copy(x, o, g):
        if x == 0:
            src = dst = scaled_ref.at[block(tok ^ g, 2 * o + core)]
        else:
            src, dst = from_line(1, o), near_cot_ref.at[pl.ds(pl.multiple_of(o * length, length), length)]
        return remote(src, dst, near_send.at[x, g, o], near_recv.at[x, g, o], (tok, ch ^ 1))

    def tok_copy(o, side):
        ref = scaled_ref.at[block(tok, 2 * o + core)]
        return remote(ref, ref, tok_send.at[side, o], tok_recv.at[side, o], (tok ^ (1 + side), ch))

    def half_block(g, o, side):
        start = g * group + (2 * o + core) * length + side * (length // 2)
        return pl.ds(pl.multiple_of(start, length // 2), length // 2)

    def diag_copy(o, side):
        ref = scaled_ref.at[half_block(tok ^ (1 + side), o, side)]
        return remote(ref, ref, diag_send.at[side, o], diag_recv.at[side, o], (tok ^ (2 - side), ch))

    def goes(o, side):
        return (o <= chip) & (chip < chips - 1) if side == 0 else (o >= chip) & (chip > 0)

    def launch(x, o):
        for side in range(2):
            pl.when(goes(o, side))(line_copy(x, o, side).start)
        near_copy(x, o, 0).start()
        if x == 0:
            for side in range(2):
                tok_copy(o, side).start()

    def accept(x, o):
        arrive(from_line(x, o), line_recv.at[x, o])
        launch(x, o)

    def pass_on(o):
        for side in range(2):
            arrive(scaled_ref.at[block(tok ^ (1 + side), 2 * o + core)], tok_recv.at[side, o])
            diag_copy(o, side).start()
            near_copy(0, o, 1 + side).start()

    def pass_last(o):
        for side in range(2):
            arrive(scaled_ref.at[half_block(tok ^ 3, o, side)], diag_recv.at[side, o])
        near_copy(0, o, 3).start()

    def load(x, o):
        if x == 0:
            arrive(scaled_ref.at[block(tok, 2 * o + 1 - core)], near_recv.at[0, 0, o])
            source = scaled_ref.at[pl.ds(pl.multiple_of(tok * group + o * chunk, chunk), chunk)]
            copies = [pltpu.make_async_copy(source, chunk_rows, load_sem.at[0])]
        else:
            other = near_cot_ref.at[pl.ds(pl.multiple_of(o * length, length), length)]
            arrive(other, near_recv.at[1, 0, o])
            copies = [
                pltpu.make_async_copy(
                    ref, chunk_rows.at[pl.ds(pl.multiple_of(q * length, length), length)], load_sem.at[at]
                )
                for at, (ref, q) in enumerate(((from_line(1, o), core), (other, 1 - core)))
            ]
        for copy in copies:
            copy.start()
        for copy in copies:
            copy.wait()

    def label_column(o):
        return jnp.concatenate(
            [labels_ref[tok, 2 * o + q].astype(F32).T[:, 0:1] for q in range(2)], axis=0
        )

    kind = ch // chips
    pair = ch % chips

    def xz_copies(o, h):
        target = 2 * pair + h
        src = staged.at[o, h]
        dst = xz.at[kind, pl.ds(pl.multiple_of(o * chunk, chunk), chunk)]
        return target, remote(src, dst, xz_send.at[o, h], xz_recv.at[kind, o], (tok, target)), pltpu.make_async_copy(
            src, dst, xz_recv.at[kind, o]
        )

    def project(o):
        load(0, o)
        label = label_column(o)
        for h in range(2):
            x = chunk_rows[...]
            parts = [dot(x, in_w[m, :, pl.ds(h * width, width)]) for m in range(mods)]
            staged[o, h] = pick(parts, label).astype(BF16)
            target, copy, local = xz_copies(o, h)
            pl.when(target != ch)(copy.start)
            pl.when(target == ch)(local.start)

    def project_back(o):
        load(1, o)
        label = label_column(o)
        x = chunk_rows[...]
        parts = [dot_bt(x, out_w[m]) for m in range(mods)]
        gated_grad_ref[pl.ds(pl.multiple_of(o * chunk, chunk), chunk), :] = pick(parts, label).astype(BF16)

    def both_sides(i, fn):
        for o in (chip - i, chip + i):
            pl.when((o >= 0) & (o < chips))(functools.partial(fn, o))

    def every_distance(fn):
        fn(chip)

        def body(i, carry):
            both_sides(i, fn)
            return carry

        lax.fori_loop(1, chips, body, 0)

    own[0].wait()
    launch(0, chip)
    for e in range(1, n):
        arrive(labels_ref.at[tok, ch ^ e], lab_recv.at[e - 1])
    fetch_in.wait()
    project(chip)

    def step(i, carry):
        both_sides(i, functools.partial(accept, 0))
        both_sides(i, project)
        pl.when(i == 1)(functools.partial(pass_on, chip))
        pl.when(i > 1)(functools.partial(both_sides, i - 1, pass_on))
        return carry

    lax.fori_loop(1, chips, step, 0)
    own[1].wait()
    launch(1, chip)
    label_tok = [
        remote(labels_ref.at[tok], labels_ref.at[tok], lab_tok_send.at[g - 1], lab_tok_recv.at[g - 1], (tok ^ g, ch))
        for g in range(1, 4)
    ]
    for copy in label_tok:
        copy.start()
    fetch_out.wait()
    project_back(chip)
    both_sides(chips - 1, pass_on)

    def step_back(i, carry):
        both_sides(i, functools.partial(accept, 1))
        both_sides(i, project_back)
        return carry

    lax.fori_loop(1, chips - 1, step_back, 0)
    every_distance(pass_last)

    for o in range(chips):
        for a in range(2):
            arrive(xz.at[a, pl.ds(o * chunk, chunk)], xz_recv.at[a, o])
    gate_ref[...] = xz[1]
    taps = cw_ref.shape[0]
    lead = (taps - 1) * GROUP
    inner = by_time(xz[0])
    inner_out_ref[...] = inner.astype(BF16)
    pad[pl.ds(0, lead), :] = jnp.zeros((lead, width), F32)
    pad[pl.ds(lead, group), :] = inner
    conv = jnp.broadcast_to(cb_ref[...].astype(F32), (group, width))
    for tap in range(taps):
        conv = conv + cw_ref[pl.ds(tap, 1), :].astype(F32) * pad[pl.ds(tap * GROUP, group), :]
    conv_ref[...] = conv
    act = conv * sigmoid(conv)
    label = jnp.concatenate(
        [jnp.broadcast_to(labels_ref[tok, d].astype(F32).T[:, 0:1], (length, 128)) for d in range(n)], axis=0
    )
    label = jnp.concatenate([by_time(label)] * (width // 128), axis=1)
    total = None
    for m in range(mods):
        high, low = halves(jnp.where(label == m, act, 0.0))
        part = dot_bt(xw_ref[m], high) + dot_bt(xw_ref[m], low)
        total = part if total is None else total + part
    proj_part[...] = total

    both_sides(chips - 1, functools.partial(accept, 1))
    sum_body(chips, proj_part, proj_ref, *sum_refs)
    both_sides(chips - 1, project_back)

    def finish(o, carry):
        for g in range(4):
            if g > 0:
                arrive(scaled_ref.at[block(tok ^ g, 2 * o + 1 - core)], near_recv.at[0, g, o])
            near_copy(0, o, g).wait_send()
        near_copy(1, o, 0).wait_send()
        for side in range(2):
            for x in range(2):
                pl.when(goes(o, side))(line_copy(x, o, side).wait_send)
            tok_copy(o, side).wait_send()
            diag_copy(o, side).wait_send()
        return carry

    lax.fori_loop(0, chips, finish, 0)
    for o in range(chips):
        for h in range(2):
            target, copy, _ = xz_copies(o, h)
            pl.when(target != ch)(copy.wait_send)
    for copy in label_copies:
        copy.wait_send()
    for g in range(1, 4):
        arrive(labels_ref.at[tok ^ g], lab_tok_recv.at[g - 1])
        label_tok[g - 1].wait_send()


def way_in(block_input, gain, cotangent, modality, in_weight, out_weight, conv_weight, conv_bias, x_weight, n, collective_id):
    length, deep = block_input.shape
    mods, width = out_weight.shape[0], out_weight.shape[1]
    group, chips = n * length, n // 2
    wide = x_weight.shape[1]
    lead = (conv_weight.shape[0] - 1) * GROUP
    dma = pltpu.SemaphoreType.DMA
    vmem = pl.BlockSpec(memory_space=pltpu.VMEM)
    any_space = pl.BlockSpec(memory_space=pl.ANY)
    return pl.pallas_call(
        functools.partial(front_kernel, chips),
        out_shape=(
            jax.ShapeDtypeStruct((4 * group, deep), BF16),
            jax.ShapeDtypeStruct((chips * length, deep), BF16),
            jax.ShapeDtypeStruct((chips * length, deep), BF16),
            jax.ShapeDtypeStruct((4, n, 8, length), jnp.int32),
            jax.ShapeDtypeStruct((group, width), BF16),
            jax.ShapeDtypeStruct((group, width), BF16),
            jax.ShapeDtypeStruct((group, width), F32),
            jax.ShapeDtypeStruct((group, width), BF16),
            jax.ShapeDtypeStruct((wide, group), F32),
        ),
        in_specs=[vmem, vmem, any_space, vmem, any_space, any_space, vmem, vmem, vmem],
        out_specs=(any_space, any_space, any_space, vmem, vmem, vmem, vmem, vmem, vmem),
        scratch_shapes=[
            pltpu.VMEM((length, deep), BF16),
            pltpu.VMEM(in_weight.shape, BF16),
            pltpu.VMEM(out_weight.shape, BF16),
            pltpu.VMEM((2 * length, deep), BF16),
            pltpu.VMEM((chips, 2, 2 * length, width), BF16),
            pltpu.VMEM((2, group, width), BF16),
            pltpu.VMEM((wide, group), F32),
            pltpu.VMEM((group + lead, width), F32),
            dma, dma, dma((2,)), dma((2,)),
            dma((2, 2, chips)), dma((2, chips)), dma((2, 4, chips)), dma((2, 4, chips)),
            dma((2, chips)), dma((2, chips)), dma((2, chips)), dma((2, chips)),
            dma((chips, 2)), dma((2, chips)), dma((n - 1,)), dma((n - 1,)), dma((3,)), dma((3,)),
        ] + sum_scratch(wide, group, chips),
        compiler_params=params(collective_id=collective_id, has_side_effects=True),
        cost_estimate=pl.CostEstimate(flops=10**11, bytes_accessed=10**8, transcendentals=0),
        name="way_in",
    )(
        block_input, gain[None, :], cotangent, jnp.broadcast_to(modality[None, :], (8, length)),
        in_weight, out_weight, conv_weight, conv_bias[None, :], x_weight,
    )


def back_kernel(
    chips, dinner_ref, dgate_ref, w_ref, label_ref, input_ref, cot_ref, gain_ref, half_cot_ref,
    xall_ref, row_grad_ref, gain_sum_ref, near_cot_ref,
    weights, sends, near_part, chip_sums, arrived, mine, gain_send, gain_arrived, gain_mine, gain_others,
    w_sem, to_col, from_own, to_tok, from_tok, to_diag, from_diag, to_near, from_near, to_row, from_row, to_gain, from_gain, to_gain_tok, from_gain_tok, cot_sems,
):
    n = 2 * chips
    group, width = dinner_ref.shape
    mods, deep = w_ref.shape[0], w_ref.shape[1]
    length = group // n
    chunk = 2 * length
    tok, ch = lax.axis_index("tok"), lax.axis_index("ch")
    chip, core = ch // 2, ch % 2
    beside, below = tok ^ 1, tok ^ 2

    fetch = pltpu.make_async_copy(w_ref, weights, w_sem)
    fetch.start()

    barrier = pltpu.get_barrier_semaphore()
    peers = [(tok, ch ^ e) for e in range(1, n)] + [(tok ^ g, ch) for g in range(1, 4)]
    for device in peers:
        pl.semaphore_signal(barrier, inc=1, device_id=device, device_id_type=MESH)
    pl.semaphore_wait(barrier, len(peers))

    def remote(src, dst, send_sem, recv_sem, device):
        return pltpu.make_async_remote_copy(
            src_ref=src, dst_ref=dst, send_sem=send_sem, recv_sem=recv_sem, device_id=device, device_id_type=MESH
        )

    def rows_of(index, size):
        return pl.ds(pl.multiple_of(index * size, size), size)

    def all_rows(group_index, chunk_index):
        return pl.ds(pl.multiple_of(group_index * group + chunk_index * chunk, chunk), chunk)

    cot_near = remote(half_cot_ref, near_cot_ref, cot_sems.at[0], cot_sems.at[1], (tok, ch ^ 1))

    order = [2, 3, 1, 0]
    owners = [ch // 2, chips + ch // 2]
    out_copies = []

    def give(j):
        for a, src_ref in enumerate((dinner_ref, dgate_ref)):
            owner = owners[a]
            k = owner // 2 ^ j
            src = src_ref.at[rows_of(k, chunk)]
            dst = xall_ref.at[core, all_rows(tok, k)]
            copy = remote(src, dst, to_col.at[j, a], from_own.at[j, core], (tok, owner))
            local = pltpu.make_async_copy(src, dst, from_own.at[j, core])
            pl.when(owner != ch)(copy.start)
            pl.when(owner == ch)(local.start)
            out_copies.append((owner, copy))

    give(order[0])
    give(order[1])
    fetch.wait()
    cot_near.start()
    tok_copies, row_copies, diag_copies, near_copies = [], [], [], []

    def pass_on(j):
        k = chip ^ j
        for side, (source, target) in enumerate(((beside, below), (below, beside))):
            whole = xall_ref.at[:, all_rows(source, k)]
            pltpu.make_async_copy(whole, whole, from_tok.at[side, j]).wait()
            part = xall_ref.at[side, all_rows(source, k)]
            copy = remote(part, part, to_diag.at[side, j], from_diag.at[side, j], (target, ch))
            copy.start()
            diag_copies.append(copy)

    def both_cores(j):
        pltpu.make_async_copy(near_part.at[j], near_part.at[j], from_near.at[j]).wait()
        value = sends[j, rows_of(core, length), :].astype(F32) + near_part[j].astype(F32)
        if j == 0:
            mine[...] = value
        else:
            chip_sums[j - 1] = value.astype(BF16)
            target = 2 * (chip ^ j) + core
            copy = remote(chip_sums.at[j - 1], arrived.at[j - 1], to_row.at[j - 1], from_row.at[j - 1], (tok, target))
            copy.start()
            row_copies.append(copy)

    for at, j in enumerate(order):
        k = chip ^ j
        for h in range(2):
            half = xall_ref.at[h, all_rows(tok, k)]
            pltpu.make_async_copy(half, half, from_own.at[j, h]).wait()
        whole = xall_ref.at[:, all_rows(tok, k)]
        for side, target in enumerate((beside, below)):
            copy = remote(whole, whole, to_tok.at[side, j], from_tok.at[side, j], (target, ch))
            copy.start()
            tok_copies.append(copy)
        if at + 2 < chips:
            give(order[at + 2])
        label = label_ref[rows_of(k, chunk), :]
        halves_of = [xall_ref[h, all_rows(tok, k), :] for h in range(2)]
        tile = min(deep, 512)

        def product(i, carry, label=label, halves_of=halves_of, j=j):
            at = pl.ds(pl.multiple_of(i * tile, tile), tile)
            total = None
            for m in range(mods):
                for h in range(2):
                    x = jnp.where(label == m, halves_of[h], jnp.zeros_like(halves_of[h]))
                    part = dot_bt(x, weights[m, at, pl.ds(h * width, width)])
                    total = part if total is None else total + part
            sends[j, :, at] = total.astype(BF16)
            return carry

        lax.fori_loop(0, deep // tile, product, 0)
        copy = remote(
            sends.at[j, rows_of(1 - core, length)], near_part.at[j], to_near.at[j], from_near.at[j], (tok, ch ^ 1)
        )
        copy.start()
        near_copies.append(copy)
        if at >= 1:
            pass_on(order[at - 1])
            both_cores(order[at - 1])
    pass_on(order[-1])
    both_cores(order[-1])

    total = mine[...]
    for e in range(chips - 1):
        pltpu.make_async_copy(arrived.at[e], arrived.at[e], from_row.at[e]).wait()
        total = total + arrived[e].astype(F32)
    rows = input_ref[...].astype(F32)
    inverse = lax.rsqrt(jnp.mean(rows * rows, axis=-1, keepdims=True) + 1e-05)
    normed = rows * inverse
    ng = total * gain_ref[...].astype(F32)
    row_grad_ref[...] = cot_ref[...].astype(F32) + inverse * (
        ng - normed * jnp.mean(ng * normed, axis=-1, keepdims=True)
    )
    own = deep // n
    gain_term = jnp.sum(total * normed, axis=0, keepdims=True)
    for d in range(n):
        gain_send[d] = jnp.broadcast_to(gain_term[:, d * own : (d + 1) * own], (8, own))
    gain_copies = []
    for e in range(1, n):
        copy = remote(gain_send.at[ch ^ e], gain_arrived.at[e - 1], to_gain.at[e - 1], from_gain.at[e - 1], (tok, ch ^ e))
        copy.start()
        gain_copies.append(copy)
    value = gain_send[ch]
    for e in range(1, n):
        gain_copies[e - 1].wait()
        value = value + gain_arrived[e - 1]
    gain_mine[...] = value
    gain_copies = []
    for g in range(1, 4):
        copy = remote(gain_mine, gain_others.at[g - 1], to_gain_tok.at[g - 1], from_gain_tok.at[g - 1], (tok ^ g, ch))
        copy.start()
        gain_copies.append(copy)
    for copy in gain_copies:
        copy.wait()
    even, odd = gain_mine[...] + gain_others[0], gain_others[1] + gain_others[2]
    gain_sum_ref[...] = even + odd

    for j in range(chips):
        for side in range(2):
            part = xall_ref.at[side, all_rows(tok ^ 3, chip ^ j)]
            pltpu.make_async_copy(part, part, from_diag.at[side, j]).wait()
    for owner, copy in out_copies:
        pl.when(owner != ch)(copy.wait_send)
    for copy in tok_copies + diag_copies + row_copies + near_copies:
        copy.wait_send()
    cot_near.wait()


def way_back(dinner, dgate, w, label, block_input, cotangent, gain, half_cot, n, collective_id):
    group, width = dinner.shape
    mods, deep, _ = w.shape
    chips, length = n // 2, group // n
    dma = pltpu.SemaphoreType.DMA
    vmem = pl.BlockSpec(memory_space=pltpu.VMEM)
    any_space = pl.BlockSpec(memory_space=pl.ANY)
    return pl.pallas_call(
        functools.partial(back_kernel, chips),
        out_shape=(
            jax.ShapeDtypeStruct((2, 4 * group, width), BF16),
            jax.ShapeDtypeStruct((length, deep), F32),
            jax.ShapeDtypeStruct((8, deep // n), F32),
            jax.ShapeDtypeStruct(half_cot.shape, BF16),
        ),
        in_specs=[vmem, vmem, any_space, vmem, vmem, vmem, vmem, any_space],
        out_specs=(vmem, vmem, vmem, any_space),
        scratch_shapes=[
            pltpu.VMEM(w.shape, BF16),
            pltpu.VMEM((chips, 2 * length, deep), BF16),
            pltpu.VMEM((chips, length, deep), BF16),
            pltpu.VMEM((chips - 1, length, deep), BF16),
            pltpu.VMEM((chips - 1, length, deep), BF16),
            pltpu.VMEM((length, deep), F32),
            pltpu.VMEM((n, 8, deep // n), F32),
            pltpu.VMEM((n - 1, 8, deep // n), F32),
            pltpu.VMEM((8, deep // n), F32),
            pltpu.VMEM((3, 8, deep // n), F32),
            dma, dma((chips, 2)), dma((chips, 2)), dma((2, chips)), dma((2, chips)), dma((2, chips)), dma((2, chips)),
            dma((chips,)), dma((chips,)), dma((chips - 1,)), dma((chips - 1,)), dma((n - 1,)), dma((n - 1,)), dma((3,)), dma((3,)), dma((2,)),
        ],
        compiler_params=params(collective_id=collective_id, has_side_effects=True),
        cost_estimate=pl.CostEstimate(flops=10**11, bytes_accessed=10**8, transcendentals=0),
        name="way_back",
    )(dinner, dgate, w, label, block_input, cotangent, gain[None, :], half_cot)


def grad_two_kernel(left_ref, right_ref, other_ref, label_ref, out_ref):
    half = right_ref.shape[0]
    turned, label = left_ref[...].T, label_ref[...]
    for m in range(out_ref.shape[0]):
        masked = jnp.where(label == m, turned, jnp.zeros_like(turned))
        out_ref[m] = dot(masked[:, :half], right_ref[...]) + dot(masked[:, half:], other_ref[...])


def weight_grad_two(left, right, other, label, mods, tile):
    rows, deep = left.shape
    half, wide = right.shape
    whole = pl.BlockSpec((half, wide), lambda i: (0, 0), pipeline_mode=pl.Buffered(1))
    return pl.pallas_call(
        grad_two_kernel,
        out_shape=jax.ShapeDtypeStruct((mods, deep, wide), F32),
        grid=(deep // tile,),
        in_specs=[pl.BlockSpec((rows, tile), lambda i: (0, i)), whole, whole, pl.BlockSpec((1, rows), lambda i: (0, 0))],
        out_specs=pl.BlockSpec((mods, tile, wide), lambda i: (0, i, 0)),
        compiler_params=params(),
        cost_estimate=pl.CostEstimate(
            flops=2 * mods * rows * deep * wide,
            bytes_accessed=2 * rows * (deep + wide) + 4 * mods * deep * wide,
            transcendentals=0,
        ),
        name="weight_grad_two",
    )(left, right, other, label)


def grad_kernel(left_ref, right_ref, label_ref, out_ref):
    left, label = left_ref[...], label_ref[...]
    wide = right_ref.shape[2]
    turned = left.T
    for m in range(out_ref.shape[0]):
        masked = jnp.where(label == m, turned, jnp.zeros_like(turned))
        for h in range(right_ref.shape[0]):
            out_ref[m, :, pl.ds(h * wide, wide)] = dot(masked, right_ref[h])


def grad_part_kernel(left_ref, right_ref, label_ref, out_ref):
    left, label = left_ref[...], label_ref[...]
    wide = right_ref.shape[2]
    turned = left.T
    first = pl.program_id(1) == 0
    for m in range(out_ref.shape[0]):
        masked = jnp.where(label == m, turned, jnp.zeros_like(turned))
        for h in range(right_ref.shape[0]):
            at = pl.ds(h * wide, wide)
            part = dot(masked, right_ref[h])
            out_ref[m, :, at] = jnp.where(first, part, out_ref[m, :, at] + part)


def weight_grad(left, right, label, mods, tile):
    rows, deep = left.shape
    wide = right.shape[0] * right.shape[2]
    block = min(rows, 4096)
    tile = min(tile, deep)
    return pl.pallas_call(
        grad_kernel if block == rows else grad_part_kernel,
        out_shape=jax.ShapeDtypeStruct((mods, deep, wide), F32),
        grid=(deep // tile, rows // block),
        in_specs=[
            pl.BlockSpec((block, tile), lambda i, j: (j, i)),
            pl.BlockSpec((right.shape[0], block, right.shape[2]), lambda i, j: (0, j, 0)),
            pl.BlockSpec((1, block), lambda i, j: (0, j)),
        ],
        out_specs=pl.BlockSpec((mods, tile, wide), lambda i, j: (0, i, 0)),
        compiler_params=params(),
        cost_estimate=pl.CostEstimate(
            flops=2 * mods * rows * deep * wide,
            bytes_accessed=2 * rows * (deep + wide) + 4 * mods * deep * wide,
            transcendentals=0,
        ),
        name="weight_grad",
    )(left, right, label)


def by_groups(fn, count, arrays, axes, joined):
    if count == 1:
        return fn(*arrays)

    def cut(a, axis, i):
        size = a.shape[axis] // count
        return lax.slice_in_dim(a, i * size, (i + 1) * size, axis=axis)

    outs = [fn(*(cut(a, axis, i) for a, axis in zip(arrays, axes, strict=True))) for i in range(count)]
    return tuple(
        jnp.concatenate(values, axis=joined[at]) if at < len(joined) else functools.reduce(jnp.add, values)
        for at, values in enumerate(zip(*outs, strict=True))
    )


def exchange_pairs(n):
    half = n // 2
    first = [(c, 2 * c) if c < half else (c, 2 * (c - half) + 1) for c in range(n)]
    second = [(c, 2 * c + 1) if c < half else (c, 2 * (c - half)) for c in range(n)]
    return first, second


def to_owners(xz, n):
    first, second = exchange_pairs(n)
    c = lax.axis_index("ch")
    width = xz.shape[1] // 2
    left, right = xz[:, :width], xz[:, width:]
    lower = c < n // 2
    one = lax.ppermute(jnp.where(lower, left, right), "ch", first)
    two = lax.ppermute(jnp.where(lower, right, left), "ch", second)
    even = c % 2 == 0
    return jnp.where(even, one, two), jnp.where(even, two, one)


def to_columns(dinner, dgate, n):
    first, second = exchange_pairs(n)
    c = lax.axis_index("ch")
    even = c % 2 == 0
    one = lax.ppermute(jnp.where(even, dinner, dgate), "ch", [(b, a) for a, b in first])
    two = lax.ppermute(jnp.where(even, dgate, dinner), "ch", [(b, a) for a, b in second])
    lower = c < n // 2
    return jnp.concatenate([jnp.where(lower, one, two), jnp.where(lower, two, one)], axis=1)


def on_device(
    n,
    block_input,
    norm_gain,
    in_weight,
    x_weight,
    dt_weight,
    dt_bias,
    conv_weight,
    conv_bias,
    a_log,
    skip_gain,
    out_weight,
    modality,
    cotangent,
):
    mods = in_weight.shape[0]
    length = block_input.shape[0]
    count = n // GROUP
    fast = n == GROUP and lax.axis_size("tok") == 4 and length % 128 == 0
    rows_float = block_input.astype(F32)
    gain = norm_gain.astype(F32)
    inverse = lax.rsqrt(jnp.mean(rows_float * rows_float, axis=-1, keepdims=True) + 1e-05)
    normed = rows_float * inverse
    scaled = (normed * gain[None, :]).astype(BF16)

    token_group = n * length
    if fast:
        every_scaled, core_cot, _, labels, gate, gated_grad, conv, inner_by_time, proj = way_in(
            block_input, norm_gain, cotangent, modality, in_weight, out_weight, conv_weight, conv_bias, x_weight, n, 0
        )
        every_label = labels[:, :, 0, :].reshape(4 * token_group)
        half_cot = lax.all_gather(core_cot, "tok", axis=0, tiled=False)
    else:
        every_label = lax.all_gather(modality, ("tok", "ch"), axis=0, tiled=True)
    group_label = lax.dynamic_slice_in_dim(every_label, lax.axis_index("tok") * token_group, token_group, 0)
    label = group_label[:, None]
    label_by_time = group_label.reshape(count, GROUP, length).transpose(0, 2, 1).reshape(token_group, 1)
    label_row = label_by_time.reshape(1, token_group)

    if not fast:
        group_rows = lax.all_gather(scaled, "ch", axis=0, tiled=True)
        every_scaled = lax.all_gather(scaled, ("tok", "ch"), axis=0, tiled=True)
        every_cot = lax.all_gather(cotangent, ("tok", "ch"), axis=0, tiled=True)
        xz = routed_select(group_rows, label, in_weight, 256, False)
        inner, gate = to_owners(xz, n)
        group_cot = lax.all_gather(cotangent, "ch", axis=0, tiled=True)
        gated_grad = routed_select(group_cot, label, out_weight, 128, True)
        conv, inner_by_time, proj_part = by_groups(
            lambda a, b: conv_forward(a, b, conv_weight, conv_bias, x_weight), count, (inner, label_row), (0, 1), (0, 0, 1)
        )
        proj = lax.psum(proj_part, "ch")

    gated, dgate, dact, dproj_part, ddtw, ddtb, dalog, dskip = by_groups(
        lambda a, b, c, d, e, f: scan_both(a, b, c, d, e, f, dt_weight, dt_bias, a_log, skip_gain),
        count,
        (conv, proj, gate, gated_grad, label_by_time, label_row),
        (0, 1, 0, 0, 0, 1),
        (0, 0, 0, 1),
    )
    dproj = sum_over_ch(dproj_part, n, 1) if fast else lax.psum(dproj_part, "ch")

    dinner, dxw, dcw, dcb = by_groups(
        lambda a, b, c, d, e, f: conv_backward(a, b, c, d, e, f, conv_weight, x_weight),
        count,
        (conv, inner_by_time, dact, dproj, label_by_time, label_row),
        (0, 0, 0, 1, 0, 1),
        (0,),
    )
    every_label = every_label[None, :]
    if fast:
        half_cot = half_cot.reshape(2 * token_group, half_cot.shape[-1])
        every_grad, row_grad, gain_grad, near_cot = way_back(
            dinner, dgate, in_weight, label, block_input, cotangent, norm_gain, half_cot, n, 2
        )
        gain_grad = gain_grad[0]
    else:
        xz_grad = to_columns(dinner, dgate, n)
        scaled_part = routed_spread(xz_grad, label, in_weight, 256, True, BF16)
        scaled_grad = lax.psum_scatter(scaled_part, "ch", scatter_dimension=0, tiled=True).astype(F32)
        gain_grad = lax.psum_scatter(jnp.sum(scaled_grad * normed, axis=0), "ch", scatter_dimension=0, tiled=True)
        ng = scaled_grad * gain[None, :]
        row_grad = cotangent.astype(F32) + inverse * (ng - normed * jnp.mean(ng * normed, axis=-1, keepdims=True))
        every_grad = lax.all_gather(xz_grad, "tok", axis=0, tiled=True)[None]

    small = (dxw, ddtw, ddtb, dcw, dcb, dalog, dskip)
    every_gated = lax.all_gather(gated, "tok", axis=0, tiled=True)
    if fast:
        gated, row_grad, small = lax.optimization_barrier((gated, row_grad, small))
    branch_part = routed_spread(gated, label, out_weight, 512, False, BF16)
    branch = lax.psum_scatter(branch_part, "ch", scatter_dimension=0, tiled=True).astype(F32)
    block_out = (rows_float + branch).astype(BF16)
    if fast:
        core = lax.axis_index("ch") % 2

        def own_first(value):
            halved = value.reshape((-1, 2, length) + value.shape[1:])
            swapped = jnp.where(core == 0, halved, halved[:, ::-1])
            return jnp.moveaxis(swapped, 1, 0).reshape(value.shape)

        out_weight_grad = weight_grad_two(
            own_first(every_gated), half_cot, near_cot, own_first(every_label[0])[None, :], mods, 128
        )
    else:
        out_weight_grad = weight_grad(every_gated, every_cot[None], every_label, mods, 128)
    in_weight_grad = weight_grad(every_scaled, every_grad, every_label, mods, 256)
    if not fast:
        gain_grad = lax.psum(gain_grad, "tok")
    flat = [value.reshape(-1, value.shape[-1]) for value in small]
    total = lax.psum(jnp.concatenate(flat, axis=0), "tok")
    start, sums = 0, []
    for value, rows in zip(small, flat, strict=True):
        sums.append(lax.slice_in_dim(total, start, start + rows.shape[0], axis=0).reshape(value.shape))
        start += rows.shape[0]
    dxw, ddtw, ddtb, dcw, dcb, dalog, dskip = sums
    return (
        block_out,
        row_grad,
        gain_grad,
        in_weight_grad,
        dxw,
        ddtw,
        ddtb,
        dcw,
        dcb[0],
        dalog,
        dskip[0],
        out_weight_grad,
    )


def solution(mesh):
    placed = (
        P(("tok", "ch"), None),
        P(),
        P(None, None, "ch"),
        P(None, None, "ch"),
        P(None, None, "ch"),
        P(None, "ch"),
        P(None, "ch"),
        P("ch"),
        P(None, "ch"),
        P("ch"),
        P(None, "ch", None),
        P(("tok", "ch")),
        P(("tok", "ch"), None),
    )
    return jax.shard_map(
        functools.partial(on_device, mesh.shape["ch"]),
        mesh=mesh,
        in_specs=placed,
        out_specs=(
            P(("tok", "ch"), None),
            P(("tok", "ch"), None),
            P("ch"),
            P(None, None, "ch"),
            P(None, None, "ch"),
            P(None, None, "ch"),
            P(None, "ch"),
            P(None, "ch"),
            P("ch"),
            P(None, "ch"),
            P("ch"),
            P(None, "ch", None),
        ),
        check_vma=False,
    )
```

```python
import functools
import math

import jax
import jax.numpy as jnp
from jax import lax
from jax.experimental import pallas as pl
from jax.experimental.pallas import tpu as pltpu
from jax.sharding import PartitionSpec as P

F32 = jnp.float32
BF16 = jnp.bfloat16
LOG2E = math.log2(math.e)
LN2 = math.log(2.0)
GROUP = 8
VMEM_LIMIT = 58 << 20


def params(**kw):
    return pltpu.CompilerParams(vmem_limit_bytes=VMEM_LIMIT, **kw)


def dot(a, b):
    return lax.dot_general(a, b, (((1,), (0,)), ((), ())), preferred_element_type=F32)


def dot_bt(a, b):
    return lax.dot_general(a, b, (((1,), (1,)), ((), ())), preferred_element_type=F32)


def dot_at(a, b):
    return lax.dot_general(a, b, (((0,), (0,)), ((), ())), preferred_element_type=F32)


def halves(x):
    high = x.astype(BF16)
    return high, (x - high.astype(F32)).astype(BF16)


def pick(parts, label):
    total = parts[-1]
    for index in range(len(parts) - 2, -1, -1):
        total = jnp.where(label == index, parts[index], total)
    return total


def sigmoid(x):
    return 0.5 * jnp.tanh(0.5 * x) + 0.5


def select_kernel(transposed, x_ref, label_ref, w_ref, out_ref):
    x = x_ref[...]
    label = label_ref[...]
    product = dot_bt if transposed else dot
    parts = [product(x, w_ref[m]) for m in range(w_ref.shape[0])]
    out_ref[...] = pick(parts, label).astype(out_ref.dtype)


def routed_select(x, label, w, tile, transposed):
    rows, depth = x.shape
    mods = w.shape[0]
    outer = w.shape[1] if transposed else w.shape[2]
    tile = min(tile, outer)
    block = min(rows, 1024)
    if transposed:
        w_spec = pl.BlockSpec((mods, tile, depth), lambda i, j: (0, j, 0))
    else:
        w_spec = pl.BlockSpec((mods, depth, tile), lambda i, j: (0, 0, j))
    return pl.pallas_call(
        functools.partial(select_kernel, transposed),
        out_shape=jax.ShapeDtypeStruct((rows, outer), BF16),
        grid=(rows // block, outer // tile),
        in_specs=[
            pl.BlockSpec((block, depth), lambda i, j: (i, 0)),
            pl.BlockSpec((block, 1), lambda i, j: (i, 0)),
            w_spec,
        ],
        out_specs=pl.BlockSpec((block, tile), lambda i, j: (i, j)),
        compiler_params=params(),
        cost_estimate=pl.CostEstimate(
            flops=2 * rows * depth * outer * mods, bytes_accessed=2 * mods * depth * outer + 2 * rows * (depth + outer), transcendentals=0
        ),
        name="routed_select",
    )(x, label, w)


def spread_kernel(transposed, x_ref, label_ref, w_ref, out_ref):
    x = x_ref[...]
    label = label_ref[...]
    product = dot_bt if transposed else dot
    total = None
    for m in range(w_ref.shape[0]):
        part = product(jnp.where(label == m, x, jnp.zeros_like(x)), w_ref[m])
        total = part if total is None else total + part
    out_ref[...] = total.astype(out_ref.dtype)


def routed_spread(x, label, w, tile, transposed, dtype):
    rows, depth = x.shape
    mods = w.shape[0]
    outer = w.shape[1] if transposed else w.shape[2]
    tile = min(tile, outer)
    block = min(rows, 1024)
    if transposed:
        w_spec = pl.BlockSpec((mods, tile, depth), lambda i, j: (0, j, 0))
    else:
        w_spec = pl.BlockSpec((mods, depth, tile), lambda i, j: (0, 0, j))
    return pl.pallas_call(
        functools.partial(spread_kernel, transposed),
        out_shape=jax.ShapeDtypeStruct((rows, outer), dtype),
        grid=(rows // block, outer // tile),
        in_specs=[
            pl.BlockSpec((block, depth), lambda i, j: (i, 0)),
            pl.BlockSpec((block, 1), lambda i, j: (i, 0)),
            w_spec,
        ],
        out_specs=pl.BlockSpec((block, tile), lambda i, j: (i, j)),
        compiler_params=params(),
        cost_estimate=pl.CostEstimate(
            flops=2 * rows * depth * outer * mods, bytes_accessed=2 * mods * depth * outer + 2 * rows * (depth + outer), transcendentals=0
        ),
        name="routed_spread",
    )(x, label, w)


def by_time(x):
    rows, width = x.shape
    return jnp.swapaxes(x.astype(F32).reshape(GROUP, rows // GROUP, width), 0, 1).reshape(rows, width)


def by_sequence(x):
    rows, width = x.shape
    return jnp.swapaxes(x.reshape(rows // GROUP, GROUP, width), 0, 1).reshape(rows, width)


def conv_kernel(inner_ref, label_ref, cw_ref, cb_ref, xw_ref, conv_ref, inner_out_ref, proj_ref, pad_ref):
    rows, channels = inner_ref.shape
    taps = cw_ref.shape[0]
    lead = (taps - 1) * GROUP
    inner = by_time(inner_ref[...])
    inner_out_ref[...] = inner.astype(BF16)
    pad_ref[pl.ds(0, lead), :] = jnp.zeros((lead, channels), F32)
    pad_ref[pl.ds(lead, rows), :] = inner
    conv = jnp.broadcast_to(cb_ref[...].astype(F32), (rows, channels))
    for tap in range(taps):
        conv = conv + cw_ref[pl.ds(tap, 1), :].astype(F32) * pad_ref[pl.ds(tap * GROUP, rows), :]
    conv_ref[...] = conv
    high, low = halves(conv * sigmoid(conv))
    label = label_ref[...]
    parts = [dot_bt(xw_ref[m], high) + dot_bt(xw_ref[m], low) for m in range(xw_ref.shape[0])]
    proj_ref[...] = pick(parts, label)


def conv_forward(inner, label, cw, cb, xw):
    rows, channels = inner.shape
    wide = xw.shape[1]
    lead = (cw.shape[0] - 1) * GROUP
    return pl.pallas_call(
        conv_kernel,
        out_shape=(
            jax.ShapeDtypeStruct((rows, channels), F32),
            jax.ShapeDtypeStruct((rows, channels), BF16),
            jax.ShapeDtypeStruct((wide, rows), F32),
        ),
        scratch_shapes=[pltpu.VMEM((rows + lead, channels), F32)],
        compiler_params=params(),
        name="conv_forward",
    )(inner, label, cw, cb[None, :], xw)


def scan_kernel(
    conv_ref, proj_ref, gate_ref, grad_ref, label_ref, dtw_ref, dtb_ref, alog_ref, skip_ref,
    gated_ref, dgate_ref, dact_ref, dproj_ref, ddtw_ref, ddtb_ref, dalog_ref, dskip_ref,
    hist, mix, prod, rate, act, step, slope, dout, scanned, dstep, dlow, low_turned, low_rank, label,
):
    rows, width = conv_ref.shape
    length = rows // GROUP
    states = alog_ref.shape[0]
    mods, low_width = dtw_ref.shape[0], dtw_ref.shape[1]
    tile = pl.program_id(0)
    ddrive = scanned

    @pl.when(tile == 0)
    def _():
        prod[...] = jnp.zeros_like(prod)
        dlow[...] = jnp.zeros_like(dlow)
        label[...] = jnp.broadcast_to(label_ref[...], (rows, width))
        low_rank[...] = proj_ref[pl.ds(0, low_width), :].astype(BF16)
        low_turned[...] = proj_ref[pl.ds(0, low_width), :].T.astype(BF16)
        turned = proj_ref[pl.ds(low_width, 2 * states), :].T.astype(BF16)
        row = lax.broadcasted_iota(jnp.int32, (2 * states, 2 * width), 0)
        column = lax.broadcasted_iota(jnp.int32, (2 * states, 2 * width), 1)
        for s in range(0, 2 * states, 2):
            spread = dot(turned, (row == s + (column >= width).astype(jnp.int32)).astype(BF16))
            mix[s] = spread[:, :width]
            mix[s + 1] = spread[:, width:]

    kind = label[...]
    parts = [dot(low_turned[...], dtw_ref[m]) + dtb_ref[pl.ds(m, 1), :].astype(F32) for m in range(mods)]
    speed = pick(parts, kind)
    step[...] = jnp.maximum(speed, 0.0) + jnp.log1p(jnp.exp(-jnp.abs(speed)))
    slope[...] = sigmoid(speed)
    conv = conv_ref[...]
    act[...] = conv * sigmoid(conv)
    for s in range(states):
        rate[s] = jnp.broadcast_to(-LOG2E * jnp.exp(alog_ref[pl.ds(s, 1), :].astype(F32)), (GROUP, width))
        hist[0, s] = jnp.zeros((GROUP, width), F32)

    def forward(t, state):
        at = pl.ds(pl.multiple_of(t * GROUP, GROUP), GROUP)
        now = step[at, :]
        drive = now * act[at, :]
        total = None
        new = []
        for s in range(states):
            value = jnp.exp2(now * rate[s]) * state[s] + mix[s, at, :] * drive
            hist[t + 1, s] = value
            new.append(value)
            term = mix[states + s, at, :] * value
            total = term if total is None else total + term
        scanned[at, :] = total
        return tuple(new)

    zero = jnp.zeros((GROUP, width), F32)
    lax.fori_loop(0, length, forward, (zero,) * states, unroll=8)

    gate = by_time(gate_ref[...])
    grad = by_time(grad_ref[...])
    soft = sigmoid(gate)
    opened = gate * soft
    skip = skip_ref[...].astype(F32)
    summed = scanned[...] + skip * act[...]
    gated_ref[...] = by_sequence(summed * opened).astype(BF16)
    dgate = grad * summed * (soft + opened * (1.0 - soft))
    dgate_ref[...] = by_sequence(dgate).astype(BF16)
    dsummed = grad * opened
    dout[...] = dsummed
    dskip_ref[...] = jnp.sum(dsummed * act[...], axis=0, keepdims=True)

    def backward(i, carry):
        t = length - 1 - i
        at = pl.ds(pl.multiple_of(t * GROUP, GROUP), GROUP)
        now = step[at, :]
        drive = now * act[at, :]
        out = dout[at, :]
        dd, ds = None, None
        new, drates = [], []
        for s in range(states):
            decay = jnp.exp2(now * rate[s])
            dstate = carry[s] + mix[states + s, at, :] * out
            prod[states + s, at, :] += out * hist[t + 1, s]
            prod[s, at, :] += dstate * drive
            term = dstate * mix[s, at, :]
            dd = term if dd is None else dd + term
            passed = dstate * decay
            new.append(passed)
            change = passed * hist[t, s]
            term = change * rate[s]
            ds = term if ds is None else ds + term
            drates.append(carry[states + s] + change * now)
        ddrive[at, :] = dd
        dstep[at, :] = ds
        return tuple(new + drates)

    final = lax.fori_loop(0, length, backward, (zero,) * (2 * states), unroll=4)

    for s in range(states):
        dalog_ref[pl.ds(s, 1), :] = LN2 * jnp.sum(final[states + s] * rate[s], axis=0, keepdims=True)
    dact_ref[...] = ddrive[...] * step[...] + skip * dout[...]
    dspeed = (dstep[...] * LN2 + ddrive[...] * act[...]) * slope[...]
    rounded = dspeed.astype(BF16)
    of_rank = kind if width == low_width else label_ref[...]
    dlow[...] += pick([dot_bt(rounded, dtw_ref[m]) for m in range(mods)], of_rank)
    for m in range(mods):
        own = kind == m
        masked = jnp.where(own, dspeed, 0.0)
        ddtw_ref[m] = dot(low_rank[...], masked.astype(BF16))
        ddtb_ref[pl.ds(m, 1), :] = jnp.sum(masked, axis=0, keepdims=True)

    @pl.when(tile == pl.num_programs(0) - 1)
    def _():
        column = lax.broadcasted_iota(jnp.int32, (width, 2 * states), 1)
        sums = jnp.zeros((rows, 2 * states), F32)
        for s in range(2 * states):
            sums = sums + dot(prod[s].astype(BF16), (column == s).astype(BF16))
        dproj_ref[pl.ds(0, low_width), :] = dlow[...].T
        dproj_ref[pl.ds(low_width, 2 * states), :] = sums.T


def scan_both(conv, proj, gate, grad, label, dtw, dtb, alog, skip):
    rows, channels = conv.shape
    width = min(128, channels)
    length = rows // GROUP
    states = alog.shape[0]
    mods, low_width = dtw.shape[0], dtw.shape[1]
    wide = proj.shape[0]

    def whole(shape):
        return pl.BlockSpec(shape, lambda j: (0,) * len(shape), pipeline_mode=pl.Buffered(1))

    def cut(*shape):
        return pl.BlockSpec(shape + (width,), lambda j: (0,) * len(shape) + (j,))

    plane = (GROUP, width)
    flat = pltpu.VMEM((rows, width), F32)
    return pl.pallas_call(
        scan_kernel,
        out_shape=(
            jax.ShapeDtypeStruct((rows, channels), BF16),
            jax.ShapeDtypeStruct((rows, channels), BF16),
            jax.ShapeDtypeStruct((rows, channels), F32),
            jax.ShapeDtypeStruct((wide, rows), F32),
            jax.ShapeDtypeStruct((mods, low_width, channels), F32),
            jax.ShapeDtypeStruct((mods, channels), F32),
            jax.ShapeDtypeStruct((states, channels), F32),
            jax.ShapeDtypeStruct((1, channels), F32),
        ),
        grid=(channels // width,),
        in_specs=[
            cut(rows), whole((wide, rows)), cut(rows), cut(rows), whole((rows, 1)),
            cut(mods, low_width), cut(mods), cut(states), cut(1),
        ],
        out_specs=(
            cut(rows), cut(rows), cut(rows), whole((wide, rows)), cut(mods, low_width), cut(mods), cut(states), cut(1),
        ),
        scratch_shapes=[
            pltpu.VMEM((length + 1, states) + plane, F32),
            pltpu.VMEM((2 * states, rows, width), F32),
            pltpu.VMEM((2 * states, rows, width), F32),
            pltpu.VMEM((states,) + plane, F32),
            flat, flat, flat, flat, flat, flat,
            pltpu.VMEM((rows, low_width), F32),
            pltpu.VMEM((rows, low_width), BF16),
            pltpu.VMEM((low_width, rows), BF16),
            pltpu.VMEM((rows, width), jnp.int32),
        ],
        compiler_params=params(),
        cost_estimate=pl.CostEstimate(flops=5000 * rows * channels * states, bytes_accessed=20 * rows * channels, transcendentals=0),
        name="scan_both",
    )(conv, proj, gate, grad, label, dtw, dtb, alog, skip[None, :])


def conv_back_kernel(
    conv_ref, inner_ref, dact_ref, dproj_ref, label_ref, label_row_ref, cw_ref, xw_ref,
    dinner_ref, dxw_ref, dcw_ref, dcb_ref, pad_ref,
):
    rows, channels = conv_ref.shape
    taps = cw_ref.shape[0]
    tail = (taps - 1) * GROUP
    label, label_row = label_ref[...], label_row_ref[...]
    conv = conv_ref[...]
    soft = sigmoid(conv)
    act = conv * soft
    dproj = dproj_ref[...]
    turned = dproj.T.astype(BF16)
    parts = [dot(turned, xw_ref[m]) for m in range(xw_ref.shape[0])]
    dact = dact_ref[...] + pick(parts, label)
    rounded = act.astype(BF16)
    for m in range(xw_ref.shape[0]):
        dxw_ref[m] = dot(jnp.where(label_row == m, dproj, 0.0).astype(BF16), rounded)
    dconv = dact * (soft + act * (1.0 - soft))
    dcb_ref[...] = jnp.sum(dconv, axis=0, keepdims=True)
    pad_ref[pl.ds(0, rows), :] = dconv
    pad_ref[pl.ds(rows, tail), :] = jnp.zeros((tail, channels), F32)
    inner = inner_ref[...].astype(F32)
    total = None
    for tap in range(taps):
        shift = (taps - 1 - tap) * GROUP
        later = pad_ref[pl.ds(shift, rows), :]
        term = cw_ref[pl.ds(tap, 1), :].astype(F32) * later
        total = term if total is None else total + term
        dcw_ref[pl.ds(tap, 1), :] = jnp.sum(later * inner, axis=0, keepdims=True)
    dinner_ref[...] = by_sequence(total).astype(BF16)


def conv_backward(conv, inner, dact, dproj, label, label_row, cw, xw):
    rows, channels = conv.shape
    mods, wide = xw.shape[0], xw.shape[1]
    taps = cw.shape[0]
    return pl.pallas_call(
        conv_back_kernel,
        out_shape=(
            jax.ShapeDtypeStruct((rows, channels), BF16),
            jax.ShapeDtypeStruct((mods, wide, channels), F32),
            jax.ShapeDtypeStruct((taps, channels), F32),
            jax.ShapeDtypeStruct((1, channels), F32),
        ),
        scratch_shapes=[pltpu.VMEM((rows + (taps - 1) * GROUP, channels), F32)],
        compiler_params=params(),
        name="conv_backward",
    )(conv, inner, dact, dproj, label, label_row, cw, xw)


MESH = pl.DeviceIdType.MESH


def sum_body(
    chips, x_ref, out_ref, near, mine, far, total, every, other, near_sems, far_sems, back_sems, other_sems,
    work=lambda i: None,
):
    wide, rows = x_ref.shape
    half, part = rows // 2, rows // 2 // chips
    tok, ch = lax.axis_index("tok"), lax.axis_index("ch")
    chip, core = ch // 2, ch % 2
    partner = (tok, 2 * chip + 1 - core)
    chips_away = [(tok, 2 * (chip ^ d) + core) for d in range(1, chips)]

    def send(src, dst, sems, device):
        copy = pltpu.make_async_remote_copy(
            src_ref=src, dst_ref=dst, send_sem=sems.at[0], recv_sem=sems.at[1], device_id=device, device_id_type=MESH
        )
        copy.start()
        return copy

    def columns(index, size):
        return pl.ds(pl.multiple_of(index * size, size), size)

    copy = send(x_ref.at[:, columns(1 - core, half)], near, near_sems, partner)
    work(0)
    copy.wait()
    mine[...] = (x_ref[:, columns(core, half)] + near[...]).astype(BF16)
    copies = [
        send(mine.at[:, columns(chip ^ d, part)], far.at[d - 1], far_sems.at[d - 1], chips_away[d - 1])
        for d in range(1, chips)
    ]
    work(1)
    work(2)
    value = mine[:, columns(chip, part)].astype(F32)
    for d, copy in enumerate(copies):
        copy.wait()
        value = value + far[d].astype(F32)
    total[...] = value.astype(BF16)
    copies = [send(total, every.at[d - 1], back_sems.at[d - 1], chips_away[d - 1]) for d in range(1, chips)]
    copies += [send(total, other.at[0], other_sems.at[0], partner)]
    out_ref[:, columns(core * chips + chip, part)] = total[...].astype(F32)
    work(3)
    for d in range(1, chips):
        copies[d - 1].wait()
        copies += [send(every.at[d - 1], other.at[d], other_sems.at[d], partner)]
        out_ref[:, columns(core * chips + (chip ^ d), part)] = every[d - 1].astype(F32)
    for d in range(chips):
        copies[chips - 1 + d].wait()
        out_ref[:, columns((1 - core) * chips + (chip ^ d), part)] = other[d].astype(F32)


def sum_scratch(wide, rows, chips):
    half, part = rows // 2, rows // 2 // chips
    dma = pltpu.SemaphoreType.DMA
    return [
        pltpu.VMEM((wide, half), F32),
        pltpu.VMEM((wide, half), BF16),
        pltpu.VMEM((chips - 1, wide, part), BF16),
        pltpu.VMEM((wide, part), BF16),
        pltpu.VMEM((chips - 1, wide, part), BF16),
        pltpu.VMEM((chips, wide, part), BF16),
        dma((2,)),
        dma((chips - 1, 2)),
        dma((chips - 1, 2)),
        dma((chips, 2)),
    ]


def middle_kernel(
    chips, dproj_part_ref, gated_ref, label_seq_ref, ow_ref, conv_ref, inner_ref, dact_ref, label_ref, label_row_ref, cw_ref, xw_ref,
    branch_ref, every_gated_ref, dinner_ref, dxw_ref, dcw_ref, dcb_ref,
    weights, dproj, pad, w_sem, own_sem, tok_send, tok_recv, *sum_refs,
):
    group = gated_ref.shape[0]
    deep = ow_ref.shape[2]
    tok, ch = lax.axis_index("tok"), lax.axis_index("ch")
    fetch = pltpu.make_async_copy(ow_ref, weights, w_sem)
    fetch.start()

    def rows_of(index):
        return pl.ds(pl.multiple_of(index * group, group), group)

    own = pltpu.make_async_copy(gated_ref, every_gated_ref.at[rows_of(tok)], own_sem)
    own.start()
    barrier = pltpu.get_barrier_semaphore()
    peers = [(tok, ch ^ 1)] + [(tok, ch ^ (2 * d)) for d in range(1, chips)] + [(tok ^ g, ch) for g in (1, 2)]
    for device in peers:
        pl.semaphore_signal(barrier, inc=1, device_id=device, device_id_type=MESH)
    pl.semaphore_wait(barrier, len(peers))
    copies = [
        pltpu.make_async_remote_copy(
            src_ref=gated_ref,
            dst_ref=every_gated_ref.at[rows_of(tok)],
            send_sem=tok_send.at[side],
            recv_sem=tok_recv.at[side],
            device_id=(tok ^ (1 + side), ch),
            device_id_type=MESH,
        )
        for side in range(2)
    ]
    for copy in copies:
        copy.start()
    wide = deep // 4

    def work(i):
        if i == 0:
            fetch.wait()
        x, label = gated_ref[...], label_seq_ref[...]
        total = None
        for m in range(ow_ref.shape[0]):
            part = dot(jnp.where(label == m, x, jnp.zeros_like(x)), weights[m, :, pl.ds(i * wide, wide)])
            total = part if total is None else total + part
        branch_ref[:, pl.ds(i * wide, wide)] = total.astype(BF16)

    sum_body(chips, dproj_part_ref, dproj, *sum_refs, work=work)
    conv_back_kernel(
        conv_ref, inner_ref, dact_ref, dproj, label_ref, label_row_ref, cw_ref, xw_ref,
        dinner_ref, dxw_ref, dcw_ref, dcb_ref, pad,
    )
    for side in range(2):
        whole = every_gated_ref.at[rows_of(tok ^ (1 + side))]
        pltpu.make_async_copy(whole, whole, tok_recv.at[side]).wait()
        copies[side].wait_send()
    own.wait()


def middle(dproj_part, gated, label_seq, ow, conv, inner, dact, label, label_row, cw, xw, n, collective_id):
    group, channels = conv.shape
    mods, wide = xw.shape[0], xw.shape[1]
    taps, deep = cw.shape[0], ow.shape[2]
    dma = pltpu.SemaphoreType.DMA
    vmem = pl.BlockSpec(memory_space=pltpu.VMEM)
    any_space = pl.BlockSpec(memory_space=pl.ANY)
    return pl.pallas_call(
        functools.partial(middle_kernel, n // 2),
        out_shape=(
            jax.ShapeDtypeStruct((group, deep), BF16),
            jax.ShapeDtypeStruct((4 * group, channels), BF16),
            jax.ShapeDtypeStruct((group, channels), BF16),
            jax.ShapeDtypeStruct((mods, wide, channels), F32),
            jax.ShapeDtypeStruct((taps, channels), F32),
            jax.ShapeDtypeStruct((1, channels), F32),
        ),
        in_specs=[vmem, vmem, vmem, any_space] + [vmem] * 7,
        out_specs=(vmem, any_space, vmem, vmem, vmem, vmem),
        scratch_shapes=[
            pltpu.VMEM(ow.shape, BF16),
            pltpu.VMEM((wide, group), F32),
            pltpu.VMEM((group + (taps - 1) * GROUP, channels), F32),
            dma, dma, dma((2,)), dma((2,)),
        ] + sum_scratch(wide, group, n // 2),
        compiler_params=params(collective_id=collective_id, has_side_effects=True),
        cost_estimate=pl.CostEstimate(flops=2 * 10**10, bytes_accessed=10**7, transcendentals=0),
        name="middle",
    )(dproj_part, gated, label_seq, ow, conv, inner, dact, label, label_row, cw, xw)


def front_kernel(
    chips, input_ref, gain_ref, cot_ref, label_ref, iw_ref, ow_ref, cw_ref, cb_ref, xw_ref,
    scaled_ref, core_cot_ref, near_cot_ref, pair_cot_ref, labels_ref, gate_ref, gated_grad_ref, conv_ref, inner_out_ref, proj_ref,
    own_rows, in_w, out_w, chunk_rows, staged, xz, proj_part, pad,
    in_sem, out_sem, load_sem, own_sem,
    line_send, line_recv, near_send, near_recv, tok_send, tok_recv, diag_send, diag_recv,
    xz_send, xz_recv, lab_send, lab_recv, lab_tok_send, lab_tok_recv,
    keep_sem, pair_send, pair_recv, pair_diag_send, pair_diag_recv, *sum_refs,
):
    n = 2 * chips
    length, deep = input_ref.shape
    group, chunk = n * length, 2 * length
    mods, width = ow_ref.shape[0], ow_ref.shape[1]
    tok, ch = lax.axis_index("tok"), lax.axis_index("ch")
    chip, core = ch // 2, ch % 2

    fetch_in = pltpu.make_async_copy(iw_ref, in_w, in_sem)
    fetch_in.start()
    fetch_out = pltpu.make_async_copy(ow_ref, out_w, out_sem)
    fetch_out.start()

    rows = input_ref[...].astype(F32)
    inverse = lax.rsqrt(jnp.mean(rows * rows, axis=-1, keepdims=True) + 1e-05)
    own_rows[...] = (rows * inverse * gain_ref[...].astype(F32)).astype(BF16)
    labels_ref[tok, ch] = label_ref[...]

    def block(g, device):
        return pl.ds(pl.multiple_of(g * group + device * length, length), length)

    own = (
        pltpu.make_async_copy(own_rows, scaled_ref.at[block(tok, ch)], own_sem.at[0]),
        pltpu.make_async_copy(cot_ref, core_cot_ref.at[pl.ds(pl.multiple_of(chip * length, length), length)], own_sem.at[1]),
    )
    for copy in own:
        copy.start()

    barrier = pltpu.get_barrier_semaphore()
    peers = [(tok, ch ^ e) for e in range(1, n)] + [(tok ^ g, ch) for g in range(1, 4)]
    for device in peers:
        pl.semaphore_signal(barrier, inc=1, device_id=device, device_id_type=MESH)
    pl.semaphore_wait(barrier, len(peers))

    def remote(src, dst, send_sem, recv_sem, device):
        return pltpu.make_async_remote_copy(
            src_ref=src, dst_ref=dst, send_sem=send_sem, recv_sem=recv_sem, device_id=device, device_id_type=MESH
        )

    def arrive(ref, sem):
        pltpu.make_async_copy(ref, ref, sem).wait()

    label_copies = [
        remote(labels_ref.at[tok, ch], labels_ref.at[tok, ch], lab_send.at[e - 1], lab_recv.at[e - 1], (tok, ch ^ e))
        for e in range(1, n)
    ]
    for copy in label_copies:
        copy.start()

    def from_line(x, o):
        if x == 0:
            return scaled_ref.at[block(tok, 2 * o + core)]
        return core_cot_ref.at[pl.ds(pl.multiple_of(o * length, length), length)]

    def line_copy(x, o, side):
        ref = from_line(x, o)
        target = lax.rem(ch + (2 if side == 0 else n - 2), n)
        return remote(ref, ref, line_send.at[x, side, o], line_recv.at[x, o], (tok, target))

    def near_copy(x, o, g):
        if x == 0:
            src = dst = scaled_ref.at[block(tok ^ g, 2 * o + core)]
        else:
            src, dst = from_line(1, o), near_cot_ref.at[pl.ds(pl.multiple_of(o * length, length), length)]
        return remote(src, dst, near_send.at[x, g, o], near_recv.at[x, g, o], (tok, ch ^ 1))

    def tok_copy(o, side):
        ref = scaled_ref.at[block(tok, 2 * o + core)]
        return remote(ref, ref, tok_send.at[side, o], tok_recv.at[side, o], (tok ^ (1 + side), ch))

    def half_block(g, o, side):
        start = g * group + (2 * o + core) * length + side * (length // 2)
        return pl.ds(pl.multiple_of(start, length // 2), length // 2)

    def diag_copy(o, side):
        ref = scaled_ref.at[half_block(tok ^ (1 + side), o, side)]
        return remote(ref, ref, diag_send.at[side, o], diag_recv.at[side, o], (tok ^ (2 - side), ch))

    def goes(o, side):
        return (o <= chip) & (chip < chips - 1) if side == 0 else (o >= chip) & (chip > 0)

    def launch(x, o):
        for side in range(2):
            pl.when(goes(o, side))(line_copy(x, o, side).start)
        near_copy(x, o, 0).start()
        if x == 0:
            for side in range(2):
                tok_copy(o, side).start()

    base = chip - chip % 2

    def pair_copy(i, side):
        src, dst = from_line(1, base + i), pair_cot_ref.at[tok, i]
        return remote(src, dst, pair_send.at[side, i], pair_recv.at[side, i], (tok ^ (1 + side), ch))

    def pair_diag(i, side):
        ref = pair_cot_ref.at[tok ^ (1 + side), i, pl.ds(side * (length // 2), length // 2)]
        return remote(ref, ref, pair_diag_send.at[side, i], pair_diag_recv.at[side, i], (tok ^ (2 - side), ch))

    def pair_pass(i):
        for side in range(2):
            arrive(pair_cot_ref.at[tok ^ (1 + side), i], pair_recv.at[side, i])
            pair_diag(i, side).start()

    def accept(x, o):
        arrive(from_line(x, o), line_recv.at[x, o])
        launch(x, o)
        if x == 1:
            for side in range(2):
                pl.when(o // 2 == chip // 2)(pair_copy(o % 2, side).start)

    def pass_on(o):
        for side in range(2):
            arrive(scaled_ref.at[block(tok ^ (1 + side), 2 * o + core)], tok_recv.at[side, o])
            diag_copy(o, side).start()
            near_copy(0, o, 1 + side).start()

    def pass_last(o):
        for side in range(2):
            arrive(scaled_ref.at[half_block(tok ^ 3, o, side)], diag_recv.at[side, o])
        near_copy(0, o, 3).start()

    def load(x, o):
        if x == 0:
            arrive(scaled_ref.at[block(tok, 2 * o + 1 - core)], near_recv.at[0, 0, o])
            source = scaled_ref.at[pl.ds(pl.multiple_of(tok * group + o * chunk, chunk), chunk)]
            copies = [pltpu.make_async_copy(source, chunk_rows, load_sem.at[0])]
        else:
            other = near_cot_ref.at[pl.ds(pl.multiple_of(o * length, length), length)]
            arrive(other, near_recv.at[1, 0, o])
            copies = [
                pltpu.make_async_copy(
                    ref, chunk_rows.at[pl.ds(pl.multiple_of(q * length, length), length)], load_sem.at[at]
                )
                for at, (ref, q) in enumerate(((from_line(1, o), core), (other, 1 - core)))
            ]
        for copy in copies:
            copy.start()
        for copy in copies:
            copy.wait()

    def label_column(o):
        return jnp.concatenate(
            [labels_ref[tok, 2 * o + q].astype(F32).T[:, 0:1] for q in range(2)], axis=0
        )

    kind = ch // chips
    pair = ch % chips

    def xz_copies(o, h):
        target = 2 * pair + h
        src = staged.at[o, h]
        dst = xz.at[kind, pl.ds(pl.multiple_of(o * chunk, chunk), chunk)]
        return target, remote(src, dst, xz_send.at[o, h], xz_recv.at[kind, o], (tok, target)), pltpu.make_async_copy(
            src, dst, xz_recv.at[kind, o]
        )

    def project(o):
        load(0, o)
        label = label_column(o)
        for h in range(2):
            x = chunk_rows[...]
            parts = [dot(x, in_w[m, :, pl.ds(h * width, width)]) for m in range(mods)]
            staged[o, h] = pick(parts, label).astype(BF16)
            target, copy, local = xz_copies(o, h)
            pl.when(target != ch)(copy.start)
            pl.when(target == ch)(local.start)

    def project_back(o):
        load(1, o)
        label = label_column(o)
        x = chunk_rows[...]
        parts = [dot_bt(x, out_w[m]) for m in range(mods)]
        gated_grad_ref[pl.ds(pl.multiple_of(o * chunk, chunk), chunk), :] = pick(parts, label).astype(BF16)

        @pl.when(o // 2 == chip // 2)
        def _():
            mine = chunk_rows.at[pl.ds(pl.multiple_of(core * length, length), length)]
            copy = pltpu.make_async_copy(mine, pair_cot_ref.at[tok, o % 2], keep_sem)
            copy.start()
            copy.wait()

    def both_sides(i, fn):
        for o in (chip - i, chip + i):
            pl.when((o >= 0) & (o < chips))(functools.partial(fn, o))

    def every_distance(fn):
        fn(chip)

        def body(i, carry):
            both_sides(i, fn)
            return carry

        lax.fori_loop(1, chips, body, 0)

    own[0].wait()
    launch(0, chip)
    for e in range(1, n):
        arrive(labels_ref.at[tok, ch ^ e], lab_recv.at[e - 1])
    fetch_in.wait()
    project(chip)

    def step(i, carry):
        both_sides(i, functools.partial(accept, 0))
        both_sides(i, project)
        pl.when(i == 1)(functools.partial(pass_on, chip))
        pl.when(i > 1)(functools.partial(both_sides, i - 1, pass_on))
        return carry

    lax.fori_loop(1, chips, step, 0)
    own[1].wait()
    launch(1, chip)
    for side in range(2):
        pair_copy(chip % 2, side).start()
    label_tok = [
        remote(labels_ref.at[tok], labels_ref.at[tok], lab_tok_send.at[g - 1], lab_tok_recv.at[g - 1], (tok ^ g, ch))
        for g in range(1, 4)
    ]
    for copy in label_tok:
        copy.start()
    fetch_out.wait()
    project_back(chip)
    both_sides(chips - 1, pass_on)

    def step_back(i, carry):
        both_sides(i, functools.partial(accept, 1))
        both_sides(i, project_back)
        return carry

    lax.fori_loop(1, chips - 1, step_back, 0)
    every_distance(pass_last)
    pair_pass(chip % 2)

    for o in range(chips):
        for a in range(2):
            arrive(xz.at[a, pl.ds(o * chunk, chunk)], xz_recv.at[a, o])
    gate_ref[...] = xz[1]
    taps = cw_ref.shape[0]
    lead = (taps - 1) * GROUP
    inner = by_time(xz[0])
    inner_out_ref[...] = inner.astype(BF16)
    pad[pl.ds(0, lead), :] = jnp.zeros((lead, width), F32)
    pad[pl.ds(lead, group), :] = inner
    conv = jnp.broadcast_to(cb_ref[...].astype(F32), (group, width))
    for tap in range(taps):
        conv = conv + cw_ref[pl.ds(tap, 1), :].astype(F32) * pad[pl.ds(tap * GROUP, group), :]
    conv_ref[...] = conv
    act = conv * sigmoid(conv)
    label = jnp.concatenate(
        [jnp.broadcast_to(labels_ref[tok, d].astype(F32).T[:, 0:1], (length, 128)) for d in range(n)], axis=0
    )
    label = jnp.concatenate([by_time(label)] * (width // 128), axis=1)
    total = None
    for m in range(mods):
        high, low = halves(jnp.where(label == m, act, 0.0))
        part = dot_bt(xw_ref[m], high) + dot_bt(xw_ref[m], low)
        total = part if total is None else total + part
    proj_part[...] = total

    both_sides(chips - 1, functools.partial(accept, 1))
    pair_pass(1 - chip % 2)
    sum_body(chips, proj_part, proj_ref, *sum_refs)
    both_sides(chips - 1, project_back)

    def finish(o, carry):
        for g in range(4):
            if g > 0:
                arrive(scaled_ref.at[block(tok ^ g, 2 * o + 1 - core)], near_recv.at[0, g, o])
            near_copy(0, o, g).wait_send()
        near_copy(1, o, 0).wait_send()
        for side in range(2):
            for x in range(2):
                pl.when(goes(o, side))(line_copy(x, o, side).wait_send)
            tok_copy(o, side).wait_send()
            diag_copy(o, side).wait_send()
        return carry

    lax.fori_loop(0, chips, finish, 0)
    for i in range(2):
        for side in range(2):
            pair_copy(i, side).wait_send()
            pair_diag(i, side).wait_send()
            part = pair_cot_ref.at[tok ^ 3, i, pl.ds(side * (length // 2), length // 2)]
            arrive(part, pair_diag_recv.at[side, i])
    for o in range(chips):
        for h in range(2):
            target, copy, _ = xz_copies(o, h)
            pl.when(target != ch)(copy.wait_send)
    for copy in label_copies:
        copy.wait_send()
    for g in range(1, 4):
        arrive(labels_ref.at[tok ^ g], lab_tok_recv.at[g - 1])
        label_tok[g - 1].wait_send()


def way_in(block_input, gain, cotangent, modality, in_weight, out_weight, conv_weight, conv_bias, x_weight, n, collective_id):
    length, deep = block_input.shape
    mods, width = out_weight.shape[0], out_weight.shape[1]
    group, chips = n * length, n // 2
    wide = x_weight.shape[1]
    lead = (conv_weight.shape[0] - 1) * GROUP
    dma = pltpu.SemaphoreType.DMA
    vmem = pl.BlockSpec(memory_space=pltpu.VMEM)
    any_space = pl.BlockSpec(memory_space=pl.ANY)
    return pl.pallas_call(
        functools.partial(front_kernel, chips),
        out_shape=(
            jax.ShapeDtypeStruct((4 * group, deep), BF16),
            jax.ShapeDtypeStruct((chips * length, deep), BF16),
            jax.ShapeDtypeStruct((chips * length, deep), BF16),
            jax.ShapeDtypeStruct((4, 2, length, deep), BF16),
            jax.ShapeDtypeStruct((4, n, 8, length), jnp.int32),
            jax.ShapeDtypeStruct((group, width), BF16),
            jax.ShapeDtypeStruct((group, width), BF16),
            jax.ShapeDtypeStruct((group, width), F32),
            jax.ShapeDtypeStruct((group, width), BF16),
            jax.ShapeDtypeStruct((wide, group), F32),
        ),
        in_specs=[vmem, vmem, any_space, vmem, any_space, any_space, vmem, vmem, vmem],
        out_specs=(any_space, any_space, any_space, any_space, vmem, vmem, vmem, vmem, vmem, vmem),
        scratch_shapes=[
            pltpu.VMEM((length, deep), BF16),
            pltpu.VMEM(in_weight.shape, BF16),
            pltpu.VMEM(out_weight.shape, BF16),
            pltpu.VMEM((2 * length, deep), BF16),
            pltpu.VMEM((chips, 2, 2 * length, width), BF16),
            pltpu.VMEM((2, group, width), BF16),
            pltpu.VMEM((wide, group), F32),
            pltpu.VMEM((group + lead, width), F32),
            dma, dma, dma((2,)), dma((2,)),
            dma((2, 2, chips)), dma((2, chips)), dma((2, 4, chips)), dma((2, 4, chips)),
            dma((2, chips)), dma((2, chips)), dma((2, chips)), dma((2, chips)),
            dma((chips, 2)), dma((2, chips)), dma((n - 1,)), dma((n - 1,)), dma((3,)), dma((3,)),
            dma, dma((2, 2)), dma((2, 2)), dma((2, 2)), dma((2, 2)),
        ] + sum_scratch(wide, group, chips),
        compiler_params=params(collective_id=collective_id, has_side_effects=True),
        cost_estimate=pl.CostEstimate(flops=10**11, bytes_accessed=10**8, transcendentals=0),
        name="way_in",
    )(
        block_input, gain[None, :], cotangent, jnp.broadcast_to(modality[None, :], (8, length)),
        in_weight, out_weight, conv_weight, conv_bias[None, :], x_weight,
    )


def small_places(values):
    start, places = 0, []
    for value in values:
        for m in range(value.shape[0]) if len(value.shape) == 3 else [None]:
            places.append((start, (value, m)))
            start += -(-value.shape[-2] // 8) * 8
    return places


def back_kernel(
    chips, dinner_ref, dgate_ref, w_ref, label_ref, input_ref, cot_ref, gain_ref, pair_cot_ref, rest_cot_ref, scaled_ref, label_row_ref, every_gated_ref,
    dxw_ref, ddtw_ref, ddtb_ref, dcw_ref, dcb_ref, dalog_ref, dskip_ref,
    xall_ref, row_grad_ref, gain_sum_ref, near_pair_ref, near_rest_ref, grad_part_ref, small_ref, diag_gated_ref,
    weights, sends, near_part, chip_sums, arrived, mine, gain_send, gain_arrived, gain_mine, gain_others, left, made,
    packed, rounded, small_in, small_all,
    w_sem, to_col, from_own, to_tok, from_tok, to_diag, from_diag, to_near, from_near, to_row, from_row, to_gain, from_gain, to_gain_tok, from_gain_tok, cot_sems, left_sems, made_sems, to_small, from_small, to_all, from_all,
    to_gated_diag, from_gated_diag,
):
    n = 2 * chips
    group, width = dinner_ref.shape
    mods, deep = w_ref.shape[0], w_ref.shape[1]
    length = group // n
    chunk = 2 * length
    tok, ch = lax.axis_index("tok"), lax.axis_index("ch")
    chip, core = ch // 2, ch % 2
    beside, below = tok ^ 1, tok ^ 2

    fetch = pltpu.make_async_copy(w_ref, weights, w_sem)
    fetch.start()

    first = tok - tok % 2
    tile_rows = left.shape[3]
    tiles = deep // tile_rows

    def left_copies(i):
        at = pl.ds(pl.multiple_of(i * tile_rows, tile_rows), tile_rows)
        return [
            pltpu.make_async_copy(
                scaled_ref.at[pl.ds(pl.multiple_of((first + g) * group, group), group), at],
                left.at[lax.rem(i, 2), g],
                left_sems.at[lax.rem(i, 2), g],
            )
            for g in range(2)
        ]

    def made_copy(i):
        at = pl.ds(pl.multiple_of(i * tile_rows, tile_rows), tile_rows)
        return pltpu.make_async_copy(made.at[lax.rem(i, 2)], grad_part_ref.at[:, at], made_sems.at[lax.rem(i, 2)])

    def grad_tile(i, carry):
        for copy in left_copies(i):
            copy.wait()
        pl.when(i >= 2)(made_copy(i - 2).wait)
        slot = lax.rem(i, 2)
        lanes = [pl.ds(pl.multiple_of((first + g) * group, group), group) for g in range(2)]
        turned = [left[slot, g].T for g in range(2)]
        for m in range(mods):
            masked = [
                jnp.where(label_row_ref[:, lanes[g]] == m, turned[g], jnp.zeros_like(turned[g])) for g in range(2)
            ]
            for h in range(2):
                total = dot(masked[0], xall_ref[h, lanes[0], :]) + dot(masked[1], xall_ref[h, lanes[1], :])
                made[slot, m, :, pl.ds(h * width, width)] = total
        made_copy(i).start()

        @pl.when(i + 2 < tiles)
        def _():
            for copy in left_copies(i + 2):
                copy.start()

        return carry

    for i in range(2):
        for copy in left_copies(i):
            copy.start()

    barrier = pltpu.get_barrier_semaphore()
    peers = [(tok, ch ^ e) for e in range(1, n)] + [(tok ^ g, ch) for g in range(1, 4)]
    for device in peers:
        pl.semaphore_signal(barrier, inc=1, device_id=device, device_id_type=MESH)
    pl.semaphore_wait(barrier, len(peers))

    def remote(src, dst, send_sem, recv_sem, device):
        return pltpu.make_async_remote_copy(
            src_ref=src, dst_ref=dst, send_sem=send_sem, recv_sem=recv_sem, device_id=device, device_id_type=MESH
        )

    def rows_of(index, size):
        return pl.ds(pl.multiple_of(index * size, size), size)

    def all_rows(group_index, chunk_index):
        return pl.ds(pl.multiple_of(group_index * group + chunk_index * chunk, chunk), chunk)

    cot_copies = [
        remote(src, dst, cot_sems.at[i, 0], cot_sems.at[i, 1], (tok, ch ^ 1))
        for i, (src, dst) in enumerate(((pair_cot_ref, near_pair_ref), (rest_cot_ref, near_rest_ref)))
    ]

    order = [2, 3, 1, 0]
    owners = [ch // 2, chips + ch // 2]
    out_copies = []

    def give(j):
        for a, src_ref in enumerate((dinner_ref, dgate_ref)):
            owner = owners[a]
            k = owner // 2 ^ j
            src = src_ref.at[rows_of(k, chunk)]
            dst = xall_ref.at[core, all_rows(tok, k)]
            copy = remote(src, dst, to_col.at[j, a], from_own.at[j, core], (tok, owner))
            local = pltpu.make_async_copy(src, dst, from_own.at[j, core])
            pl.when(owner != ch)(copy.start)
            pl.when(owner == ch)(local.start)
            out_copies.append((owner, copy))

    give(order[0])
    give(order[1])
    half = group // 2
    gated_copies = []
    for side, (source, target) in enumerate(((beside, below), (below, beside))):
        src = every_gated_ref.at[rows_of(2 * source + side, half)]
        dst = diag_gated_ref.at[pl.ds(side * half, half)]
        copy = remote(src, dst, to_gated_diag.at[side], from_gated_diag.at[side], (target, ch))
        copy.start()
        gated_copies.append(copy)
    quarter = rounded.shape[0] // 4
    packed[...] = jnp.zeros_like(packed)
    for start, (ref, m) in small_places(
        (dxw_ref, ddtw_ref, ddtb_ref, dcw_ref, dcb_ref, dalog_ref, dskip_ref)
    ):
        value = ref[...] if m is None else ref[m]
        packed[pl.ds(start, value.shape[0]), :] = value
    rounded[...] = packed[...].astype(BF16)
    fetch.wait()
    for copy in cot_copies:
        copy.start()
    tok_copies, row_copies, diag_copies, near_copies = [], [], [], []

    def pass_on(j):
        k = chip ^ j
        for side, (source, target) in enumerate(((beside, below), (below, beside))):
            whole = xall_ref.at[:, all_rows(source, k)]
            pltpu.make_async_copy(whole, whole, from_tok.at[side, j]).wait()
            part = xall_ref.at[side, all_rows(source, k)]
            copy = remote(part, part, to_diag.at[side, j], from_diag.at[side, j], (target, ch))
            copy.start()
            diag_copies.append(copy)

    def both_cores(j):
        pltpu.make_async_copy(near_part.at[j], near_part.at[j], from_near.at[j]).wait()
        value = sends[j, rows_of(core, length), :].astype(F32) + near_part[j].astype(F32)
        if j == 0:
            mine[...] = value
        else:
            chip_sums[j - 1] = value.astype(BF16)
            target = 2 * (chip ^ j) + core
            copy = remote(chip_sums.at[j - 1], arrived.at[j - 1], to_row.at[j - 1], from_row.at[j - 1], (tok, target))
            copy.start()
            row_copies.append(copy)

    for at, j in enumerate(order):
        k = chip ^ j
        for h in range(2):
            half = xall_ref.at[h, all_rows(tok, k)]
            pltpu.make_async_copy(half, half, from_own.at[j, h]).wait()
        whole = xall_ref.at[:, all_rows(tok, k)]
        for side, target in enumerate((beside, below)):
            copy = remote(whole, whole, to_tok.at[side, j], from_tok.at[side, j], (target, ch))
            copy.start()
            tok_copies.append(copy)
        if at + 2 < chips:
            give(order[at + 2])
        label = label_ref[rows_of(k, chunk), :]
        halves_of = [xall_ref[h, all_rows(tok, k), :] for h in range(2)]
        tile = min(deep, 512)

        def product(i, carry, label=label, halves_of=halves_of, j=j):
            at = pl.ds(pl.multiple_of(i * tile, tile), tile)
            total = None
            for m in range(mods):
                for h in range(2):
                    x = jnp.where(label == m, halves_of[h], jnp.zeros_like(halves_of[h]))
                    part = dot_bt(x, weights[m, at, pl.ds(h * width, width)])
                    total = part if total is None else total + part
            sends[j, :, at] = total.astype(BF16)
            return carry

        lax.fori_loop(0, deep // tile, product, 0)
        copy = remote(
            sends.at[j, rows_of(1 - core, length)], near_part.at[j], to_near.at[j], from_near.at[j], (tok, ch ^ 1)
        )
        copy.start()
        near_copies.append(copy)
    for j in order:
        both_cores(j)
    for j in order:
        pass_on(j)
    small_copies = [
        remote(
            rounded.at[rows_of(tok ^ g, quarter)],
            small_in.at[g - 1],
            to_small.at[g - 1],
            from_small.at[g - 1],
            (tok ^ g, ch),
        )
        for g in range(1, 4)
    ]
    for copy in small_copies:
        copy.start()

    lax.fori_loop(0, tiles - 4, grad_tile, 0)
    value = packed[rows_of(tok, quarter), :]
    for copy in small_copies:
        copy.wait()
    for g in range(3):
        value = value + small_in[g].astype(F32)
    small_all[tok] = value.astype(BF16)
    small_copies = [
        remote(small_all.at[tok], small_all.at[tok], to_all.at[g - 1], from_all.at[g - 1], (tok ^ g, ch))
        for g in range(1, 4)
    ]
    for copy in small_copies:
        copy.start()
    lax.fori_loop(tiles - 4, tiles - 2, grad_tile, 0)
    total = mine[...]
    for e in range(chips - 1):
        pltpu.make_async_copy(arrived.at[e], arrived.at[e], from_row.at[e]).wait()
        total = total + arrived[e].astype(F32)
    rows = input_ref[...].astype(F32)
    inverse = lax.rsqrt(jnp.mean(rows * rows, axis=-1, keepdims=True) + 1e-05)
    normed = rows * inverse
    ng = total * gain_ref[...].astype(F32)
    row_grad_ref[...] = cot_ref[...].astype(F32) + inverse * (
        ng - normed * jnp.mean(ng * normed, axis=-1, keepdims=True)
    )
    own = deep // n
    gain_term = jnp.sum(total * normed, axis=0, keepdims=True)
    for d in range(n):
        gain_send[d] = jnp.broadcast_to(gain_term[:, d * own : (d + 1) * own], (8, own))
    gain_copies = []
    for e in range(1, n):
        copy = remote(gain_send.at[ch ^ e], gain_arrived.at[e - 1], to_gain.at[e - 1], from_gain.at[e - 1], (tok, ch ^ e))
        copy.start()
        gain_copies.append(copy)
    grad_tile(tiles - 2, 0)
    value = gain_send[ch]
    for e in range(1, n):
        gain_copies[e - 1].wait()
        value = value + gain_arrived[e - 1]
    gain_mine[...] = value
    gain_copies = []
    for g in range(1, 4):
        copy = remote(gain_mine, gain_others.at[g - 1], to_gain_tok.at[g - 1], from_gain_tok.at[g - 1], (tok ^ g, ch))
        copy.start()
        gain_copies.append(copy)
    grad_tile(tiles - 1, 0)
    for copy in gain_copies:
        copy.wait()
    even, odd = gain_mine[...] + gain_others[0], gain_others[1] + gain_others[2]
    gain_sum_ref[...] = even + odd

    for j in range(chips):
        for side in range(2):
            part = xall_ref.at[side, all_rows(tok ^ 3, chip ^ j)]
            pltpu.make_async_copy(part, part, from_diag.at[side, j]).wait()
    for owner, copy in out_copies:
        pl.when(owner != ch)(copy.wait_send)
    for copy in tok_copies + diag_copies + row_copies + near_copies:
        copy.wait_send()
    for copy in cot_copies:
        copy.wait()
    for copy in gated_copies:
        copy.wait()
    for g in range(1, 4):
        pltpu.make_async_copy(small_all.at[tok ^ g], small_all.at[tok ^ g], from_all.at[g - 1]).wait()
        small_copies[g - 1].wait_send()
    for g in range(4):
        small_ref[pl.ds(g * quarter, quarter), :] = small_all[g].astype(F32)
    for i in (tiles - 2, tiles - 1):
        made_copy(i).wait()


def way_back(
    dinner, dgate, w, label, block_input, cotangent, gain, pair_cot, rest_cot, every_scaled, every_label, every_gated, small, n, collective_id
):
    group, width = dinner.shape
    mods, deep, _ = w.shape
    chips, length = n // 2, group // n
    dma = pltpu.SemaphoreType.DMA
    vmem = pl.BlockSpec(memory_space=pltpu.VMEM)
    tile = min(256, deep)
    last, (value, _) = small_places(small)[-1]
    quarter = -(-(last + value.shape[-2]) // 64) * 16
    any_space = pl.BlockSpec(memory_space=pl.ANY)
    return pl.pallas_call(
        functools.partial(back_kernel, chips),
        out_shape=(
            jax.ShapeDtypeStruct((2, 4 * group, width), BF16),
            jax.ShapeDtypeStruct((length, deep), F32),
            jax.ShapeDtypeStruct((8, deep // n), F32),
            jax.ShapeDtypeStruct(pair_cot.shape, BF16),
            jax.ShapeDtypeStruct(rest_cot.shape, BF16),
            jax.ShapeDtypeStruct(w.shape, F32),
            jax.ShapeDtypeStruct((4 * quarter, width), F32),
            jax.ShapeDtypeStruct((group, width), BF16),
        ),
        in_specs=[vmem, vmem, any_space, vmem, vmem, vmem, vmem, any_space, any_space, any_space, vmem, any_space]
        + [vmem] * len(small),
        out_specs=(vmem, vmem, vmem, any_space, any_space, any_space, vmem, any_space),
        scratch_shapes=[
            pltpu.VMEM(w.shape, BF16),
            pltpu.VMEM((chips, 2 * length, deep), BF16),
            pltpu.VMEM((chips, length, deep), BF16),
            pltpu.VMEM((chips - 1, length, deep), BF16),
            pltpu.VMEM((chips - 1, length, deep), BF16),
            pltpu.VMEM((length, deep), F32),
            pltpu.VMEM((n, 8, deep // n), F32),
            pltpu.VMEM((n - 1, 8, deep // n), F32),
            pltpu.VMEM((8, deep // n), F32),
            pltpu.VMEM((3, 8, deep // n), F32),
            pltpu.VMEM((2, 2, group, tile), BF16),
            pltpu.VMEM((2, mods, tile, 2 * width), F32),
            pltpu.VMEM((4 * quarter, width), F32),
            pltpu.VMEM((4 * quarter, width), BF16),
            pltpu.VMEM((3, quarter, width), BF16),
            pltpu.VMEM((4, quarter, width), BF16),
            dma, dma((chips, 2)), dma((chips, 2)), dma((2, chips)), dma((2, chips)), dma((2, chips)), dma((2, chips)),
            dma((chips,)), dma((chips,)), dma((chips - 1,)), dma((chips - 1,)), dma((n - 1,)), dma((n - 1,)), dma((3,)), dma((3,)), dma((2, 2)), dma((2, 2)), dma((2,)),
            dma((3,)), dma((3,)), dma((3,)), dma((3,)),
            dma((2,)), dma((2,)),
        ],
        compiler_params=params(collective_id=collective_id, has_side_effects=True),
        cost_estimate=pl.CostEstimate(flops=10**11, bytes_accessed=10**8, transcendentals=0),
        name="way_back",
    )(dinner, dgate, w, label, block_input, cotangent, gain[None, :], pair_cot, rest_cot, every_scaled, every_label, every_gated, *small)


def grad_parts_kernel(left_ref, label_ref, *refs):
    right_refs, out_ref = refs[:-1], refs[-1]
    size = right_refs[0].shape[0]
    turned, label = left_ref[...].T, label_ref[...]
    for m in range(out_ref.shape[0]):
        masked = jnp.where(label == m, turned, jnp.zeros_like(turned))
        total = None
        for i, right_ref in enumerate(right_refs):
            part = dot(masked[:, i * size : (i + 1) * size], right_ref[...])
            total = part if total is None else total + part
        out_ref[m] = total


def weight_grad_parts(left, rights, label, mods, tile):
    rows, deep = left.shape
    size, wide = rights[0].shape
    whole = pl.BlockSpec((size, wide), lambda i: (0, 0), pipeline_mode=pl.Buffered(1))
    return pl.pallas_call(
        grad_parts_kernel,
        out_shape=jax.ShapeDtypeStruct((mods, deep, wide), F32),
        grid=(deep // tile,),
        in_specs=[pl.BlockSpec((rows, tile), lambda i: (0, i)), pl.BlockSpec((1, rows), lambda i: (0, 0))]
        + [whole] * len(rights),
        out_specs=pl.BlockSpec((mods, tile, wide), lambda i: (0, i, 0)),
        compiler_params=params(),
        cost_estimate=pl.CostEstimate(
            flops=2 * mods * rows * deep * wide,
            bytes_accessed=2 * rows * (deep + wide) + 4 * mods * deep * wide,
            transcendentals=0,
        ),
        name="weight_grad_parts",
    )(left, label, *rights)


def grad_last_kernel(which_ref, left_ref, right_ref, label_ref, left2_ref, right2_ref, label2_ref, part_ref, out_ref, made):
    del which_ref
    turned = [left_ref[...].T, left2_ref[...].T]
    labels = [label_ref[...], label2_ref[...]]
    wide = right_ref.shape[2]
    for m in range(out_ref.shape[0]):
        masked = [jnp.where(label == m, x, jnp.zeros_like(x)) for label, x in zip(labels, turned, strict=True)]
        for h in range(right_ref.shape[0]):
            at = pl.ds(h * wide, wide)
            made[...] = dot(masked[0], right_ref[h]) + dot(masked[1], right2_ref[h])
            out_ref[m, :, at] = part_ref[m, :, at] + made[...]


def weight_grad_last(left, right, label, part, which, tile):
    mods, deep, wide = part.shape
    group = left.shape[0] // 4
    of_group = [
        spec
        for g in range(2)
        for spec in (
            pl.BlockSpec((group, tile), lambda i, which, g=g: (which[g], i)),
            pl.BlockSpec((right.shape[0], group, right.shape[2]), lambda i, which, g=g: (0, which[g], 0)),
            pl.BlockSpec((1, group), lambda i, which, g=g: (0, which[g])),
        )
    ]
    return pl.pallas_call(
        grad_last_kernel,
        out_shape=jax.ShapeDtypeStruct(part.shape, F32),
        grid_spec=pltpu.PrefetchScalarGridSpec(
            num_scalar_prefetch=1,
            grid=(deep // tile,),
            in_specs=of_group + [pl.BlockSpec((mods, tile, wide), lambda i, which: (0, i, 0))],
            out_specs=pl.BlockSpec((mods, tile, wide), lambda i, which: (0, i, 0)),
            scratch_shapes=[pltpu.VMEM((tile, right.shape[2]), F32)],
        ),
        compiler_params=params(),
        cost_estimate=pl.CostEstimate(
            flops=4 * mods * group * deep * wide,
            bytes_accessed=8 * mods * deep * wide,
            transcendentals=0,
        ),
        name="weight_grad_last",
    )(which, left, right, label, left, right, label, part)


def grad_kernel(left_ref, right_ref, label_ref, out_ref):
    left, label = left_ref[...], label_ref[...]
    wide = right_ref.shape[2]
    turned = left.T
    for m in range(out_ref.shape[0]):
        masked = jnp.where(label == m, turned, jnp.zeros_like(turned))
        for h in range(right_ref.shape[0]):
            out_ref[m, :, pl.ds(h * wide, wide)] = dot(masked, right_ref[h])


def grad_part_kernel(left_ref, right_ref, label_ref, out_ref):
    left, label = left_ref[...], label_ref[...]
    wide = right_ref.shape[2]
    turned = left.T
    first = pl.program_id(1) == 0
    for m in range(out_ref.shape[0]):
        masked = jnp.where(label == m, turned, jnp.zeros_like(turned))
        for h in range(right_ref.shape[0]):
            at = pl.ds(h * wide, wide)
            part = dot(masked, right_ref[h])
            out_ref[m, :, at] = jnp.where(first, part, out_ref[m, :, at] + part)


def weight_grad(left, right, label, mods, tile):
    rows, deep = left.shape
    wide = right.shape[0] * right.shape[2]
    block = min(rows, 4096)
    tile = min(tile, deep)
    return pl.pallas_call(
        grad_kernel if block == rows else grad_part_kernel,
        out_shape=jax.ShapeDtypeStruct((mods, deep, wide), F32),
        grid=(deep // tile, rows // block),
        in_specs=[
            pl.BlockSpec((block, tile), lambda i, j: (j, i)),
            pl.BlockSpec((right.shape[0], block, right.shape[2]), lambda i, j: (0, j, 0)),
            pl.BlockSpec((1, block), lambda i, j: (0, j)),
        ],
        out_specs=pl.BlockSpec((mods, tile, wide), lambda i, j: (0, i, 0)),
        compiler_params=params(),
        cost_estimate=pl.CostEstimate(
            flops=2 * mods * rows * deep * wide,
            bytes_accessed=2 * rows * (deep + wide) + 4 * mods * deep * wide,
            transcendentals=0,
        ),
        name="weight_grad",
    )(left, right, label)


def by_groups(fn, count, arrays, axes, joined):
    if count == 1:
        return fn(*arrays)

    def cut(a, axis, i):
        size = a.shape[axis] // count
        return lax.slice_in_dim(a, i * size, (i + 1) * size, axis=axis)

    outs = [fn(*(cut(a, axis, i) for a, axis in zip(arrays, axes, strict=True))) for i in range(count)]
    return tuple(
        jnp.concatenate(values, axis=joined[at]) if at < len(joined) else functools.reduce(jnp.add, values)
        for at, values in enumerate(zip(*outs, strict=True))
    )


def exchange_pairs(n):
    half = n // 2
    first = [(c, 2 * c) if c < half else (c, 2 * (c - half) + 1) for c in range(n)]
    second = [(c, 2 * c + 1) if c < half else (c, 2 * (c - half)) for c in range(n)]
    return first, second


def to_owners(xz, n):
    first, second = exchange_pairs(n)
    c = lax.axis_index("ch")
    width = xz.shape[1] // 2
    left, right = xz[:, :width], xz[:, width:]
    lower = c < n // 2
    one = lax.ppermute(jnp.where(lower, left, right), "ch", first)
    two = lax.ppermute(jnp.where(lower, right, left), "ch", second)
    even = c % 2 == 0
    return jnp.where(even, one, two), jnp.where(even, two, one)


def to_columns(dinner, dgate, n):
    first, second = exchange_pairs(n)
    c = lax.axis_index("ch")
    even = c % 2 == 0
    one = lax.ppermute(jnp.where(even, dinner, dgate), "ch", [(b, a) for a, b in first])
    two = lax.ppermute(jnp.where(even, dgate, dinner), "ch", [(b, a) for a, b in second])
    lower = c < n // 2
    return jnp.concatenate([jnp.where(lower, one, two), jnp.where(lower, two, one)], axis=1)


def on_device(
    n,
    block_input,
    norm_gain,
    in_weight,
    x_weight,
    dt_weight,
    dt_bias,
    conv_weight,
    conv_bias,
    a_log,
    skip_gain,
    out_weight,
    modality,
    cotangent,
):
    mods = in_weight.shape[0]
    length = block_input.shape[0]
    count = n // GROUP
    fast = n == GROUP and lax.axis_size("tok") == 4 and length % 128 == 0
    rows_float = block_input.astype(F32)
    gain = norm_gain.astype(F32)
    inverse = lax.rsqrt(jnp.mean(rows_float * rows_float, axis=-1, keepdims=True) + 1e-05)
    normed = rows_float * inverse
    scaled = (normed * gain[None, :]).astype(BF16)

    token_group = n * length
    if fast:
        every_scaled, core_cot, _, pair_cot, labels, gate, gated_grad, conv, inner_by_time, proj = way_in(
            block_input, norm_gain, cotangent, modality, in_weight, out_weight, conv_weight, conv_bias, x_weight, n, 0
        )
        every_label = labels[:, :, 0, :].reshape(4 * token_group)
        rest = (1 - lax.axis_index("ch") // 4) * 2 * length
        rest_cot = lax.all_gather(lax.dynamic_slice_in_dim(core_cot, rest, 2 * length, 0), "tok", axis=0, tiled=True)
    else:
        every_label = lax.all_gather(modality, ("tok", "ch"), axis=0, tiled=True)
    group_label = lax.dynamic_slice_in_dim(every_label, lax.axis_index("tok") * token_group, token_group, 0)
    label = group_label[:, None]
    label_by_time = group_label.reshape(count, GROUP, length).transpose(0, 2, 1).reshape(token_group, 1)
    label_row = label_by_time.reshape(1, token_group)

    if not fast:
        group_rows = lax.all_gather(scaled, "ch", axis=0, tiled=True)
        every_scaled = lax.all_gather(scaled, ("tok", "ch"), axis=0, tiled=True)
        every_cot = lax.all_gather(cotangent, ("tok", "ch"), axis=0, tiled=True)
        xz = routed_select(group_rows, label, in_weight, 256, False)
        inner, gate = to_owners(xz, n)
        group_cot = lax.all_gather(cotangent, "ch", axis=0, tiled=True)
        gated_grad = routed_select(group_cot, label, out_weight, 128, True)
        conv, inner_by_time, proj_part = by_groups(
            lambda a, b: conv_forward(a, b, conv_weight, conv_bias, x_weight), count, (inner, label_row), (0, 1), (0, 0, 1)
        )
        proj = lax.psum(proj_part, "ch")

    gated, dgate, dact, dproj_part, ddtw, ddtb, dalog, dskip = by_groups(
        lambda a, b, c, d, e: scan_both(a, b, c, d, e, dt_weight, dt_bias, a_log, skip_gain),
        count,
        (conv, proj, gate, gated_grad, label_by_time),
        (0, 1, 0, 0, 0),
        (0, 0, 0, 1),
    )
    if fast:
        branch_part, every_gated, dinner, dxw, dcw, dcb = middle(
            dproj_part, gated, label, out_weight, conv, inner_by_time, dact, label_by_time, label_row, conv_weight, x_weight, n, 1
        )
    else:
        dproj = lax.psum(dproj_part, "ch")
        dinner, dxw, dcw, dcb = by_groups(
            lambda a, b, c, d, e, f: conv_backward(a, b, c, d, e, f, conv_weight, x_weight),
            count,
            (conv, inner_by_time, dact, dproj, label_by_time, label_row),
            (0, 0, 0, 1, 0, 1),
            (0,),
        )
        branch_part = routed_spread(gated, label, out_weight, 512, False, BF16)
        every_gated = lax.all_gather(gated, "tok", axis=0, tiled=True)
    every_label = every_label[None, :]
    small = (dxw, ddtw, ddtb, dcw, dcb, dalog, dskip)
    if fast:
        pair_cot = pair_cot.reshape(rest_cot.shape)
        every_grad, row_grad, gain_grad, near_pair, near_rest, grad_part, total, diag_gated = way_back(
            dinner, dgate, in_weight, label, block_input, cotangent, norm_gain, pair_cot, rest_cot, every_scaled, every_label,
            every_gated, small, n, 2,
        )
        fourth = (lax.axis_index("tok") ^ 3) * token_group
        every_gated = lax.dynamic_update_slice_in_dim(every_gated, diag_gated, fourth, 0)
        gain_grad = gain_grad[0]
    else:
        xz_grad = to_columns(dinner, dgate, n)
        scaled_part = routed_spread(xz_grad, label, in_weight, 256, True, BF16)
        scaled_grad = lax.psum_scatter(scaled_part, "ch", scatter_dimension=0, tiled=True).astype(F32)
        gain_grad = lax.psum_scatter(jnp.sum(scaled_grad * normed, axis=0), "ch", scatter_dimension=0, tiled=True)
        ng = scaled_grad * gain[None, :]
        row_grad = cotangent.astype(F32) + inverse * (ng - normed * jnp.mean(ng * normed, axis=-1, keepdims=True))
        every_grad = lax.all_gather(xz_grad, "tok", axis=0, tiled=True)[None]

    if fast:
        branch_part, row_grad = lax.optimization_barrier((branch_part, row_grad))
    branch = lax.psum_scatter(branch_part, "ch", scatter_dimension=0, tiled=True).astype(F32)
    block_out = (rows_float + branch).astype(BF16)
    if fast:
        ch = lax.axis_index("ch")

        def own_first(value):
            split = value.reshape((4, 2, 2, 2, length) + value.shape[1:])
            split = jnp.where(ch // 4 == 0, split, split[:, ::-1])
            split = jnp.where(ch % 2 == 0, split, split[:, :, :, ::-1])
            return jnp.moveaxis(split, (1, 3), (0, 1)).reshape(value.shape)

        out_weight_grad = weight_grad_parts(
            own_first(every_gated),
            (pair_cot, near_pair, rest_cot, near_rest),
            own_first(every_label[0])[None, :],
            mods,
            128,
        )
    else:
        out_weight_grad = weight_grad(every_gated, every_cot[None], every_label, mods, 128)
    if fast:
        others = (2 - lax.axis_index("tok") // 2 * 2 + jnp.arange(2)).astype(jnp.int32)
        in_weight_grad = weight_grad_last(every_scaled, every_grad, every_label, grad_part, others, 256)
    else:
        in_weight_grad = weight_grad(every_scaled, every_grad, every_label, mods, 256)
    sums = []
    if fast:
        for start, (value, m) in small_places(small):
            rows = lax.slice_in_dim(total, start, start + value.shape[-2], axis=0)
            if not m:
                sums.append([])
            sums[-1].append(rows)
        sums = [rows[0] if len(value.shape) == 2 else jnp.stack(rows) for rows, value in zip(sums, small, strict=True)]
    else:
        gain_grad = lax.psum(gain_grad, "tok")
        flat = [value.reshape(-1, value.shape[-1]) for value in small]
        total = lax.psum(jnp.concatenate(flat, axis=0), "tok")
        start = 0
        for value, rows in zip(small, flat, strict=True):
            sums.append(lax.slice_in_dim(total, start, start + rows.shape[0], axis=0).reshape(value.shape))
            start += rows.shape[0]
    dxw, ddtw, ddtb, dcw, dcb, dalog, dskip = sums
    return (
        block_out,
        row_grad,
        gain_grad,
        in_weight_grad,
        dxw,
        ddtw,
        ddtb,
        dcw,
        dcb[0],
        dalog,
        dskip[0],
        out_weight_grad,
    )


def solution(mesh):
    placed = (
        P(("tok", "ch"), None),
        P(),
        P(None, None, "ch"),
        P(None, None, "ch"),
        P(None, None, "ch"),
        P(None, "ch"),
        P(None, "ch"),
        P("ch"),
        P(None, "ch"),
        P("ch"),
        P(None, "ch", None),
        P(("tok", "ch")),
        P(("tok", "ch"), None),
    )
    return jax.shard_map(
        functools.partial(on_device, mesh.shape["ch"]),
        mesh=mesh,
        in_specs=placed,
        out_specs=(
            P(("tok", "ch"), None),
            P(("tok", "ch"), None),
            P("ch"),
            P(None, None, "ch"),
            P(None, None, "ch"),
            P(None, None, "ch"),
            P(None, "ch"),
            P(None, "ch"),
            P("ch"),
            P(None, "ch"),
            P("ch"),
            P(None, "ch", None),
        ),
        check_vma=False,
    )
```

```python
import functools
import math

import jax
import jax.numpy as jnp
from jax import lax
from jax.experimental import pallas as pl
from jax.experimental.pallas import tpu as pltpu
from jax.sharding import PartitionSpec as P

F32 = jnp.float32
BF16 = jnp.bfloat16
LOG2E = math.log2(math.e)
LN2 = math.log(2.0)
GROUP = 8
VMEM_LIMIT = 58 << 20


def params(**kw):
    return pltpu.CompilerParams(vmem_limit_bytes=VMEM_LIMIT, **kw)


def dot(a, b):
    return lax.dot_general(a, b, (((1,), (0,)), ((), ())), preferred_element_type=F32)


def dot_bt(a, b):
    return lax.dot_general(a, b, (((1,), (1,)), ((), ())), preferred_element_type=F32)


def dot_at(a, b):
    return lax.dot_general(a, b, (((0,), (0,)), ((), ())), preferred_element_type=F32)


def halves(x):
    high = x.astype(BF16)
    return high, (x - high.astype(F32)).astype(BF16)


def pick(parts, label):
    total = parts[-1]
    for index in range(len(parts) - 2, -1, -1):
        total = jnp.where(label == index, parts[index], total)
    return total


def by_kind(turned, label, mods):
    return jnp.concatenate([jnp.where(label == m, turned, jnp.zeros_like(turned)) for m in range(mods)], axis=0)


def sigmoid(x):
    return 0.5 * jnp.tanh(0.5 * x) + 0.5


def select_kernel(transposed, x_ref, label_ref, w_ref, out_ref):
    x = x_ref[...]
    label = label_ref[...]
    product = dot_bt if transposed else dot
    parts = [product(x, w_ref[m]) for m in range(w_ref.shape[0])]
    out_ref[...] = pick(parts, label).astype(out_ref.dtype)


def routed_select(x, label, w, tile, transposed):
    rows, depth = x.shape
    mods = w.shape[0]
    outer = w.shape[1] if transposed else w.shape[2]
    tile = min(tile, outer)
    block = min(rows, 1024)
    if transposed:
        w_spec = pl.BlockSpec((mods, tile, depth), lambda i, j: (0, j, 0))
    else:
        w_spec = pl.BlockSpec((mods, depth, tile), lambda i, j: (0, 0, j))
    return pl.pallas_call(
        functools.partial(select_kernel, transposed),
        out_shape=jax.ShapeDtypeStruct((rows, outer), BF16),
        grid=(rows // block, outer // tile),
        in_specs=[
            pl.BlockSpec((block, depth), lambda i, j: (i, 0)),
            pl.BlockSpec((block, 1), lambda i, j: (i, 0)),
            w_spec,
        ],
        out_specs=pl.BlockSpec((block, tile), lambda i, j: (i, j)),
        compiler_params=params(),
        cost_estimate=pl.CostEstimate(
            flops=2 * rows * depth * outer * mods, bytes_accessed=2 * mods * depth * outer + 2 * rows * (depth + outer), transcendentals=0
        ),
        name="routed_select",
    )(x, label, w)


def spread_kernel(transposed, x_ref, label_ref, w_ref, out_ref):
    x = x_ref[...]
    label = label_ref[...]
    product = dot_bt if transposed else dot
    total = None
    for m in range(w_ref.shape[0]):
        part = product(jnp.where(label == m, x, jnp.zeros_like(x)), w_ref[m])
        total = part if total is None else total + part
    out_ref[...] = total.astype(out_ref.dtype)


def routed_spread(x, label, w, tile, transposed, dtype):
    rows, depth = x.shape
    mods = w.shape[0]
    outer = w.shape[1] if transposed else w.shape[2]
    tile = min(tile, outer)
    block = min(rows, 1024)
    if transposed:
        w_spec = pl.BlockSpec((mods, tile, depth), lambda i, j: (0, j, 0))
    else:
        w_spec = pl.BlockSpec((mods, depth, tile), lambda i, j: (0, 0, j))
    return pl.pallas_call(
        functools.partial(spread_kernel, transposed),
        out_shape=jax.ShapeDtypeStruct((rows, outer), dtype),
        grid=(rows // block, outer // tile),
        in_specs=[
            pl.BlockSpec((block, depth), lambda i, j: (i, 0)),
            pl.BlockSpec((block, 1), lambda i, j: (i, 0)),
            w_spec,
        ],
        out_specs=pl.BlockSpec((block, tile), lambda i, j: (i, j)),
        compiler_params=params(),
        cost_estimate=pl.CostEstimate(
            flops=2 * rows * depth * outer * mods, bytes_accessed=2 * mods * depth * outer + 2 * rows * (depth + outer), transcendentals=0
        ),
        name="routed_spread",
    )(x, label, w)


def by_time(x):
    rows, width = x.shape
    return jnp.swapaxes(x.astype(F32).reshape(GROUP, rows // GROUP, width), 0, 1).reshape(rows, width)


def by_sequence(x):
    rows, width = x.shape
    return jnp.swapaxes(x.reshape(rows // GROUP, GROUP, width), 0, 1).reshape(rows, width)


def conv_kernel(inner_ref, label_ref, cw_ref, cb_ref, xw_ref, conv_ref, inner_out_ref, proj_ref, pad_ref):
    rows, channels = inner_ref.shape
    taps = cw_ref.shape[0]
    lead = (taps - 1) * GROUP
    inner = by_time(inner_ref[...])
    inner_out_ref[...] = inner.astype(BF16)
    pad_ref[pl.ds(0, lead), :] = jnp.zeros((lead, channels), F32)
    pad_ref[pl.ds(lead, rows), :] = inner
    conv = jnp.broadcast_to(cb_ref[...].astype(F32), (rows, channels))
    for tap in range(taps):
        conv = conv + cw_ref[pl.ds(tap, 1), :].astype(F32) * pad_ref[pl.ds(tap * GROUP, rows), :]
    conv_ref[...] = conv
    high, low = halves(conv * sigmoid(conv))
    label = label_ref[...]
    parts = [dot_bt(xw_ref[m], high) + dot_bt(xw_ref[m], low) for m in range(xw_ref.shape[0])]
    proj_ref[...] = pick(parts, label)


def conv_forward(inner, label, cw, cb, xw):
    rows, channels = inner.shape
    wide = xw.shape[1]
    lead = (cw.shape[0] - 1) * GROUP
    return pl.pallas_call(
        conv_kernel,
        out_shape=(
            jax.ShapeDtypeStruct((rows, channels), F32),
            jax.ShapeDtypeStruct((rows, channels), BF16),
            jax.ShapeDtypeStruct((wide, rows), F32),
        ),
        scratch_shapes=[pltpu.VMEM((rows + lead, channels), F32)],
        compiler_params=params(),
        name="conv_forward",
    )(inner, label, cw, cb[None, :], xw)


def scan_kernel(
    conv_ref, proj_ref, gate_ref, grad_ref, label_ref, dtw_ref, dtb_ref, alog_ref, skip_ref,
    gated_ref, dgate_ref, dact_ref, dproj_ref, ddtw_ref, ddtb_ref, dalog_ref, dskip_ref,
    hist, mix, prod, rate, act, step, slope, dout, scanned, dstep, dlow, low_turned, low_rank, label,
):
    rows, width = conv_ref.shape
    length = rows // GROUP
    states = alog_ref.shape[0]
    mods, low_width = dtw_ref.shape[0], dtw_ref.shape[1]
    tile = pl.program_id(0)
    ddrive = scanned

    @pl.when(tile == 0)
    def _():
        prod[...] = jnp.zeros_like(prod)
        dlow[...] = jnp.zeros_like(dlow)
        label[...] = jnp.broadcast_to(label_ref[...], (rows, width))
        low_rank[...] = proj_ref[pl.ds(0, low_width), :].astype(BF16)
        low_turned[...] = proj_ref[pl.ds(0, low_width), :].T.astype(BF16)
        turned = proj_ref[pl.ds(low_width, 2 * states), :].T.astype(BF16)
        row = lax.broadcasted_iota(jnp.int32, (2 * states, 2 * width), 0)
        column = lax.broadcasted_iota(jnp.int32, (2 * states, 2 * width), 1)
        for s in range(0, 2 * states, 2):
            spread = dot(turned, (row == s + (column >= width).astype(jnp.int32)).astype(BF16))
            mix[s] = spread[:, :width]
            mix[s + 1] = spread[:, width:]

    kind = label[...]
    parts = [dot(low_turned[...], dtw_ref[m]) + dtb_ref[pl.ds(m, 1), :].astype(F32) for m in range(mods)]
    speed = pick(parts, kind)
    step[...] = jnp.maximum(speed, 0.0) + jnp.log1p(jnp.exp(-jnp.abs(speed)))
    slope[...] = sigmoid(speed)
    conv = conv_ref[...]
    act[...] = conv * sigmoid(conv)
    for s in range(states):
        rate[s] = jnp.broadcast_to(-LOG2E * jnp.exp(alog_ref[pl.ds(s, 1), :].astype(F32)), (GROUP, width))
        hist[0, s] = jnp.zeros((GROUP, width), F32)

    def forward(t, state):
        at = pl.ds(pl.multiple_of(t * GROUP, GROUP), GROUP)
        now = step[at, :]
        drive = now * act[at, :]
        total = None
        new = []
        for s in range(states):
            value = jnp.exp2(now * rate[s]) * state[s] + mix[s, at, :] * drive
            hist[t + 1, s] = value
            new.append(value)
            term = mix[states + s, at, :] * value
            total = term if total is None else total + term
        scanned[at, :] = total
        return tuple(new)

    zero = jnp.zeros((GROUP, width), F32)
    lax.fori_loop(0, length, forward, (zero,) * states, unroll=8)

    gate = by_time(gate_ref[...])
    grad = by_time(grad_ref[...])
    soft = sigmoid(gate)
    opened = gate * soft
    skip = skip_ref[...].astype(F32)
    summed = scanned[...] + skip * act[...]
    gated_ref[...] = by_sequence(summed * opened).astype(BF16)
    dgate = grad * summed * (soft + opened * (1.0 - soft))
    dgate_ref[...] = by_sequence(dgate).astype(BF16)
    dsummed = grad * opened
    dout[...] = dsummed
    dskip_ref[...] = jnp.sum(dsummed * act[...], axis=0, keepdims=True)

    def backward(i, carry):
        t = length - 1 - i
        at = pl.ds(pl.multiple_of(t * GROUP, GROUP), GROUP)
        now = step[at, :]
        drive = now * act[at, :]
        out = dout[at, :]
        dd, ds = None, None
        new, drates = [], []
        for s in range(states):
            decay = jnp.exp2(now * rate[s])
            dstate = carry[s] + mix[states + s, at, :] * out
            prod[states + s, at, :] += out * hist[t + 1, s]
            prod[s, at, :] += dstate * drive
            term = dstate * mix[s, at, :]
            dd = term if dd is None else dd + term
            passed = dstate * decay
            new.append(passed)
            change = passed * hist[t, s]
            term = change * rate[s]
            ds = term if ds is None else ds + term
            drates.append(carry[states + s] + change * now)
        ddrive[at, :] = dd
        dstep[at, :] = ds
        return tuple(new + drates)

    final = lax.fori_loop(0, length, backward, (zero,) * (2 * states), unroll=4)

    for s in range(states):
        dalog_ref[pl.ds(s, 1), :] = LN2 * jnp.sum(final[states + s] * rate[s], axis=0, keepdims=True)
    dact_ref[...] = ddrive[...] * step[...] + skip * dout[...]
    dspeed = (dstep[...] * LN2 + ddrive[...] * act[...]) * slope[...]
    rounded = dspeed.astype(BF16)
    of_rank = kind if width == low_width else label_ref[...]
    dlow[...] += pick([dot_bt(rounded, dtw_ref[m]) for m in range(mods)], of_rank)
    for m in range(mods):
        own = kind == m
        masked = jnp.where(own, dspeed, 0.0)
        ddtw_ref[m] = dot(low_rank[...], masked.astype(BF16))
        ddtb_ref[pl.ds(m, 1), :] = jnp.sum(masked, axis=0, keepdims=True)

    @pl.when(tile == pl.num_programs(0) - 1)
    def _():
        column = lax.broadcasted_iota(jnp.int32, (width, 2 * states), 1)
        sums = jnp.zeros((rows, 2 * states), F32)
        for s in range(2 * states):
            sums = sums + dot(prod[s].astype(BF16), (column == s).astype(BF16))
        dproj_ref[pl.ds(0, low_width), :] = dlow[...].T
        dproj_ref[pl.ds(low_width, 2 * states), :] = sums.T


def scan_both(conv, proj, gate, grad, label, dtw, dtb, alog, skip):
    rows, channels = conv.shape
    width = min(128, channels)
    length = rows // GROUP
    states = alog.shape[0]
    mods, low_width = dtw.shape[0], dtw.shape[1]
    wide = proj.shape[0]

    def whole(shape):
        return pl.BlockSpec(shape, lambda j: (0,) * len(shape), pipeline_mode=pl.Buffered(1))

    def cut(*shape):
        return pl.BlockSpec(shape + (width,), lambda j: (0,) * len(shape) + (j,))

    plane = (GROUP, width)
    flat = pltpu.VMEM((rows, width), F32)
    return pl.pallas_call(
        scan_kernel,
        out_shape=(
            jax.ShapeDtypeStruct((rows, channels), BF16),
            jax.ShapeDtypeStruct((rows, channels), BF16),
            jax.ShapeDtypeStruct((rows, channels), F32),
            jax.ShapeDtypeStruct((wide, rows), F32),
            jax.ShapeDtypeStruct((mods, low_width, channels), F32),
            jax.ShapeDtypeStruct((mods, channels), F32),
            jax.ShapeDtypeStruct((states, channels), F32),
            jax.ShapeDtypeStruct((1, channels), F32),
        ),
        grid=(channels // width,),
        in_specs=[
            cut(rows), whole((wide, rows)), cut(rows), cut(rows), whole((rows, 1)),
            cut(mods, low_width), cut(mods), cut(states), cut(1),
        ],
        out_specs=(
            cut(rows), cut(rows), cut(rows), whole((wide, rows)), cut(mods, low_width), cut(mods), cut(states), cut(1),
        ),
        scratch_shapes=[
            pltpu.VMEM((length + 1, states) + plane, F32),
            pltpu.VMEM((2 * states, rows, width), F32),
            pltpu.VMEM((2 * states, rows, width), F32),
            pltpu.VMEM((states,) + plane, F32),
            flat, flat, flat, flat, flat, flat,
            pltpu.VMEM((rows, low_width), F32),
            pltpu.VMEM((rows, low_width), BF16),
            pltpu.VMEM((low_width, rows), BF16),
            pltpu.VMEM((rows, width), jnp.int32),
        ],
        compiler_params=params(),
        cost_estimate=pl.CostEstimate(flops=5000 * rows * channels * states, bytes_accessed=20 * rows * channels, transcendentals=0),
        name="scan_both",
    )(conv, proj, gate, grad, label, dtw, dtb, alog, skip[None, :])


def conv_back_kernel(
    conv_ref, inner_ref, dact_ref, dproj_ref, label_ref, label_row_ref, cw_ref, xw_ref,
    dinner_ref, dxw_ref, dcw_ref, dcb_ref, pad_ref,
):
    rows, channels = conv_ref.shape
    taps = cw_ref.shape[0]
    tail = (taps - 1) * GROUP
    label, label_row = label_ref[...], label_row_ref[...]
    conv = conv_ref[...]
    soft = sigmoid(conv)
    act = conv * soft
    dproj = dproj_ref[...]
    turned = dproj.T.astype(BF16)
    parts = [dot(turned, xw_ref[m]) for m in range(xw_ref.shape[0])]
    dact = dact_ref[...] + pick(parts, label)
    rounded = act.astype(BF16)
    for m in range(xw_ref.shape[0]):
        dxw_ref[m] = dot(jnp.where(label_row == m, dproj, 0.0).astype(BF16), rounded)
    dconv = dact * (soft + act * (1.0 - soft))
    dcb_ref[...] = jnp.sum(dconv, axis=0, keepdims=True)
    pad_ref[pl.ds(0, rows), :] = dconv
    pad_ref[pl.ds(rows, tail), :] = jnp.zeros((tail, channels), F32)
    inner = inner_ref[...].astype(F32)
    total = None
    for tap in range(taps):
        shift = (taps - 1 - tap) * GROUP
        later = pad_ref[pl.ds(shift, rows), :]
        term = cw_ref[pl.ds(tap, 1), :].astype(F32) * later
        total = term if total is None else total + term
        dcw_ref[pl.ds(tap, 1), :] = jnp.sum(later * inner, axis=0, keepdims=True)
    dinner_ref[...] = by_sequence(total).astype(BF16)


def conv_backward(conv, inner, dact, dproj, label, label_row, cw, xw):
    rows, channels = conv.shape
    mods, wide = xw.shape[0], xw.shape[1]
    taps = cw.shape[0]
    return pl.pallas_call(
        conv_back_kernel,
        out_shape=(
            jax.ShapeDtypeStruct((rows, channels), BF16),
            jax.ShapeDtypeStruct((mods, wide, channels), F32),
            jax.ShapeDtypeStruct((taps, channels), F32),
            jax.ShapeDtypeStruct((1, channels), F32),
        ),
        scratch_shapes=[pltpu.VMEM((rows + (taps - 1) * GROUP, channels), F32)],
        compiler_params=params(),
        name="conv_backward",
    )(conv, inner, dact, dproj, label, label_row, cw, xw)


MESH = pl.DeviceIdType.MESH


def sum_body(
    chips, x_ref, out_ref, near, mine, far, total, every, other, near_sems, far_sems, back_sems, other_sems,
    work=lambda i: None,
):
    wide, rows = x_ref.shape
    half, part = rows // 2, rows // 2 // chips
    tok, ch = lax.axis_index("tok"), lax.axis_index("ch")
    chip, core = ch // 2, ch % 2
    partner = (tok, 2 * chip + 1 - core)
    chips_away = [(tok, 2 * (chip ^ d) + core) for d in range(1, chips)]

    def send(src, dst, sems, device):
        copy = pltpu.make_async_remote_copy(
            src_ref=src, dst_ref=dst, send_sem=sems.at[0], recv_sem=sems.at[1], device_id=device, device_id_type=MESH
        )
        copy.start()
        return copy

    def columns(index, size):
        return pl.ds(pl.multiple_of(index * size, size), size)

    copy = send(x_ref.at[:, columns(1 - core, half)], near, near_sems, partner)
    work(0)
    copy.wait()
    mine[...] = (x_ref[:, columns(core, half)] + near[...]).astype(BF16)
    copies = [
        send(mine.at[:, columns(chip ^ d, part)], far.at[d - 1], far_sems.at[d - 1], chips_away[d - 1])
        for d in range(1, chips)
    ]
    work(1)
    work(2)
    value = mine[:, columns(chip, part)].astype(F32)
    for d, copy in enumerate(copies):
        copy.wait()
        value = value + far[d].astype(F32)
    total[...] = value.astype(BF16)
    copies = [send(total, every.at[d - 1], back_sems.at[d - 1], chips_away[d - 1]) for d in range(1, chips)]
    copies += [send(total, other.at[0], other_sems.at[0], partner)]
    out_ref[:, columns(core * chips + chip, part)] = total[...].astype(F32)
    work(3)
    for d in range(1, chips):
        copies[d - 1].wait()
        copies += [send(every.at[d - 1], other.at[d], other_sems.at[d], partner)]
        out_ref[:, columns(core * chips + (chip ^ d), part)] = every[d - 1].astype(F32)
    for d in range(chips):
        copies[chips - 1 + d].wait()
        out_ref[:, columns((1 - core) * chips + (chip ^ d), part)] = other[d].astype(F32)


def sum_scratch(wide, rows, chips):
    half, part = rows // 2, rows // 2 // chips
    dma = pltpu.SemaphoreType.DMA
    return [
        pltpu.VMEM((wide, half), F32),
        pltpu.VMEM((wide, half), BF16),
        pltpu.VMEM((chips - 1, wide, part), BF16),
        pltpu.VMEM((wide, part), BF16),
        pltpu.VMEM((chips - 1, wide, part), BF16),
        pltpu.VMEM((chips, wide, part), BF16),
        dma((2,)),
        dma((chips - 1, 2)),
        dma((chips - 1, 2)),
        dma((chips, 2)),
    ]


def middle_kernel(
    chips, dproj_part_ref, gated_ref, label_seq_ref, ow_ref, conv_ref, inner_ref, dact_ref, label_ref, label_row_ref, cw_ref, xw_ref,
    branch_ref, every_gated_ref, dinner_ref, dxw_ref, dcw_ref, dcb_ref,
    weights, dproj, pad, w_sem, own_sem, tok_send, tok_recv, *sum_refs,
):
    group = gated_ref.shape[0]
    deep = ow_ref.shape[2]
    tok, ch = lax.axis_index("tok"), lax.axis_index("ch")
    fetch = pltpu.make_async_copy(ow_ref, weights, w_sem)
    fetch.start()

    def rows_of(index):
        return pl.ds(pl.multiple_of(index * group, group), group)

    own = pltpu.make_async_copy(gated_ref, every_gated_ref.at[rows_of(tok)], own_sem)
    own.start()
    barrier = pltpu.get_barrier_semaphore()
    peers = [(tok, ch ^ 1)] + [(tok, ch ^ (2 * d)) for d in range(1, chips)] + [(tok ^ g, ch) for g in (1, 2)]
    for device in peers:
        pl.semaphore_signal(barrier, inc=1, device_id=device, device_id_type=MESH)
    pl.semaphore_wait(barrier, len(peers))
    copies = [
        pltpu.make_async_remote_copy(
            src_ref=gated_ref,
            dst_ref=every_gated_ref.at[rows_of(tok)],
            send_sem=tok_send.at[side],
            recv_sem=tok_recv.at[side],
            device_id=(tok ^ (1 + side), ch),
            device_id_type=MESH,
        )
        for side in range(2)
    ]
    for copy in copies:
        copy.start()
    wide = deep // 4

    def work(i):
        if i == 0:
            fetch.wait()
        x, label = gated_ref[...], label_seq_ref[...]
        total = None
        for m in range(ow_ref.shape[0]):
            part = dot(jnp.where(label == m, x, jnp.zeros_like(x)), weights[m, :, pl.ds(i * wide, wide)])
            total = part if total is None else total + part
        branch_ref[:, pl.ds(i * wide, wide)] = total.astype(BF16)

    sum_body(chips, dproj_part_ref, dproj, *sum_refs, work=work)
    conv_back_kernel(
        conv_ref, inner_ref, dact_ref, dproj, label_ref, label_row_ref, cw_ref, xw_ref,
        dinner_ref, dxw_ref, dcw_ref, dcb_ref, pad,
    )
    for side in range(2):
        whole = every_gated_ref.at[rows_of(tok ^ (1 + side))]
        pltpu.make_async_copy(whole, whole, tok_recv.at[side]).wait()
        copies[side].wait_send()
    own.wait()


def middle(dproj_part, gated, label_seq, ow, conv, inner, dact, label, label_row, cw, xw, n, collective_id):
    group, channels = conv.shape
    mods, wide = xw.shape[0], xw.shape[1]
    taps, deep = cw.shape[0], ow.shape[2]
    dma = pltpu.SemaphoreType.DMA
    vmem = pl.BlockSpec(memory_space=pltpu.VMEM)
    any_space = pl.BlockSpec(memory_space=pl.ANY)
    return pl.pallas_call(
        functools.partial(middle_kernel, n // 2),
        out_shape=(
            jax.ShapeDtypeStruct((group, deep), BF16),
            jax.ShapeDtypeStruct((4 * group, channels), BF16),
            jax.ShapeDtypeStruct((group, channels), BF16),
            jax.ShapeDtypeStruct((mods, wide, channels), F32),
            jax.ShapeDtypeStruct((taps, channels), F32),
            jax.ShapeDtypeStruct((1, channels), F32),
        ),
        in_specs=[vmem, vmem, vmem, any_space] + [vmem] * 7,
        out_specs=(vmem, any_space, vmem, vmem, vmem, vmem),
        scratch_shapes=[
            pltpu.VMEM(ow.shape, BF16),
            pltpu.VMEM((wide, group), F32),
            pltpu.VMEM((group + (taps - 1) * GROUP, channels), F32),
            dma, dma, dma((2,)), dma((2,)),
        ] + sum_scratch(wide, group, n // 2),
        compiler_params=params(collective_id=collective_id, has_side_effects=True),
        cost_estimate=pl.CostEstimate(flops=2 * 10**10, bytes_accessed=10**7, transcendentals=0),
        name="middle",
    )(dproj_part, gated, label_seq, ow, conv, inner, dact, label, label_row, cw, xw)


def front_kernel(
    chips, input_ref, gain_ref, cot_ref, label_ref, iw_ref, ow_ref, cw_ref, cb_ref, xw_ref,
    scaled_ref, core_cot_ref, near_cot_ref, pair_cot_ref, labels_ref, label_ref_seq, label_ref_time, label_ref_row, gate_ref, gated_grad_ref, conv_ref, inner_out_ref, proj_ref,
    own_rows, in_w, out_w, chunk_rows, staged, xz, proj_part, pad,
    in_sem, out_sem, load_sem, own_sem,
    line_send, line_recv, near_send, near_recv, tok_send, tok_recv, diag_send, diag_recv,
    xz_send, xz_recv, lab_send, lab_recv, lab_tok_send, lab_tok_recv,
    keep_sem, pair_send, pair_recv, pair_diag_send, pair_diag_recv, *sum_refs,
):
    n = 2 * chips
    length, deep = input_ref.shape
    group, chunk = n * length, 2 * length
    mods, width = ow_ref.shape[0], ow_ref.shape[1]
    tok, ch = lax.axis_index("tok"), lax.axis_index("ch")
    chip, core = ch // 2, ch % 2

    fetch_in = pltpu.make_async_copy(iw_ref, in_w, in_sem)
    fetch_in.start()
    fetch_out = pltpu.make_async_copy(ow_ref, out_w, out_sem)
    fetch_out.start()

    rows = input_ref[...].astype(F32)
    inverse = lax.rsqrt(jnp.mean(rows * rows, axis=-1, keepdims=True) + 1e-05)
    own_rows[...] = (rows * inverse * gain_ref[...].astype(F32)[None, :]).astype(BF16)
    labels_ref[tok, ch] = jnp.broadcast_to(label_ref[...][None, :], (8, length))

    def block(g, device):
        return pl.ds(pl.multiple_of(g * group + device * length, length), length)

    own = (
        pltpu.make_async_copy(own_rows, scaled_ref.at[block(tok, ch)], own_sem.at[0]),
        pltpu.make_async_copy(cot_ref, core_cot_ref.at[pl.ds(pl.multiple_of(chip * length, length), length)], own_sem.at[1]),
    )
    for copy in own:
        copy.start()

    barrier = pltpu.get_barrier_semaphore()
    peers = [(tok, ch ^ e) for e in range(1, n)] + [(tok ^ g, ch) for g in range(1, 4)]
    for device in peers:
        pl.semaphore_signal(barrier, inc=1, device_id=device, device_id_type=MESH)
    pl.semaphore_wait(barrier, len(peers))

    def remote(src, dst, send_sem, recv_sem, device):
        return pltpu.make_async_remote_copy(
            src_ref=src, dst_ref=dst, send_sem=send_sem, recv_sem=recv_sem, device_id=device, device_id_type=MESH
        )

    def arrive(ref, sem):
        pltpu.make_async_copy(ref, ref, sem).wait()

    label_copies = [
        remote(labels_ref.at[tok, ch], labels_ref.at[tok, ch], lab_send.at[e - 1], lab_recv.at[e - 1], (tok, ch ^ e))
        for e in range(1, n)
    ]
    for copy in label_copies:
        copy.start()

    def from_line(x, o):
        if x == 0:
            return scaled_ref.at[block(tok, 2 * o + core)]
        return core_cot_ref.at[pl.ds(pl.multiple_of(o * length, length), length)]

    def line_copy(x, o, side):
        ref = from_line(x, o)
        target = lax.rem(ch + (2 if side == 0 else n - 2), n)
        return remote(ref, ref, line_send.at[x, side, o], line_recv.at[x, o], (tok, target))

    def near_copy(x, o, g):
        if x == 0:
            src = dst = scaled_ref.at[block(tok ^ g, 2 * o + core)]
        else:
            src, dst = from_line(1, o), near_cot_ref.at[pl.ds(pl.multiple_of(o * length, length), length)]
        return remote(src, dst, near_send.at[x, g, o], near_recv.at[x, g, o], (tok, ch ^ 1))

    def tok_copy(o, side):
        ref = scaled_ref.at[block(tok, 2 * o + core)]
        return remote(ref, ref, tok_send.at[side, o], tok_recv.at[side, o], (tok ^ (1 + side), ch))

    def half_block(g, o, side):
        start = g * group + (2 * o + core) * length + side * (length // 2)
        return pl.ds(pl.multiple_of(start, length // 2), length // 2)

    def diag_copy(o, side):
        ref = scaled_ref.at[half_block(tok ^ (1 + side), o, side)]
        return remote(ref, ref, diag_send.at[side, o], diag_recv.at[side, o], (tok ^ (2 - side), ch))

    def goes(o, side):
        return (o <= chip) & (chip < chips - 1) if side == 0 else (o >= chip) & (chip > 0)

    def launch(x, o):
        for side in range(2):
            pl.when(goes(o, side))(line_copy(x, o, side).start)
        near_copy(x, o, 0).start()
        if x == 0:
            for side in range(2):
                tok_copy(o, side).start()

    base = chip - chip % 2

    def pair_copy(i, side):
        src, dst = from_line(1, base + i), pair_cot_ref.at[tok, i]
        return remote(src, dst, pair_send.at[side, i], pair_recv.at[side, i], (tok ^ (1 + side), ch))

    def pair_diag(i, side):
        ref = pair_cot_ref.at[tok ^ (1 + side), i, pl.ds(side * (length // 2), length // 2)]
        return remote(ref, ref, pair_diag_send.at[side, i], pair_diag_recv.at[side, i], (tok ^ (2 - side), ch))

    def pair_pass(i):
        for side in range(2):
            arrive(pair_cot_ref.at[tok ^ (1 + side), i], pair_recv.at[side, i])
            pair_diag(i, side).start()

    def accept(x, o):
        arrive(from_line(x, o), line_recv.at[x, o])
        launch(x, o)
        if x == 1:
            for side in range(2):
                pl.when(o // 2 == chip // 2)(pair_copy(o % 2, side).start)

    def pass_on(o):
        for side in range(2):
            arrive(scaled_ref.at[block(tok ^ (1 + side), 2 * o + core)], tok_recv.at[side, o])
            diag_copy(o, side).start()
            near_copy(0, o, 1 + side).start()

    def pass_last(o):
        for side in range(2):
            arrive(scaled_ref.at[half_block(tok ^ 3, o, side)], diag_recv.at[side, o])
        near_copy(0, o, 3).start()

    def load(x, o):
        if x == 0:
            arrive(scaled_ref.at[block(tok, 2 * o + 1 - core)], near_recv.at[0, 0, o])
            source = scaled_ref.at[pl.ds(pl.multiple_of(tok * group + o * chunk, chunk), chunk)]
            copies = [pltpu.make_async_copy(source, chunk_rows, load_sem.at[0])]
        else:
            other = near_cot_ref.at[pl.ds(pl.multiple_of(o * length, length), length)]
            arrive(other, near_recv.at[1, 0, o])
            copies = [
                pltpu.make_async_copy(
                    ref, chunk_rows.at[pl.ds(pl.multiple_of(q * length, length), length)], load_sem.at[at]
                )
                for at, (ref, q) in enumerate(((from_line(1, o), core), (other, 1 - core)))
            ]
        for copy in copies:
            copy.start()
        for copy in copies:
            copy.wait()

    def label_column(o):
        return jnp.concatenate(
            [labels_ref[tok, 2 * o + q].astype(F32).T[:, 0:1] for q in range(2)], axis=0
        )

    kind = ch // chips
    pair = ch % chips

    def xz_copies(o, h):
        target = 2 * pair + h
        src = staged.at[o, h]
        dst = xz.at[kind, pl.ds(pl.multiple_of(o * chunk, chunk), chunk)]
        return target, remote(src, dst, xz_send.at[o, h], xz_recv.at[kind, o], (tok, target)), pltpu.make_async_copy(
            src, dst, xz_recv.at[kind, o]
        )

    def project(o):
        load(0, o)
        label = label_column(o)
        for h in range(2):
            x = chunk_rows[...]
            parts = [dot(x, in_w[m, :, pl.ds(h * width, width)]) for m in range(mods)]
            staged[o, h] = pick(parts, label).astype(BF16)
            target, copy, local = xz_copies(o, h)
            pl.when(target != ch)(copy.start)
            pl.when(target == ch)(local.start)

    def project_back(o):
        load(1, o)
        label = label_column(o)
        x = chunk_rows[...]
        parts = [dot_bt(x, out_w[m]) for m in range(mods)]
        gated_grad_ref[pl.ds(pl.multiple_of(o * chunk, chunk), chunk), :] = pick(parts, label).astype(BF16)

        @pl.when(o // 2 == chip // 2)
        def _():
            mine = chunk_rows.at[pl.ds(pl.multiple_of(core * length, length), length)]
            copy = pltpu.make_async_copy(mine, pair_cot_ref.at[tok, o % 2], keep_sem)
            copy.start()
            copy.wait()

    def both_sides(i, fn):
        for o in (chip - i, chip + i):
            pl.when((o >= 0) & (o < chips))(functools.partial(fn, o))

    def every_distance(fn):
        fn(chip)

        def body(i, carry):
            both_sides(i, fn)
            return carry

        lax.fori_loop(1, chips, body, 0)

    own[0].wait()
    launch(0, chip)
    for e in range(1, n):
        arrive(labels_ref.at[tok, ch ^ e], lab_recv.at[e - 1])
    fetch_in.wait()
    project(chip)

    def step(i, carry):
        both_sides(i, functools.partial(accept, 0))
        both_sides(i, project)
        pl.when(i == 1)(functools.partial(pass_on, chip))
        pl.when(i > 1)(functools.partial(both_sides, i - 1, pass_on))
        return carry

    lax.fori_loop(1, chips, step, 0)
    own[1].wait()
    launch(1, chip)
    for side in range(2):
        pair_copy(chip % 2, side).start()
    label_tok = [
        remote(labels_ref.at[tok], labels_ref.at[tok], lab_tok_send.at[g - 1], lab_tok_recv.at[g - 1], (tok ^ g, ch))
        for g in range(1, 4)
    ]
    for copy in label_tok:
        copy.start()
    fetch_out.wait()
    project_back(chip)
    both_sides(chips - 1, pass_on)

    def step_back(i, carry):
        both_sides(i, functools.partial(accept, 1))
        both_sides(i, project_back)
        return carry

    lax.fori_loop(1, chips - 1, step_back, 0)
    every_distance(pass_last)
    pair_pass(chip % 2)

    for o in range(chips):
        for a in range(2):
            arrive(xz.at[a, pl.ds(o * chunk, chunk)], xz_recv.at[a, o])
    gate_ref[...] = xz[1]
    taps = cw_ref.shape[0]
    lead = (taps - 1) * GROUP
    inner = by_time(xz[0])
    inner_out_ref[...] = inner.astype(BF16)
    pad[pl.ds(0, lead), :] = jnp.zeros((lead, width), F32)
    pad[pl.ds(lead, group), :] = inner
    conv = jnp.broadcast_to(cb_ref[...].astype(F32)[None, :], (group, width))
    for tap in range(taps):
        conv = conv + cw_ref[pl.ds(tap, 1), :].astype(F32) * pad[pl.ds(tap * GROUP, group), :]
    conv_ref[...] = conv
    act = conv * sigmoid(conv)
    label = jnp.concatenate(
        [jnp.broadcast_to(labels_ref[tok, d].astype(F32).T[:, 0:1], (length, 128)) for d in range(n)], axis=0
    )
    label_ref_seq[...] = label[:, 0:1].astype(jnp.int32)
    label = by_time(label)
    label_ref_time[...] = label[:, 0:1].astype(jnp.int32)
    label_ref_row[...] = label.T[0:1, :].astype(jnp.int32)
    label = jnp.concatenate([label] * (width // 128), axis=1)
    total = None
    for m in range(mods):
        high, low = halves(jnp.where(label == m, act, 0.0))
        part = dot_bt(xw_ref[m], high) + dot_bt(xw_ref[m], low)
        total = part if total is None else total + part
    proj_part[...] = total

    both_sides(chips - 1, functools.partial(accept, 1))
    pair_pass(1 - chip % 2)
    sum_body(chips, proj_part, proj_ref, *sum_refs)
    both_sides(chips - 1, project_back)

    def finish(o, carry):
        for g in range(4):
            if g > 0:
                arrive(scaled_ref.at[block(tok ^ g, 2 * o + 1 - core)], near_recv.at[0, g, o])
            near_copy(0, o, g).wait_send()
        near_copy(1, o, 0).wait_send()
        for side in range(2):
            for x in range(2):
                pl.when(goes(o, side))(line_copy(x, o, side).wait_send)
            tok_copy(o, side).wait_send()
            diag_copy(o, side).wait_send()
        return carry

    lax.fori_loop(0, chips, finish, 0)
    for i in range(2):
        for side in range(2):
            pair_copy(i, side).wait_send()
            pair_diag(i, side).wait_send()
            part = pair_cot_ref.at[tok ^ 3, i, pl.ds(side * (length // 2), length // 2)]
            arrive(part, pair_diag_recv.at[side, i])
    for o in range(chips):
        for h in range(2):
            target, copy, _ = xz_copies(o, h)
            pl.when(target != ch)(copy.wait_send)
    for copy in label_copies:
        copy.wait_send()
    for g in range(1, 4):
        arrive(labels_ref.at[tok ^ g], lab_tok_recv.at[g - 1])
        label_tok[g - 1].wait_send()


def way_in(block_input, gain, cotangent, modality, in_weight, out_weight, conv_weight, conv_bias, x_weight, n, collective_id):
    length, deep = block_input.shape
    mods, width = out_weight.shape[0], out_weight.shape[1]
    group, chips = n * length, n // 2
    wide = x_weight.shape[1]
    lead = (conv_weight.shape[0] - 1) * GROUP
    dma = pltpu.SemaphoreType.DMA
    vmem = pl.BlockSpec(memory_space=pltpu.VMEM)
    any_space = pl.BlockSpec(memory_space=pl.ANY)
    return pl.pallas_call(
        functools.partial(front_kernel, chips),
        out_shape=(
            jax.ShapeDtypeStruct((4 * group, deep), BF16),
            jax.ShapeDtypeStruct((chips * length, deep), BF16),
            jax.ShapeDtypeStruct((chips * length, deep), BF16),
            jax.ShapeDtypeStruct((4, 2, length, deep), BF16),
            jax.ShapeDtypeStruct((4, n, 8, length), jnp.int32),
            jax.ShapeDtypeStruct((group, 1), jnp.int32),
            jax.ShapeDtypeStruct((group, 1), jnp.int32),
            jax.ShapeDtypeStruct((1, group), jnp.int32),
            jax.ShapeDtypeStruct((group, width), BF16),
            jax.ShapeDtypeStruct((group, width), BF16),
            jax.ShapeDtypeStruct((group, width), F32),
            jax.ShapeDtypeStruct((group, width), BF16),
            jax.ShapeDtypeStruct((wide, group), F32),
        ),
        in_specs=[vmem, vmem, any_space, vmem, any_space, any_space, vmem, vmem, vmem],
        out_specs=(any_space,) * 4 + (vmem,) * 9,
        scratch_shapes=[
            pltpu.VMEM((length, deep), BF16),
            pltpu.VMEM(in_weight.shape, BF16),
            pltpu.VMEM(out_weight.shape, BF16),
            pltpu.VMEM((2 * length, deep), BF16),
            pltpu.VMEM((chips, 2, 2 * length, width), BF16),
            pltpu.VMEM((2, group, width), BF16),
            pltpu.VMEM((wide, group), F32),
            pltpu.VMEM((group + lead, width), F32),
            dma, dma, dma((2,)), dma((2,)),
            dma((2, 2, chips)), dma((2, chips)), dma((2, 4, chips)), dma((2, 4, chips)),
            dma((2, chips)), dma((2, chips)), dma((2, chips)), dma((2, chips)),
            dma((chips, 2)), dma((2, chips)), dma((n - 1,)), dma((n - 1,)), dma((3,)), dma((3,)),
            dma, dma((2, 2)), dma((2, 2)), dma((2, 2)), dma((2, 2)),
        ] + sum_scratch(wide, group, chips),
        compiler_params=params(collective_id=collective_id, has_side_effects=True),
        cost_estimate=pl.CostEstimate(flops=10**11, bytes_accessed=10**8, transcendentals=0),
        name="way_in",
    )(
        block_input, gain, cotangent, modality, in_weight, out_weight, conv_weight, conv_bias, x_weight,
    )


def small_places(values):
    start, places = 0, []
    for value in values:
        for m in range(value.shape[0]) if len(value.shape) == 3 else [None]:
            places.append((start, (value, m)))
            start += -(-value.shape[-2] // 8) * 8
    return places


def back_kernel(
    chips, dinner_ref, dgate_ref, w_ref, label_ref, input_ref, cot_ref, gain_ref, pair_cot_ref, rest_cot_ref, scaled_ref, label_row_ref, every_gated_ref,
    dxw_ref, ddtw_ref, ddtb_ref, dcw_ref, dcb_ref, dalog_ref, dskip_ref,
    xall_ref, row_grad_ref, gain_sum_ref, near_pair_ref, near_rest_ref, grad_part_ref, small_ref, diag_gated_ref,
    weights, sends, near_part, chip_sums, arrived, mine, gain_send, gain_arrived, gain_mine, gain_others, left, made,
    packed, rounded, small_in, small_all,
    w_sem, to_col, from_own, to_tok, from_tok, to_diag, from_diag, to_near, from_near, to_row, from_row, to_gain, from_gain, to_gain_tok, from_gain_tok, cot_sems, left_sems, made_sems, to_small, from_small, to_all, from_all,
    to_gated_diag, from_gated_diag,
):
    n = 2 * chips
    group, width = dinner_ref.shape
    mods, deep = w_ref.shape[0], w_ref.shape[1]
    length = group // n
    chunk = 2 * length
    tok, ch = lax.axis_index("tok"), lax.axis_index("ch")
    chip, core = ch // 2, ch % 2
    beside, below = tok ^ 1, tok ^ 2

    fetch = pltpu.make_async_copy(w_ref, weights, w_sem)
    fetch.start()

    first = tok - tok % 2
    tile_rows = left.shape[3]
    tiles = deep // tile_rows

    def left_copies(i):
        at = pl.ds(pl.multiple_of(i * tile_rows, tile_rows), tile_rows)
        return [
            pltpu.make_async_copy(
                scaled_ref.at[pl.ds(pl.multiple_of((first + g) * group, group), group), at],
                left.at[lax.rem(i, 2), g],
                left_sems.at[lax.rem(i, 2), g],
            )
            for g in range(2)
        ]

    def made_copy(i):
        at = pl.ds(pl.multiple_of(i * tile_rows, tile_rows), tile_rows)
        return pltpu.make_async_copy(made.at[lax.rem(i, 2)], grad_part_ref.at[:, at], made_sems.at[lax.rem(i, 2)])

    def grad_tile(i, carry):
        for copy in left_copies(i):
            copy.wait()
        pl.when(i >= 2)(made_copy(i - 2).wait)
        slot = lax.rem(i, 2)
        lanes = [pl.ds(pl.multiple_of((first + g) * group, group), group) for g in range(2)]
        stacked = [by_kind(left[slot, g].T, label_row_ref[:, lanes[g]], mods) for g in range(2)]
        for h in range(2):
            total = dot(stacked[0], xall_ref[h, lanes[0], :]) + dot(stacked[1], xall_ref[h, lanes[1], :])
            for m in range(mods):
                made[slot, m, :, pl.ds(h * width, width)] = total[m * tile_rows : (m + 1) * tile_rows]
        made_copy(i).start()

        @pl.when(i + 2 < tiles)
        def _():
            for copy in left_copies(i + 2):
                copy.start()

        return carry

    for i in range(2):
        for copy in left_copies(i):
            copy.start()

    barrier = pltpu.get_barrier_semaphore()
    peers = [(tok, ch ^ e) for e in range(1, n)] + [(tok ^ g, ch) for g in range(1, 4)]
    for device in peers:
        pl.semaphore_signal(barrier, inc=1, device_id=device, device_id_type=MESH)
    pl.semaphore_wait(barrier, len(peers))

    def remote(src, dst, send_sem, recv_sem, device):
        return pltpu.make_async_remote_copy(
            src_ref=src, dst_ref=dst, send_sem=send_sem, recv_sem=recv_sem, device_id=device, device_id_type=MESH
        )

    def rows_of(index, size):
        return pl.ds(pl.multiple_of(index * size, size), size)

    def all_rows(group_index, chunk_index):
        return pl.ds(pl.multiple_of(group_index * group + chunk_index * chunk, chunk), chunk)

    cot_copies = [
        remote(src, dst, cot_sems.at[i, 0], cot_sems.at[i, 1], (tok, ch ^ 1))
        for i, (src, dst) in enumerate(((pair_cot_ref, near_pair_ref), (rest_cot_ref, near_rest_ref)))
    ]

    order = [2, 3, 1, 0]
    owners = [ch // 2, chips + ch // 2]
    out_copies = []

    def give(j):
        for a, src_ref in enumerate((dinner_ref, dgate_ref)):
            owner = owners[a]
            k = owner // 2 ^ j
            src = src_ref.at[rows_of(k, chunk)]
            dst = xall_ref.at[core, all_rows(tok, k)]
            copy = remote(src, dst, to_col.at[j, a], from_own.at[j, core], (tok, owner))
            local = pltpu.make_async_copy(src, dst, from_own.at[j, core])
            pl.when(owner != ch)(copy.start)
            pl.when(owner == ch)(local.start)
            out_copies.append((owner, copy))

    give(order[0])
    give(order[1])
    half = group // 2
    gated_copies = []
    for side, (source, target) in enumerate(((beside, below), (below, beside))):
        src = every_gated_ref.at[rows_of(2 * source + side, half)]
        dst = diag_gated_ref.at[pl.ds(side * half, half)]
        copy = remote(src, dst, to_gated_diag.at[side], from_gated_diag.at[side], (target, ch))
        copy.start()
        gated_copies.append(copy)
    quarter = rounded.shape[0] // 4
    packed[...] = jnp.zeros_like(packed)
    for start, (ref, m) in small_places(
        (dxw_ref, ddtw_ref, ddtb_ref, dcw_ref, dcb_ref, dalog_ref, dskip_ref)
    ):
        value = ref[...] if m is None else ref[m]
        packed[pl.ds(start, value.shape[0]), :] = value
    rounded[...] = packed[...].astype(BF16)
    small_copies = [
        remote(
            rounded.at[rows_of(tok ^ g, quarter)],
            small_in.at[g - 1],
            to_small.at[g - 1],
            from_small.at[g - 1],
            (tok ^ g, ch),
        )
        for g in range(1, 4)
    ]
    for copy in small_copies:
        copy.start()

    fetch.wait()
    for copy in cot_copies:
        copy.start()
    tok_copies, row_copies, diag_copies, near_copies = [], [], [], []

    def pass_on(j):
        k = chip ^ j
        for side, (source, target) in enumerate(((beside, below), (below, beside))):
            whole = xall_ref.at[:, all_rows(source, k)]
            pltpu.make_async_copy(whole, whole, from_tok.at[side, j]).wait()
            part = xall_ref.at[side, all_rows(source, k)]
            copy = remote(part, part, to_diag.at[side, j], from_diag.at[side, j], (target, ch))
            copy.start()
            diag_copies.append(copy)

    def both_cores(j):
        pltpu.make_async_copy(near_part.at[j], near_part.at[j], from_near.at[j]).wait()
        value = sends[j, rows_of(core, length), :].astype(F32) + near_part[j].astype(F32)
        if j == 0:
            mine[...] = value
        else:
            chip_sums[j - 1] = value.astype(BF16)
            target = 2 * (chip ^ j) + core
            copy = remote(chip_sums.at[j - 1], arrived.at[j - 1], to_row.at[j - 1], from_row.at[j - 1], (tok, target))
            copy.start()
            row_copies.append(copy)

    for at, j in enumerate(order):
        k = chip ^ j
        for h in range(2):
            half = xall_ref.at[h, all_rows(tok, k)]
            pltpu.make_async_copy(half, half, from_own.at[j, h]).wait()
        whole = xall_ref.at[:, all_rows(tok, k)]
        for side, target in enumerate((beside, below)):
            copy = remote(whole, whole, to_tok.at[side, j], from_tok.at[side, j], (target, ch))
            copy.start()
            tok_copies.append(copy)
        if at + 2 < chips:
            give(order[at + 2])
        label = label_ref[rows_of(k, chunk), :]
        halves_of = [xall_ref[h, all_rows(tok, k), :] for h in range(2)]
        tile = min(deep, 512)

        def product(i, carry, label=label, halves_of=halves_of, j=j):
            at = pl.ds(pl.multiple_of(i * tile, tile), tile)
            total = None
            for m in range(mods):
                for h in range(2):
                    x = jnp.where(label == m, halves_of[h], jnp.zeros_like(halves_of[h]))
                    part = dot_bt(x, weights[m, at, pl.ds(h * width, width)])
                    total = part if total is None else total + part
            sends[j, :, at] = total.astype(BF16)
            return carry

        lax.fori_loop(0, deep // tile, product, 0)
        copy = remote(
            sends.at[j, rows_of(1 - core, length)], near_part.at[j], to_near.at[j], from_near.at[j], (tok, ch ^ 1)
        )
        copy.start()
        near_copies.append(copy)
    for j in order:
        both_cores(j)
    value = packed[rows_of(tok, quarter), :]
    for copy in small_copies:
        copy.wait()
    for g in range(3):
        value = value + small_in[g].astype(F32)
    small_all[tok] = value.astype(BF16)
    small_copies = [
        remote(small_all.at[tok], small_all.at[tok], to_all.at[g - 1], from_all.at[g - 1], (tok ^ g, ch))
        for g in range(1, 4)
    ]
    for copy in small_copies:
        copy.start()
    for j in order:
        pass_on(j)
    lax.fori_loop(0, tiles - 2, grad_tile, 0)
    total = mine[...]
    for e in range(chips - 1):
        pltpu.make_async_copy(arrived.at[e], arrived.at[e], from_row.at[e]).wait()
        total = total + arrived[e].astype(F32)
    rows = input_ref[...].astype(F32)
    inverse = lax.rsqrt(jnp.mean(rows * rows, axis=-1, keepdims=True) + 1e-05)
    normed = rows * inverse
    ng = total * gain_ref[...].astype(F32)
    row_grad_ref[...] = cot_ref[...].astype(F32) + inverse * (
        ng - normed * jnp.mean(ng * normed, axis=-1, keepdims=True)
    )
    own = deep // n
    gain_term = jnp.sum(total * normed, axis=0, keepdims=True)
    for d in range(n):
        gain_send[d] = jnp.broadcast_to(gain_term[:, d * own : (d + 1) * own], (8, own))
    gain_copies = []
    for e in range(1, n):
        copy = remote(gain_send.at[ch ^ e], gain_arrived.at[e - 1], to_gain.at[e - 1], from_gain.at[e - 1], (tok, ch ^ e))
        copy.start()
        gain_copies.append(copy)
    grad_tile(tiles - 2, 0)
    value = gain_send[ch]
    for e in range(1, n):
        gain_copies[e - 1].wait()
        value = value + gain_arrived[e - 1]
    gain_mine[...] = value
    gain_copies = []
    for g in range(1, 4):
        copy = remote(gain_mine, gain_others.at[g - 1], to_gain_tok.at[g - 1], from_gain_tok.at[g - 1], (tok ^ g, ch))
        copy.start()
        gain_copies.append(copy)
    grad_tile(tiles - 1, 0)
    for copy in gain_copies:
        copy.wait()
    even, odd = gain_mine[...] + gain_others[0], gain_others[1] + gain_others[2]
    gain_sum_ref[...] = even + odd

    for j in range(chips):
        for side in range(2):
            part = xall_ref.at[side, all_rows(tok ^ 3, chip ^ j)]
            pltpu.make_async_copy(part, part, from_diag.at[side, j]).wait()
    for owner, copy in out_copies:
        pl.when(owner != ch)(copy.wait_send)
    for copy in tok_copies + diag_copies + row_copies + near_copies:
        copy.wait_send()
    for copy in cot_copies:
        copy.wait()
    for copy in gated_copies:
        copy.wait()
    for g in range(1, 4):
        pltpu.make_async_copy(small_all.at[tok ^ g], small_all.at[tok ^ g], from_all.at[g - 1]).wait()
        small_copies[g - 1].wait_send()
    for g in range(4):
        small_ref[pl.ds(g * quarter, quarter), :] = small_all[g].astype(F32)
    for i in (tiles - 2, tiles - 1):
        made_copy(i).wait()


def way_back(
    dinner, dgate, w, label, block_input, cotangent, gain, pair_cot, rest_cot, every_scaled, every_label, every_gated, small, n, collective_id
):
    group, width = dinner.shape
    mods, deep, _ = w.shape
    chips, length = n // 2, group // n
    dma = pltpu.SemaphoreType.DMA
    vmem = pl.BlockSpec(memory_space=pltpu.VMEM)
    tile = min(256, deep)
    last, (value, _) = small_places(small)[-1]
    quarter = -(-(last + value.shape[-2]) // 64) * 16
    any_space = pl.BlockSpec(memory_space=pl.ANY)
    return pl.pallas_call(
        functools.partial(back_kernel, chips),
        out_shape=(
            jax.ShapeDtypeStruct((2, 4 * group, width), BF16),
            jax.ShapeDtypeStruct((length, deep), F32),
            jax.ShapeDtypeStruct((8, deep // n), F32),
            jax.ShapeDtypeStruct(pair_cot.shape, BF16),
            jax.ShapeDtypeStruct(rest_cot.shape, BF16),
            jax.ShapeDtypeStruct(w.shape, F32),
            jax.ShapeDtypeStruct((4 * quarter, width), F32),
            jax.ShapeDtypeStruct((group, width), BF16),
        ),
        in_specs=[vmem, vmem, any_space, vmem, vmem, vmem, vmem, any_space, any_space, any_space, vmem, any_space]
        + [vmem] * len(small),
        out_specs=(vmem, vmem, vmem, any_space, any_space, any_space, vmem, any_space),
        scratch_shapes=[
            pltpu.VMEM(w.shape, BF16),
            pltpu.VMEM((chips, 2 * length, deep), BF16),
            pltpu.VMEM((chips, length, deep), BF16),
            pltpu.VMEM((chips - 1, length, deep), BF16),
            pltpu.VMEM((chips - 1, length, deep), BF16),
            pltpu.VMEM((length, deep), F32),
            pltpu.VMEM((n, 8, deep // n), F32),
            pltpu.VMEM((n - 1, 8, deep // n), F32),
            pltpu.VMEM((8, deep // n), F32),
            pltpu.VMEM((3, 8, deep // n), F32),
            pltpu.VMEM((2, 2, group, tile), BF16),
            pltpu.VMEM((2, mods, tile, 2 * width), F32),
            pltpu.VMEM((4 * quarter, width), F32),
            pltpu.VMEM((4 * quarter, width), BF16),
            pltpu.VMEM((3, quarter, width), BF16),
            pltpu.VMEM((4, quarter, width), BF16),
            dma, dma((chips, 2)), dma((chips, 2)), dma((2, chips)), dma((2, chips)), dma((2, chips)), dma((2, chips)),
            dma((chips,)), dma((chips,)), dma((chips - 1,)), dma((chips - 1,)), dma((n - 1,)), dma((n - 1,)), dma((3,)), dma((3,)), dma((2, 2)), dma((2, 2)), dma((2,)),
            dma((3,)), dma((3,)), dma((3,)), dma((3,)),
            dma((2,)), dma((2,)),
        ],
        compiler_params=params(collective_id=collective_id, has_side_effects=True),
        cost_estimate=pl.CostEstimate(flops=10**11, bytes_accessed=10**8, transcendentals=0),
        name="way_back",
    )(dinner, dgate, w, label, block_input, cotangent, gain[None, :], pair_cot, rest_cot, every_scaled, every_label, every_gated, *small)


def grad_parts_kernel(which_ref, *refs):
    del which_ref
    count = (len(refs) - 1) // 3
    out_ref = refs[-1]
    mods, tile, wide = out_ref.shape
    stacked = []
    for left_ref, label_ref in zip(refs[:count], refs[count : 2 * count], strict=True):
        groups, _, chips, _, length, _ = left_ref.shape
        turned = left_ref[...].reshape(groups * chips * length, tile).T
        blocks = [
            by_kind(turned[:, (g * chips + o) * length : (g * chips + o + 1) * length], label_ref[g, 0, o, 0], mods)
            for g in range(groups)
            for o in range(chips)
        ]
        stacked.append(jnp.concatenate(blocks, axis=1))
    step = min(512, wide)
    for start in range(0, wide, step):
        at = pl.ds(start, step)
        total = None
        for rows, right_ref in zip(stacked, refs[2 * count : -1], strict=True):
            part = dot(rows, right_ref[:, at])
            total = part if total is None else total + part
        for m in range(mods):
            out_ref[m, :, at] = total[m * tile : (m + 1) * tile]


def weight_grad_parts(left, rights, label, which, mods, tile):
    groups, pairs, chips, cores, length, deep = left.shape
    size, wide = rights[0].shape
    rows = left.size // deep
    chosen = [(flip, turn) for flip in range(2) for turn in range(2)]

    def block(last, moves, flip, turn):
        def index(i, which):
            return (0, which[0] ^ flip, 0, which[1] ^ turn, 0, i if moves else 0)

        return pl.BlockSpec((groups, 1, chips, 1) + last, index)

    whole = pl.BlockSpec((size, wide), lambda i, which: (0, 0), pipeline_mode=pl.Buffered(1))
    return pl.pallas_call(
        grad_parts_kernel,
        out_shape=jax.ShapeDtypeStruct((mods, deep, wide), F32),
        grid_spec=pltpu.PrefetchScalarGridSpec(
            num_scalar_prefetch=1,
            grid=(deep // tile,),
            in_specs=[block((length, tile), True, *c) for c in chosen]
            + [block((1, length), False, *c) for c in chosen]
            + [whole] * len(rights),
            out_specs=pl.BlockSpec((mods, tile, wide), lambda i, which: (0, i, 0)),
        ),
        compiler_params=params(),
        cost_estimate=pl.CostEstimate(
            flops=2 * mods * rows * deep * wide,
            bytes_accessed=2 * rows * (deep + wide) + 4 * mods * deep * wide,
            transcendentals=0,
        ),
        name="weight_grad_parts",
    )(which, *[left] * 4, *[label] * 4, *rights)


def grad_last_kernel(which_ref, left_ref, right_ref, label_ref, left2_ref, right2_ref, label2_ref, part_ref, out_ref, made):
    del which_ref
    mods, tile, _ = out_ref.shape
    wide = right_ref.shape[2]
    stacked = [
        by_kind(x[...].T, label[...], mods) for x, label in ((left_ref, label_ref), (left2_ref, label2_ref))
    ]
    for h in range(right_ref.shape[0]):
        at = pl.ds(h * wide, wide)
        made[...] = dot(stacked[0], right_ref[h]) + dot(stacked[1], right2_ref[h])
        for m in range(mods):
            out_ref[m, :, at] = part_ref[m, :, at] + made[pl.ds(m * tile, tile), :]


def weight_grad_last(left, right, label, part, which, tile):
    mods, deep, wide = part.shape
    group = left.shape[0] // 4
    of_group = [
        spec
        for g in range(2)
        for spec in (
            pl.BlockSpec((group, tile), lambda i, which, g=g: (which[g], i)),
            pl.BlockSpec((right.shape[0], group, right.shape[2]), lambda i, which, g=g: (0, which[g], 0)),
            pl.BlockSpec((1, group), lambda i, which, g=g: (0, which[g])),
        )
    ]
    return pl.pallas_call(
        grad_last_kernel,
        out_shape=jax.ShapeDtypeStruct(part.shape, F32),
        grid_spec=pltpu.PrefetchScalarGridSpec(
            num_scalar_prefetch=1,
            grid=(deep // tile,),
            in_specs=of_group + [pl.BlockSpec((mods, tile, wide), lambda i, which: (0, i, 0))],
            out_specs=pl.BlockSpec((mods, tile, wide), lambda i, which: (0, i, 0)),
            scratch_shapes=[pltpu.VMEM((mods * tile, right.shape[2]), F32)],
        ),
        compiler_params=params(),
        cost_estimate=pl.CostEstimate(
            flops=4 * mods * group * deep * wide,
            bytes_accessed=8 * mods * deep * wide,
            transcendentals=0,
        ),
        name="weight_grad_last",
    )(which, left, right, label, left, right, label, part)


def grad_kernel(left_ref, right_ref, label_ref, out_ref):
    left, label = left_ref[...], label_ref[...]
    wide = right_ref.shape[2]
    turned = left.T
    for m in range(out_ref.shape[0]):
        masked = jnp.where(label == m, turned, jnp.zeros_like(turned))
        for h in range(right_ref.shape[0]):
            out_ref[m, :, pl.ds(h * wide, wide)] = dot(masked, right_ref[h])


def grad_part_kernel(left_ref, right_ref, label_ref, out_ref):
    left, label = left_ref[...], label_ref[...]
    wide = right_ref.shape[2]
    turned = left.T
    first = pl.program_id(1) == 0
    for m in range(out_ref.shape[0]):
        masked = jnp.where(label == m, turned, jnp.zeros_like(turned))
        for h in range(right_ref.shape[0]):
            at = pl.ds(h * wide, wide)
            part = dot(masked, right_ref[h])
            out_ref[m, :, at] = jnp.where(first, part, out_ref[m, :, at] + part)


def weight_grad(left, right, label, mods, tile):
    rows, deep = left.shape
    wide = right.shape[0] * right.shape[2]
    block = min(rows, 4096)
    tile = min(tile, deep)
    return pl.pallas_call(
        grad_kernel if block == rows else grad_part_kernel,
        out_shape=jax.ShapeDtypeStruct((mods, deep, wide), F32),
        grid=(deep // tile, rows // block),
        in_specs=[
            pl.BlockSpec((block, tile), lambda i, j: (j, i)),
            pl.BlockSpec((right.shape[0], block, right.shape[2]), lambda i, j: (0, j, 0)),
            pl.BlockSpec((1, block), lambda i, j: (0, j)),
        ],
        out_specs=pl.BlockSpec((mods, tile, wide), lambda i, j: (0, i, 0)),
        compiler_params=params(),
        cost_estimate=pl.CostEstimate(
            flops=2 * mods * rows * deep * wide,
            bytes_accessed=2 * rows * (deep + wide) + 4 * mods * deep * wide,
            transcendentals=0,
        ),
        name="weight_grad",
    )(left, right, label)


def by_groups(fn, count, arrays, axes, joined):
    if count == 1:
        return fn(*arrays)

    def cut(a, axis, i):
        size = a.shape[axis] // count
        return lax.slice_in_dim(a, i * size, (i + 1) * size, axis=axis)

    outs = [fn(*(cut(a, axis, i) for a, axis in zip(arrays, axes, strict=True))) for i in range(count)]
    return tuple(
        jnp.concatenate(values, axis=joined[at]) if at < len(joined) else functools.reduce(jnp.add, values)
        for at, values in enumerate(zip(*outs, strict=True))
    )


def exchange_pairs(n):
    half = n // 2
    first = [(c, 2 * c) if c < half else (c, 2 * (c - half) + 1) for c in range(n)]
    second = [(c, 2 * c + 1) if c < half else (c, 2 * (c - half)) for c in range(n)]
    return first, second


def to_owners(xz, n):
    first, second = exchange_pairs(n)
    c = lax.axis_index("ch")
    width = xz.shape[1] // 2
    left, right = xz[:, :width], xz[:, width:]
    lower = c < n // 2
    one = lax.ppermute(jnp.where(lower, left, right), "ch", first)
    two = lax.ppermute(jnp.where(lower, right, left), "ch", second)
    even = c % 2 == 0
    return jnp.where(even, one, two), jnp.where(even, two, one)


def to_columns(dinner, dgate, n):
    first, second = exchange_pairs(n)
    c = lax.axis_index("ch")
    even = c % 2 == 0
    one = lax.ppermute(jnp.where(even, dinner, dgate), "ch", [(b, a) for a, b in first])
    two = lax.ppermute(jnp.where(even, dgate, dinner), "ch", [(b, a) for a, b in second])
    lower = c < n // 2
    return jnp.concatenate([jnp.where(lower, one, two), jnp.where(lower, two, one)], axis=1)


def on_device(
    n,
    block_input,
    norm_gain,
    in_weight,
    x_weight,
    dt_weight,
    dt_bias,
    conv_weight,
    conv_bias,
    a_log,
    skip_gain,
    out_weight,
    modality,
    cotangent,
):
    mods = in_weight.shape[0]
    length = block_input.shape[0]
    count = n // GROUP
    fast = n == GROUP and lax.axis_size("tok") == 4 and length % 128 == 0
    rows_float = block_input.astype(F32)
    gain = norm_gain.astype(F32)
    inverse = lax.rsqrt(jnp.mean(rows_float * rows_float, axis=-1, keepdims=True) + 1e-05)
    normed = rows_float * inverse
    scaled = (normed * gain[None, :]).astype(BF16)

    token_group = n * length
    if fast:
        every_scaled, core_cot, _, pair_cot, labels, label, label_by_time, label_row, gate, gated_grad, conv, inner_by_time, proj = way_in(
            block_input, norm_gain, cotangent, modality, in_weight, out_weight, conv_weight, conv_bias, x_weight, n, 0
        )
        every_label = labels[:, :, 0, :].reshape(4 * token_group)
        rest = (1 - lax.axis_index("ch") // 4) * 2 * length
        rest_cot = lax.all_gather(lax.dynamic_slice_in_dim(core_cot, rest, 2 * length, 0), "tok", axis=0, tiled=True)
    else:
        every_label = lax.all_gather(modality, ("tok", "ch"), axis=0, tiled=True)
    if not fast:
        group_label = lax.dynamic_slice_in_dim(every_label, lax.axis_index("tok") * token_group, token_group, 0)
        label = group_label[:, None]
        label_by_time = group_label.reshape(count, GROUP, length).transpose(0, 2, 1).reshape(token_group, 1)
        label_row = label_by_time.reshape(1, token_group)
        group_rows = lax.all_gather(scaled, "ch", axis=0, tiled=True)
        every_scaled = lax.all_gather(scaled, ("tok", "ch"), axis=0, tiled=True)
        every_cot = lax.all_gather(cotangent, ("tok", "ch"), axis=0, tiled=True)
        xz = routed_select(group_rows, label, in_weight, 256, False)
        inner, gate = to_owners(xz, n)
        group_cot = lax.all_gather(cotangent, "ch", axis=0, tiled=True)
        gated_grad = routed_select(group_cot, label, out_weight, 128, True)
        conv, inner_by_time, proj_part = by_groups(
            lambda a, b: conv_forward(a, b, conv_weight, conv_bias, x_weight), count, (inner, label_row), (0, 1), (0, 0, 1)
        )
        proj = lax.psum(proj_part, "ch")

    gated, dgate, dact, dproj_part, ddtw, ddtb, dalog, dskip = by_groups(
        lambda a, b, c, d, e: scan_both(a, b, c, d, e, dt_weight, dt_bias, a_log, skip_gain),
        count,
        (conv, proj, gate, gated_grad, label_by_time),
        (0, 1, 0, 0, 0),
        (0, 0, 0, 1),
    )
    if fast:
        branch_part, every_gated, dinner, dxw, dcw, dcb = middle(
            dproj_part, gated, label, out_weight, conv, inner_by_time, dact, label_by_time, label_row, conv_weight, x_weight, n, 1
        )
    else:
        dproj = lax.psum(dproj_part, "ch")
        dinner, dxw, dcw, dcb = by_groups(
            lambda a, b, c, d, e, f: conv_backward(a, b, c, d, e, f, conv_weight, x_weight),
            count,
            (conv, inner_by_time, dact, dproj, label_by_time, label_row),
            (0, 0, 0, 1, 0, 1),
            (0,),
        )
        branch_part = routed_spread(gated, label, out_weight, 512, False, BF16)
        every_gated = lax.all_gather(gated, "tok", axis=0, tiled=True)
    every_label = every_label[None, :]
    small = (dxw, ddtw, ddtb, dcw, dcb, dalog, dskip)
    if fast:
        pair_cot = pair_cot.reshape(rest_cot.shape)
        every_grad, row_grad, gain_grad, near_pair, near_rest, grad_part, total, diag_gated = way_back(
            dinner, dgate, in_weight, label, block_input, cotangent, norm_gain, pair_cot, rest_cot, every_scaled, every_label,
            every_gated, small, n, 2,
        )
        fourth = (lax.axis_index("tok") ^ 3) * token_group
        every_gated = lax.dynamic_update_slice_in_dim(every_gated, diag_gated, fourth, 0)
        gain_grad = gain_grad[0]
    else:
        xz_grad = to_columns(dinner, dgate, n)
        scaled_part = routed_spread(xz_grad, label, in_weight, 256, True, BF16)
        scaled_grad = lax.psum_scatter(scaled_part, "ch", scatter_dimension=0, tiled=True).astype(F32)
        gain_grad = lax.psum_scatter(jnp.sum(scaled_grad * normed, axis=0), "ch", scatter_dimension=0, tiled=True)
        ng = scaled_grad * gain[None, :]
        row_grad = cotangent.astype(F32) + inverse * (ng - normed * jnp.mean(ng * normed, axis=-1, keepdims=True))
        every_grad = lax.all_gather(xz_grad, "tok", axis=0, tiled=True)[None]

    if fast:
        branch_part, row_grad = lax.optimization_barrier((branch_part, row_grad))
    branch = lax.psum_scatter(branch_part, "ch", scatter_dimension=0, tiled=True).astype(F32)
    block_out = (rows_float + branch).astype(BF16)
    if fast:
        ch = lax.axis_index("ch")
        split = (4, 2, 2, 2)
        out_weight_grad = weight_grad_parts(
            every_gated.reshape(split + (length, every_gated.shape[1])),
            (pair_cot, near_pair, rest_cot, near_rest),
            every_label.reshape(split + (1, length)),
            jnp.stack([ch // 4, ch % 2]).astype(jnp.int32),
            mods,
            256,
        )
    else:
        out_weight_grad = weight_grad(every_gated, every_cot[None], every_label, mods, 128)
    if fast:
        others = (2 - lax.axis_index("tok") // 2 * 2 + jnp.arange(2)).astype(jnp.int32)
        in_weight_grad = weight_grad_last(every_scaled, every_grad, every_label, grad_part, others, 256)
    else:
        in_weight_grad = weight_grad(every_scaled, every_grad, every_label, mods, 256)
    sums = []
    if fast:
        starts = [start for start, (_, m) in small_places(small) if not m]
        for start, value in zip(starts, small, strict=True):
            size = math.prod(value.shape[:-1])
            sums.append(lax.slice_in_dim(total, start, start + size, axis=0).reshape(value.shape))
    else:
        gain_grad = lax.psum(gain_grad, "tok")
        flat = [value.reshape(-1, value.shape[-1]) for value in small]
        total = lax.psum(jnp.concatenate(flat, axis=0), "tok")
        start = 0
        for value, rows in zip(small, flat, strict=True):
            sums.append(lax.slice_in_dim(total, start, start + rows.shape[0], axis=0).reshape(value.shape))
            start += rows.shape[0]
    dxw, ddtw, ddtb, dcw, dcb, dalog, dskip = sums
    return (
        block_out,
        row_grad,
        gain_grad,
        in_weight_grad,
        dxw,
        ddtw,
        ddtb,
        dcw,
        dcb[0],
        dalog,
        dskip[0],
        out_weight_grad,
    )


def solution(mesh):
    placed = (
        P(("tok", "ch"), None),
        P(),
        P(None, None, "ch"),
        P(None, None, "ch"),
        P(None, None, "ch"),
        P(None, "ch"),
        P(None, "ch"),
        P("ch"),
        P(None, "ch"),
        P("ch"),
        P(None, "ch", None),
        P(("tok", "ch")),
        P(("tok", "ch"), None),
    )
    return jax.shard_map(
        functools.partial(on_device, mesh.shape["ch"]),
        mesh=mesh,
        in_specs=placed,
        out_specs=(
            P(("tok", "ch"), None),
            P(("tok", "ch"), None),
            P("ch"),
            P(None, None, "ch"),
            P(None, None, "ch"),
            P(None, None, "ch"),
            P(None, "ch"),
            P(None, "ch"),
            P("ch"),
            P(None, "ch"),
            P("ch"),
            P(None, "ch", None),
        ),
        check_vma=False,
    )
```

```python
import functools
import math

import jax
import jax.numpy as jnp
from jax import lax
from jax.experimental import pallas as pl
from jax.experimental.pallas import tpu as pltpu
from jax.sharding import PartitionSpec as P

F32 = jnp.float32
BF16 = jnp.bfloat16
LOG2E = math.log2(math.e)
LN2 = math.log(2.0)
GROUP = 8
VMEM_LIMIT = 58 << 20


def params(**kw):
    return pltpu.CompilerParams(vmem_limit_bytes=VMEM_LIMIT, **kw)


def dot(a, b):
    return lax.dot_general(a, b, (((1,), (0,)), ((), ())), preferred_element_type=F32)


def dot_bt(a, b):
    return lax.dot_general(a, b, (((1,), (1,)), ((), ())), preferred_element_type=F32)


def dot_at(a, b):
    return lax.dot_general(a, b, (((0,), (0,)), ((), ())), preferred_element_type=F32)


def halves(x):
    high = x.astype(BF16)
    return high, (x - high.astype(F32)).astype(BF16)


def pick(parts, label):
    total = parts[-1]
    for index in range(len(parts) - 2, -1, -1):
        total = jnp.where(label == index, parts[index], total)
    return total


def by_kind(turned, label, mods):
    return jnp.concatenate([jnp.where(label == m, turned, jnp.zeros_like(turned)) for m in range(mods)], axis=0)


def sigmoid(x):
    return 0.5 * jnp.tanh(0.5 * x) + 0.5


def select_kernel(transposed, x_ref, label_ref, w_ref, out_ref):
    x = x_ref[...]
    label = label_ref[...]
    product = dot_bt if transposed else dot
    parts = [product(x, w_ref[m]) for m in range(w_ref.shape[0])]
    out_ref[...] = pick(parts, label).astype(out_ref.dtype)


def routed_select(x, label, w, tile, transposed):
    rows, depth = x.shape
    mods = w.shape[0]
    outer = w.shape[1] if transposed else w.shape[2]
    tile = min(tile, outer)
    block = min(rows, 1024)
    if transposed:
        w_spec = pl.BlockSpec((mods, tile, depth), lambda i, j: (0, j, 0))
    else:
        w_spec = pl.BlockSpec((mods, depth, tile), lambda i, j: (0, 0, j))
    return pl.pallas_call(
        functools.partial(select_kernel, transposed),
        out_shape=jax.ShapeDtypeStruct((rows, outer), BF16),
        grid=(rows // block, outer // tile),
        in_specs=[
            pl.BlockSpec((block, depth), lambda i, j: (i, 0)),
            pl.BlockSpec((block, 1), lambda i, j: (i, 0)),
            w_spec,
        ],
        out_specs=pl.BlockSpec((block, tile), lambda i, j: (i, j)),
        compiler_params=params(),
        cost_estimate=pl.CostEstimate(
            flops=2 * rows * depth * outer * mods, bytes_accessed=2 * mods * depth * outer + 2 * rows * (depth + outer), transcendentals=0
        ),
        name="routed_select",
    )(x, label, w)


def spread_kernel(transposed, x_ref, label_ref, w_ref, out_ref):
    x = x_ref[...]
    label = label_ref[...]
    product = dot_bt if transposed else dot
    total = None
    for m in range(w_ref.shape[0]):
        part = product(jnp.where(label == m, x, jnp.zeros_like(x)), w_ref[m])
        total = part if total is None else total + part
    out_ref[...] = total.astype(out_ref.dtype)


def routed_spread(x, label, w, tile, transposed, dtype):
    rows, depth = x.shape
    mods = w.shape[0]
    outer = w.shape[1] if transposed else w.shape[2]
    tile = min(tile, outer)
    block = min(rows, 1024)
    if transposed:
        w_spec = pl.BlockSpec((mods, tile, depth), lambda i, j: (0, j, 0))
    else:
        w_spec = pl.BlockSpec((mods, depth, tile), lambda i, j: (0, 0, j))
    return pl.pallas_call(
        functools.partial(spread_kernel, transposed),
        out_shape=jax.ShapeDtypeStruct((rows, outer), dtype),
        grid=(rows // block, outer // tile),
        in_specs=[
            pl.BlockSpec((block, depth), lambda i, j: (i, 0)),
            pl.BlockSpec((block, 1), lambda i, j: (i, 0)),
            w_spec,
        ],
        out_specs=pl.BlockSpec((block, tile), lambda i, j: (i, j)),
        compiler_params=params(),
        cost_estimate=pl.CostEstimate(
            flops=2 * rows * depth * outer * mods, bytes_accessed=2 * mods * depth * outer + 2 * rows * (depth + outer), transcendentals=0
        ),
        name="routed_spread",
    )(x, label, w)


def by_time(x):
    rows, width = x.shape
    return jnp.swapaxes(x.astype(F32).reshape(GROUP, rows // GROUP, width), 0, 1).reshape(rows, width)


def by_sequence(x):
    rows, width = x.shape
    return jnp.swapaxes(x.reshape(rows // GROUP, GROUP, width), 0, 1).reshape(rows, width)


def conv_kernel(inner_ref, label_ref, cw_ref, cb_ref, xw_ref, conv_ref, inner_out_ref, proj_ref, pad_ref):
    rows, channels = inner_ref.shape
    taps = cw_ref.shape[0]
    lead = (taps - 1) * GROUP
    inner = by_time(inner_ref[...])
    inner_out_ref[...] = inner.astype(BF16)
    pad_ref[pl.ds(0, lead), :] = jnp.zeros((lead, channels), F32)
    pad_ref[pl.ds(lead, rows), :] = inner
    conv = jnp.broadcast_to(cb_ref[...].astype(F32), (rows, channels))
    for tap in range(taps):
        conv = conv + cw_ref[pl.ds(tap, 1), :].astype(F32) * pad_ref[pl.ds(tap * GROUP, rows), :]
    conv_ref[...] = conv
    high, low = halves(conv * sigmoid(conv))
    label = label_ref[...]
    parts = [dot_bt(xw_ref[m], high) + dot_bt(xw_ref[m], low) for m in range(xw_ref.shape[0])]
    proj_ref[...] = pick(parts, label)


def conv_forward(inner, label, cw, cb, xw):
    rows, channels = inner.shape
    wide = xw.shape[1]
    lead = (cw.shape[0] - 1) * GROUP
    return pl.pallas_call(
        conv_kernel,
        out_shape=(
            jax.ShapeDtypeStruct((rows, channels), F32),
            jax.ShapeDtypeStruct((rows, channels), BF16),
            jax.ShapeDtypeStruct((wide, rows), F32),
        ),
        scratch_shapes=[pltpu.VMEM((rows + lead, channels), F32)],
        compiler_params=params(),
        name="conv_forward",
    )(inner, label, cw, cb[None, :], xw)


def scan_kernel(
    conv_ref, proj_ref, gate_ref, grad_ref, label_ref, dtw_ref, dtb_ref, alog_ref, skip_ref,
    gated_ref, dgate_ref, dact_ref, dproj_ref, ddtw_ref, ddtb_ref, dalog_ref, dskip_ref,
    hist, mix, prod, rate, act, step, slope, dout, scanned, dstep, dlow, low_turned, low_rank, label,
):
    rows, width = conv_ref.shape
    length = rows // GROUP
    states = alog_ref.shape[0]
    mods, low_width = dtw_ref.shape[0], dtw_ref.shape[1]
    tile = pl.program_id(0)
    ddrive = scanned

    @pl.when(tile == 0)
    def _():
        prod[...] = jnp.zeros_like(prod)
        dlow[...] = jnp.zeros_like(dlow)
        label[...] = jnp.broadcast_to(label_ref[...], (rows, width))
        low_rank[...] = proj_ref[pl.ds(0, low_width), :].astype(BF16)
        low_turned[...] = proj_ref[pl.ds(0, low_width), :].T.astype(BF16)
        turned = proj_ref[pl.ds(low_width, 2 * states), :].T.astype(BF16)
        row = lax.broadcasted_iota(jnp.int32, (2 * states, 2 * width), 0)
        column = lax.broadcasted_iota(jnp.int32, (2 * states, 2 * width), 1)
        for s in range(0, 2 * states, 2):
            spread = dot(turned, (row == s + (column >= width).astype(jnp.int32)).astype(BF16))
            mix[s] = spread[:, :width]
            mix[s + 1] = spread[:, width:]

    kind = label[...]
    parts = [dot(low_turned[...], dtw_ref[m]) + dtb_ref[pl.ds(m, 1), :].astype(F32) for m in range(mods)]
    speed = pick(parts, kind)
    step[...] = jnp.maximum(speed, 0.0) + jnp.log1p(jnp.exp(-jnp.abs(speed)))
    slope[...] = sigmoid(speed)
    conv = conv_ref[...]
    act[...] = conv * sigmoid(conv)
    for s in range(states):
        rate[s] = jnp.broadcast_to(-LOG2E * jnp.exp(alog_ref[pl.ds(s, 1), :].astype(F32)), (GROUP, width))
        hist[0, s] = jnp.zeros((GROUP, width), F32)

    def forward(t, state):
        at = pl.ds(pl.multiple_of(t * GROUP, GROUP), GROUP)
        now = step[at, :]
        drive = now * act[at, :]
        total = None
        new = []
        for s in range(states):
            value = jnp.exp2(now * rate[s]) * state[s] + mix[s, at, :] * drive
            hist[t + 1, s] = value
            new.append(value)
            term = mix[states + s, at, :] * value
            total = term if total is None else total + term
        scanned[at, :] = total
        return tuple(new)

    zero = jnp.zeros((GROUP, width), F32)
    lax.fori_loop(0, length, forward, (zero,) * states, unroll=8)

    gate = gate_ref[...].astype(F32)
    grad = by_time(grad_ref[...])
    soft = sigmoid(gate)
    opened = gate * soft
    skip = skip_ref[...].astype(F32)
    summed = scanned[...] + skip * act[...]
    gated_ref[...] = by_sequence(summed * opened).astype(BF16)
    dgate = grad * summed * (soft + opened * (1.0 - soft))
    dgate_ref[...] = by_sequence(dgate).astype(BF16)
    dsummed = grad * opened
    dout[...] = dsummed
    dskip_ref[...] = jnp.sum(dsummed * act[...], axis=0, keepdims=True)

    def backward(i, carry):
        t = length - 1 - i
        at = pl.ds(pl.multiple_of(t * GROUP, GROUP), GROUP)
        now = step[at, :]
        drive = now * act[at, :]
        out = dout[at, :]
        dd, ds = None, None
        new, drates = [], []
        for s in range(states):
            decay = jnp.exp2(now * rate[s])
            dstate = carry[s] + mix[states + s, at, :] * out
            prod[states + s, at, :] += out * hist[t + 1, s]
            prod[s, at, :] += dstate * drive
            term = dstate * mix[s, at, :]
            dd = term if dd is None else dd + term
            passed = dstate * decay
            new.append(passed)
            change = passed * hist[t, s]
            term = change * rate[s]
            ds = term if ds is None else ds + term
            drates.append(carry[states + s] + change * now)
        ddrive[at, :] = dd
        dstep[at, :] = ds
        return tuple(new + drates)

    final = lax.fori_loop(0, length, backward, (zero,) * (2 * states), unroll=4)

    for s in range(states):
        dalog_ref[pl.ds(s, 1), :] = LN2 * jnp.sum(final[states + s] * rate[s], axis=0, keepdims=True)
    dact_ref[...] = ddrive[...] * step[...] + skip * dout[...]
    dspeed = (dstep[...] * LN2 + ddrive[...] * act[...]) * slope[...]
    rounded = dspeed.astype(BF16)
    of_rank = kind if width == low_width else label_ref[...]
    dlow[...] += pick([dot_bt(rounded, dtw_ref[m]) for m in range(mods)], of_rank)
    for m in range(mods):
        own = kind == m
        masked = jnp.where(own, dspeed, 0.0)
        ddtw_ref[m] = dot(low_rank[...], masked.astype(BF16))
        ddtb_ref[pl.ds(m, 1), :] = jnp.sum(masked, axis=0, keepdims=True)

    @pl.when(tile == pl.num_programs(0) - 1)
    def _():
        column = lax.broadcasted_iota(jnp.int32, (width, 2 * states), 1)
        sums = jnp.zeros((rows, 2 * states), F32)
        for s in range(2 * states):
            sums = sums + dot(prod[s].astype(BF16), (column == s).astype(BF16))
        dproj_ref[pl.ds(0, low_width), :] = dlow[...].T
        dproj_ref[pl.ds(low_width, 2 * states), :] = sums.T


def scan_both(conv, proj, gate, grad, label, dtw, dtb, alog, skip):
    rows, channels = conv.shape
    width = min(128, channels)
    length = rows // GROUP
    states = alog.shape[0]
    mods, low_width = dtw.shape[0], dtw.shape[1]
    wide = proj.shape[0]

    def whole(shape):
        return pl.BlockSpec(shape, lambda j: (0,) * len(shape), pipeline_mode=pl.Buffered(1))

    def cut(*shape):
        return pl.BlockSpec(shape + (width,), lambda j: (0,) * len(shape) + (j,))

    plane = (GROUP, width)
    flat = pltpu.VMEM((rows, width), F32)
    return pl.pallas_call(
        scan_kernel,
        out_shape=(
            jax.ShapeDtypeStruct((rows, channels), BF16),
            jax.ShapeDtypeStruct((rows, channels), BF16),
            jax.ShapeDtypeStruct((rows, channels), F32),
            jax.ShapeDtypeStruct((wide, rows), F32),
            jax.ShapeDtypeStruct((mods, low_width, channels), F32),
            jax.ShapeDtypeStruct((mods, channels), F32),
            jax.ShapeDtypeStruct((states, channels), F32),
            jax.ShapeDtypeStruct((1, channels), F32),
        ),
        grid=(channels // width,),
        in_specs=[
            cut(rows), whole((wide, rows)), cut(rows), cut(rows), whole((rows, 1)),
            cut(mods, low_width), cut(mods), cut(states), cut(1),
        ],
        out_specs=(
            cut(rows), cut(rows), cut(rows), whole((wide, rows)), cut(mods, low_width), cut(mods), cut(states), cut(1),
        ),
        scratch_shapes=[
            pltpu.VMEM((length + 1, states) + plane, F32),
            pltpu.VMEM((2 * states, rows, width), F32),
            pltpu.VMEM((2 * states, rows, width), F32),
            pltpu.VMEM((states,) + plane, F32),
            flat, flat, flat, flat, flat, flat,
            pltpu.VMEM((rows, low_width), F32),
            pltpu.VMEM((rows, low_width), BF16),
            pltpu.VMEM((low_width, rows), BF16),
            pltpu.VMEM((rows, width), jnp.int32),
        ],
        compiler_params=params(),
        cost_estimate=pl.CostEstimate(flops=5000 * rows * channels * states, bytes_accessed=20 * rows * channels, transcendentals=0),
        name="scan_both",
    )(conv, proj, gate, grad, label, dtw, dtb, alog, skip[None, :])


def conv_back_kernel(
    conv_ref, inner_ref, dact_ref, dproj_ref, label_ref, label_row_ref, cw_ref, xw_ref,
    dinner_ref, dxw_ref, dcw_ref, dcb_ref, pad_ref,
):
    rows, channels = conv_ref.shape
    taps = cw_ref.shape[0]
    tail = (taps - 1) * GROUP
    label, label_row = label_ref[...], label_row_ref[...]
    conv = conv_ref[...]
    soft = sigmoid(conv)
    act = conv * soft
    dproj = dproj_ref[...]
    turned = dproj.T.astype(BF16)
    parts = [dot(turned, xw_ref[m]) for m in range(xw_ref.shape[0])]
    dact = dact_ref[...] + pick(parts, label)
    rounded = act.astype(BF16)
    for m in range(xw_ref.shape[0]):
        dxw_ref[m] = dot(jnp.where(label_row == m, dproj, 0.0).astype(BF16), rounded)
    dconv = dact * (soft + act * (1.0 - soft))
    dcb_ref[...] = jnp.sum(dconv, axis=0, keepdims=True)
    pad_ref[pl.ds(0, rows), :] = dconv
    pad_ref[pl.ds(rows, tail), :] = jnp.zeros((tail, channels), F32)
    inner = inner_ref[...].astype(F32)
    total = None
    for tap in range(taps):
        shift = (taps - 1 - tap) * GROUP
        later = pad_ref[pl.ds(shift, rows), :]
        term = cw_ref[pl.ds(tap, 1), :].astype(F32) * later
        total = term if total is None else total + term
        dcw_ref[pl.ds(tap, 1), :] = jnp.sum(later * inner, axis=0, keepdims=True)
    dinner_ref[...] = by_sequence(total).astype(BF16)


def conv_backward(conv, inner, dact, dproj, label, label_row, cw, xw):
    rows, channels = conv.shape
    mods, wide = xw.shape[0], xw.shape[1]
    taps = cw.shape[0]
    return pl.pallas_call(
        conv_back_kernel,
        out_shape=(
            jax.ShapeDtypeStruct((rows, channels), BF16),
            jax.ShapeDtypeStruct((mods, wide, channels), F32),
            jax.ShapeDtypeStruct((taps, channels), F32),
            jax.ShapeDtypeStruct((1, channels), F32),
        ),
        scratch_shapes=[pltpu.VMEM((rows + (taps - 1) * GROUP, channels), F32)],
        compiler_params=params(),
        name="conv_backward",
    )(conv, inner, dact, dproj, label, label_row, cw, xw)


MESH = pl.DeviceIdType.MESH


def sum_body(
    chips, x_ref, out_ref, near, mine, far, total, every, other, near_sems, far_sems, back_sems, other_sems,
    work=lambda i: None,
):
    wide, rows = x_ref.shape
    half, part = rows // 2, rows // 2 // chips
    tok, ch = lax.axis_index("tok"), lax.axis_index("ch")
    chip, core = ch // 2, ch % 2
    partner = (tok, 2 * chip + 1 - core)
    chips_away = [(tok, 2 * (chip ^ d) + core) for d in range(1, chips)]

    def send(src, dst, sems, device):
        copy = pltpu.make_async_remote_copy(
            src_ref=src, dst_ref=dst, send_sem=sems.at[0], recv_sem=sems.at[1], device_id=device, device_id_type=MESH
        )
        copy.start()
        return copy

    def columns(index, size):
        return pl.ds(pl.multiple_of(index * size, size), size)

    copy = send(x_ref.at[:, columns(1 - core, half)], near, near_sems, partner)
    work(0)
    copy.wait()
    mine[...] = (x_ref[:, columns(core, half)] + near[...]).astype(BF16)
    copies = [
        send(mine.at[:, columns(chip ^ d, part)], far.at[d - 1], far_sems.at[d - 1], chips_away[d - 1])
        for d in range(1, chips)
    ]
    work(1)
    work(2)
    value = mine[:, columns(chip, part)].astype(F32)
    for d, copy in enumerate(copies):
        copy.wait()
        value = value + far[d].astype(F32)
    total[...] = value.astype(BF16)
    copies = [send(total, every.at[d - 1], back_sems.at[d - 1], chips_away[d - 1]) for d in range(1, chips)]
    copies += [send(total, other.at[0], other_sems.at[0], partner)]
    out_ref[:, columns(core * chips + chip, part)] = total[...].astype(F32)
    work(3)
    for d in range(1, chips):
        copies[d - 1].wait()
        copies += [send(every.at[d - 1], other.at[d], other_sems.at[d], partner)]
        out_ref[:, columns(core * chips + (chip ^ d), part)] = every[d - 1].astype(F32)
    for d in range(chips):
        copies[chips - 1 + d].wait()
        out_ref[:, columns((1 - core) * chips + (chip ^ d), part)] = other[d].astype(F32)


def sum_scratch(wide, rows, chips):
    half, part = rows // 2, rows // 2 // chips
    dma = pltpu.SemaphoreType.DMA
    return [
        pltpu.VMEM((wide, half), F32),
        pltpu.VMEM((wide, half), BF16),
        pltpu.VMEM((chips - 1, wide, part), BF16),
        pltpu.VMEM((wide, part), BF16),
        pltpu.VMEM((chips - 1, wide, part), BF16),
        pltpu.VMEM((chips, wide, part), BF16),
        dma((2,)),
        dma((chips - 1, 2)),
        dma((chips - 1, 2)),
        dma((chips, 2)),
    ]


def middle_kernel(
    chips, dproj_part_ref, gated_ref, label_seq_ref, ow_ref, conv_ref, inner_ref, dact_ref, label_ref, label_row_ref, cw_ref, xw_ref,
    branch_ref, every_gated_ref, dinner_ref, dxw_ref, dcw_ref, dcb_ref,
    weights, dproj, pad, w_sem, own_sem, tok_send, tok_recv, *sum_refs,
):
    group = gated_ref.shape[0]
    deep = ow_ref.shape[2]
    tok, ch = lax.axis_index("tok"), lax.axis_index("ch")
    fetch = pltpu.make_async_copy(ow_ref, weights, w_sem)
    fetch.start()

    def rows_of(index):
        return pl.ds(pl.multiple_of(index * group, group), group)

    own = pltpu.make_async_copy(gated_ref, every_gated_ref.at[rows_of(tok)], own_sem)
    own.start()
    barrier = pltpu.get_barrier_semaphore()
    peers = [(tok, ch ^ 1)] + [(tok, ch ^ (2 * d)) for d in range(1, chips)] + [(tok ^ g, ch) for g in (1, 2)]
    for device in peers:
        pl.semaphore_signal(barrier, inc=1, device_id=device, device_id_type=MESH)
    pl.semaphore_wait(barrier, len(peers))
    copies = [
        pltpu.make_async_remote_copy(
            src_ref=gated_ref,
            dst_ref=every_gated_ref.at[rows_of(tok)],
            send_sem=tok_send.at[side],
            recv_sem=tok_recv.at[side],
            device_id=(tok ^ (1 + side), ch),
            device_id_type=MESH,
        )
        for side in range(2)
    ]
    for copy in copies:
        copy.start()
    wide = deep // 4

    def work(i):
        if i == 0:
            fetch.wait()
        x, label = gated_ref[...], label_seq_ref[...]
        total = None
        for m in range(ow_ref.shape[0]):
            part = dot(jnp.where(label == m, x, jnp.zeros_like(x)), weights[m, :, pl.ds(i * wide, wide)])
            total = part if total is None else total + part
        branch_ref[:, pl.ds(i * wide, wide)] = total.astype(BF16)

    sum_body(chips, dproj_part_ref, dproj, *sum_refs, work=work)
    conv_back_kernel(
        conv_ref, inner_ref, dact_ref, dproj, label_ref, label_row_ref, cw_ref, xw_ref,
        dinner_ref, dxw_ref, dcw_ref, dcb_ref, pad,
    )
    for side in range(2):
        whole = every_gated_ref.at[rows_of(tok ^ (1 + side))]
        pltpu.make_async_copy(whole, whole, tok_recv.at[side]).wait()
        copies[side].wait_send()
    own.wait()


def middle(dproj_part, gated, label_seq, ow, conv, inner, dact, label, label_row, cw, xw, n, collective_id):
    group, channels = conv.shape
    mods, wide = xw.shape[0], xw.shape[1]
    taps, deep = cw.shape[0], ow.shape[2]
    dma = pltpu.SemaphoreType.DMA
    vmem = pl.BlockSpec(memory_space=pltpu.VMEM)
    any_space = pl.BlockSpec(memory_space=pl.ANY)
    return pl.pallas_call(
        functools.partial(middle_kernel, n // 2),
        out_shape=(
            jax.ShapeDtypeStruct((group, deep), BF16),
            jax.ShapeDtypeStruct((4 * group, channels), BF16),
            jax.ShapeDtypeStruct((group, channels), BF16),
            jax.ShapeDtypeStruct((mods, wide, channels), F32),
            jax.ShapeDtypeStruct((taps, channels), F32),
            jax.ShapeDtypeStruct((1, channels), F32),
        ),
        in_specs=[vmem, vmem, vmem, any_space] + [vmem] * 7,
        out_specs=(vmem, any_space, vmem, vmem, vmem, vmem),
        scratch_shapes=[
            pltpu.VMEM(ow.shape, BF16),
            pltpu.VMEM((wide, group), F32),
            pltpu.VMEM((group + (taps - 1) * GROUP, channels), F32),
            dma, dma, dma((2,)), dma((2,)),
        ] + sum_scratch(wide, group, n // 2),
        compiler_params=params(collective_id=collective_id, has_side_effects=True),
        cost_estimate=pl.CostEstimate(flops=2 * 10**10, bytes_accessed=10**7, transcendentals=0),
        name="middle",
    )(dproj_part, gated, label_seq, ow, conv, inner, dact, label, label_row, cw, xw)


def front_kernel(
    chips, input_ref, gain_ref, cot_ref, label_ref, iw_ref, ow_ref, cw_ref, cb_ref, xw_ref,
    scaled_ref, core_cot_ref, near_cot_ref, pair_cot_ref, rest_cot_ref, labels_ref, label_ref_all, label_ref_seq, label_ref_time, label_ref_row, gate_ref, gated_grad_ref, conv_ref, inner_out_ref, proj_ref,
    own_rows, in_w, out_w, chunk_rows, staged, xz, proj_part, pad,
    in_sem, out_sem, load_sem, own_sem,
    line_send, line_recv, near_send, near_recv, tok_send, tok_recv, diag_send, diag_recv,
    xz_send, xz_recv, lab_send, lab_recv, lab_tok_send, lab_tok_recv,
    keep_sem, pair_send, pair_recv, pair_diag_send, pair_diag_recv, *sum_refs,
):
    n = 2 * chips
    length, deep = input_ref.shape
    group, chunk = n * length, 2 * length
    mods, width = ow_ref.shape[0], ow_ref.shape[1]
    tok, ch = lax.axis_index("tok"), lax.axis_index("ch")
    chip, core = ch // 2, ch % 2

    fetch_in = pltpu.make_async_copy(iw_ref, in_w, in_sem)
    fetch_in.start()
    fetch_out = pltpu.make_async_copy(ow_ref, out_w, out_sem)
    fetch_out.start()

    rows = input_ref[...].astype(F32)
    inverse = lax.rsqrt(jnp.mean(rows * rows, axis=-1, keepdims=True) + 1e-05)
    own_rows[...] = (rows * inverse * gain_ref[...].astype(F32)[None, :]).astype(BF16)
    labels_ref[tok, ch] = jnp.broadcast_to(label_ref[...][None, :], (8, length))

    def block(g, device):
        return pl.ds(pl.multiple_of(g * group + device * length, length), length)

    own = (
        pltpu.make_async_copy(own_rows, scaled_ref.at[block(tok, ch)], own_sem.at[0]),
        pltpu.make_async_copy(cot_ref, core_cot_ref.at[pl.ds(pl.multiple_of(chip * length, length), length)], own_sem.at[1]),
    )
    for copy in own:
        copy.start()

    barrier = pltpu.get_barrier_semaphore()
    peers = [(tok, ch ^ e) for e in range(1, n)] + [(tok ^ g, ch) for g in range(1, 4)]
    for device in peers:
        pl.semaphore_signal(barrier, inc=1, device_id=device, device_id_type=MESH)
    pl.semaphore_wait(barrier, len(peers))

    def remote(src, dst, send_sem, recv_sem, device):
        return pltpu.make_async_remote_copy(
            src_ref=src, dst_ref=dst, send_sem=send_sem, recv_sem=recv_sem, device_id=device, device_id_type=MESH
        )

    def arrive(ref, sem):
        pltpu.make_async_copy(ref, ref, sem).wait()

    label_copies = [
        remote(labels_ref.at[tok, ch], labels_ref.at[tok, ch], lab_send.at[e - 1], lab_recv.at[e - 1], (tok, ch ^ e))
        for e in range(1, n)
    ]
    for copy in label_copies:
        copy.start()

    def from_line(x, o):
        if x == 0:
            return scaled_ref.at[block(tok, 2 * o + core)]
        return core_cot_ref.at[pl.ds(pl.multiple_of(o * length, length), length)]

    def line_copy(x, o, side):
        ref = from_line(x, o)
        target = lax.rem(ch + (2 if side == 0 else n - 2), n)
        return remote(ref, ref, line_send.at[x, side, o], line_recv.at[x, o], (tok, target))

    def near_copy(x, o, g):
        if x == 0:
            src = dst = scaled_ref.at[block(tok ^ g, 2 * o + core)]
        else:
            src, dst = from_line(1, o), near_cot_ref.at[pl.ds(pl.multiple_of(o * length, length), length)]
        return remote(src, dst, near_send.at[x, g, o], near_recv.at[x, g, o], (tok, ch ^ 1))

    def tok_copy(o, side):
        ref = scaled_ref.at[block(tok, 2 * o + core)]
        return remote(ref, ref, tok_send.at[side, o], tok_recv.at[side, o], (tok ^ (1 + side), ch))

    def half_block(g, o, side):
        start = g * group + (2 * o + core) * length + side * (length // 2)
        return pl.ds(pl.multiple_of(start, length // 2), length // 2)

    def diag_copy(o, side):
        ref = scaled_ref.at[half_block(tok ^ (1 + side), o, side)]
        return remote(ref, ref, diag_send.at[side, o], diag_recv.at[side, o], (tok ^ (2 - side), ch))

    def goes(o, side):
        return (o <= chip) & (chip < chips - 1) if side == 0 else (o >= chip) & (chip > 0)

    def launch(x, o):
        for side in range(2):
            pl.when(goes(o, side))(line_copy(x, o, side).start)
        near_copy(x, o, 0).start()
        if x == 0:
            for side in range(2):
                tok_copy(o, side).start()

    base = chip - chip % 2

    def pair_copy(i, side):
        src, dst = from_line(1, base + i), pair_cot_ref.at[tok, i]
        return remote(src, dst, pair_send.at[side, i], pair_recv.at[side, i], (tok ^ (1 + side), ch))

    def pair_diag(i, side):
        ref = pair_cot_ref.at[tok ^ (1 + side), i, pl.ds(side * (length // 2), length // 2)]
        return remote(ref, ref, pair_diag_send.at[side, i], pair_diag_recv.at[side, i], (tok ^ (2 - side), ch))

    def pair_pass(i):
        for side in range(2):
            arrive(pair_cot_ref.at[tok ^ (1 + side), i], pair_recv.at[side, i])
            pair_diag(i, side).start()

    def accept(x, o):
        arrive(from_line(x, o), line_recv.at[x, o])
        launch(x, o)
        if x == 1:
            for side in range(2):
                pl.when(o // 2 == chip // 2)(pair_copy(o % 2, side).start)

    def pass_on(o):
        for side in range(2):
            arrive(scaled_ref.at[block(tok ^ (1 + side), 2 * o + core)], tok_recv.at[side, o])
            diag_copy(o, side).start()
            near_copy(0, o, 1 + side).start()

    def pass_last(o):
        for side in range(2):
            arrive(scaled_ref.at[half_block(tok ^ 3, o, side)], diag_recv.at[side, o])
        near_copy(0, o, 3).start()

    def load(x, o):
        if x == 0:
            arrive(scaled_ref.at[block(tok, 2 * o + 1 - core)], near_recv.at[0, 0, o])
            source = scaled_ref.at[pl.ds(pl.multiple_of(tok * group + o * chunk, chunk), chunk)]
            copies = [pltpu.make_async_copy(source, chunk_rows, load_sem.at[0])]
        else:
            other = near_cot_ref.at[pl.ds(pl.multiple_of(o * length, length), length)]
            arrive(other, near_recv.at[1, 0, o])
            copies = [
                pltpu.make_async_copy(
                    ref, chunk_rows.at[pl.ds(pl.multiple_of(q * length, length), length)], load_sem.at[at]
                )
                for at, (ref, q) in enumerate(((from_line(1, o), core), (other, 1 - core)))
            ]
        for copy in copies:
            copy.start()
        for copy in copies:
            copy.wait()

    def label_column(o):
        return jnp.concatenate(
            [labels_ref[tok, 2 * o + q].astype(F32).T[:, 0:1] for q in range(2)], axis=0
        )

    kind = ch // chips
    pair = ch % chips

    def xz_copies(o, h):
        target = 2 * pair + h
        src = staged.at[o, h]
        dst = xz.at[kind, pl.ds(pl.multiple_of(o * chunk, chunk), chunk)]
        return target, remote(src, dst, xz_send.at[o, h], xz_recv.at[kind, o], (tok, target)), pltpu.make_async_copy(
            src, dst, xz_recv.at[kind, o]
        )

    def project(o):
        load(0, o)
        label = label_column(o)
        for h in range(2):
            x = chunk_rows[...]
            parts = [dot(x, in_w[m, :, pl.ds(h * width, width)]) for m in range(mods)]
            staged[o, h] = pick(parts, label).astype(BF16)
            target, copy, local = xz_copies(o, h)
            pl.when(target != ch)(copy.start)
            pl.when(target == ch)(local.start)

    def keep(dst):
        copy = pltpu.make_async_copy(chunk_rows.at[pl.ds(pl.multiple_of(core * length, length), length)], dst, keep_sem)
        copy.start()
        copy.wait()

    def project_back(o):
        load(1, o)
        label = label_column(o)
        x = chunk_rows[...]
        parts = [dot_bt(x, out_w[m]) for m in range(mods)]
        gated_grad_ref[pl.ds(pl.multiple_of(o * chunk, chunk), chunk), :] = pick(parts, label).astype(BF16)

        @pl.when(o // 2 == chip // 2)
        def _():
            keep(pair_cot_ref.at[tok, o % 2])

        @pl.when(o // 2 != chip // 2)
        def _():
            keep(rest_cot_ref.at[pl.ds(pl.multiple_of(o % 2 * length, length), length)])

    def both_sides(i, fn):
        for o in (chip - i, chip + i):
            pl.when((o >= 0) & (o < chips))(functools.partial(fn, o))

    def every_distance(fn):
        fn(chip)

        def body(i, carry):
            both_sides(i, fn)
            return carry

        lax.fori_loop(1, chips, body, 0)

    own[0].wait()
    launch(0, chip)
    for e in range(1, n):
        arrive(labels_ref.at[tok, ch ^ e], lab_recv.at[e - 1])
    fetch_in.wait()
    project(chip)

    def step(i, carry):
        both_sides(i, functools.partial(accept, 0))
        both_sides(i, project)
        pl.when(i == 1)(functools.partial(pass_on, chip))
        pl.when(i > 1)(functools.partial(both_sides, i - 1, pass_on))
        return carry

    lax.fori_loop(1, chips, step, 0)
    own[1].wait()
    launch(1, chip)
    for side in range(2):
        pair_copy(chip % 2, side).start()
    label_tok = [
        remote(labels_ref.at[tok], labels_ref.at[tok], lab_tok_send.at[g - 1], lab_tok_recv.at[g - 1], (tok ^ g, ch))
        for g in range(1, 4)
    ]
    for copy in label_tok:
        copy.start()
    fetch_out.wait()
    project_back(chip)
    both_sides(chips - 1, pass_on)

    def step_back(i, carry):
        both_sides(i, functools.partial(accept, 1))
        both_sides(i, project_back)
        return carry

    lax.fori_loop(1, chips - 1, step_back, 0)
    every_distance(pass_last)
    pair_pass(chip % 2)

    for o in range(chips):
        for a in range(2):
            arrive(xz.at[a, pl.ds(o * chunk, chunk)], xz_recv.at[a, o])
    gate_ref[...] = by_time(xz[1]).astype(BF16)
    taps = cw_ref.shape[0]
    lead = (taps - 1) * GROUP
    inner = by_time(xz[0])
    inner_out_ref[...] = inner.astype(BF16)
    pad[pl.ds(0, lead), :] = jnp.zeros((lead, width), F32)
    pad[pl.ds(lead, group), :] = inner
    conv = jnp.broadcast_to(cb_ref[...].astype(F32)[None, :], (group, width))
    for tap in range(taps):
        conv = conv + cw_ref[pl.ds(tap, 1), :].astype(F32) * pad[pl.ds(tap * GROUP, group), :]
    conv_ref[...] = conv
    act = conv * sigmoid(conv)
    label = jnp.concatenate(
        [jnp.broadcast_to(labels_ref[tok, d].astype(F32).T[:, 0:1], (length, 128)) for d in range(n)], axis=0
    )
    label_ref_seq[...] = label[:, 0:1].astype(jnp.int32)
    label = by_time(label)
    label_ref_time[...] = label[:, 0:1].astype(jnp.int32)
    label_ref_row[...] = label.T[0:1, :].astype(jnp.int32)
    label = jnp.concatenate([label] * (width // 128), axis=1)
    total = None
    for m in range(mods):
        high, low = halves(jnp.where(label == m, act, 0.0))
        part = dot_bt(xw_ref[m], high) + dot_bt(xw_ref[m], low)
        total = part if total is None else total + part
    proj_part[...] = total

    both_sides(chips - 1, functools.partial(accept, 1))
    pair_pass(1 - chip % 2)
    sum_body(
        chips, proj_part, proj_ref, *sum_refs, work=lambda i: both_sides(chips - 1, project_back) if i == 1 else None
    )

    def finish(o, carry):
        for g in range(4):
            if g > 0:
                arrive(scaled_ref.at[block(tok ^ g, 2 * o + 1 - core)], near_recv.at[0, g, o])
            near_copy(0, o, g).wait_send()
        near_copy(1, o, 0).wait_send()
        for side in range(2):
            for x in range(2):
                pl.when(goes(o, side))(line_copy(x, o, side).wait_send)
            tok_copy(o, side).wait_send()
            diag_copy(o, side).wait_send()
        return carry

    lax.fori_loop(0, chips, finish, 0)
    for i in range(2):
        for side in range(2):
            pair_copy(i, side).wait_send()
            pair_diag(i, side).wait_send()
            part = pair_cot_ref.at[tok ^ 3, i, pl.ds(side * (length // 2), length // 2)]
            arrive(part, pair_diag_recv.at[side, i])
    for o in range(chips):
        for h in range(2):
            target, copy, _ = xz_copies(o, h)
            pl.when(target != ch)(copy.wait_send)
    for copy in label_copies:
        copy.wait_send()
    for g in range(1, 4):
        arrive(labels_ref.at[tok ^ g], lab_tok_recv.at[g - 1])
        label_tok[g - 1].wait_send()
    for g in range(4):
        for d in range(n):
            label_ref_all[:, pl.ds((g * n + d) * length, length)] = labels_ref[g, d, 0:1, :]


def way_in(block_input, gain, cotangent, modality, in_weight, out_weight, conv_weight, conv_bias, x_weight, n, collective_id):
    length, deep = block_input.shape
    mods, width = out_weight.shape[0], out_weight.shape[1]
    group, chips = n * length, n // 2
    wide = x_weight.shape[1]
    lead = (conv_weight.shape[0] - 1) * GROUP
    dma = pltpu.SemaphoreType.DMA
    vmem = pl.BlockSpec(memory_space=pltpu.VMEM)
    any_space = pl.BlockSpec(memory_space=pl.ANY)
    return pl.pallas_call(
        functools.partial(front_kernel, chips),
        out_shape=(
            jax.ShapeDtypeStruct((4 * group, deep), BF16),
            jax.ShapeDtypeStruct((chips * length, deep), BF16),
            jax.ShapeDtypeStruct((chips * length, deep), BF16),
            jax.ShapeDtypeStruct((4, 2, length, deep), BF16),
            jax.ShapeDtypeStruct((2 * length, deep), BF16),
            jax.ShapeDtypeStruct((4, n, 8, length), jnp.int32),
            jax.ShapeDtypeStruct((1, 4 * group), jnp.int32),
            jax.ShapeDtypeStruct((group, 1), jnp.int32),
            jax.ShapeDtypeStruct((group, 1), jnp.int32),
            jax.ShapeDtypeStruct((1, group), jnp.int32),
            jax.ShapeDtypeStruct((group, width), BF16),
            jax.ShapeDtypeStruct((group, width), BF16),
            jax.ShapeDtypeStruct((group, width), F32),
            jax.ShapeDtypeStruct((group, width), BF16),
            jax.ShapeDtypeStruct((wide, group), F32),
        ),
        in_specs=[vmem, vmem, any_space, vmem, any_space, any_space, vmem, vmem, vmem],
        out_specs=(any_space,) * 5 + (vmem,) * 10,
        scratch_shapes=[
            pltpu.VMEM((length, deep), BF16),
            pltpu.VMEM(in_weight.shape, BF16),
            pltpu.VMEM(out_weight.shape, BF16),
            pltpu.VMEM((2 * length, deep), BF16),
            pltpu.VMEM((chips, 2, 2 * length, width), BF16),
            pltpu.VMEM((2, group, width), BF16),
            pltpu.VMEM((wide, group), F32),
            pltpu.VMEM((group + lead, width), F32),
            dma, dma, dma((2,)), dma((2,)),
            dma((2, 2, chips)), dma((2, chips)), dma((2, 4, chips)), dma((2, 4, chips)),
            dma((2, chips)), dma((2, chips)), dma((2, chips)), dma((2, chips)),
            dma((chips, 2)), dma((2, chips)), dma((n - 1,)), dma((n - 1,)), dma((3,)), dma((3,)),
            dma, dma((2, 2)), dma((2, 2)), dma((2, 2)), dma((2, 2)),
        ] + sum_scratch(wide, group, chips),
        compiler_params=params(collective_id=collective_id, has_side_effects=True),
        cost_estimate=pl.CostEstimate(flops=10**11, bytes_accessed=10**8, transcendentals=0),
        name="way_in",
    )(
        block_input, gain, cotangent, modality, in_weight, out_weight, conv_weight, conv_bias, x_weight,
    )


def small_places(values):
    start, places = 0, []
    for value in values:
        for m in range(value.shape[0]) if len(value.shape) == 3 else [None]:
            places.append((start, (value, m)))
            start += -(-value.shape[-2] // 8) * 8
    return places


def back_kernel(
    chips, dinner_ref, dgate_ref, w_ref, label_ref, input_ref, cot_ref, gain_ref, pair_cot_ref, rest_cot_ref, scaled_ref, label_row_ref, every_gated_ref,
    dxw_ref, ddtw_ref, ddtb_ref, dcw_ref, dcb_ref, dalog_ref, dskip_ref,
    xall_ref, row_grad_ref, gain_sum_ref, near_pair_ref, near_rest_ref, grad_part_ref, small_ref, diag_gated_ref,
    weights, sends, near_part, chip_sums, arrived, mine, gain_send, gain_arrived, gain_mine, gain_others, left, made,
    packed, rounded, small_in, small_all,
    w_sem, to_col, from_own, to_tok, from_tok, to_diag, from_diag, to_near, from_near, to_row, from_row, to_gain, from_gain, to_gain_tok, from_gain_tok, cot_sems, left_sems, made_sems, to_small, from_small, to_all, from_all,
    to_gated_diag, from_gated_diag,
):
    n = 2 * chips
    group, width = dinner_ref.shape
    mods, deep = w_ref.shape[0], w_ref.shape[1]
    length = group // n
    chunk = 2 * length
    tok, ch = lax.axis_index("tok"), lax.axis_index("ch")
    chip, core = ch // 2, ch % 2
    beside, below = tok ^ 1, tok ^ 2

    fetch = pltpu.make_async_copy(w_ref, weights, w_sem)
    fetch.start()

    first = tok - tok % 2
    tile_rows = left.shape[3]
    tiles = deep // tile_rows

    def left_copies(i):
        at = pl.ds(pl.multiple_of(i * tile_rows, tile_rows), tile_rows)
        return [
            pltpu.make_async_copy(
                scaled_ref.at[pl.ds(pl.multiple_of((first + g) * group, group), group), at],
                left.at[lax.rem(i, 2), g],
                left_sems.at[lax.rem(i, 2), g],
            )
            for g in range(2)
        ]

    def made_copy(i):
        at = pl.ds(pl.multiple_of(i * tile_rows, tile_rows), tile_rows)
        return pltpu.make_async_copy(made.at[lax.rem(i, 2)], grad_part_ref.at[:, at], made_sems.at[lax.rem(i, 2)])

    def grad_tile(i, carry):
        for copy in left_copies(i):
            copy.wait()
        pl.when(i >= 2)(made_copy(i - 2).wait)
        slot = lax.rem(i, 2)
        lanes = [pl.ds(pl.multiple_of((first + g) * group, group), group) for g in range(2)]
        stacked = [by_kind(left[slot, g].T, label_row_ref[:, lanes[g]], mods) for g in range(2)]
        for h in range(2):
            total = dot(stacked[0], xall_ref[h, lanes[0], :]) + dot(stacked[1], xall_ref[h, lanes[1], :])
            for m in range(mods):
                made[slot, m, :, pl.ds(h * width, width)] = total[m * tile_rows : (m + 1) * tile_rows]
        made_copy(i).start()

        @pl.when(i + 2 < tiles)
        def _():
            for copy in left_copies(i + 2):
                copy.start()

        return carry

    for i in range(2):
        for copy in left_copies(i):
            copy.start()

    barrier = pltpu.get_barrier_semaphore()
    peers = [(tok, ch ^ e) for e in range(1, n)] + [(tok ^ g, ch) for g in range(1, 4)]
    for device in peers:
        pl.semaphore_signal(barrier, inc=1, device_id=device, device_id_type=MESH)
    pl.semaphore_wait(barrier, len(peers))

    def remote(src, dst, send_sem, recv_sem, device):
        return pltpu.make_async_remote_copy(
            src_ref=src, dst_ref=dst, send_sem=send_sem, recv_sem=recv_sem, device_id=device, device_id_type=MESH
        )

    def rows_of(index, size):
        return pl.ds(pl.multiple_of(index * size, size), size)

    def all_rows(group_index, chunk_index):
        return pl.ds(pl.multiple_of(group_index * group + chunk_index * chunk, chunk), chunk)

    cot_copies = [
        remote(src, dst, cot_sems.at[i, 0], cot_sems.at[i, 1], (tok, ch ^ 1))
        for i, (src, dst) in enumerate(((pair_cot_ref, near_pair_ref), (rest_cot_ref, near_rest_ref)))
    ]

    order = [2, 3, 1, 0]
    owners = [ch // 2, chips + ch // 2]
    out_copies = []

    def give(j):
        for a, src_ref in enumerate((dinner_ref, dgate_ref)):
            owner = owners[a]
            k = owner // 2 ^ j
            src = src_ref.at[rows_of(k, chunk)]
            dst = xall_ref.at[core, all_rows(tok, k)]
            copy = remote(src, dst, to_col.at[j, a], from_own.at[j, core], (tok, owner))
            local = pltpu.make_async_copy(src, dst, from_own.at[j, core])
            pl.when(owner != ch)(copy.start)
            pl.when(owner == ch)(local.start)
            out_copies.append((owner, copy))

    give(order[0])
    give(order[1])
    half = group // 2
    gated_copies = []
    for side, (source, target) in enumerate(((beside, below), (below, beside))):
        src = every_gated_ref.at[rows_of(2 * source + side, half)]
        dst = diag_gated_ref.at[pl.ds(side * half, half)]
        copy = remote(src, dst, to_gated_diag.at[side], from_gated_diag.at[side], (target, ch))
        copy.start()
        gated_copies.append(copy)
    quarter = rounded.shape[0] // 4
    packed[...] = jnp.zeros_like(packed)
    for start, (ref, m) in small_places(
        (dxw_ref, ddtw_ref, ddtb_ref, dcw_ref, dcb_ref, dalog_ref, dskip_ref)
    ):
        value = ref[...] if m is None else ref[m]
        packed[pl.ds(start, value.shape[0]), :] = value
    rounded[...] = packed[...].astype(BF16)
    small_copies = [
        remote(
            rounded.at[rows_of(tok ^ g, quarter)],
            small_in.at[g - 1],
            to_small.at[g - 1],
            from_small.at[g - 1],
            (tok ^ g, ch),
        )
        for g in range(1, 4)
    ]
    for copy in small_copies:
        copy.start()

    fetch.wait()
    for copy in cot_copies:
        copy.start()
    tok_copies, row_copies, diag_copies, near_copies = [], [], [], []

    def pass_on(j):
        k = chip ^ j
        for side, (source, target) in enumerate(((beside, below), (below, beside))):
            whole = xall_ref.at[:, all_rows(source, k)]
            pltpu.make_async_copy(whole, whole, from_tok.at[side, j]).wait()
            part = xall_ref.at[side, all_rows(source, k)]
            copy = remote(part, part, to_diag.at[side, j], from_diag.at[side, j], (target, ch))
            copy.start()
            diag_copies.append(copy)

    def both_cores(j):
        pltpu.make_async_copy(near_part.at[j], near_part.at[j], from_near.at[j]).wait()
        value = sends[j, rows_of(core, length), :].astype(F32) + near_part[j].astype(F32)
        if j == 0:
            mine[...] = value
        else:
            chip_sums[j - 1] = value.astype(BF16)
            target = 2 * (chip ^ j) + core
            copy = remote(chip_sums.at[j - 1], arrived.at[j - 1], to_row.at[j - 1], from_row.at[j - 1], (tok, target))
            copy.start()
            row_copies.append(copy)

    for at, j in enumerate(order):
        k = chip ^ j
        for h in range(2):
            half = xall_ref.at[h, all_rows(tok, k)]
            pltpu.make_async_copy(half, half, from_own.at[j, h]).wait()
        whole = xall_ref.at[:, all_rows(tok, k)]
        for side, target in enumerate((beside, below)):
            copy = remote(whole, whole, to_tok.at[side, j], from_tok.at[side, j], (target, ch))
            copy.start()
            tok_copies.append(copy)
        if at + 2 < chips:
            give(order[at + 2])
        label = label_ref[rows_of(k, chunk), :]
        halves_of = [xall_ref[h, all_rows(tok, k), :] for h in range(2)]
        tile = min(deep, 512)

        def product(i, carry, label=label, halves_of=halves_of, j=j):
            at = pl.ds(pl.multiple_of(i * tile, tile), tile)
            total = None
            for m in range(mods):
                for h in range(2):
                    x = jnp.where(label == m, halves_of[h], jnp.zeros_like(halves_of[h]))
                    part = dot_bt(x, weights[m, at, pl.ds(h * width, width)])
                    total = part if total is None else total + part
            sends[j, :, at] = total.astype(BF16)
            return carry

        lax.fori_loop(0, deep // tile, product, 0)
        copy = remote(
            sends.at[j, rows_of(1 - core, length)], near_part.at[j], to_near.at[j], from_near.at[j], (tok, ch ^ 1)
        )
        copy.start()
        near_copies.append(copy)
    for j in order:
        both_cores(j)
    value = packed[rows_of(tok, quarter), :]
    for copy in small_copies:
        copy.wait()
    for g in range(3):
        value = value + small_in[g].astype(F32)
    small_all[tok] = value.astype(BF16)
    small_copies = [
        remote(small_all.at[tok], small_all.at[tok], to_all.at[g - 1], from_all.at[g - 1], (tok ^ g, ch))
        for g in range(1, 4)
    ]
    for copy in small_copies:
        copy.start()
    for j in order:
        pass_on(j)
    lax.fori_loop(0, tiles - 2, grad_tile, 0)
    total = mine[...]
    for e in range(chips - 1):
        pltpu.make_async_copy(arrived.at[e], arrived.at[e], from_row.at[e]).wait()
        total = total + arrived[e].astype(F32)
    rows = input_ref[...].astype(F32)
    inverse = lax.rsqrt(jnp.mean(rows * rows, axis=-1, keepdims=True) + 1e-05)
    normed = rows * inverse
    ng = total * gain_ref[...].astype(F32)
    row_grad_ref[...] = cot_ref[...].astype(F32) + inverse * (
        ng - normed * jnp.mean(ng * normed, axis=-1, keepdims=True)
    )
    own = deep // n
    gain_term = jnp.sum(total * normed, axis=0, keepdims=True)
    for d in range(n):
        gain_send[d] = jnp.broadcast_to(gain_term[:, d * own : (d + 1) * own], (8, own))
    gain_copies = []
    for e in range(1, n):
        copy = remote(gain_send.at[ch ^ e], gain_arrived.at[e - 1], to_gain.at[e - 1], from_gain.at[e - 1], (tok, ch ^ e))
        copy.start()
        gain_copies.append(copy)
    grad_tile(tiles - 2, 0)
    value = gain_send[ch]
    for e in range(1, n):
        gain_copies[e - 1].wait()
        value = value + gain_arrived[e - 1]
    gain_mine[...] = value
    gain_copies = []
    for g in range(1, 4):
        copy = remote(gain_mine, gain_others.at[g - 1], to_gain_tok.at[g - 1], from_gain_tok.at[g - 1], (tok ^ g, ch))
        copy.start()
        gain_copies.append(copy)
    grad_tile(tiles - 1, 0)
    for copy in gain_copies:
        copy.wait()
    even, odd = gain_mine[...] + gain_others[0], gain_others[1] + gain_others[2]
    gain_sum_ref[...] = even + odd

    for j in range(chips):
        for side in range(2):
            part = xall_ref.at[side, all_rows(tok ^ 3, chip ^ j)]
            pltpu.make_async_copy(part, part, from_diag.at[side, j]).wait()
    for owner, copy in out_copies:
        pl.when(owner != ch)(copy.wait_send)
    for copy in tok_copies + diag_copies + row_copies + near_copies:
        copy.wait_send()
    for copy in cot_copies:
        copy.wait()
    for copy in gated_copies:
        copy.wait()
    for g in range(1, 4):
        pltpu.make_async_copy(small_all.at[tok ^ g], small_all.at[tok ^ g], from_all.at[g - 1]).wait()
        small_copies[g - 1].wait_send()
    for g in range(4):
        small_ref[pl.ds(g * quarter, quarter), :] = small_all[g].astype(F32)
    for i in (tiles - 2, tiles - 1):
        made_copy(i).wait()


def way_back(
    dinner, dgate, w, label, block_input, cotangent, gain, pair_cot, rest_cot, every_scaled, every_label, every_gated, small, n, collective_id
):
    group, width = dinner.shape
    mods, deep, _ = w.shape
    chips, length = n // 2, group // n
    dma = pltpu.SemaphoreType.DMA
    vmem = pl.BlockSpec(memory_space=pltpu.VMEM)
    tile = min(256, deep)
    last, (value, _) = small_places(small)[-1]
    quarter = -(-(last + value.shape[-2]) // 64) * 16
    any_space = pl.BlockSpec(memory_space=pl.ANY)
    return pl.pallas_call(
        functools.partial(back_kernel, chips),
        out_shape=(
            jax.ShapeDtypeStruct((2, 4 * group, width), BF16),
            jax.ShapeDtypeStruct((length, deep), F32),
            jax.ShapeDtypeStruct((8, deep // n), F32),
            jax.ShapeDtypeStruct(pair_cot.shape, BF16),
            jax.ShapeDtypeStruct(rest_cot.shape, BF16),
            jax.ShapeDtypeStruct(w.shape, F32),
            jax.ShapeDtypeStruct((4 * quarter, width), F32),
            jax.ShapeDtypeStruct((group, width), BF16),
        ),
        in_specs=[vmem, vmem, any_space, vmem, vmem, vmem, vmem, any_space, any_space, any_space, vmem, any_space]
        + [vmem] * len(small),
        out_specs=(vmem, vmem, vmem, any_space, any_space, any_space, vmem, any_space),
        scratch_shapes=[
            pltpu.VMEM(w.shape, BF16),
            pltpu.VMEM((chips, 2 * length, deep), BF16),
            pltpu.VMEM((chips, length, deep), BF16),
            pltpu.VMEM((chips - 1, length, deep), BF16),
            pltpu.VMEM((chips - 1, length, deep), BF16),
            pltpu.VMEM((length, deep), F32),
            pltpu.VMEM((n, 8, deep // n), F32),
            pltpu.VMEM((n - 1, 8, deep // n), F32),
            pltpu.VMEM((8, deep // n), F32),
            pltpu.VMEM((3, 8, deep // n), F32),
            pltpu.VMEM((2, 2, group, tile), BF16),
            pltpu.VMEM((2, mods, tile, 2 * width), F32),
            pltpu.VMEM((4 * quarter, width), F32),
            pltpu.VMEM((4 * quarter, width), BF16),
            pltpu.VMEM((3, quarter, width), BF16),
            pltpu.VMEM((4, quarter, width), BF16),
            dma, dma((chips, 2)), dma((chips, 2)), dma((2, chips)), dma((2, chips)), dma((2, chips)), dma((2, chips)),
            dma((chips,)), dma((chips,)), dma((chips - 1,)), dma((chips - 1,)), dma((n - 1,)), dma((n - 1,)), dma((3,)), dma((3,)), dma((2, 2)), dma((2, 2)), dma((2,)),
            dma((3,)), dma((3,)), dma((3,)), dma((3,)),
            dma((2,)), dma((2,)),
        ],
        compiler_params=params(collective_id=collective_id, has_side_effects=True),
        cost_estimate=pl.CostEstimate(flops=10**11, bytes_accessed=10**8, transcendentals=0),
        name="way_back",
    )(dinner, dgate, w, label, block_input, cotangent, gain[None, :], pair_cot, rest_cot, every_scaled, every_label, every_gated, *small)


def grad_parts_kernel(which_ref, *refs):
    del which_ref
    count = (len(refs) - 1) // 3
    out_ref = refs[-1]
    mods, tile, wide = out_ref.shape
    stacked = []
    for left_ref, label_ref in zip(refs[:count], refs[count : 2 * count], strict=True):
        groups, _, chips, _, length, _ = left_ref.shape
        turned = left_ref[...].reshape(groups * chips * length, tile).T
        blocks = [
            by_kind(turned[:, (g * chips + o) * length : (g * chips + o + 1) * length], label_ref[g, 0, o, 0], mods)
            for g in range(groups)
            for o in range(chips)
        ]
        stacked.append(jnp.concatenate(blocks, axis=1))
    step = min(512, wide)
    for start in range(0, wide, step):
        at = pl.ds(start, step)
        total = None
        for rows, right_ref in zip(stacked, refs[2 * count : -1], strict=True):
            part = dot(rows, right_ref[:, at])
            total = part if total is None else total + part
        for m in range(mods):
            out_ref[m, :, at] = total[m * tile : (m + 1) * tile]


def weight_grad_parts(left, rights, label, which, mods, tile):
    groups, pairs, chips, cores, length, deep = left.shape
    size, wide = rights[0].shape
    rows = left.size // deep
    chosen = [(flip, turn) for flip in range(2) for turn in range(2)]

    def block(last, moves, flip, turn):
        def index(i, which):
            return (0, which[0] ^ flip, 0, which[1] ^ turn, 0, i if moves else 0)

        return pl.BlockSpec((groups, 1, chips, 1) + last, index)

    whole = pl.BlockSpec((size, wide), lambda i, which: (0, 0), pipeline_mode=pl.Buffered(1))
    return pl.pallas_call(
        grad_parts_kernel,
        out_shape=jax.ShapeDtypeStruct((mods, deep, wide), F32),
        grid_spec=pltpu.PrefetchScalarGridSpec(
            num_scalar_prefetch=1,
            grid=(deep // tile,),
            in_specs=[block((length, tile), True, *c) for c in chosen]
            + [block((1, length), False, *c) for c in chosen]
            + [whole] * len(rights),
            out_specs=pl.BlockSpec((mods, tile, wide), lambda i, which: (0, i, 0)),
        ),
        compiler_params=params(),
        cost_estimate=pl.CostEstimate(
            flops=2 * mods * rows * deep * wide,
            bytes_accessed=2 * rows * (deep + wide) + 4 * mods * deep * wide,
            transcendentals=0,
        ),
        name="weight_grad_parts",
    )(which, *[left] * 4, *[label] * 4, *rights)


def grad_last_kernel(which_ref, left_ref, right_ref, label_ref, left2_ref, right2_ref, label2_ref, part_ref, out_ref, made):
    del which_ref
    mods, tile, _ = out_ref.shape
    wide = right_ref.shape[2]
    stacked = [
        by_kind(x[...].T, label[...], mods) for x, label in ((left_ref, label_ref), (left2_ref, label2_ref))
    ]
    for h in range(right_ref.shape[0]):
        at = pl.ds(h * wide, wide)
        made[...] = dot(stacked[0], right_ref[h]) + dot(stacked[1], right2_ref[h])
        for m in range(mods):
            out_ref[m, :, at] = part_ref[m, :, at] + made[pl.ds(m * tile, tile), :]


def weight_grad_last(left, right, label, part, which, tile):
    mods, deep, wide = part.shape
    group = left.shape[0] // 4
    of_group = [
        spec
        for g in range(2)
        for spec in (
            pl.BlockSpec((group, tile), lambda i, which, g=g: (which[g], i)),
            pl.BlockSpec((right.shape[0], group, right.shape[2]), lambda i, which, g=g: (0, which[g], 0)),
            pl.BlockSpec((1, group), lambda i, which, g=g: (0, which[g])),
        )
    ]
    return pl.pallas_call(
        grad_last_kernel,
        out_shape=jax.ShapeDtypeStruct(part.shape, F32),
        grid_spec=pltpu.PrefetchScalarGridSpec(
            num_scalar_prefetch=1,
            grid=(deep // tile,),
            in_specs=of_group + [pl.BlockSpec((mods, tile, wide), lambda i, which: (0, i, 0))],
            out_specs=pl.BlockSpec((mods, tile, wide), lambda i, which: (0, i, 0)),
            scratch_shapes=[pltpu.VMEM((mods * tile, right.shape[2]), F32)],
        ),
        compiler_params=params(),
        cost_estimate=pl.CostEstimate(
            flops=4 * mods * group * deep * wide,
            bytes_accessed=8 * mods * deep * wide,
            transcendentals=0,
        ),
        name="weight_grad_last",
    )(which, left, right, label, left, right, label, part)


def grad_kernel(left_ref, right_ref, label_ref, out_ref):
    left, label = left_ref[...], label_ref[...]
    wide = right_ref.shape[2]
    turned = left.T
    for m in range(out_ref.shape[0]):
        masked = jnp.where(label == m, turned, jnp.zeros_like(turned))
        for h in range(right_ref.shape[0]):
            out_ref[m, :, pl.ds(h * wide, wide)] = dot(masked, right_ref[h])


def grad_part_kernel(left_ref, right_ref, label_ref, out_ref):
    left, label = left_ref[...], label_ref[...]
    wide = right_ref.shape[2]
    turned = left.T
    first = pl.program_id(1) == 0
    for m in range(out_ref.shape[0]):
        masked = jnp.where(label == m, turned, jnp.zeros_like(turned))
        for h in range(right_ref.shape[0]):
            at = pl.ds(h * wide, wide)
            part = dot(masked, right_ref[h])
            out_ref[m, :, at] = jnp.where(first, part, out_ref[m, :, at] + part)


def weight_grad(left, right, label, mods, tile):
    rows, deep = left.shape
    wide = right.shape[0] * right.shape[2]
    block = min(rows, 4096)
    tile = min(tile, deep)
    return pl.pallas_call(
        grad_kernel if block == rows else grad_part_kernel,
        out_shape=jax.ShapeDtypeStruct((mods, deep, wide), F32),
        grid=(deep // tile, rows // block),
        in_specs=[
            pl.BlockSpec((block, tile), lambda i, j: (j, i)),
            pl.BlockSpec((right.shape[0], block, right.shape[2]), lambda i, j: (0, j, 0)),
            pl.BlockSpec((1, block), lambda i, j: (0, j)),
        ],
        out_specs=pl.BlockSpec((mods, tile, wide), lambda i, j: (0, i, 0)),
        compiler_params=params(),
        cost_estimate=pl.CostEstimate(
            flops=2 * mods * rows * deep * wide,
            bytes_accessed=2 * rows * (deep + wide) + 4 * mods * deep * wide,
            transcendentals=0,
        ),
        name="weight_grad",
    )(left, right, label)


def by_groups(fn, count, arrays, axes, joined):
    if count == 1:
        return fn(*arrays)

    def cut(a, axis, i):
        size = a.shape[axis] // count
        return lax.slice_in_dim(a, i * size, (i + 1) * size, axis=axis)

    outs = [fn(*(cut(a, axis, i) for a, axis in zip(arrays, axes, strict=True))) for i in range(count)]
    return tuple(
        jnp.concatenate(values, axis=joined[at]) if at < len(joined) else functools.reduce(jnp.add, values)
        for at, values in enumerate(zip(*outs, strict=True))
    )


def exchange_pairs(n):
    half = n // 2
    first = [(c, 2 * c) if c < half else (c, 2 * (c - half) + 1) for c in range(n)]
    second = [(c, 2 * c + 1) if c < half else (c, 2 * (c - half)) for c in range(n)]
    return first, second


def to_owners(xz, n):
    first, second = exchange_pairs(n)
    c = lax.axis_index("ch")
    width = xz.shape[1] // 2
    left, right = xz[:, :width], xz[:, width:]
    lower = c < n // 2
    one = lax.ppermute(jnp.where(lower, left, right), "ch", first)
    two = lax.ppermute(jnp.where(lower, right, left), "ch", second)
    even = c % 2 == 0
    return jnp.where(even, one, two), jnp.where(even, two, one)


def to_columns(dinner, dgate, n):
    first, second = exchange_pairs(n)
    c = lax.axis_index("ch")
    even = c % 2 == 0
    one = lax.ppermute(jnp.where(even, dinner, dgate), "ch", [(b, a) for a, b in first])
    two = lax.ppermute(jnp.where(even, dgate, dinner), "ch", [(b, a) for a, b in second])
    lower = c < n // 2
    return jnp.concatenate([jnp.where(lower, one, two), jnp.where(lower, two, one)], axis=1)


def on_device(
    n,
    block_input,
    norm_gain,
    in_weight,
    x_weight,
    dt_weight,
    dt_bias,
    conv_weight,
    conv_bias,
    a_log,
    skip_gain,
    out_weight,
    modality,
    cotangent,
):
    mods = in_weight.shape[0]
    length = block_input.shape[0]
    count = n // GROUP
    fast = n == GROUP and lax.axis_size("tok") == 4 and length % 128 == 0
    rows_float = block_input.astype(F32)
    gain = norm_gain.astype(F32)
    inverse = lax.rsqrt(jnp.mean(rows_float * rows_float, axis=-1, keepdims=True) + 1e-05)
    normed = rows_float * inverse
    scaled = (normed * gain[None, :]).astype(BF16)

    token_group = n * length
    if fast:
        every_scaled, _, _, pair_cot, rest_cot, _, every_label, label, label_by_time, label_row, gate, gated_grad, conv, inner_by_time, proj = way_in(
            block_input, norm_gain, cotangent, modality, in_weight, out_weight, conv_weight, conv_bias, x_weight, n, 0
        )
        rest_cot = lax.all_gather(rest_cot, "tok", axis=0, tiled=True)
    else:
        every_label = lax.all_gather(modality, ("tok", "ch"), axis=0, tiled=True)
    if not fast:
        group_label = lax.dynamic_slice_in_dim(every_label, lax.axis_index("tok") * token_group, token_group, 0)
        label = group_label[:, None]
        label_by_time = group_label.reshape(count, GROUP, length).transpose(0, 2, 1).reshape(token_group, 1)
        label_row = label_by_time.reshape(1, token_group)
        group_rows = lax.all_gather(scaled, "ch", axis=0, tiled=True)
        every_scaled = lax.all_gather(scaled, ("tok", "ch"), axis=0, tiled=True)
        every_cot = lax.all_gather(cotangent, ("tok", "ch"), axis=0, tiled=True)
        xz = routed_select(group_rows, label, in_weight, 256, False)
        inner, gate = to_owners(xz, n)
        gate = gate.reshape(count, GROUP, length, -1).swapaxes(1, 2).reshape(gate.shape)
        group_cot = lax.all_gather(cotangent, "ch", axis=0, tiled=True)
        gated_grad = routed_select(group_cot, label, out_weight, 128, True)
        conv, inner_by_time, proj_part = by_groups(
            lambda a, b: conv_forward(a, b, conv_weight, conv_bias, x_weight), count, (inner, label_row), (0, 1), (0, 0, 1)
        )
        proj = lax.psum(proj_part, "ch")

    gated, dgate, dact, dproj_part, ddtw, ddtb, dalog, dskip = by_groups(
        lambda a, b, c, d, e: scan_both(a, b, c, d, e, dt_weight, dt_bias, a_log, skip_gain),
        count,
        (conv, proj, gate, gated_grad, label_by_time),
        (0, 1, 0, 0, 0),
        (0, 0, 0, 1),
    )
    if fast:
        branch_part, every_gated, dinner, dxw, dcw, dcb = middle(
            dproj_part, gated, label, out_weight, conv, inner_by_time, dact, label_by_time, label_row, conv_weight, x_weight, n, 1
        )
    else:
        dproj = lax.psum(dproj_part, "ch")
        dinner, dxw, dcw, dcb = by_groups(
            lambda a, b, c, d, e, f: conv_backward(a, b, c, d, e, f, conv_weight, x_weight),
            count,
            (conv, inner_by_time, dact, dproj, label_by_time, label_row),
            (0, 0, 0, 1, 0, 1),
            (0,),
        )
        branch_part = routed_spread(gated, label, out_weight, 512, False, BF16)
        every_gated = lax.all_gather(gated, "tok", axis=0, tiled=True)
    if not fast:
        every_label = every_label[None, :]
    small = (dxw, ddtw, ddtb, dcw, dcb, dalog, dskip)
    if fast:
        pair_cot = pair_cot.reshape(rest_cot.shape)
        every_grad, row_grad, gain_grad, near_pair, near_rest, grad_part, total, diag_gated = way_back(
            dinner, dgate, in_weight, label, block_input, cotangent, norm_gain, pair_cot, rest_cot, every_scaled, every_label,
            every_gated, small, n, 2,
        )
        fourth = (lax.axis_index("tok") ^ 3) * token_group
        every_gated = lax.dynamic_update_slice_in_dim(every_gated, diag_gated, fourth, 0)
        gain_grad = gain_grad[0]
    else:
        xz_grad = to_columns(dinner, dgate, n)
        scaled_part = routed_spread(xz_grad, label, in_weight, 256, True, BF16)
        scaled_grad = lax.psum_scatter(scaled_part, "ch", scatter_dimension=0, tiled=True).astype(F32)
        gain_grad = lax.psum_scatter(jnp.sum(scaled_grad * normed, axis=0), "ch", scatter_dimension=0, tiled=True)
        ng = scaled_grad * gain[None, :]
        row_grad = cotangent.astype(F32) + inverse * (ng - normed * jnp.mean(ng * normed, axis=-1, keepdims=True))
        every_grad = lax.all_gather(xz_grad, "tok", axis=0, tiled=True)[None]

    if fast:
        branch_part, row_grad = lax.optimization_barrier((branch_part, row_grad))
    branch = lax.psum_scatter(branch_part, "ch", scatter_dimension=0, tiled=True).astype(F32)
    block_out = (rows_float + branch).astype(BF16)
    if fast:
        ch = lax.axis_index("ch")
        split = (4, 2, 2, 2)
        out_weight_grad = weight_grad_parts(
            every_gated.reshape(split + (length, every_gated.shape[1])),
            (pair_cot, near_pair, rest_cot, near_rest),
            every_label.reshape(split + (1, length)),
            jnp.stack([ch // 4, ch % 2]).astype(jnp.int32),
            mods,
            256,
        )
    else:
        out_weight_grad = weight_grad(every_gated, every_cot[None], every_label, mods, 128)
    if fast:
        others = (2 - lax.axis_index("tok") // 2 * 2 + jnp.arange(2)).astype(jnp.int32)
        in_weight_grad = weight_grad_last(every_scaled, every_grad, every_label, grad_part, others, 256)
    else:
        in_weight_grad = weight_grad(every_scaled, every_grad, every_label, mods, 256)
    sums = []
    if fast:
        starts = [start for start, (_, m) in small_places(small) if not m]
        for start, value in zip(starts, small, strict=True):
            size = math.prod(value.shape[:-1])
            sums.append(lax.slice_in_dim(total, start, start + size, axis=0).reshape(value.shape))
    else:
        gain_grad = lax.psum(gain_grad, "tok")
        flat = [value.reshape(-1, value.shape[-1]) for value in small]
        total = lax.psum(jnp.concatenate(flat, axis=0), "tok")
        start = 0
        for value, rows in zip(small, flat, strict=True):
            sums.append(lax.slice_in_dim(total, start, start + rows.shape[0], axis=0).reshape(value.shape))
            start += rows.shape[0]
    dxw, ddtw, ddtb, dcw, dcb, dalog, dskip = sums
    return (
        block_out,
        row_grad,
        gain_grad,
        in_weight_grad,
        dxw,
        ddtw,
        ddtb,
        dcw,
        dcb[0],
        dalog,
        dskip[0],
        out_weight_grad,
    )


def solution(mesh):
    placed = (
        P(("tok", "ch"), None),
        P(),
        P(None, None, "ch"),
        P(None, None, "ch"),
        P(None, None, "ch"),
        P(None, "ch"),
        P(None, "ch"),
        P("ch"),
        P(None, "ch"),
        P("ch"),
        P(None, "ch", None),
        P(("tok", "ch")),
        P(("tok", "ch"), None),
    )
    return jax.shard_map(
        functools.partial(on_device, mesh.shape["ch"]),
        mesh=mesh,
        in_specs=placed,
        out_specs=(
            P(("tok", "ch"), None),
            P(("tok", "ch"), None),
            P("ch"),
            P(None, None, "ch"),
            P(None, None, "ch"),
            P(None, None, "ch"),
            P(None, "ch"),
            P(None, "ch"),
            P("ch"),
            P(None, "ch"),
            P("ch"),
            P(None, "ch", None),
        ),
        check_vma=False,
    )
```

```python
import functools
import math

import jax
import jax.numpy as jnp
from jax import lax
from jax.experimental import pallas as pl
from jax.experimental.pallas import tpu as pltpu
from jax.sharding import PartitionSpec as P

F32 = jnp.float32
BF16 = jnp.bfloat16
LOG2E = math.log2(math.e)
LN2 = math.log(2.0)
GROUP = 8
VMEM_LIMIT = 58 << 20


def params(**kw):
    return pltpu.CompilerParams(vmem_limit_bytes=VMEM_LIMIT, **kw)


def dot(a, b):
    return lax.dot_general(a, b, (((1,), (0,)), ((), ())), preferred_element_type=F32)


def dot_bt(a, b):
    return lax.dot_general(a, b, (((1,), (1,)), ((), ())), preferred_element_type=F32)


def dot_at(a, b):
    return lax.dot_general(a, b, (((0,), (0,)), ((), ())), preferred_element_type=F32)


def halves(x):
    high = x.astype(BF16)
    return high, (x - high.astype(F32)).astype(BF16)


def pick(parts, label):
    total = parts[-1]
    for index in range(len(parts) - 2, -1, -1):
        total = jnp.where(label == index, parts[index], total)
    return total


def by_kind(turned, label, mods):
    return jnp.concatenate([jnp.where(label == m, turned, jnp.zeros_like(turned)) for m in range(mods)], axis=0)


def sigmoid(x):
    return 0.5 * jnp.tanh(0.5 * x) + 0.5


def select_kernel(transposed, x_ref, label_ref, w_ref, out_ref):
    x = x_ref[...]
    label = label_ref[...]
    product = dot_bt if transposed else dot
    parts = [product(x, w_ref[m]) for m in range(w_ref.shape[0])]
    out_ref[...] = pick(parts, label).astype(out_ref.dtype)


def routed_select(x, label, w, tile, transposed):
    rows, depth = x.shape
    mods = w.shape[0]
    outer = w.shape[1] if transposed else w.shape[2]
    tile = min(tile, outer)
    block = min(rows, 1024)
    if transposed:
        w_spec = pl.BlockSpec((mods, tile, depth), lambda i, j: (0, j, 0))
    else:
        w_spec = pl.BlockSpec((mods, depth, tile), lambda i, j: (0, 0, j))
    return pl.pallas_call(
        functools.partial(select_kernel, transposed),
        out_shape=jax.ShapeDtypeStruct((rows, outer), BF16),
        grid=(rows // block, outer // tile),
        in_specs=[
            pl.BlockSpec((block, depth), lambda i, j: (i, 0)),
            pl.BlockSpec((block, 1), lambda i, j: (i, 0)),
            w_spec,
        ],
        out_specs=pl.BlockSpec((block, tile), lambda i, j: (i, j)),
        compiler_params=params(),
        cost_estimate=pl.CostEstimate(
            flops=2 * rows * depth * outer * mods, bytes_accessed=2 * mods * depth * outer + 2 * rows * (depth + outer), transcendentals=0
        ),
        name="routed_select",
    )(x, label, w)


def spread_kernel(transposed, x_ref, label_ref, w_ref, out_ref):
    x = x_ref[...]
    label = label_ref[...]
    product = dot_bt if transposed else dot
    total = None
    for m in range(w_ref.shape[0]):
        part = product(jnp.where(label == m, x, jnp.zeros_like(x)), w_ref[m])
        total = part if total is None else total + part
    out_ref[...] = total.astype(out_ref.dtype)


def routed_spread(x, label, w, tile, transposed, dtype):
    rows, depth = x.shape
    mods = w.shape[0]
    outer = w.shape[1] if transposed else w.shape[2]
    tile = min(tile, outer)
    block = min(rows, 1024)
    if transposed:
        w_spec = pl.BlockSpec((mods, tile, depth), lambda i, j: (0, j, 0))
    else:
        w_spec = pl.BlockSpec((mods, depth, tile), lambda i, j: (0, 0, j))
    return pl.pallas_call(
        functools.partial(spread_kernel, transposed),
        out_shape=jax.ShapeDtypeStruct((rows, outer), dtype),
        grid=(rows // block, outer // tile),
        in_specs=[
            pl.BlockSpec((block, depth), lambda i, j: (i, 0)),
            pl.BlockSpec((block, 1), lambda i, j: (i, 0)),
            w_spec,
        ],
        out_specs=pl.BlockSpec((block, tile), lambda i, j: (i, j)),
        compiler_params=params(),
        cost_estimate=pl.CostEstimate(
            flops=2 * rows * depth * outer * mods, bytes_accessed=2 * mods * depth * outer + 2 * rows * (depth + outer), transcendentals=0
        ),
        name="routed_spread",
    )(x, label, w)


def by_time(x):
    rows, width = x.shape
    return jnp.swapaxes(x.astype(F32).reshape(GROUP, rows // GROUP, width), 0, 1).reshape(rows, width)


def by_sequence(x):
    rows, width = x.shape
    return jnp.swapaxes(x.reshape(rows // GROUP, GROUP, width), 0, 1).reshape(rows, width)


def conv_kernel(inner_ref, label_ref, cw_ref, cb_ref, xw_ref, conv_ref, inner_out_ref, proj_ref, pad_ref):
    rows, channels = inner_ref.shape
    taps = cw_ref.shape[0]
    lead = (taps - 1) * GROUP
    inner = by_time(inner_ref[...])
    inner_out_ref[...] = inner.astype(BF16)
    pad_ref[pl.ds(0, lead), :] = jnp.zeros((lead, channels), F32)
    pad_ref[pl.ds(lead, rows), :] = inner
    conv = jnp.broadcast_to(cb_ref[...].astype(F32), (rows, channels))
    for tap in range(taps):
        conv = conv + cw_ref[pl.ds(tap, 1), :].astype(F32) * pad_ref[pl.ds(tap * GROUP, rows), :]
    conv_ref[...] = conv
    high, low = halves(conv * sigmoid(conv))
    label = label_ref[...]
    parts = [dot_bt(xw_ref[m], high) + dot_bt(xw_ref[m], low) for m in range(xw_ref.shape[0])]
    proj_ref[...] = pick(parts, label)


def conv_forward(inner, label, cw, cb, xw):
    rows, channels = inner.shape
    wide = xw.shape[1]
    lead = (cw.shape[0] - 1) * GROUP
    return pl.pallas_call(
        conv_kernel,
        out_shape=(
            jax.ShapeDtypeStruct((rows, channels), F32),
            jax.ShapeDtypeStruct((rows, channels), BF16),
            jax.ShapeDtypeStruct((wide, rows), F32),
        ),
        scratch_shapes=[pltpu.VMEM((rows + lead, channels), F32)],
        compiler_params=params(),
        name="conv_forward",
    )(inner, label, cw, cb[None, :], xw)


def scan_kernel(
    conv_ref, proj_ref, gate_ref, grad_ref, label_ref, dtw_ref, dtb_ref, alog_ref, skip_ref,
    gated_ref, dgate_ref, dact_ref, dproj_ref, ddtw_ref, ddtb_ref, dalog_ref, dskip_ref,
    hist, mix, prod, rate, act, step, slope, dout, scanned, dstep, dlow, low_turned, low_rank, label,
):
    rows, width = conv_ref.shape
    length = rows // GROUP
    states = alog_ref.shape[0]
    mods, low_width = dtw_ref.shape[0], dtw_ref.shape[1]
    tile = pl.program_id(0)
    ddrive = scanned

    @pl.when(tile == 0)
    def _():
        prod[...] = jnp.zeros_like(prod)
        dlow[...] = jnp.zeros_like(dlow)
        label[...] = jnp.broadcast_to(label_ref[...], (rows, width))
        low_rank[...] = proj_ref[pl.ds(0, low_width), :].astype(BF16)
        low_turned[...] = proj_ref[pl.ds(0, low_width), :].T.astype(BF16)
        turned = proj_ref[pl.ds(low_width, 2 * states), :].T.astype(BF16)
        row = lax.broadcasted_iota(jnp.int32, (2 * states, 2 * width), 0)
        column = lax.broadcasted_iota(jnp.int32, (2 * states, 2 * width), 1)
        for s in range(0, 2 * states, 2):
            spread = dot(turned, (row == s + (column >= width).astype(jnp.int32)).astype(BF16))
            mix[s] = spread[:, :width]
            mix[s + 1] = spread[:, width:]

    kind = label[...]
    parts = [dot(low_turned[...], dtw_ref[m]) + dtb_ref[pl.ds(m, 1), :].astype(F32) for m in range(mods)]
    speed = pick(parts, kind)
    step[...] = jnp.maximum(speed, 0.0) + jnp.log1p(jnp.exp(-jnp.abs(speed)))
    slope[...] = sigmoid(speed)
    conv = conv_ref[...]
    act[...] = conv * sigmoid(conv)
    for s in range(states):
        rate[s] = jnp.broadcast_to(-LOG2E * jnp.exp(alog_ref[pl.ds(s, 1), :].astype(F32)), (GROUP, width))
        hist[0, s] = jnp.zeros((GROUP, width), F32)

    def forward(t, state):
        at = pl.ds(pl.multiple_of(t * GROUP, GROUP), GROUP)
        now = step[at, :]
        drive = now * act[at, :]
        total = None
        new = []
        for s in range(states):
            value = jnp.exp2(now * rate[s]) * state[s] + mix[s, at, :] * drive
            hist[t + 1, s] = value
            new.append(value)
            term = mix[states + s, at, :] * value
            total = term if total is None else total + term
        scanned[at, :] = total
        return tuple(new)

    zero = jnp.zeros((GROUP, width), F32)
    lax.fori_loop(0, length, forward, (zero,) * states, unroll=8)

    gate = gate_ref[...].astype(F32)
    grad = by_time(grad_ref[...])
    soft = sigmoid(gate)
    opened = gate * soft
    skip = skip_ref[...].astype(F32)
    summed = scanned[...] + skip * act[...]
    gated_ref[...] = by_sequence(summed * opened).astype(BF16)
    dgate = grad * summed * (soft + opened * (1.0 - soft))
    dgate_ref[...] = by_sequence(dgate).astype(BF16)
    dsummed = grad * opened
    dout[...] = dsummed
    dskip_ref[...] = jnp.sum(dsummed * act[...], axis=0, keepdims=True)

    def backward(i, carry):
        t = length - 1 - i
        at = pl.ds(pl.multiple_of(t * GROUP, GROUP), GROUP)
        now = step[at, :]
        drive = now * act[at, :]
        out = dout[at, :]
        dd, ds = None, None
        new, drates = [], []
        for s in range(states):
            decay = jnp.exp2(now * rate[s])
            dstate = carry[s] + mix[states + s, at, :] * out
            prod[states + s, at, :] += out * hist[t + 1, s]
            prod[s, at, :] += dstate * drive
            term = dstate * mix[s, at, :]
            dd = term if dd is None else dd + term
            passed = dstate * decay
            new.append(passed)
            change = passed * hist[t, s]
            term = change * rate[s]
            ds = term if ds is None else ds + term
            drates.append(carry[states + s] + change * now)
        ddrive[at, :] = dd
        dstep[at, :] = ds
        return tuple(new + drates)

    final = lax.fori_loop(0, length, backward, (zero,) * (2 * states), unroll=4)

    for s in range(states):
        dalog_ref[pl.ds(s, 1), :] = LN2 * jnp.sum(final[states + s] * rate[s], axis=0, keepdims=True)
    dact_ref[...] = ddrive[...] * step[...] + skip * dout[...]
    dspeed = (dstep[...] * LN2 + ddrive[...] * act[...]) * slope[...]
    rounded = dspeed.astype(BF16)
    of_rank = kind if width == low_width else label_ref[...]
    dlow[...] += pick([dot_bt(rounded, dtw_ref[m]) for m in range(mods)], of_rank)
    for m in range(mods):
        own = kind == m
        masked = jnp.where(own, dspeed, 0.0)
        ddtw_ref[m] = dot(low_rank[...], masked.astype(BF16))
        ddtb_ref[pl.ds(m, 1), :] = jnp.sum(masked, axis=0, keepdims=True)

    @pl.when(tile == pl.num_programs(0) - 1)
    def _():
        column = lax.broadcasted_iota(jnp.int32, (width, 2 * states), 1)
        sums = jnp.zeros((rows, 2 * states), F32)
        for s in range(2 * states):
            sums = sums + dot(prod[s].astype(BF16), (column == s).astype(BF16))
        dproj_ref[pl.ds(0, low_width), :] = dlow[...].T
        dproj_ref[pl.ds(low_width, 2 * states), :] = sums.T


def scan_both(conv, proj, gate, grad, label, dtw, dtb, alog, skip):
    rows, channels = conv.shape
    width = min(128, channels)
    length = rows // GROUP
    states = alog.shape[0]
    mods, low_width = dtw.shape[0], dtw.shape[1]
    wide = proj.shape[0]

    def whole(shape):
        return pl.BlockSpec(shape, lambda j: (0,) * len(shape), pipeline_mode=pl.Buffered(1))

    def cut(*shape):
        return pl.BlockSpec(shape + (width,), lambda j: (0,) * len(shape) + (j,))

    plane = (GROUP, width)
    flat = pltpu.VMEM((rows, width), F32)
    return pl.pallas_call(
        scan_kernel,
        out_shape=(
            jax.ShapeDtypeStruct((rows, channels), BF16),
            jax.ShapeDtypeStruct((rows, channels), BF16),
            jax.ShapeDtypeStruct((rows, channels), F32),
            jax.ShapeDtypeStruct((wide, rows), F32),
            jax.ShapeDtypeStruct((mods, low_width, channels), F32),
            jax.ShapeDtypeStruct((mods, channels), F32),
            jax.ShapeDtypeStruct((states, channels), F32),
            jax.ShapeDtypeStruct((1, channels), F32),
        ),
        grid=(channels // width,),
        in_specs=[
            cut(rows), whole((wide, rows)), cut(rows), cut(rows), whole((rows, 1)),
            cut(mods, low_width), cut(mods), cut(states), cut(1),
        ],
        out_specs=(
            cut(rows), cut(rows), cut(rows), whole((wide, rows)), cut(mods, low_width), cut(mods), cut(states), cut(1),
        ),
        scratch_shapes=[
            pltpu.VMEM((length + 1, states) + plane, F32),
            pltpu.VMEM((2 * states, rows, width), F32),
            pltpu.VMEM((2 * states, rows, width), F32),
            pltpu.VMEM((states,) + plane, F32),
            flat, flat, flat, flat, flat, flat,
            pltpu.VMEM((rows, low_width), F32),
            pltpu.VMEM((rows, low_width), BF16),
            pltpu.VMEM((low_width, rows), BF16),
            pltpu.VMEM((rows, width), jnp.int32),
        ],
        compiler_params=params(),
        cost_estimate=pl.CostEstimate(flops=5000 * rows * channels * states, bytes_accessed=20 * rows * channels, transcendentals=0),
        name="scan_both",
    )(conv, proj, gate, grad, label, dtw, dtb, alog, skip[None, :])


def conv_back_kernel(
    conv_ref, inner_ref, dact_ref, dproj_ref, label_ref, label_row_ref, cw_ref, xw_ref,
    dinner_ref, dxw_ref, dcw_ref, dcb_ref, pad_ref,
):
    rows, channels = conv_ref.shape
    taps = cw_ref.shape[0]
    tail = (taps - 1) * GROUP
    label, label_row = label_ref[...], label_row_ref[...]
    conv = conv_ref[...]
    soft = sigmoid(conv)
    act = conv * soft
    dproj = dproj_ref[...]
    turned = dproj.T.astype(BF16)
    parts = [dot(turned, xw_ref[m]) for m in range(xw_ref.shape[0])]
    dact = dact_ref[...] + pick(parts, label)
    rounded = act.astype(BF16)
    for m in range(xw_ref.shape[0]):
        dxw_ref[m] = dot(jnp.where(label_row == m, dproj, 0.0).astype(BF16), rounded)
    dconv = dact * (soft + act * (1.0 - soft))
    dcb_ref[...] = jnp.sum(dconv, axis=0, keepdims=True)
    pad_ref[pl.ds(0, rows), :] = dconv
    pad_ref[pl.ds(rows, tail), :] = jnp.zeros((tail, channels), F32)
    inner = inner_ref[...].astype(F32)
    total = None
    for tap in range(taps):
        shift = (taps - 1 - tap) * GROUP
        later = pad_ref[pl.ds(shift, rows), :]
        term = cw_ref[pl.ds(tap, 1), :].astype(F32) * later
        total = term if total is None else total + term
        dcw_ref[pl.ds(tap, 1), :] = jnp.sum(later * inner, axis=0, keepdims=True)
    dinner_ref[...] = by_sequence(total).astype(BF16)


def conv_backward(conv, inner, dact, dproj, label, label_row, cw, xw):
    rows, channels = conv.shape
    mods, wide = xw.shape[0], xw.shape[1]
    taps = cw.shape[0]
    return pl.pallas_call(
        conv_back_kernel,
        out_shape=(
            jax.ShapeDtypeStruct((rows, channels), BF16),
            jax.ShapeDtypeStruct((mods, wide, channels), F32),
            jax.ShapeDtypeStruct((taps, channels), F32),
            jax.ShapeDtypeStruct((1, channels), F32),
        ),
        scratch_shapes=[pltpu.VMEM((rows + (taps - 1) * GROUP, channels), F32)],
        compiler_params=params(),
        name="conv_backward",
    )(conv, inner, dact, dproj, label, label_row, cw, xw)


MESH = pl.DeviceIdType.MESH


def sum_body(
    chips, x_ref, out_ref, near, mine, far, total, every, other, near_sems, far_sems, back_sems, other_sems,
    work=lambda i: None,
):
    wide, rows = x_ref.shape
    half, part = rows // 2, rows // 2 // chips
    tok, ch = lax.axis_index("tok"), lax.axis_index("ch")
    chip, core = ch // 2, ch % 2
    partner = (tok, 2 * chip + 1 - core)
    chips_away = [(tok, 2 * (chip ^ d) + core) for d in range(1, chips)]

    def send(src, dst, sems, device):
        copy = pltpu.make_async_remote_copy(
            src_ref=src, dst_ref=dst, send_sem=sems.at[0], recv_sem=sems.at[1], device_id=device, device_id_type=MESH
        )
        copy.start()
        return copy

    def columns(index, size):
        return pl.ds(pl.multiple_of(index * size, size), size)

    copy = send(x_ref.at[:, columns(1 - core, half)], near, near_sems, partner)
    work(0)
    copy.wait()
    mine[...] = (x_ref[:, columns(core, half)] + near[...]).astype(BF16)
    copies = [
        send(mine.at[:, columns(chip ^ d, part)], far.at[d - 1], far_sems.at[d - 1], chips_away[d - 1])
        for d in range(1, chips)
    ]
    work(1)
    work(2)
    value = mine[:, columns(chip, part)].astype(F32)
    for d, copy in enumerate(copies):
        copy.wait()
        value = value + far[d].astype(F32)
    total[...] = value.astype(BF16)
    copies = [send(total, every.at[d - 1], back_sems.at[d - 1], chips_away[d - 1]) for d in range(1, chips)]
    copies += [send(total, other.at[0], other_sems.at[0], partner)]
    out_ref[:, columns(core * chips + chip, part)] = total[...].astype(F32)
    work(3)
    for d in range(1, chips):
        copies[d - 1].wait()
        copies += [send(every.at[d - 1], other.at[d], other_sems.at[d], partner)]
        out_ref[:, columns(core * chips + (chip ^ d), part)] = every[d - 1].astype(F32)
    for d in range(chips):
        copies[chips - 1 + d].wait()
        out_ref[:, columns((1 - core) * chips + (chip ^ d), part)] = other[d].astype(F32)


def sum_scratch(wide, rows, chips):
    half, part = rows // 2, rows // 2 // chips
    dma = pltpu.SemaphoreType.DMA
    return [
        pltpu.VMEM((wide, half), F32),
        pltpu.VMEM((wide, half), BF16),
        pltpu.VMEM((chips - 1, wide, part), BF16),
        pltpu.VMEM((wide, part), BF16),
        pltpu.VMEM((chips - 1, wide, part), BF16),
        pltpu.VMEM((chips, wide, part), BF16),
        dma((2,)),
        dma((chips - 1, 2)),
        dma((chips - 1, 2)),
        dma((chips, 2)),
    ]


def middle_kernel(
    chips, dproj_part_ref, gated_ref, label_seq_ref, ow_ref, conv_ref, inner_ref, dact_ref, label_ref, label_row_ref, cw_ref, xw_ref,
    branch_ref, every_gated_ref, dinner_ref, dxw_ref, dcw_ref, dcb_ref,
    weights, dproj, pad, w_sem, own_sem, tok_send, tok_recv, *sum_refs,
):
    group = gated_ref.shape[0]
    deep = ow_ref.shape[2]
    tok, ch = lax.axis_index("tok"), lax.axis_index("ch")
    fetch = pltpu.make_async_copy(ow_ref, weights, w_sem)
    fetch.start()

    def rows_of(index):
        return pl.ds(pl.multiple_of(index * group, group), group)

    own = pltpu.make_async_copy(gated_ref, every_gated_ref.at[rows_of(tok)], own_sem)
    own.start()
    barrier = pltpu.get_barrier_semaphore()
    peers = [(tok, ch ^ 1)] + [(tok, ch ^ (2 * d)) for d in range(1, chips)] + [(tok ^ g, ch) for g in (1, 2)]
    for device in peers:
        pl.semaphore_signal(barrier, inc=1, device_id=device, device_id_type=MESH)
    pl.semaphore_wait(barrier, len(peers))
    copies = [
        pltpu.make_async_remote_copy(
            src_ref=gated_ref,
            dst_ref=every_gated_ref.at[rows_of(tok)],
            send_sem=tok_send.at[side],
            recv_sem=tok_recv.at[side],
            device_id=(tok ^ (1 + side), ch),
            device_id_type=MESH,
        )
        for side in range(2)
    ]
    for copy in copies:
        copy.start()
    wide = deep // 4

    def work(i):
        if i == 0:
            fetch.wait()
        x, label = gated_ref[...], label_seq_ref[...]
        total = None
        for m in range(ow_ref.shape[0]):
            part = dot(jnp.where(label == m, x, jnp.zeros_like(x)), weights[m, :, pl.ds(i * wide, wide)])
            total = part if total is None else total + part
        branch_ref[:, pl.ds(i * wide, wide)] = total.astype(BF16)

    sum_body(chips, dproj_part_ref, dproj, *sum_refs, work=work)
    conv_back_kernel(
        conv_ref, inner_ref, dact_ref, dproj, label_ref, label_row_ref, cw_ref, xw_ref,
        dinner_ref, dxw_ref, dcw_ref, dcb_ref, pad,
    )
    for side in range(2):
        whole = every_gated_ref.at[rows_of(tok ^ (1 + side))]
        pltpu.make_async_copy(whole, whole, tok_recv.at[side]).wait()
        copies[side].wait_send()
    own.wait()


def middle(dproj_part, gated, label_seq, ow, conv, inner, dact, label, label_row, cw, xw, n, collective_id):
    group, channels = conv.shape
    mods, wide = xw.shape[0], xw.shape[1]
    taps, deep = cw.shape[0], ow.shape[2]
    dma = pltpu.SemaphoreType.DMA
    vmem = pl.BlockSpec(memory_space=pltpu.VMEM)
    any_space = pl.BlockSpec(memory_space=pl.ANY)
    return pl.pallas_call(
        functools.partial(middle_kernel, n // 2),
        out_shape=(
            jax.ShapeDtypeStruct((group, deep), BF16),
            jax.ShapeDtypeStruct((4 * group, channels), BF16),
            jax.ShapeDtypeStruct((group, channels), BF16),
            jax.ShapeDtypeStruct((mods, wide, channels), F32),
            jax.ShapeDtypeStruct((taps, channels), F32),
            jax.ShapeDtypeStruct((1, channels), F32),
        ),
        in_specs=[vmem, vmem, vmem, any_space] + [vmem] * 7,
        out_specs=(vmem, any_space, vmem, vmem, vmem, vmem),
        scratch_shapes=[
            pltpu.VMEM(ow.shape, BF16),
            pltpu.VMEM((wide, group), F32),
            pltpu.VMEM((group + (taps - 1) * GROUP, channels), F32),
            dma, dma, dma((2,)), dma((2,)),
        ] + sum_scratch(wide, group, n // 2),
        compiler_params=params(collective_id=collective_id, has_side_effects=True),
        cost_estimate=pl.CostEstimate(flops=2 * 10**10, bytes_accessed=10**7, transcendentals=0),
        name="middle",
    )(dproj_part, gated, label_seq, ow, conv, inner, dact, label, label_row, cw, xw)


def front_kernel(
    chips, input_ref, gain_ref, cot_ref, label_ref, iw_ref, ow_ref, cw_ref, cb_ref, xw_ref,
    scaled_ref, core_cot_ref, near_cot_ref, pair_cot_ref, rest_cot_ref, labels_ref, label_ref_all, label_ref_seq, label_ref_time, label_ref_row, gate_ref, gated_grad_ref, conv_ref, inner_out_ref, proj_ref,
    own_rows, in_w, out_w, chunk_rows, staged, xz, proj_part, pad,
    in_sem, out_sem, load_sem, own_sem,
    line_send, line_recv, near_send, near_recv, tok_send, tok_recv, diag_send, diag_recv,
    xz_send, xz_recv, lab_send, lab_recv, lab_tok_send, lab_tok_recv,
    keep_sem, pair_send, pair_recv, pair_diag_send, pair_diag_recv, *sum_refs,
):
    n = 2 * chips
    length, deep = input_ref.shape
    group, chunk = n * length, 2 * length
    mods, width = ow_ref.shape[0], ow_ref.shape[1]
    tok, ch = lax.axis_index("tok"), lax.axis_index("ch")
    chip, core = ch // 2, ch % 2

    fetch_in = pltpu.make_async_copy(iw_ref, in_w, in_sem)
    fetch_in.start()
    fetch_out = pltpu.make_async_copy(ow_ref, out_w, out_sem)
    fetch_out.start()

    rows = input_ref[...].astype(F32)
    inverse = lax.rsqrt(jnp.mean(rows * rows, axis=-1, keepdims=True) + 1e-05)
    own_rows[...] = (rows * inverse * gain_ref[...].astype(F32)[None, :]).astype(BF16)
    labels_ref[tok, ch] = jnp.broadcast_to(label_ref[...][None, :], (8, length))

    def block(g, device):
        return pl.ds(pl.multiple_of(g * group + device * length, length), length)

    own = (
        pltpu.make_async_copy(own_rows, scaled_ref.at[block(tok, ch)], own_sem.at[0]),
        pltpu.make_async_copy(cot_ref, core_cot_ref.at[pl.ds(pl.multiple_of(chip * length, length), length)], own_sem.at[1]),
    )
    for copy in own:
        copy.start()

    barrier = pltpu.get_barrier_semaphore()
    peers = [(tok, ch ^ e) for e in range(1, n)] + [(tok ^ g, ch) for g in range(1, 4)]
    for device in peers:
        pl.semaphore_signal(barrier, inc=1, device_id=device, device_id_type=MESH)
    pl.semaphore_wait(barrier, len(peers))

    def remote(src, dst, send_sem, recv_sem, device):
        return pltpu.make_async_remote_copy(
            src_ref=src, dst_ref=dst, send_sem=send_sem, recv_sem=recv_sem, device_id=device, device_id_type=MESH
        )

    def arrive(ref, sem):
        pltpu.make_async_copy(ref, ref, sem).wait()

    label_copies = [
        remote(labels_ref.at[tok, ch], labels_ref.at[tok, ch], lab_send.at[e - 1], lab_recv.at[e - 1], (tok, ch ^ e))
        for e in range(1, n)
    ]
    for copy in label_copies:
        copy.start()

    def from_line(x, o):
        if x == 0:
            return scaled_ref.at[block(tok, 2 * o + core)]
        return core_cot_ref.at[pl.ds(pl.multiple_of(o * length, length), length)]

    def line_copy(x, o, side):
        ref = from_line(x, o)
        target = lax.rem(ch + (2 if side == 0 else n - 2), n)
        return remote(ref, ref, line_send.at[x, side, o], line_recv.at[x, o], (tok, target))

    def near_copy(x, o, g):
        if x == 0:
            src = dst = scaled_ref.at[block(tok ^ g, 2 * o + core)]
        else:
            src, dst = from_line(1, o), near_cot_ref.at[pl.ds(pl.multiple_of(o * length, length), length)]
        return remote(src, dst, near_send.at[x, g, o], near_recv.at[x, g, o], (tok, ch ^ 1))

    def tok_copy(o, side):
        ref = scaled_ref.at[block(tok, 2 * o + core)]
        return remote(ref, ref, tok_send.at[side, o], tok_recv.at[side, o], (tok ^ (1 + side), ch))

    def half_block(g, o, side):
        start = g * group + (2 * o + core) * length + side * (length // 2)
        return pl.ds(pl.multiple_of(start, length // 2), length // 2)

    def diag_copy(o, side):
        ref = scaled_ref.at[half_block(tok ^ (1 + side), o, side)]
        return remote(ref, ref, diag_send.at[side, o], diag_recv.at[side, o], (tok ^ (2 - side), ch))

    def goes(o, side):
        return (o <= chip) & (chip < chips - 1) if side == 0 else (o >= chip) & (chip > 0)

    def launch(x, o):
        for side in range(2):
            pl.when(goes(o, side))(line_copy(x, o, side).start)
        near_copy(x, o, 0).start()
        if x == 0:
            for side in range(2):
                tok_copy(o, side).start()

    base = chip - chip % 2

    def pair_copy(i, side):
        src, dst = from_line(1, base + i), pair_cot_ref.at[tok, i]
        return remote(src, dst, pair_send.at[side, i], pair_recv.at[side, i], (tok ^ (1 + side), ch))

    def pair_diag(i, side):
        ref = pair_cot_ref.at[tok ^ (1 + side), i, pl.ds(side * (length // 2), length // 2)]
        return remote(ref, ref, pair_diag_send.at[side, i], pair_diag_recv.at[side, i], (tok ^ (2 - side), ch))

    def pair_pass(i):
        for side in range(2):
            arrive(pair_cot_ref.at[tok ^ (1 + side), i], pair_recv.at[side, i])
            pair_diag(i, side).start()

    def accept(x, o):
        arrive(from_line(x, o), line_recv.at[x, o])
        launch(x, o)
        if x == 1:
            for side in range(2):
                pl.when(o // 2 == chip // 2)(pair_copy(o % 2, side).start)

    def pass_on(o):
        for side in range(2):
            arrive(scaled_ref.at[block(tok ^ (1 + side), 2 * o + core)], tok_recv.at[side, o])
            diag_copy(o, side).start()
            near_copy(0, o, 1 + side).start()

    def pass_last(o):
        for side in range(2):
            arrive(scaled_ref.at[half_block(tok ^ 3, o, side)], diag_recv.at[side, o])
        near_copy(0, o, 3).start()

    def load(x, o):
        if x == 0:
            arrive(scaled_ref.at[block(tok, 2 * o + 1 - core)], near_recv.at[0, 0, o])
            source = scaled_ref.at[pl.ds(pl.multiple_of(tok * group + o * chunk, chunk), chunk)]
            copies = [pltpu.make_async_copy(source, chunk_rows, load_sem.at[0])]
        else:
            other = near_cot_ref.at[pl.ds(pl.multiple_of(o * length, length), length)]
            arrive(other, near_recv.at[1, 0, o])
            copies = [
                pltpu.make_async_copy(
                    ref, chunk_rows.at[pl.ds(pl.multiple_of(q * length, length), length)], load_sem.at[at]
                )
                for at, (ref, q) in enumerate(((from_line(1, o), core), (other, 1 - core)))
            ]
        for copy in copies:
            copy.start()
        for copy in copies:
            copy.wait()

    def label_column(o):
        return jnp.concatenate(
            [labels_ref[tok, 2 * o + q].astype(F32).T[:, 0:1] for q in range(2)], axis=0
        )

    kind = ch // chips
    pair = ch % chips

    def xz_copies(o, h):
        target = 2 * pair + h
        src = staged.at[o, h]
        dst = xz.at[kind, pl.ds(pl.multiple_of(o * chunk, chunk), chunk)]
        return target, remote(src, dst, xz_send.at[o, h], xz_recv.at[kind, o], (tok, target)), pltpu.make_async_copy(
            src, dst, xz_recv.at[kind, o]
        )

    def project(o):
        load(0, o)
        label = label_column(o)
        for h in range(2):
            x = chunk_rows[...]
            parts = [dot(x, in_w[m, :, pl.ds(h * width, width)]) for m in range(mods)]
            staged[o, h] = pick(parts, label).astype(BF16)
            target, copy, local = xz_copies(o, h)
            pl.when(target != ch)(copy.start)
            pl.when(target == ch)(local.start)

    def keep(dst):
        copy = pltpu.make_async_copy(chunk_rows.at[pl.ds(pl.multiple_of(core * length, length), length)], dst, keep_sem)
        copy.start()
        copy.wait()

    def project_back(o):
        load(1, o)
        label = label_column(o)
        x = chunk_rows[...]
        parts = [dot_bt(x, out_w[m]) for m in range(mods)]
        gated_grad_ref[pl.ds(pl.multiple_of(o * chunk, chunk), chunk), :] = pick(parts, label).astype(BF16)

        @pl.when(o // 2 == chip // 2)
        def _():
            keep(pair_cot_ref.at[tok, o % 2])

        @pl.when(o // 2 != chip // 2)
        def _():
            keep(rest_cot_ref.at[pl.ds(pl.multiple_of(o % 2 * length, length), length)])

    def both_sides(i, fn):
        for o in (chip - i, chip + i):
            pl.when((o >= 0) & (o < chips))(functools.partial(fn, o))

    def every_distance(fn):
        fn(chip)

        def body(i, carry):
            both_sides(i, fn)
            return carry

        lax.fori_loop(1, chips, body, 0)

    own[0].wait()
    launch(0, chip)
    for e in range(1, n):
        arrive(labels_ref.at[tok, ch ^ e], lab_recv.at[e - 1])
    fetch_in.wait()
    project(chip)

    def step(i, carry):
        both_sides(i, functools.partial(accept, 0))
        both_sides(i, project)
        pl.when(i == 1)(functools.partial(pass_on, chip))
        pl.when(i > 1)(functools.partial(both_sides, i - 1, pass_on))
        return carry

    lax.fori_loop(1, chips, step, 0)
    own[1].wait()
    launch(1, chip)
    for side in range(2):
        pair_copy(chip % 2, side).start()
    label_tok = [
        remote(labels_ref.at[tok], labels_ref.at[tok], lab_tok_send.at[g - 1], lab_tok_recv.at[g - 1], (tok ^ g, ch))
        for g in range(1, 4)
    ]
    for copy in label_tok:
        copy.start()
    fetch_out.wait()
    project_back(chip)
    both_sides(chips - 1, pass_on)

    def step_back(i, carry):
        both_sides(i, functools.partial(accept, 1))
        both_sides(i, project_back)
        return carry

    lax.fori_loop(1, chips - 1, step_back, 0)
    every_distance(pass_last)
    pair_pass(chip % 2)

    for o in range(chips):
        for a in range(2):
            arrive(xz.at[a, pl.ds(o * chunk, chunk)], xz_recv.at[a, o])
    gate_ref[...] = by_time(xz[1]).astype(BF16)
    taps = cw_ref.shape[0]
    lead = (taps - 1) * GROUP
    inner = by_time(xz[0])
    inner_out_ref[...] = inner.astype(BF16)
    pad[pl.ds(0, lead), :] = jnp.zeros((lead, width), F32)
    pad[pl.ds(lead, group), :] = inner
    conv = jnp.broadcast_to(cb_ref[...].astype(F32)[None, :], (group, width))
    for tap in range(taps):
        conv = conv + cw_ref[pl.ds(tap, 1), :].astype(F32) * pad[pl.ds(tap * GROUP, group), :]
    conv_ref[...] = conv
    act = conv * sigmoid(conv)
    label = jnp.concatenate(
        [jnp.broadcast_to(labels_ref[tok, d].astype(F32).T[:, 0:1], (length, 128)) for d in range(n)], axis=0
    )
    label_ref_seq[...] = label[:, 0:1].astype(jnp.int32)
    label = by_time(label)
    label_ref_time[...] = label[:, 0:1].astype(jnp.int32)
    label_ref_row[...] = label.T[0:1, :].astype(jnp.int32)
    label = jnp.concatenate([label] * (width // 128), axis=1)
    total = None
    for m in range(mods):
        high, low = halves(jnp.where(label == m, act, 0.0))
        part = dot_bt(xw_ref[m], high) + dot_bt(xw_ref[m], low)
        total = part if total is None else total + part
    proj_part[...] = total

    both_sides(chips - 1, functools.partial(accept, 1))
    pair_pass(1 - chip % 2)
    sum_body(
        chips, proj_part, proj_ref, *sum_refs, work=lambda i: both_sides(chips - 1, project_back) if i == 1 else None
    )

    def finish(o, carry):
        for g in range(4):
            if g > 0:
                arrive(scaled_ref.at[block(tok ^ g, 2 * o + 1 - core)], near_recv.at[0, g, o])
            near_copy(0, o, g).wait_send()
        near_copy(1, o, 0).wait_send()
        for side in range(2):
            for x in range(2):
                pl.when(goes(o, side))(line_copy(x, o, side).wait_send)
            tok_copy(o, side).wait_send()
            diag_copy(o, side).wait_send()
        return carry

    lax.fori_loop(0, chips, finish, 0)
    for i in range(2):
        for side in range(2):
            pair_copy(i, side).wait_send()
            pair_diag(i, side).wait_send()
            part = pair_cot_ref.at[tok ^ 3, i, pl.ds(side * (length // 2), length // 2)]
            arrive(part, pair_diag_recv.at[side, i])
    for o in range(chips):
        for h in range(2):
            target, copy, _ = xz_copies(o, h)
            pl.when(target != ch)(copy.wait_send)
    for copy in label_copies:
        copy.wait_send()
    for g in range(1, 4):
        arrive(labels_ref.at[tok ^ g], lab_tok_recv.at[g - 1])
        label_tok[g - 1].wait_send()
    for g in range(4):
        for d in range(n):
            label_ref_all[:, pl.ds((g * n + d) * length, length)] = labels_ref[g, d, 0:1, :]


def way_in(block_input, gain, cotangent, modality, in_weight, out_weight, conv_weight, conv_bias, x_weight, n, collective_id):
    length, deep = block_input.shape
    mods, width = out_weight.shape[0], out_weight.shape[1]
    group, chips = n * length, n // 2
    wide = x_weight.shape[1]
    lead = (conv_weight.shape[0] - 1) * GROUP
    dma = pltpu.SemaphoreType.DMA
    vmem = pl.BlockSpec(memory_space=pltpu.VMEM)
    any_space = pl.BlockSpec(memory_space=pl.ANY)
    return pl.pallas_call(
        functools.partial(front_kernel, chips),
        out_shape=(
            jax.ShapeDtypeStruct((4 * group, deep), BF16),
            jax.ShapeDtypeStruct((chips * length, deep), BF16),
            jax.ShapeDtypeStruct((chips * length, deep), BF16),
            jax.ShapeDtypeStruct((4, 2, length, deep), BF16),
            jax.ShapeDtypeStruct((2 * length, deep), BF16),
            jax.ShapeDtypeStruct((4, n, 8, length), jnp.int32),
            jax.ShapeDtypeStruct((1, 4 * group), jnp.int32),
            jax.ShapeDtypeStruct((group, 1), jnp.int32),
            jax.ShapeDtypeStruct((group, 1), jnp.int32),
            jax.ShapeDtypeStruct((1, group), jnp.int32),
            jax.ShapeDtypeStruct((group, width), BF16),
            jax.ShapeDtypeStruct((group, width), BF16),
            jax.ShapeDtypeStruct((group, width), F32),
            jax.ShapeDtypeStruct((group, width), BF16),
            jax.ShapeDtypeStruct((wide, group), F32),
        ),
        in_specs=[vmem, vmem, any_space, vmem, any_space, any_space, vmem, vmem, vmem],
        out_specs=(any_space,) * 5 + (vmem,) * 10,
        scratch_shapes=[
            pltpu.VMEM((length, deep), BF16),
            pltpu.VMEM(in_weight.shape, BF16),
            pltpu.VMEM(out_weight.shape, BF16),
            pltpu.VMEM((2 * length, deep), BF16),
            pltpu.VMEM((chips, 2, 2 * length, width), BF16),
            pltpu.VMEM((2, group, width), BF16),
            pltpu.VMEM((wide, group), F32),
            pltpu.VMEM((group + lead, width), F32),
            dma, dma, dma((2,)), dma((2,)),
            dma((2, 2, chips)), dma((2, chips)), dma((2, 4, chips)), dma((2, 4, chips)),
            dma((2, chips)), dma((2, chips)), dma((2, chips)), dma((2, chips)),
            dma((chips, 2)), dma((2, chips)), dma((n - 1,)), dma((n - 1,)), dma((3,)), dma((3,)),
            dma, dma((2, 2)), dma((2, 2)), dma((2, 2)), dma((2, 2)),
        ] + sum_scratch(wide, group, chips),
        compiler_params=params(collective_id=collective_id, has_side_effects=True),
        cost_estimate=pl.CostEstimate(flops=10**11, bytes_accessed=10**8, transcendentals=0),
        name="way_in",
    )(
        block_input, gain, cotangent, modality, in_weight, out_weight, conv_weight, conv_bias, x_weight,
    )


def small_places(values):
    start, places = 0, []
    for value in values:
        for m in range(value.shape[0]) if len(value.shape) == 3 else [None]:
            places.append((start, (value, m)))
            start += -(-value.shape[-2] // 8) * 8
    return places


def back_kernel(
    chips, dinner_ref, dgate_ref, w_ref, label_ref, input_ref, cot_ref, gain_ref, pair_cot_ref, rest_cot_ref, scaled_ref, label_row_ref, every_gated_ref,
    dxw_ref, ddtw_ref, ddtb_ref, dcw_ref, dcb_ref, dalog_ref, dskip_ref,
    xall_ref, row_grad_ref, gain_sum_ref, near_pair_ref, near_rest_ref, grad_part_ref, small_ref, diag_gated_ref,
    weights, sends, near_part, chip_sums, arrived, mine, gain_send, gain_arrived, gain_mine, gain_others, left, made,
    packed, rounded, small_in, small_all,
    w_sem, to_col, from_own, to_tok, from_tok, to_diag, from_diag, to_near, from_near, to_row, from_row, to_gain, from_gain, to_gain_tok, from_gain_tok, cot_sems, left_sems, made_sems, to_small, from_small, to_all, from_all,
    to_gated_diag, from_gated_diag,
):
    n = 2 * chips
    group, width = dinner_ref.shape
    mods, deep = w_ref.shape[0], w_ref.shape[1]
    length = group // n
    chunk = 2 * length
    tok, ch = lax.axis_index("tok"), lax.axis_index("ch")
    chip, core = ch // 2, ch % 2
    beside, below = tok ^ 1, tok ^ 2

    fetch = pltpu.make_async_copy(w_ref, weights, w_sem)
    fetch.start()

    first = tok - tok % 2
    tile_rows = left.shape[3]
    tiles = deep // tile_rows

    def left_copies(i):
        at = pl.ds(pl.multiple_of(i * tile_rows, tile_rows), tile_rows)
        return [
            pltpu.make_async_copy(
                scaled_ref.at[pl.ds(pl.multiple_of((first + g) * group, group), group), at],
                left.at[lax.rem(i, 2), g],
                left_sems.at[lax.rem(i, 2), g],
            )
            for g in range(2)
        ]

    def made_copy(i):
        at = pl.ds(pl.multiple_of(i * tile_rows, tile_rows), tile_rows)
        return pltpu.make_async_copy(made.at[lax.rem(i, 2)], grad_part_ref.at[:, at], made_sems.at[lax.rem(i, 2)])

    def grad_tile(i, carry):
        for copy in left_copies(i):
            copy.wait()
        pl.when(i >= 2)(made_copy(i - 2).wait)
        slot = lax.rem(i, 2)
        lanes = [pl.ds(pl.multiple_of((first + g) * group, group), group) for g in range(2)]
        stacked = [by_kind(left[slot, g].T, label_row_ref[:, lanes[g]], mods) for g in range(2)]
        for h in range(2):
            total = dot(stacked[0], xall_ref[h, lanes[0], :]) + dot(stacked[1], xall_ref[h, lanes[1], :])
            for m in range(mods):
                made[slot, m, :, pl.ds(h * width, width)] = total[m * tile_rows : (m + 1) * tile_rows]
        made_copy(i).start()

        @pl.when(i + 2 < tiles)
        def _():
            for copy in left_copies(i + 2):
                copy.start()

        return carry

    for i in range(2):
        for copy in left_copies(i):
            copy.start()

    barrier = pltpu.get_barrier_semaphore()
    peers = [(tok, ch ^ e) for e in range(1, n)] + [(tok ^ g, ch) for g in range(1, 4)]
    for device in peers:
        pl.semaphore_signal(barrier, inc=1, device_id=device, device_id_type=MESH)
    pl.semaphore_wait(barrier, len(peers))

    def remote(src, dst, send_sem, recv_sem, device):
        return pltpu.make_async_remote_copy(
            src_ref=src, dst_ref=dst, send_sem=send_sem, recv_sem=recv_sem, device_id=device, device_id_type=MESH
        )

    def rows_of(index, size):
        return pl.ds(pl.multiple_of(index * size, size), size)

    def all_rows(group_index, chunk_index):
        return pl.ds(pl.multiple_of(group_index * group + chunk_index * chunk, chunk), chunk)

    cot_copies = [
        remote(src, dst, cot_sems.at[i, 0], cot_sems.at[i, 1], (tok, ch ^ 1))
        for i, (src, dst) in enumerate(((pair_cot_ref, near_pair_ref), (rest_cot_ref, near_rest_ref)))
    ]

    order = [2, 3, 1, 0]
    owners = [ch // 2, chips + ch // 2]
    out_copies = []

    def give(j):
        for a, src_ref in enumerate((dinner_ref, dgate_ref)):
            owner = owners[a]
            k = owner // 2 ^ j
            src = src_ref.at[rows_of(k, chunk)]
            dst = xall_ref.at[core, all_rows(tok, k)]
            copy = remote(src, dst, to_col.at[j, a], from_own.at[j, core], (tok, owner))
            local = pltpu.make_async_copy(src, dst, from_own.at[j, core])
            pl.when(owner != ch)(copy.start)
            pl.when(owner == ch)(local.start)
            out_copies.append((owner, copy))

    give(order[0])
    give(order[1])
    half = group // 2
    gated_copies = []
    for side, (source, target) in enumerate(((beside, below), (below, beside))):
        src = every_gated_ref.at[rows_of(2 * source + side, half)]
        dst = diag_gated_ref.at[pl.ds(side * half, half)]
        copy = remote(src, dst, to_gated_diag.at[side], from_gated_diag.at[side], (target, ch))
        copy.start()
        gated_copies.append(copy)
    quarter = rounded.shape[0] // 4
    packed[...] = jnp.zeros_like(packed)
    for start, (ref, m) in small_places(
        (dxw_ref, ddtw_ref, ddtb_ref, dcw_ref, dcb_ref, dalog_ref, dskip_ref)
    ):
        value = ref[...] if m is None else ref[m]
        packed[pl.ds(start, value.shape[0]), :] = value
    rounded[...] = packed[...].astype(BF16)
    small_copies = [
        remote(
            rounded.at[rows_of(tok ^ g, quarter)],
            small_in.at[g - 1],
            to_small.at[g - 1],
            from_small.at[g - 1],
            (tok ^ g, ch),
        )
        for g in range(1, 4)
    ]
    for copy in small_copies:
        copy.start()

    fetch.wait()
    for copy in cot_copies:
        copy.start()
    tok_copies, row_copies, diag_copies, near_copies = [], [], [], []

    def pass_on(j):
        k = chip ^ j
        for side, (source, target) in enumerate(((beside, below), (below, beside))):
            whole = xall_ref.at[:, all_rows(source, k)]
            pltpu.make_async_copy(whole, whole, from_tok.at[side, j]).wait()
            part = xall_ref.at[side, all_rows(source, k)]
            copy = remote(part, part, to_diag.at[side, j], from_diag.at[side, j], (target, ch))
            copy.start()
            diag_copies.append(copy)

    def both_cores(j):
        pltpu.make_async_copy(near_part.at[j], near_part.at[j], from_near.at[j]).wait()
        value = sends[j, rows_of(core, length), :].astype(F32) + near_part[j].astype(F32)
        if j == 0:
            mine[...] = value
        else:
            chip_sums[j - 1] = value.astype(BF16)
            target = 2 * (chip ^ j) + core
            copy = remote(chip_sums.at[j - 1], arrived.at[j - 1], to_row.at[j - 1], from_row.at[j - 1], (tok, target))
            copy.start()
            row_copies.append(copy)

    for at, j in enumerate(order):
        k = chip ^ j
        for h in range(2):
            half = xall_ref.at[h, all_rows(tok, k)]
            pltpu.make_async_copy(half, half, from_own.at[j, h]).wait()
        whole = xall_ref.at[:, all_rows(tok, k)]
        for side, target in enumerate((beside, below)):
            copy = remote(whole, whole, to_tok.at[side, j], from_tok.at[side, j], (target, ch))
            copy.start()
            tok_copies.append(copy)
        if at + 2 < chips:
            give(order[at + 2])
        label = label_ref[rows_of(k, chunk), :]
        halves_of = [xall_ref[h, all_rows(tok, k), :] for h in range(2)]
        tile = min(deep, 512)

        def product(i, carry, label=label, halves_of=halves_of, j=j):
            at = pl.ds(pl.multiple_of(i * tile, tile), tile)
            total = None
            for m in range(mods):
                for h in range(2):
                    x = jnp.where(label == m, halves_of[h], jnp.zeros_like(halves_of[h]))
                    part = dot_bt(x, weights[m, at, pl.ds(h * width, width)])
                    total = part if total is None else total + part
            sends[j, :, at] = total.astype(BF16)
            return carry

        lax.fori_loop(0, deep // tile, product, 0)
        copy = remote(
            sends.at[j, rows_of(1 - core, length)], near_part.at[j], to_near.at[j], from_near.at[j], (tok, ch ^ 1)
        )
        copy.start()
        near_copies.append(copy)
    for j in order:
        both_cores(j)
    value = packed[rows_of(tok, quarter), :]
    for copy in small_copies:
        copy.wait()
    for g in range(3):
        value = value + small_in[g].astype(F32)
    small_all[tok] = value.astype(BF16)
    small_copies = [
        remote(small_all.at[tok], small_all.at[tok], to_all.at[g - 1], from_all.at[g - 1], (tok ^ g, ch))
        for g in range(1, 4)
    ]
    for copy in small_copies:
        copy.start()
    for j in order:
        pass_on(j)
    lax.fori_loop(0, tiles - 2, grad_tile, 0)
    total = mine[...]
    for e in range(chips - 1):
        pltpu.make_async_copy(arrived.at[e], arrived.at[e], from_row.at[e]).wait()
        total = total + arrived[e].astype(F32)
    rows = input_ref[...].astype(F32)
    inverse = lax.rsqrt(jnp.mean(rows * rows, axis=-1, keepdims=True) + 1e-05)
    normed = rows * inverse
    ng = total * gain_ref[...].astype(F32)
    row_grad_ref[...] = cot_ref[...].astype(F32) + inverse * (
        ng - normed * jnp.mean(ng * normed, axis=-1, keepdims=True)
    )
    own = deep // n
    gain_term = jnp.sum(total * normed, axis=0, keepdims=True)
    for d in range(n):
        gain_send[d] = jnp.broadcast_to(gain_term[:, d * own : (d + 1) * own], (8, own))
    gain_copies = []
    for e in range(1, n):
        copy = remote(gain_send.at[ch ^ e], gain_arrived.at[e - 1], to_gain.at[e - 1], from_gain.at[e - 1], (tok, ch ^ e))
        copy.start()
        gain_copies.append(copy)
    grad_tile(tiles - 2, 0)
    value = gain_send[ch]
    for e in range(1, n):
        gain_copies[e - 1].wait()
        value = value + gain_arrived[e - 1]
    gain_mine[...] = value
    gain_copies = []
    for g in range(1, 4):
        copy = remote(gain_mine, gain_others.at[g - 1], to_gain_tok.at[g - 1], from_gain_tok.at[g - 1], (tok ^ g, ch))
        copy.start()
        gain_copies.append(copy)
    grad_tile(tiles - 1, 0)
    for copy in gain_copies:
        copy.wait()
    even, odd = gain_mine[...] + gain_others[0], gain_others[1] + gain_others[2]
    gain_sum_ref[...] = even + odd

    for j in range(chips):
        for side in range(2):
            part = xall_ref.at[side, all_rows(tok ^ 3, chip ^ j)]
            pltpu.make_async_copy(part, part, from_diag.at[side, j]).wait()
    for owner, copy in out_copies:
        pl.when(owner != ch)(copy.wait_send)
    for copy in tok_copies + diag_copies + row_copies + near_copies:
        copy.wait_send()
    for copy in cot_copies:
        copy.wait()
    for copy in gated_copies:
        copy.wait()
    for g in range(1, 4):
        pltpu.make_async_copy(small_all.at[tok ^ g], small_all.at[tok ^ g], from_all.at[g - 1]).wait()
        small_copies[g - 1].wait_send()
    for g in range(4):
        small_ref[pl.ds(g * quarter, quarter), :] = small_all[g].astype(F32)
    for i in (tiles - 2, tiles - 1):
        made_copy(i).wait()


def way_back(
    dinner, dgate, w, label, block_input, cotangent, gain, pair_cot, rest_cot, every_scaled, every_label, every_gated, small, n, collective_id
):
    group, width = dinner.shape
    mods, deep, _ = w.shape
    chips, length = n // 2, group // n
    dma = pltpu.SemaphoreType.DMA
    vmem = pl.BlockSpec(memory_space=pltpu.VMEM)
    tile = min(256, deep)
    last, (value, _) = small_places(small)[-1]
    quarter = -(-(last + value.shape[-2]) // 64) * 16
    any_space = pl.BlockSpec(memory_space=pl.ANY)
    return pl.pallas_call(
        functools.partial(back_kernel, chips),
        out_shape=(
            jax.ShapeDtypeStruct((2, 4 * group, width), BF16),
            jax.ShapeDtypeStruct((length, deep), F32),
            jax.ShapeDtypeStruct((8, deep // n), F32),
            jax.ShapeDtypeStruct(pair_cot.shape, BF16),
            jax.ShapeDtypeStruct(rest_cot.shape, BF16),
            jax.ShapeDtypeStruct(w.shape, F32),
            jax.ShapeDtypeStruct((4 * quarter, width), F32),
            jax.ShapeDtypeStruct((group, width), BF16),
        ),
        in_specs=[vmem, vmem, any_space, vmem, vmem, vmem, vmem, any_space, any_space, any_space, vmem, any_space]
        + [vmem] * len(small),
        out_specs=(vmem, vmem, vmem, any_space, any_space, any_space, vmem, any_space),
        scratch_shapes=[
            pltpu.VMEM(w.shape, BF16),
            pltpu.VMEM((chips, 2 * length, deep), BF16),
            pltpu.VMEM((chips, length, deep), BF16),
            pltpu.VMEM((chips - 1, length, deep), BF16),
            pltpu.VMEM((chips - 1, length, deep), BF16),
            pltpu.VMEM((length, deep), F32),
            pltpu.VMEM((n, 8, deep // n), F32),
            pltpu.VMEM((n - 1, 8, deep // n), F32),
            pltpu.VMEM((8, deep // n), F32),
            pltpu.VMEM((3, 8, deep // n), F32),
            pltpu.VMEM((2, 2, group, tile), BF16),
            pltpu.VMEM((2, mods, tile, 2 * width), F32),
            pltpu.VMEM((4 * quarter, width), F32),
            pltpu.VMEM((4 * quarter, width), BF16),
            pltpu.VMEM((3, quarter, width), BF16),
            pltpu.VMEM((4, quarter, width), BF16),
            dma, dma((chips, 2)), dma((chips, 2)), dma((2, chips)), dma((2, chips)), dma((2, chips)), dma((2, chips)),
            dma((chips,)), dma((chips,)), dma((chips - 1,)), dma((chips - 1,)), dma((n - 1,)), dma((n - 1,)), dma((3,)), dma((3,)), dma((2, 2)), dma((2, 2)), dma((2,)),
            dma((3,)), dma((3,)), dma((3,)), dma((3,)),
            dma((2,)), dma((2,)),
        ],
        compiler_params=params(collective_id=collective_id, has_side_effects=True),
        cost_estimate=pl.CostEstimate(flops=10**11, bytes_accessed=10**8, transcendentals=0),
        name="way_back",
    )(dinner, dgate, w, label, block_input, cotangent, gain[None, :], pair_cot, rest_cot, every_scaled, every_label, every_gated, *small)


def grad_parts_kernel(which_ref, *refs):
    del which_ref
    count = (len(refs) - 2) // 3
    out_ref, stacked = refs[-2:]
    mods, deep, _ = out_ref.shape

    @pl.when(pl.program_id(0) == 0)
    def _():
        for i, (left_ref, label_ref) in enumerate(zip(refs[:count], refs[count : 2 * count], strict=True)):
            groups, _, chips, _, length, _ = left_ref.shape
            for g in range(groups):
                for o in range(chips):
                    at = pl.ds((g * chips + o) * length, length)
                    stacked[i, :, at] = by_kind(left_ref[g, 0, o, 0].T, label_ref[g, 0, o, 0], mods)

    total = None
    for i, right_ref in enumerate(refs[2 * count : 3 * count]):
        part = dot(stacked[i], right_ref[...])
        total = part if total is None else total + part
    for m in range(mods):
        out_ref[m] = total[m * deep : (m + 1) * deep]


def weight_grad_parts(left, rights, label, which, mods, tile):
    groups, pairs, chips, cores, length, deep = left.shape
    size, wide = rights[0].shape
    rows = left.size // deep
    chosen = [(flip, turn) for flip in range(2) for turn in range(2)]

    def block(last, flip, turn):
        def index(i, which):
            return (0, which[0] ^ flip, 0, which[1] ^ turn, 0, 0)

        return pl.BlockSpec((groups, 1, chips, 1) + last, index, pipeline_mode=pl.Buffered(1))

    cut = pl.BlockSpec((size, tile), lambda i, which: (0, i))
    return pl.pallas_call(
        grad_parts_kernel,
        out_shape=jax.ShapeDtypeStruct((mods, deep, wide), F32),
        grid_spec=pltpu.PrefetchScalarGridSpec(
            num_scalar_prefetch=1,
            grid=(wide // tile,),
            in_specs=[block((length, deep), *c) for c in chosen]
            + [block((1, length), *c) for c in chosen]
            + [cut] * len(rights),
            out_specs=pl.BlockSpec((mods, deep, tile), lambda i, which: (0, 0, i)),
            scratch_shapes=[pltpu.VMEM((len(rights), mods * deep, size), BF16)],
        ),
        compiler_params=params(),
        cost_estimate=pl.CostEstimate(
            flops=2 * mods * rows * deep * wide,
            bytes_accessed=2 * rows * (deep + wide) + 4 * mods * deep * wide,
            transcendentals=0,
        ),
        name="weight_grad_parts",
    )(which, *[left] * 4, *[label] * 4, *rights)


def grad_last_kernel(which_ref, left_ref, right_ref, label_ref, left2_ref, right2_ref, label2_ref, part_ref, out_ref, made):
    del which_ref
    mods, tile, _ = out_ref.shape
    wide = right_ref.shape[2]
    stacked = [
        by_kind(x[...].T, label[...], mods) for x, label in ((left_ref, label_ref), (left2_ref, label2_ref))
    ]
    for h in range(right_ref.shape[0]):
        at = pl.ds(h * wide, wide)
        made[...] = dot(stacked[0], right_ref[h]) + dot(stacked[1], right2_ref[h])
        for m in range(mods):
            out_ref[m, :, at] = part_ref[m, :, at] + made[pl.ds(m * tile, tile), :]


def weight_grad_last(left, right, label, part, which, tile):
    mods, deep, wide = part.shape
    group = left.shape[0] // 4
    of_group = [
        spec
        for g in range(2)
        for spec in (
            pl.BlockSpec((group, tile), lambda i, which, g=g: (which[g], i)),
            pl.BlockSpec((right.shape[0], group, right.shape[2]), lambda i, which, g=g: (0, which[g], 0)),
            pl.BlockSpec((1, group), lambda i, which, g=g: (0, which[g])),
        )
    ]
    return pl.pallas_call(
        grad_last_kernel,
        out_shape=jax.ShapeDtypeStruct(part.shape, F32),
        grid_spec=pltpu.PrefetchScalarGridSpec(
            num_scalar_prefetch=1,
            grid=(deep // tile,),
            in_specs=of_group + [pl.BlockSpec((mods, tile, wide), lambda i, which: (0, i, 0))],
            out_specs=pl.BlockSpec((mods, tile, wide), lambda i, which: (0, i, 0)),
            scratch_shapes=[pltpu.VMEM((mods * tile, right.shape[2]), F32)],
        ),
        compiler_params=params(),
        cost_estimate=pl.CostEstimate(
            flops=4 * mods * group * deep * wide,
            bytes_accessed=8 * mods * deep * wide,
            transcendentals=0,
        ),
        name="weight_grad_last",
    )(which, left, right, label, left, right, label, part)


def grad_kernel(left_ref, right_ref, label_ref, out_ref):
    left, label = left_ref[...], label_ref[...]
    wide = right_ref.shape[2]
    turned = left.T
    for m in range(out_ref.shape[0]):
        masked = jnp.where(label == m, turned, jnp.zeros_like(turned))
        for h in range(right_ref.shape[0]):
            out_ref[m, :, pl.ds(h * wide, wide)] = dot(masked, right_ref[h])


def grad_part_kernel(left_ref, right_ref, label_ref, out_ref):
    left, label = left_ref[...], label_ref[...]
    wide = right_ref.shape[2]
    turned = left.T
    first = pl.program_id(1) == 0
    for m in range(out_ref.shape[0]):
        masked = jnp.where(label == m, turned, jnp.zeros_like(turned))
        for h in range(right_ref.shape[0]):
            at = pl.ds(h * wide, wide)
            part = dot(masked, right_ref[h])
            out_ref[m, :, at] = jnp.where(first, part, out_ref[m, :, at] + part)


def weight_grad(left, right, label, mods, tile):
    rows, deep = left.shape
    wide = right.shape[0] * right.shape[2]
    block = min(rows, 4096)
    tile = min(tile, deep)
    return pl.pallas_call(
        grad_kernel if block == rows else grad_part_kernel,
        out_shape=jax.ShapeDtypeStruct((mods, deep, wide), F32),
        grid=(deep // tile, rows // block),
        in_specs=[
            pl.BlockSpec((block, tile), lambda i, j: (j, i)),
            pl.BlockSpec((right.shape[0], block, right.shape[2]), lambda i, j: (0, j, 0)),
            pl.BlockSpec((1, block), lambda i, j: (0, j)),
        ],
        out_specs=pl.BlockSpec((mods, tile, wide), lambda i, j: (0, i, 0)),
        compiler_params=params(),
        cost_estimate=pl.CostEstimate(
            flops=2 * mods * rows * deep * wide,
            bytes_accessed=2 * rows * (deep + wide) + 4 * mods * deep * wide,
            transcendentals=0,
        ),
        name="weight_grad",
    )(left, right, label)


def by_groups(fn, count, arrays, axes, joined):
    if count == 1:
        return fn(*arrays)

    def cut(a, axis, i):
        size = a.shape[axis] // count
        return lax.slice_in_dim(a, i * size, (i + 1) * size, axis=axis)

    outs = [fn(*(cut(a, axis, i) for a, axis in zip(arrays, axes, strict=True))) for i in range(count)]
    return tuple(
        jnp.concatenate(values, axis=joined[at]) if at < len(joined) else functools.reduce(jnp.add, values)
        for at, values in enumerate(zip(*outs, strict=True))
    )


def exchange_pairs(n):
    half = n // 2
    first = [(c, 2 * c) if c < half else (c, 2 * (c - half) + 1) for c in range(n)]
    second = [(c, 2 * c + 1) if c < half else (c, 2 * (c - half)) for c in range(n)]
    return first, second


def to_owners(xz, n):
    first, second = exchange_pairs(n)
    c = lax.axis_index("ch")
    width = xz.shape[1] // 2
    left, right = xz[:, :width], xz[:, width:]
    lower = c < n // 2
    one = lax.ppermute(jnp.where(lower, left, right), "ch", first)
    two = lax.ppermute(jnp.where(lower, right, left), "ch", second)
    even = c % 2 == 0
    return jnp.where(even, one, two), jnp.where(even, two, one)


def to_columns(dinner, dgate, n):
    first, second = exchange_pairs(n)
    c = lax.axis_index("ch")
    even = c % 2 == 0
    one = lax.ppermute(jnp.where(even, dinner, dgate), "ch", [(b, a) for a, b in first])
    two = lax.ppermute(jnp.where(even, dgate, dinner), "ch", [(b, a) for a, b in second])
    lower = c < n // 2
    return jnp.concatenate([jnp.where(lower, one, two), jnp.where(lower, two, one)], axis=1)


def on_device(
    n,
    block_input,
    norm_gain,
    in_weight,
    x_weight,
    dt_weight,
    dt_bias,
    conv_weight,
    conv_bias,
    a_log,
    skip_gain,
    out_weight,
    modality,
    cotangent,
):
    mods = in_weight.shape[0]
    length = block_input.shape[0]
    count = n // GROUP
    fast = n == GROUP and lax.axis_size("tok") == 4 and length % 128 == 0
    rows_float = block_input.astype(F32)
    gain = norm_gain.astype(F32)
    inverse = lax.rsqrt(jnp.mean(rows_float * rows_float, axis=-1, keepdims=True) + 1e-05)
    normed = rows_float * inverse
    scaled = (normed * gain[None, :]).astype(BF16)

    token_group = n * length
    if fast:
        every_scaled, _, _, pair_cot, rest_cot, _, every_label, label, label_by_time, label_row, gate, gated_grad, conv, inner_by_time, proj = way_in(
            block_input, norm_gain, cotangent, modality, in_weight, out_weight, conv_weight, conv_bias, x_weight, n, 0
        )
        rest_cot = lax.all_gather(rest_cot, "tok", axis=0, tiled=True)
    else:
        every_label = lax.all_gather(modality, ("tok", "ch"), axis=0, tiled=True)
    if not fast:
        group_label = lax.dynamic_slice_in_dim(every_label, lax.axis_index("tok") * token_group, token_group, 0)
        label = group_label[:, None]
        label_by_time = group_label.reshape(count, GROUP, length).transpose(0, 2, 1).reshape(token_group, 1)
        label_row = label_by_time.reshape(1, token_group)
        group_rows = lax.all_gather(scaled, "ch", axis=0, tiled=True)
        every_scaled = lax.all_gather(scaled, ("tok", "ch"), axis=0, tiled=True)
        every_cot = lax.all_gather(cotangent, ("tok", "ch"), axis=0, tiled=True)
        xz = routed_select(group_rows, label, in_weight, 256, False)
        inner, gate = to_owners(xz, n)
        gate = gate.reshape(count, GROUP, length, -1).swapaxes(1, 2).reshape(gate.shape)
        group_cot = lax.all_gather(cotangent, "ch", axis=0, tiled=True)
        gated_grad = routed_select(group_cot, label, out_weight, 128, True)
        conv, inner_by_time, proj_part = by_groups(
            lambda a, b: conv_forward(a, b, conv_weight, conv_bias, x_weight), count, (inner, label_row), (0, 1), (0, 0, 1)
        )
        proj = lax.psum(proj_part, "ch")

    gated, dgate, dact, dproj_part, ddtw, ddtb, dalog, dskip = by_groups(
        lambda a, b, c, d, e: scan_both(a, b, c, d, e, dt_weight, dt_bias, a_log, skip_gain),
        count,
        (conv, proj, gate, gated_grad, label_by_time),
        (0, 1, 0, 0, 0),
        (0, 0, 0, 1),
    )
    if fast:
        branch_part, every_gated, dinner, dxw, dcw, dcb = middle(
            dproj_part, gated, label, out_weight, conv, inner_by_time, dact, label_by_time, label_row, conv_weight, x_weight, n, 1
        )
    else:
        dproj = lax.psum(dproj_part, "ch")
        dinner, dxw, dcw, dcb = by_groups(
            lambda a, b, c, d, e, f: conv_backward(a, b, c, d, e, f, conv_weight, x_weight),
            count,
            (conv, inner_by_time, dact, dproj, label_by_time, label_row),
            (0, 0, 0, 1, 0, 1),
            (0,),
        )
        branch_part = routed_spread(gated, label, out_weight, 512, False, BF16)
        every_gated = lax.all_gather(gated, "tok", axis=0, tiled=True)
    if not fast:
        every_label = every_label[None, :]
    small = (dxw, ddtw, ddtb, dcw, dcb, dalog, dskip)
    if fast:
        pair_cot = pair_cot.reshape(rest_cot.shape)
        every_grad, row_grad, gain_grad, near_pair, near_rest, grad_part, total, diag_gated = way_back(
            dinner, dgate, in_weight, label, block_input, cotangent, norm_gain, pair_cot, rest_cot, every_scaled, every_label,
            every_gated, small, n, 2,
        )
        fourth = (lax.axis_index("tok") ^ 3) * token_group
        every_gated = lax.dynamic_update_slice_in_dim(every_gated, diag_gated, fourth, 0)
        gain_grad = gain_grad[0]
    else:
        xz_grad = to_columns(dinner, dgate, n)
        scaled_part = routed_spread(xz_grad, label, in_weight, 256, True, BF16)
        scaled_grad = lax.psum_scatter(scaled_part, "ch", scatter_dimension=0, tiled=True).astype(F32)
        gain_grad = lax.psum_scatter(jnp.sum(scaled_grad * normed, axis=0), "ch", scatter_dimension=0, tiled=True)
        ng = scaled_grad * gain[None, :]
        row_grad = cotangent.astype(F32) + inverse * (ng - normed * jnp.mean(ng * normed, axis=-1, keepdims=True))
        every_grad = lax.all_gather(xz_grad, "tok", axis=0, tiled=True)[None]

    if fast:
        branch_part, row_grad = lax.optimization_barrier((branch_part, row_grad))
    branch = lax.psum_scatter(branch_part, "ch", scatter_dimension=0, tiled=True).astype(F32)
    block_out = (rows_float + branch).astype(BF16)
    if fast:
        ch = lax.axis_index("ch")
        split = (4, 2, 2, 2)
        out_weight_grad = weight_grad_parts(
            every_gated.reshape(split + (length, every_gated.shape[1])),
            (pair_cot, near_pair, rest_cot, near_rest),
            every_label.reshape(split + (1, length)),
            jnp.stack([ch // 4, ch % 2]).astype(jnp.int32),
            mods,
            256,
        )
    else:
        out_weight_grad = weight_grad(every_gated, every_cot[None], every_label, mods, 128)
    if fast:
        others = (2 - lax.axis_index("tok") // 2 * 2 + jnp.arange(2)).astype(jnp.int32)
        in_weight_grad = weight_grad_last(every_scaled, every_grad, every_label, grad_part, others, 256)
    else:
        in_weight_grad = weight_grad(every_scaled, every_grad, every_label, mods, 256)
    sums = []
    if fast:
        starts = [start for start, (_, m) in small_places(small) if not m]
        for start, value in zip(starts, small, strict=True):
            size = math.prod(value.shape[:-1])
            sums.append(lax.slice_in_dim(total, start, start + size, axis=0).reshape(value.shape))
    else:
        gain_grad = lax.psum(gain_grad, "tok")
        flat = [value.reshape(-1, value.shape[-1]) for value in small]
        total = lax.psum(jnp.concatenate(flat, axis=0), "tok")
        start = 0
        for value, rows in zip(small, flat, strict=True):
            sums.append(lax.slice_in_dim(total, start, start + rows.shape[0], axis=0).reshape(value.shape))
            start += rows.shape[0]
    dxw, ddtw, ddtb, dcw, dcb, dalog, dskip = sums
    return (
        block_out,
        row_grad,
        gain_grad,
        in_weight_grad,
        dxw,
        ddtw,
        ddtb,
        dcw,
        dcb[0],
        dalog,
        dskip[0],
        out_weight_grad,
    )


def solution(mesh):
    placed = (
        P(("tok", "ch"), None),
        P(),
        P(None, None, "ch"),
        P(None, None, "ch"),
        P(None, None, "ch"),
        P(None, "ch"),
        P(None, "ch"),
        P("ch"),
        P(None, "ch"),
        P("ch"),
        P(None, "ch", None),
        P(("tok", "ch")),
        P(("tok", "ch"), None),
    )
    return jax.shard_map(
        functools.partial(on_device, mesh.shape["ch"]),
        mesh=mesh,
        in_specs=placed,
        out_specs=(
            P(("tok", "ch"), None),
            P(("tok", "ch"), None),
            P("ch"),
            P(None, None, "ch"),
            P(None, None, "ch"),
            P(None, None, "ch"),
            P(None, "ch"),
            P(None, "ch"),
            P("ch"),
            P(None, "ch"),
            P("ch"),
            P(None, "ch", None),
        ),
        check_vma=False,
    )
```
